128 devices in a mesh: sect: 2 (over x_lo), rr: 8 (over x_hi, y), row: 8 (over z, core).
Axes of the slice: x: 4 (x_hi: 2, x_lo: 2; x = x_hi * 2 + x_lo), y: 4, z: 4, core: 2. Of those that a mesh axis runs over, the one named last changes fastest.
Arguments:
- packet: float32 [2, 512, 256, 512], P('sect', 'rr', 'row'), may hold values from -6 to 6
- previous: float32 [2, 512, 256, 512], P('sect', 'rr', 'row'), may hold values from -6 to 6
- potential: float32 [2, 512, 256, 512], P('sect', 'rr', 'row'), may hold values from 0 to 4
- rotation: float32 [2, 512, 256], P('sect', 'rr', 'row'), may hold values from 0.1 to 1
- angular: float32 [2, 512, 512], P('sect'), as said below
- damping: float32 [2, 512, 256], P('sect', 'rr', 'row'), may hold values from 0.3 to 0.9
- absorber: int32 [2, 512, 256], P('sect', 'rr', 'row'), may hold values from 0 to 1, as said below
- stencil_index: int32 [4, 512, 256], P(None, 'rr', 'row'), may hold values from 0 to 511
- stencil_weight: float32 [4, 512, 256], P(None, 'rr', 'row'), may hold values from -3 to 3
Outputs:
- latest: float32 [2, 512, 256, 512], P('sect', 'rr', 'row')
- earlier: float32 [2, 512, 256, 512], P('sect', 'rr', 'row')
The draws below stay inside these ranges and needn't reach their ends.
Inputs may be any that keep to these rules, and one draw needn't show every extreme that they name: `absorber`: zero at every point whose R index is below 510. `angular`: symmetric.
All inputs are finite; a program needn't handle non-finite values.
Results may differ from the reference program's by a relative error of at most 0.0001.
Values sent between devices are 32-bit elements; how exact they have to be, the bound alone decides.
No kernel may reach another device: no remote copies, remote signals or barrier semaphores. Data moves between devices by JAX's collectives and lax.ppermute only.
A program may use at most 128 MiB of HBM per device.

```python
import math
import jax
import jax.numpy as jnp
from jax import lax

NA = 512
BAND = 2
ITERS = 2
NR = 512
NV = 256


def draw_angular(key, part):
    key = jax.random.fold_in(key, 11)
    key_off, key_diag = jax.random.split(key)
    raw = jax.random.normal(key_off, (2, NA, NA), jnp.float32)
    symmetric = (raw + jnp.swapaxes(raw, 1, 2)) * 0.5 * NA ** (-0.5)
    diagonal = jnp.exp(jax.random.uniform(key_diag, (2, NA), jnp.float32, 0.0, 1.3862944))
    eye = jnp.eye(NA, dtype=jnp.float32)
    return symmetric + diagonal[:, :, None] * eye[None]


def draw_absorber(key, part):
    key = jax.random.fold_in(key, 23)
    flags = jax.random.randint(key, (2, NR, NV), 0, 2)
    inside = (jnp.arange(NR) >= NR - BAND).astype(jnp.int32)
    return (flags * inside[None, :, None]).astype(jnp.int32)


def with_ends(values, key, least, high):
    longest = values.shape.index(max(values.shape))
    spots = []
    for shift in (0, 1):
        where = [jax.random.randint(jax.random.fold_in(key, axis), (), 0, length) for axis, length in enumerate(values.shape)]
        where[longest] = (where[longest] + shift) % values.shape[longest]
        spots.append(tuple(where))
    return values.at[spots[0]].set(least).at[spots[1]].set(high)


def steps_of(own_key, shape, cuts, low, high):
    loudness = 1.0
    for dim, blocks in cuts:
        heights = jax.random.uniform(jax.random.fold_in(jax.random.fold_in(own_key, 6), dim), (blocks,), jnp.float32, low / len(cuts), high / len(cuts))
        loudness = loudness * jnp.repeat(jnp.exp(heights), shape[dim] // blocks).reshape((-1,) + (1,) * (len(shape) - 1 - dim))
    return loudness


def noise(stream_key, shape, spread, reach, shards=(), kind=jnp.bfloat16):
    array = spread * jax.random.normal(stream_key, shape, jnp.float32)
    if shards:
        array = array * steps_of(stream_key, shape, shards, -0.22, 0.18)
    return jnp.clip(array, -reach, reach).astype(kind)


def setup_inputs(seed: int = 0) -> dict:
    streams_of = jax.random.split(jax.random.key(seed), 10)
    packet = noise(streams_of[0], (2, NR, NV, NA), 1.0, 6.0, ((0, 2), (1, 8), (2, 8)), jnp.float32)
    previous = noise(streams_of[1], (2, NR, NV, NA), 1.0, 6.0, ((0, 2), (1, 8), (2, 8)), jnp.float32)
    potential = jnp.clip(4.0 * jax.random.uniform(streams_of[2], (2, NR, NV, NA), jnp.float32) ** steps_of(streams_of[2], (2, NR, NV, NA), ((0, 2), (1, 8), (2, 8)), -0.2, 0.2), 0.0, 4.0)
    rotation = jnp.clip(jnp.exp(math.log(1.0) - 2.3025851 * jax.random.uniform(streams_of[3], (2, NR, NV), jnp.float32) ** steps_of(streams_of[3], (2, NR, NV), ((0, 2), (1, 8), (2, 8)), -0.2, 0.2)), 0.1, 1.0)
    angular = draw_angular(jax.random.fold_in(streams_of[9], 71), 0)
    damping = jnp.clip(0.3 + 0.59999996 * jax.random.uniform(streams_of[5], (2, NR, NV), jnp.float32) ** steps_of(streams_of[5], (2, NR, NV), ((0, 2), (1, 8), (2, 8)), -0.2, 0.2), 0.3, 0.9)
    absorber = draw_absorber(jax.random.fold_in(streams_of[9], 71), 0)
    stencil_index = with_ends(jax.random.randint(streams_of[7], (4, NR, NV), 0, NV * BAND), jax.random.fold_in(streams_of[7], 1), 0, (NV * BAND) - 1).astype(jnp.int32)
    stencil_weight = noise(streams_of[8], (4, NR, NV), 0.5, 3.0, ((1, 8), (2, 8)), jnp.float32)
    return dict(packet=packet, previous=previous, potential=potential, rotation=rotation, angular=angular, damping=damping, absorber=absorber, stencil_index=stencil_index, stencil_weight=stencil_weight)


kinetic_radial = 0.5
kinetic_vibration = 0.5
energy_middle = 7.5
energy_half = 8.0


def curvature(padded, count, axis):
    parts = [lax.slice_in_dim(padded, k, k + count, axis=axis) for k in range(5)]
    return (-parts[0] + 16.0 * parts[1] - 30.0 * parts[2] + 16.0 * parts[3] - parts[4]) / 12.0


def scaled_hamilton(field, rotation, angular, potential):
    count_r = field.shape[0]
    count_v = field.shape[1]
    width = field.shape[2]
    padded = jnp.pad(field, ((2, 2), (2, 2), (0, 0)))
    radial = curvature(padded[:, 2:-2], count_r, 0)
    vibration = curvature(padded[2:-2], count_v, 1)
    turned = jnp.dot(field.reshape(-1, width), angular, precision=lax.Precision.HIGHEST).reshape(field.shape)
    energy = -kinetic_radial * radial - kinetic_vibration * vibration + rotation[:, :, None] * turned + potential * field
    return (energy - energy_middle * field) / energy_half


def reference(packet, previous, potential, rotation, angular, damping, absorber, stencil_index, stencil_weight):
    retained = 1.0 - absorber.astype(jnp.float32) * (1.0 - damping)
    current = [packet[0], packet[1]]
    earlier = [previous[0], previous[1]]
    for iteration in range(ITERS):
        updates = []
        for section in range(2):
            scaled = scaled_hamilton(current[section], rotation[section], angular[section], potential[section])
            updates.append(2.0 * scaled - retained[section][:, :, None] * earlier[section])
        leaving = (1.0 - retained[0][:, :, None]) * updates[0]
        band_table = jnp.transpose(leaving[NR - BAND:], (1, 0, 2)).reshape(NV * BAND, NA)
        source = jnp.zeros((NR, NV, NA), jnp.float32)
        for stencil in range(4):
            picked = jnp.take(band_table, stencil_index[stencil].reshape(-1), axis=0).reshape(NR, NV, NA)
            source = source + stencil_weight[stencil][:, :, None] * picked
        advanced = [retained[0][:, :, None] * updates[0], retained[1][:, :, None] * updates[1] + source]
        earlier = current
        current = advanced
    return jnp.stack(current), jnp.stack(earlier)
```

```python
import functools

import jax
import jax.numpy as jnp
from jax import lax
from jax.experimental import pallas as pl
from jax.experimental.pallas import tpu as pltpu
from jax.sharding import PartitionSpec as P

BAND = 2
STENCILS = 4
HALO = 2
LANES = 128
CHUNK = 8
FAR = 2
POINT = 16
ROT, RET, POS, WEIGHT = 0, 1, 2, 6
MIB = 1 << 20
F32 = jnp.float32
BF16 = jnp.bfloat16

SIDE1 = -16.0 / 96.0
SIDE2 = 1.0 / 96.0
MIDDLE = 2.0 * 30.0 / 96.0 - 7.5 / 4.0


def halves(value):
    high = value.astype(BF16)
    low = (value - high.astype(F32)).astype(BF16)
    return high, low


def product(left, right_high, right_low):
    high, low = left
    total = jnp.dot(high, right_high, preferred_element_type=F32)
    total += jnp.dot(low, right_high, preferred_element_type=F32)
    return total + jnp.dot(high, right_low, preferred_element_type=F32)


def doubled_hamilton(field, index, start, count, lanes, turned, potential, rotation):
    def at(shift_r, shift_v):
        return field[index + shift_r, pl.ds(start + shift_v, count), lanes]

    middle = at(0, 0)
    near = at(-1, 0) + at(1, 0) + (at(0, -1) + at(0, 1))
    far = at(-2, 0) + at(2, 0) + (at(0, -2) + at(0, 2))
    return (
        SIDE1 * near
        + SIDE2 * far
        + (0.25 * potential + MIDDLE) * middle
        + (0.25 * rotation) * turned
    )


def split_kernel(matrix, high, low):
    high[...], low[...] = halves(matrix[...])


def split(matrix):
    return pl.pallas_call(
        split_kernel,
        out_shape=[jax.ShapeDtypeStruct(matrix.shape, BF16)] * 2,
        name="split_angular",
    )(matrix)


def band_kernel(
    flag, packet, previous, potential, points, left, right, high, low, out, field, later, turned
):
    width = packet.shape[2]
    rows = packet.shape[1]
    base = 16
    wide = rows + 16

    @pl.when(flag[0] == 1)
    def _():
        field[...] = jnp.zeros_like(field)
        later[...] = jnp.zeros_like(later)
        for k in range(2, 8):
            field[k, base : base + rows] = packet[k]
        for k in range(4):
            field[4 + k, base - 4 : base] = left[4 * k : 4 * k + 4]
            field[4 + k, base + rows : base + rows + 4] = right[4 * k : 4 * k + 4]
        window = field[4:8, base - 8 : base + rows + 8].reshape(4 * wide, width)
        turned[...] = product(halves(window), high[...], low[...])
        for k in range(4):
            own = points[(4 + k) * rows : (5 + k) * rows]
            rotation = own[:, ROT : ROT + 1]
            retained = own[:, RET : RET + 1]
            for at in range(0, width, LANES):
                lanes = slice(at, at + LANES)
                update = doubled_hamilton(
                    field, 4 + k, base, rows, lanes,
                    turned[k * wide + 8 : k * wide + 8 + rows, lanes], potential[4 + k, :, lanes], rotation,
                ) - retained * previous[4 + k, :, lanes]
                later[k, base : base + rows, lanes] = retained * update
                if k >= 2:
                    out[(k - 2) * rows : (k - 1) * rows, lanes] = (1.0 - retained) * update
        for k in range(2, 4):
            for slab, place, inside in ((left, base - 8, 6), (right, base + rows, 0)):
                at = 16 + 2 * (k - 2)
                prev, pot, rot, ret = (slab[at + 4 * n : at + 4 * n + 2] for n in range(4))
                update = doubled_hamilton(
                    field, 4 + k, place + inside, 2, slice(None),
                    turned[k * wide + place - base + 8 + inside : k * wide + place - base + 10 + inside], pot, rot,
                ) - ret * prev
                later[k, place + inside : place + inside + 2] = ret * update
        window = later[2:4, base : base + rows].reshape(2 * rows, width)
        turned[0 : 2 * rows] = product(halves(window), high[...], low[...])
        for k in range(2, 4):
            own = points[(4 + k) * rows : (5 + k) * rows]
            rotation = own[:, ROT : ROT + 1]
            retained = own[:, RET : RET + 1]
            for at in range(0, width, LANES):
                lanes = slice(at, at + LANES)
                update = doubled_hamilton(
                    later, k, base, rows, lanes,
                    turned[(k - 2) * rows : (k - 1) * rows, lanes], potential[4 + k, :, lanes], rotation,
                ) - retained * field[4 + k, base : base + rows, lanes]
                out[k * rows : (k + 1) * rows, lanes] = (1.0 - retained) * update

    @pl.when(flag[0] == 0)
    def _():
        out[...] = jnp.zeros_like(out)


def bands(flag, packet, previous, potential, points, left, right, high, low):
    count_r, count_v, width = packet.shape
    last = count_r // CHUNK - 1
    block = pl.BlockSpec((CHUNK, count_v, width), lambda i: (last, 0, 0))

    def whole(shape):
        return pl.BlockSpec(shape, lambda i: (0,) * len(shape))

    rows = 2 * BAND * count_v
    return pl.pallas_call(
        band_kernel,
        grid=(1,),
        in_specs=[
            pl.BlockSpec(memory_space=pltpu.SMEM),
            block, block, block,
            pl.BlockSpec((CHUNK * count_v, POINT), lambda i: (last, 0)),
            whole(left.shape), whole(right.shape), whole(high.shape), whole(low.shape),
        ],
        out_specs=whole((rows, width)),
        out_shape=jax.ShapeDtypeStruct((rows, width), F32),
        scratch_shapes=[
            pltpu.VMEM((CHUNK + 2, count_v + 32, width), F32),
            pltpu.VMEM((6, count_v + 32, width), F32),
            pltpu.VMEM((4 * (count_v + 16), width), F32),
        ],
        compiler_params=pltpu.CompilerParams(vmem_limit_bytes=48 * MIB),
        cost_estimate=pl.CostEstimate(flops=400_000_000, bytes_accessed=6 * MIB, transcendentals=0),
        name="both_bands",
    )(flag, packet, previous, potential, points, left, right, high, low)


def first_kernel(
    packet, before, after, previous, potential, points, up, down, left, right, high, low, out, field, turned
):
    step = pl.program_id(0)
    steps = pl.num_programs(0)
    count, rows, width = packet.shape
    base = 8
    field[HALO : HALO + count, base : base + rows] = packet[...]
    field[0:HALO, base : base + rows] = jnp.where(step == 0, up[...].reshape(before.shape), before[...])
    field[HALO + count :, base : base + rows] = jnp.where(step == steps - 1, down[...].reshape(after.shape), after[...])
    start = pl.multiple_of(step * (HALO * count), HALO * count)
    sides = (left[pl.ds(start, HALO * count)], right[pl.ds(start, HALO * count)])
    for k in range(count):
        field[HALO + k, base - HALO : base] = sides[0][HALO * k : HALO * (k + 1)]
        field[HALO + k, base + rows : base + rows + HALO] = sides[1][HALO * k : HALO * (k + 1)]
    turned[...] = product(halves(packet[...].reshape(count * rows, width)), high[...], low[...])
    for k in range(count):
        own = points[k * rows : (k + 1) * rows]
        rotation = own[:, ROT : ROT + 1]
        retained = own[:, RET : RET + 1]
        for at in range(0, width, LANES):
            lanes = slice(at, at + LANES)
            update = doubled_hamilton(
                field, HALO + k, base, rows, lanes,
                turned[k * rows : (k + 1) * rows, lanes], potential[k, :, lanes], rotation,
            ) - retained * previous[k, :, lanes]
            out[k, :, lanes] = retained * update


def first(packet, previous, potential, points, halos, high, low):
    count_r, count_v, width = packet.shape
    per = CHUNK // HALO
    steps = count_r // CHUNK
    block = pl.BlockSpec((CHUNK, count_v, width), lambda i: (i, 0, 0))
    edge = (HALO, count_v, width)

    def whole(shape):
        return pl.BlockSpec(shape, lambda i: (0,) * len(shape))

    up, down, left, right = halos
    return pl.pallas_call(
        first_kernel,
        grid=(steps,),
        in_specs=[
            block,
            pl.BlockSpec(edge, lambda i: (jnp.maximum(i * per - 1, 0), 0, 0)),
            pl.BlockSpec(edge, lambda i: (jnp.minimum((i + 1) * per, steps * per - 1), 0, 0)),
            block, block,
            pl.BlockSpec((CHUNK * count_v, POINT), lambda i: (i, 0)),
            whole(up.shape), whole(down.shape), whole(left.shape), whole(right.shape),
            whole(high.shape), whole(low.shape),
        ],
        out_specs=block,
        out_shape=jax.ShapeDtypeStruct(packet.shape, F32),
        scratch_shapes=[
            pltpu.VMEM((CHUNK + 2 * HALO, count_v + 16, width), F32),
            pltpu.VMEM((CHUNK * count_v, width), F32),
        ],
        compiler_params=pltpu.CompilerParams(vmem_limit_bytes=48 * MIB),
        cost_estimate=pl.CostEstimate(flops=7_000_000_000, bytes_accessed=20 * MIB, transcendentals=0),
        name="first_iteration",
    )(packet, packet, packet, previous, potential, points, up, down, left, right, high, low)


def stencil_kernel(points, high, low):
    rows = points.shape[0]
    width = high.shape[1]
    columns = lax.broadcasted_iota(jnp.int32, (rows, width), 1).astype(F32)
    total = jnp.zeros((rows, width), F32)
    for n in range(STENCILS):
        place = points[:, POS + n : POS + n + 1]
        weight = points[:, WEIGHT + n : WEIGHT + n + 1]
        total += jnp.where(columns == place, weight, 0.0)
    high[...], low[...] = halves(total)


def stencil_matrix(points, width):
    rows = points.shape[0]
    tile = 128
    out = pl.BlockSpec((tile, width), lambda i: (i, 0))
    return pl.pallas_call(
        stencil_kernel,
        grid=(rows // tile,),
        in_specs=[pl.BlockSpec((tile, POINT), lambda i: (i, 0))],
        out_specs=[out, out],
        out_shape=[jax.ShapeDtypeStruct((rows, width), BF16)] * 2,
        cost_estimate=pl.CostEstimate(flops=12_000_000, bytes_accessed=6 * MIB, transcendentals=0),
        name="stencil_matrix",
    )(points)


def last_kernel(
    flag, first_packet, packet, potential, points, up, down, left, right,
    high, low, stencil_high, stencil_low, edge_high, edge_low, own_table, other_table,
    earlier, latest, field, turned, table,
):
    step = pl.program_id(0)
    steps = pl.num_programs(0) // 2
    count, rows, width = packet.shape
    base = 8
    count_r = steps * count
    is_product = flag[0] == 1
    quarter = own_table.shape[1]
    half = quarter // 2
    pieces = own_table.shape[0]

    @pl.when((step == 0) & is_product)
    def _():
        for side, ref in enumerate((own_table, other_table)):
            for k in range(pieces):
                at = (side * pieces + k) * half
                for band in range(2):
                    upper, lower = halves(ref[k, band * half : (band + 1) * half])
                    table[2 * band, at : at + half] = upper
                    table[2 * band + 1, at : at + half] = lower

    @pl.when(step < steps)
    def _():
        here = pl.multiple_of(step * count, count)

        @pl.when(is_product)
        def _():
            turned[...] = product((stencil_high[...], stencil_low[...]), table[0], table[1])
            for k in range(count):
                value = first_packet[k] + turned[k * rows : (k + 1) * rows]
                field[HALO + here + k, base : base + rows] = value
                earlier[k] = value

        @pl.when(jnp.logical_not(is_product))
        def _():
            field[pl.ds(HALO + here, count), base : base + rows] = first_packet[...]
            earlier[...] = first_packet[...]

    @pl.when(step == 0)
    def _():
        edges = HALO * rows
        sides = HALO * count_r

        def put(up_value, down_value, left_value, right_value):
            for k in range(HALO):
                field[k, base : base + rows] = up_value[k * rows : (k + 1) * rows]
                field[HALO + count_r + k, base : base + rows] = down_value[k * rows : (k + 1) * rows]
            for k in range(count_r):
                field[HALO + k, base - HALO : base] = left_value[HALO * k : HALO * (k + 1)]
                field[HALO + k, base + rows : base + rows + HALO] = right_value[HALO * k : HALO * (k + 1)]

        @pl.when(is_product)
        def _():
            source = product((edge_high[...], edge_low[...]), table[0], table[1])
            put(
                up[...] + source[:edges],
                down[...] + source[edges : 2 * edges],
                left[...] + source[2 * edges : 2 * edges + sides],
                right[...] + source[2 * edges + sides :],
            )

        @pl.when(jnp.logical_not(is_product))
        def _():
            put(up[...], down[...], left[...], right[...])

    @pl.when(step >= steps)
    def _():
        here = pl.multiple_of((step - steps) * count, count)
        window = field[pl.ds(HALO + here, count), base : base + rows].reshape(count * rows, width)
        turned[...] = product(halves(window), high[...], low[...])

        for k in range(count):
            own = points[k * rows : (k + 1) * rows]
            rotation = own[:, ROT : ROT + 1]
            retained = own[:, RET : RET + 1]
            for at in range(0, width, LANES):
                lanes = slice(at, at + LANES)
                update = doubled_hamilton(
                    field, HALO + here + k, base, rows, lanes,
                    turned[k * rows : (k + 1) * rows, lanes], potential[k, :, lanes], rotation,
                ) - retained * packet[k, :, lanes]
                latest[k, :, lanes] = retained * update

        @pl.when(is_product)
        def _():
            turned[...] = product((stencil_high[...], stencil_low[...]), table[2], table[3])
            for k in range(count):
                latest[k] += turned[k * rows : (k + 1) * rows]


def last(flag, first_packet, packet, potential, points, halos, high, low, matrix, edges, tables):
    count_r, count_v, width = packet.shape
    steps = count_r // CHUNK

    def early(i):
        return jnp.minimum(i, steps - 1)

    def late(i):
        return jnp.maximum(i - steps, 0)

    def block(where):
        return pl.BlockSpec((CHUNK, count_v, width), lambda i: (where(i), 0, 0))

    def whole(shape):
        return pl.BlockSpec(shape, lambda i: (0,) * len(shape))

    rows = CHUNK * count_v
    stencil = pl.BlockSpec((rows, matrix[0].shape[1]), lambda i: (i % steps, 0))
    return pl.pallas_call(
        last_kernel,
        grid=(2 * steps,),
        in_specs=[
            pl.BlockSpec(memory_space=pltpu.SMEM),
            block(early), block(late), block(late),
            pl.BlockSpec((rows, POINT), lambda i: (late(i), 0)),
            *[whole(halo.shape) for halo in halos],
            whole(high.shape), whole(low.shape), stencil, stencil,
            *[whole(edge.shape) for edge in edges],
            *[whole(table.shape) for table in tables],
        ],
        out_specs=[block(early), block(late)],
        out_shape=[jax.ShapeDtypeStruct(packet.shape, F32)] * 2,
        scratch_shapes=[
            pltpu.VMEM((count_r + 2 * HALO, count_v + 16, width), F32),
            pltpu.VMEM((rows, width), F32),
            pltpu.VMEM((4, matrix[0].shape[1], width), BF16),
        ],
        compiler_params=pltpu.CompilerParams(vmem_limit_bytes=56 * MIB),
        cost_estimate=pl.CostEstimate(flops=20_000_000_000, bytes_accessed=36 * MIB, transcendentals=0),
        name="last_iteration",
    )(flag, first_packet, packet, potential, points, *halos, high, low, *matrix, *edges, *tables)


def neighbours(axis, upward, downward):
    count = lax.axis_size(axis)
    return (
        lax.ppermute(upward, axis, [(i, i + 1) for i in range(count - 1)]),
        lax.ppermute(downward, axis, [(i + 1, i) for i in range(count - 1)]),
    )


def exchange(edges):
    top, bottom, first_columns, last_columns = edges
    left, right = neighbours("row", last_columns, first_columns)
    up, down = neighbours("rr", bottom, top)
    return up, down, left, right


def edges_of(field):
    width = field.shape[-1]
    return (
        field[:HALO].reshape(-1, width),
        field[-HALO:].reshape(-1, width),
        field[:, :HALO].reshape(-1, width),
        field[:, -HALO:].reshape(-1, width),
    )


def with_points(slab, values):
    width = slab.shape[-1]
    rows = values.reshape(-1, width)
    return jnp.concatenate([slab, jnp.pad(rows, ((0, -rows.shape[0] % 8), (0, 0)))], axis=0)


def local(packet, previous, potential, rotation, angular, damping, absorber, stencil_index, stencil_weight):
    packet, previous, potential = packet[0], previous[0], potential[0]
    rotation, angular = rotation[0], angular[0]
    count_r, count_v, width = packet.shape
    retained = 1.0 - absorber[0].astype(F32) * (1.0 - damping[0])
    sect = lax.axis_index("sect")
    rr = lax.axis_index("rr")
    row = lax.axis_index("row")
    sections, count_rr, count_row = (lax.axis_size(name) for name in ("sect", "rr", "row"))
    cores = 2
    chips = count_row // cores
    is_source = ((sect == 0) & (rr == count_rr - 1)).astype(jnp.int32)[None]
    is_product = (sect == 1).astype(jnp.int32)[None]

    def band_slab(far, near):
        spread = jnp.concatenate(
            [value[-BAND:, near].reshape(-1, 1) for value in (rotation, retained)], axis=0
        )
        return jnp.concatenate(
            [
                packet[-2 * BAND :, far].reshape(-1, width),
                previous[-BAND:, near].reshape(-1, width),
                potential[-BAND:, near].reshape(-1, width),
                jnp.broadcast_to(spread, (spread.shape[0], width)),
            ],
            axis=0,
        )

    firsts = band_slab(slice(0, 4), slice(0, 2))
    lasts = band_slab(slice(-4, None), slice(-2, None))
    sources = (count_rr - 1) * count_row
    axes = ("sect", "rr", "row")
    band_left = lax.ppermute(lasts, axes, [(sources + i, sources + i + 1) for i in range(count_row - 1)])
    band_right = lax.ppermute(firsts, axes, [(sources + i + 1, sources + i) for i in range(count_row - 1)])

    high, low = split(angular)
    index = stencil_index
    per = count_v * BAND
    owner = index // per
    inside = index % per
    slot = (
        ((owner + row) % cores) * chips + (row // cores - owner // cores) % chips
    ) * per + (inside % BAND) * count_v + inside // BAND
    table_points = jnp.concatenate([slot.astype(F32), stencil_weight], axis=0)
    canonical = jnp.concatenate([index.astype(F32), stencil_weight], axis=0)
    points = jnp.concatenate([rotation[None], retained[None], table_points], axis=0)
    points = jnp.pad(points, ((0, POINT - points.shape[0]), (0, 0), (0, 0)))
    points = jnp.transpose(points, (1, 2, 0)).reshape(count_r * count_v, POINT)

    table = bands(is_source, packet, previous, potential, points, band_left, band_right, high, low)

    plane = ("sect", "rr")
    half = count_rr // FAR
    start = count_rr - 1
    entries = [count_rr + (k + 1) * half - 1 for k in range(FAR)]
    piece = sum(lax.ppermute(table, plane, [(start, entry)]) for entry in entries)
    spread = piece
    for shift in (1, half - 1, 2):
        spread = spread + lax.ppermute(
            piece, plane, [(entry, entry - (half - 1) + (half - 1 + shift) % half) for entry in entries]
        )
    line = ("sect", "row")

    def around(shift):
        pairs = []
        for chip in range(chips):
            for core in range(cores):
                pairs.append(
                    (count_row + chip * cores + core, count_row + ((chip + shift) % chips) * cores + core)
                )
        return lax.ppermute(spread, line, pairs)

    own = jnp.stack([spread, around(1), around(2), around(3)], axis=0)
    other = lax.ppermute(
        own, line, [(count_row + i, count_row + i + 1 - 2 * (i % cores)) for i in range(count_row)]
    )

    cut = edges_of(packet)
    cut_points = (canonical[:, :HALO], canonical[:, -HALO:], canonical[:, :, :HALO], canonical[:, :, -HALO:])
    cut_points = [jnp.transpose(value, (1, 2, 0)) for value in cut_points]
    halos = exchange([with_points(slab, value) for slab, value in zip(cut, cut_points)])
    lengths = [slab.shape[0] for slab in cut]
    one = first(packet, previous, potential, points, [h[:n] for h, n in zip(halos, lengths)], high, low)
    later = exchange(edges_of(one))

    edge_points = jnp.concatenate(
        [h[n : n + n * 8 // width].reshape(n, 8) for h, n in zip(halos, lengths)], axis=0
    )
    edge_index = edge_points[:, :STENCILS].astype(jnp.int32)
    edge_owner = edge_index // per
    edge_inside = edge_index % per
    edge_slot = (
        ((edge_owner + row) % cores) * chips + (row // cores - edge_owner // cores) % chips
    ) * per + (edge_inside % BAND) * count_v + edge_inside // BAND
    edge_points = jnp.concatenate([edge_slot.astype(F32), edge_points[:, STENCILS:]], axis=1)
    edge_points = jnp.pad(edge_points, ((0, 0), (POS, POINT - POS - 2 * STENCILS)))
    columns = count_row * per
    matrix = stencil_matrix(points, columns)
    edge_matrix = stencil_matrix(edge_points, columns)

    earlier, latest = last(
        is_product, one, packet, potential, points, later, high, low, matrix, edge_matrix, (own, other)
    )
    return latest[None], earlier[None]


def solution(mesh):
    in_specs = (
        P("sect", "rr", "row", None),
        P("sect", "rr", "row", None),
        P("sect", "rr", "row", None),
        P("sect", "rr", "row"),
        P("sect", None, None),
        P("sect", "rr", "row"),
        P("sect", "rr", "row"),
        P(None, "rr", "row"),
        P(None, "rr", "row"),
    )
    out_specs = (P("sect", "rr", "row", None), P("sect", "rr", "row", None))
    return jax.shard_map(local, mesh=mesh, in_specs=in_specs, out_specs=out_specs, check_vma=False)
```

```python
import functools

import jax
import jax.numpy as jnp
from jax import lax
from jax.experimental import pallas as pl
from jax.experimental.pallas import tpu as pltpu
from jax.sharding import PartitionSpec as P

BAND = 2
STENCILS = 4
HALO = 2
LANES = 128
CHUNK = 16
LAST = 8
CORES = 2
FAR = 2
SOURCE, PRODUCT, CORE, CHIP = range(4)
ROT, RET, INDEX, WEIGHT, TABLES = 0, 1, 2, 6, 10
EXTRA = 2 * STENCILS * HALO
MIB = 1 << 20
F32 = jnp.float32
BF16 = jnp.bfloat16
ANY = pl.BlockSpec(memory_space=pl.ANY)
SMEM = pl.BlockSpec(memory_space=pltpu.SMEM)
VMEM = pl.BlockSpec(memory_space=pltpu.VMEM)

SIDE1 = -16.0 / 96.0
SIDE2 = 1.0 / 96.0
MIDDLE = 2.0 * 30.0 / 96.0 - 7.5 / 4.0


def halves(value):
    high = value.astype(BF16)
    low = (value - high.astype(F32)).astype(BF16)
    return high, low


def product(left, right_high, right_low):
    high, low = left
    total = jnp.dot(high, right_high, preferred_element_type=F32)
    total += jnp.dot(low, right_high, preferred_element_type=F32)
    return total + jnp.dot(high, right_low, preferred_element_type=F32)


def doubled_hamilton(field, index, start, count, lanes, turned, potential, rotation):
    def at(shift_r, shift_v):
        return field[index + shift_r, pl.ds(start + shift_v, count), lanes]

    middle = at(0, 0)
    near = at(-1, 0) + at(1, 0) + (at(0, -1) + at(0, 1))
    far = at(-2, 0) + at(2, 0) + (at(0, -2) + at(0, 2))
    return (
        SIDE1 * near
        + SIDE2 * far
        + (0.25 * potential + MIDDLE) * middle
        + (0.25 * rotation) * turned
    )


def retained_of(damping, absorber):
    return 1.0 - absorber.astype(F32) * (1.0 - damping)


def band_slab_kernel(where, rotation, damping, absorber, packet, previous, potential, firsts, lasts, held, sems):
    count_r, rows, width = packet.shape

    @pl.when(where[SOURCE] == 1)
    def _():
        copies = [
            pltpu.make_async_copy(ref.at[pl.ds(count_r - 4, 4)], held.at[n], sems.at[n])
            for n, ref in enumerate((packet, previous, potential))
        ]
        for copy in copies:
            copy.start()
        for out, near in ((firsts, 0), (lasts, rows - 2)):
            for k in range(BAND):
                for r in range(2):
                    at = (count_r - BAND + k, near + r)
                    ret = retained_of(damping[at], absorber[at])
                    out[24 + 2 * k + r : 25 + 2 * k + r] = jnp.full((1, width), rotation[at], F32)
                    out[28 + 2 * k + r : 29 + 2 * k + r] = jnp.full((1, width), ret, F32)
        for copy in copies:
            copy.wait()
        for out, far, near in ((firsts, 0, 0), (lasts, rows - 4, rows - 2)):
            for k in range(4):
                out[4 * k : 4 * k + 4] = held[0, k, far : far + 4]
            for k in range(BAND):
                out[16 + 2 * k : 18 + 2 * k] = held[1, 2 + k, near : near + 2]
                out[20 + 2 * k : 22 + 2 * k] = held[2, 2 + k, near : near + 2]


def band_slabs(where, rotation, damping, absorber, packet, previous, potential):
    _, rows, width = packet.shape
    return pl.pallas_call(
        band_slab_kernel,
        in_specs=[SMEM, SMEM, SMEM, SMEM, ANY, ANY, ANY],
        out_specs=[VMEM, VMEM],
        out_shape=[jax.ShapeDtypeStruct((32, width), F32)] * 2,
        scratch_shapes=[pltpu.VMEM((3, 4, rows, width), F32), pltpu.SemaphoreType.DMA((3,))],
        name="band_slabs",
    )(where, rotation, damping, absorber, packet, previous, potential)


def band_kernel(
    where, packet, previous, potential, tables, left, right, high, low, out, field, later, turned, held, sems
):
    count_r, rows, width = packet.shape
    base = 16
    wide = rows + 16

    @pl.when(where[SOURCE] == 1)
    def _():
        copies = [
            pltpu.make_async_copy(packet.at[pl.ds(count_r - 6, 6)], field.at[pl.ds(2, 6), pl.ds(base, rows)], sems.at[0]),
            pltpu.make_async_copy(previous.at[pl.ds(count_r - 4, 4)], held.at[0], sems.at[1]),
            pltpu.make_async_copy(potential.at[pl.ds(count_r - 4, 4)], held.at[1], sems.at[2]),
        ]
        later[...] = jnp.zeros_like(later)
        field[0:2] = jnp.zeros_like(field[0:2])
        field[8:10] = jnp.zeros_like(field[8:10])
        for k in range(2, 8):
            field[k, 0:base] = jnp.zeros((base, width), F32)
            field[k, base + rows :] = jnp.zeros((base, width), F32)
        for copy in copies:
            copy.start()
        for k in range(4):
            field[4 + k, base - 4 : base] = left[4 * k : 4 * k + 4]
            field[4 + k, base + rows : base + rows + 4] = right[4 * k : 4 * k + 4]
        columns = [
            (tables[ROT, :, count_r - 4 + k : count_r - 3 + k], tables[RET, :, count_r - 4 + k : count_r - 3 + k])
            for k in range(4)
        ]
        columns = [tuple(jnp.broadcast_to(c, (rows, LANES)) for c in pair) for pair in columns]
        for copy in copies:
            copy.wait()
        window = field[4:8, base - 8 : base + rows + 8].reshape(4 * wide, width)
        turned[...] = product(halves(window), high[...], low[...])
        for k in range(4):
            rotation, retained = columns[k]
            for at in range(0, width, LANES):
                lanes = slice(at, at + LANES)
                update = doubled_hamilton(
                    field, 4 + k, base, rows, lanes,
                    turned[k * wide + 8 : k * wide + 8 + rows, lanes], held[1, k, :, lanes], rotation,
                ) - retained * held[0, k, :, lanes]
                later[k, base : base + rows, lanes] = retained * update
                if k >= 2:
                    out[(k - 2) * rows : (k - 1) * rows, lanes] = (1.0 - retained) * update
        for k in range(2, 4):
            for slab, place, inside in ((left, base - 8, 6), (right, base + rows, 0)):
                at = 16 + 2 * (k - 2)
                prev, pot, rot, ret = (slab[at + 4 * n : at + 4 * n + 2] for n in range(4))
                update = doubled_hamilton(
                    field, 4 + k, place + inside, 2, slice(None),
                    turned[k * wide + place - base + 8 + inside : k * wide + place - base + 10 + inside], pot, rot,
                ) - ret * prev
                later[k, place + inside : place + inside + 2] = ret * update
        window = later[2:4, base : base + rows].reshape(2 * rows, width)
        turned[0 : 2 * rows] = product(halves(window), high[...], low[...])
        for k in range(2, 4):
            rotation, retained = columns[k]
            for at in range(0, width, LANES):
                lanes = slice(at, at + LANES)
                update = doubled_hamilton(
                    later, k, base, rows, lanes,
                    turned[(k - 2) * rows : (k - 1) * rows, lanes], held[1, k, :, lanes], rotation,
                ) - retained * field[4 + k, base : base + rows, lanes]
                out[k * rows : (k + 1) * rows, lanes] = (1.0 - retained) * update


def bands(where, packet, previous, potential, tables, left, right, high, low):
    _, rows, width = packet.shape
    return pl.pallas_call(
        band_kernel,
        in_specs=[SMEM, ANY, ANY, ANY, VMEM, VMEM, VMEM, VMEM, VMEM],
        out_specs=VMEM,
        out_shape=jax.ShapeDtypeStruct((2 * BAND * rows, width), F32),
        scratch_shapes=[
            pltpu.VMEM((10, rows + 32, width), F32),
            pltpu.VMEM((6, rows + 32, width), F32),
            pltpu.VMEM((4 * (rows + 16), width), F32),
            pltpu.VMEM((2, 4, rows, width), F32),
            pltpu.SemaphoreType.DMA((3,)),
        ],
        compiler_params=pltpu.CompilerParams(vmem_limit_bytes=16 * MIB),
        cost_estimate=pl.CostEstimate(flops=400_000_000, bytes_accessed=4 * MIB, transcendentals=0),
        name="both_bands",
    )(where, packet, previous, potential, tables, left, right, high, low)


def prepare_kernel(
    packet, rotation, damping, absorber, index, weight, angular, after,
    top, bottom, first, last, tables, high, low, ends, sides, square, sems,
):
    count_r, rows, width = packet.shape
    copies = [
        pltpu.make_async_copy(packet.at[pl.ds(0, HALO)], ends.at[0], sems.at[0]),
        pltpu.make_async_copy(packet.at[pl.ds(count_r - HALO, HALO)], ends.at[1], sems.at[1]),
        pltpu.make_async_copy(packet.at[:, pl.ds(0, 8)], sides.at[0], sems.at[2]),
        pltpu.make_async_copy(packet.at[:, pl.ds(rows - 8, 8)], sides.at[1], sems.at[3]),
    ]
    for copy in copies:
        copy.start()
    square[...] = jnp.zeros_like(square)
    values = [rotation[...], retained_of(damping[...], absorber[...])]
    values += [index[n].astype(F32) for n in range(STENCILS)]
    values += [weight[n] for n in range(STENCILS)]
    for n, value in enumerate(values):
        square[0:count_r, 0:rows] = value
        turned = square[...].T[0:rows]
        tables[n] = turned
        if n >= INDEX:
            at = (n - INDEX) * HALO
            edges = HALO * rows
            columns = HALO * count_r
            top[edges + at : edges + at + HALO, 0:rows] = value[0:HALO]
            bottom[edges + at : edges + at + HALO, 0:rows] = value[count_r - HALO :]
            first[columns + at : columns + at + HALO, 0:LANES] = turned[0:HALO]
            last[columns + at : columns + at + HALO, 0:LANES] = turned[rows - HALO : rows]
    high[...], low[...] = halves(angular[...])
    for copy in copies:
        copy.wait()
    for out, n in ((top, 0), (bottom, 1)):
        for k in range(HALO):
            out[k * rows : (k + 1) * rows] = ends[n, k]
    for out, n, near in ((first, 0, 0), (last, 1, 8 - HALO)):
        for k in range(count_r):
            for r in range(HALO):
                out[r * count_r + k : r * count_r + k + 1] = sides[n, k, near + r : near + r + 1]


def prepare(packet, rotation, damping, absorber, index, weight, angular, after):
    count_r, rows, width = packet.shape
    ends = jax.ShapeDtypeStruct((HALO * rows + EXTRA, width), F32)
    sides = jax.ShapeDtypeStruct((HALO * count_r + EXTRA, width), F32)
    part = jax.ShapeDtypeStruct(angular.shape, BF16)
    return pl.pallas_call(
        prepare_kernel,
        in_specs=[ANY, VMEM, VMEM, VMEM, VMEM, VMEM, VMEM, ANY],
        out_specs=[VMEM] * 7,
        out_shape=[ends, ends, sides, sides, jax.ShapeDtypeStruct((TABLES, rows, LANES), F32), part, part],
        scratch_shapes=[
            pltpu.VMEM((2, HALO, rows, width), F32),
            pltpu.VMEM((2, count_r, 8, width), F32),
            pltpu.VMEM((LANES, LANES), F32),
            pltpu.SemaphoreType.DMA((4,)),
        ],
        compiler_params=pltpu.CompilerParams(vmem_limit_bytes=16 * MIB),
        cost_estimate=pl.CostEstimate(flops=1_000_000, bytes_accessed=6 * MIB, transcendentals=0),
        name="prepare",
    )(packet, rotation, damping, absorber, index, weight, angular, after)


def put_sides(sides, left, right, count_r, left_more=None, right_more=None):
    def body(k, carry):
        for r in range(HALO):
            at = pl.ds(r * count_r + k, 1)
            before, behind = left[at], right[at]
            if left_more is not None:
                before, behind = before + left_more[at], behind + right_more[at]
            sides[k, r : r + 1] = behind
            sides[k, 8 - HALO + r : 8 - HALO + r + 1] = before
        return carry

    lax.fori_loop(0, count_r, body, 0, unroll=8)


def advance(step, chunk, field, sides, previous, potential, tables, high, low, put):
    rows = previous.shape[1]
    width = previous.shape[2]
    here = step * chunk
    shift = lax.rem(LANES - here, LANES)
    columns = [pltpu.roll(tables[n], shift, 1) for n in (ROT, RET)]
    window = field[pl.ds(HALO + here, chunk)].reshape(chunk * rows, width)
    split = halves(window)
    wide = 2 * LANES
    for tile in range(0, width, wide):
        turned = product(split, high[:, tile : tile + wide], low[:, tile : tile + wide])
        for k in range(chunk):
            rotation = jnp.broadcast_to(0.25 * columns[0][:, k : k + 1], (rows, LANES))
            retained = jnp.broadcast_to(columns[1][:, k : k + 1], (rows, LANES))
            for at in range(tile, tile + wide, LANES):
                lanes = slice(at, at + LANES)

                def row(shift):
                    return field[HALO + here + k + shift, :, lanes]

                middle = row(0)
                ring = jnp.concatenate([middle, sides[here + k, :, lanes]], axis=0)
                around = [pltpu.roll(ring, s, 0)[:rows] for s in (1, rows + 7, 2, rows + 6)]
                near = row(-1) + row(1) + (around[0] + around[1])
                far = row(-2) + row(2) + (around[2] + around[3])
                update = (
                    SIDE1 * near
                    + SIDE2 * far
                    + (0.25 * potential[here + k, :, lanes] + MIDDLE) * middle
                    + rotation * turned[k * rows : (k + 1) * rows, at - tile : at - tile + LANES]
                    - retained * previous[here + k, :, lanes]
                )
                put(here + k, lanes, retained * update)


def pieces(count, chunk):
    return [pl.ds(n * chunk, chunk) for n in range(count // chunk)]


def first_kernel(
    packet, previous, potential, tables, up, down, left, right, high, low, after,
    out, top, bottom, first, last, field, prev, pot, done, sides, sems,
):
    count_r, rows, width = packet.shape
    steps = count_r // CHUNK
    into = []
    for n, part in enumerate(pieces(count_r, CHUNK)):
        into.append(
            [
                pltpu.make_async_copy(packet.at[part], field.at[pl.ds(HALO + n * CHUNK, CHUNK)], sems.at[0, n]),
                pltpu.make_async_copy(previous.at[part], prev.at[part], sems.at[1, n]),
                pltpu.make_async_copy(potential.at[part], pot.at[part], sems.at[2, n]),
            ]
        )
    for group in into:
        for copy in group:
            copy.start()
    for k in range(HALO):
        field[k] = up[k * rows : (k + 1) * rows]
        field[HALO + count_r + k] = down[k * rows : (k + 1) * rows]
    put_sides(sides, left, right, count_r)
    into[0][0].wait()
    outs = []
    for step in range(steps):
        if step + 1 < steps:
            into[step + 1][0].wait()
        into[step][1].wait()
        into[step][2].wait()

        def put(k, lanes, value):
            done[k, :, lanes] = value

        advance(step, CHUNK, field, sides, prev, pot, tables, high, low, put)
        part = pl.ds(step * CHUNK, CHUNK)
        outs.append(pltpu.make_async_copy(done.at[part], out.at[part], sems.at[3, step]))
        outs[-1].start()
        for k in range(step * CHUNK, (step + 1) * CHUNK):
            for r in range(HALO):
                first[r * count_r + k : r * count_r + k + 1] = done[k, r : r + 1]
                last[r * count_r + k : r * count_r + k + 1] = done[k, rows - HALO + r : rows - HALO + r + 1]
    for k in range(HALO):
        top[k * rows : (k + 1) * rows] = done[k]
        bottom[k * rows : (k + 1) * rows] = done[count_r - HALO + k]
    for copy in outs:
        copy.wait()


def first_iteration(packet, previous, potential, tables, halos, high, low, after):
    count_r, rows, width = packet.shape
    ends = jax.ShapeDtypeStruct((HALO * rows, width), F32)
    sides = jax.ShapeDtypeStruct((HALO * count_r, width), F32)
    return pl.pallas_call(
        first_kernel,
        in_specs=[ANY, ANY, ANY, *[VMEM] * 7, ANY],
        out_specs=[ANY, *[VMEM] * 4],
        out_shape=[jax.ShapeDtypeStruct(packet.shape, F32), ends, ends, sides, sides],
        scratch_shapes=[
            pltpu.VMEM((count_r + 2 * HALO, rows, width), F32),
            pltpu.VMEM(packet.shape, F32),
            pltpu.VMEM(packet.shape, F32),
            pltpu.VMEM(packet.shape, F32),
            pltpu.VMEM((count_r, 8, width), F32),
            pltpu.SemaphoreType.DMA((4, count_r // CHUNK)),
        ],
        compiler_params=pltpu.CompilerParams(vmem_limit_bytes=40 * MIB),
        cost_estimate=pl.CostEstimate(flops=7_000_000_000, bytes_accessed=20 * MIB, transcendentals=0),
        name="first_iteration",
    )(packet, previous, potential, tables, *halos, high, low, after)


def stencil_kernel(where, tables, up, down, left, right, after, high, low, edge_high, edge_low, square):
    _, rows, _ = tables.shape
    count_r = left.shape[0] // HALO - EXTRA // HALO
    width = high.shape[1]
    per = rows * BAND
    shift_owner = per.bit_length() - 1
    chips = width // per // CORES

    def place(value):
        index = value.astype(jnp.int32)
        owner = index >> shift_owner
        inside = index & (per - 1)
        core = (owner & 1) ^ where[CORE]
        chip = (where[CHIP] - (owner >> 1)) & (chips - 1)
        slot = ((core * chips + chip) << shift_owner) + (inside & 1) * rows + (inside >> 1)
        return slot.astype(F32)

    column = lax.broadcasted_iota(jnp.int32, (32, LANES), 1).astype(F32)

    def fill(at, places, weights, high_out, low_out):
        places = [jnp.broadcast_to(p, (32, LANES)) for p in places]
        weights = [jnp.broadcast_to(w, (32, LANES)) for w in weights]
        for tile in range(0, width, LANES):
            here = column + float(tile)
            total = jnp.where(here == places[0], weights[0], 0.0)
            for n in range(1, STENCILS):
                total += jnp.where(here == places[n], weights[n], 0.0)
            upper, lower = halves(total)
            high_out[pl.ds(at, 32), tile : tile + LANES] = upper
            low_out[pl.ds(at, 32), tile : tile + LANES] = lower

    @pl.when(where[PRODUCT] == 1)
    def _():
        places = [place(tables[INDEX + n]) for n in range(STENCILS)]
        weights = [tables[WEIGHT + n] for n in range(STENCILS)]
        group = 8

        def body(step, carry):
            shift = lax.rem(LANES - step * group, LANES)
            moved = [pltpu.roll(value, shift, 1) for value in places + weights]
            for k in range(group):
                cut = [value[:, k : k + 1] for value in moved]
                at = pl.multiple_of((step * group + k) * rows, rows)
                fill(at, cut[:STENCILS], cut[STENCILS:], high, low)
            return carry

        lax.fori_loop(0, count_r // group, body, 0)

        square[...] = jnp.zeros_like(square)
        for n, side in enumerate((up, down, left, right)):
            begin = side.shape[0] - EXTRA
            square[n * EXTRA : n * EXTRA + EXTRA // 2] = place(side[begin : begin + EXTRA // 2, 0:LANES])
            square[n * EXTRA + EXTRA // 2 : (n + 1) * EXTRA] = side[begin + EXTRA // 2 : begin + EXTRA, 0:LANES]
        turned = square[...].T
        at = 0
        for n, length in enumerate((rows, rows, count_r, count_r)):
            for e in range(HALO):
                for begin in range(0, length, 32):
                    cut = [
                        turned[begin : begin + 32, n * EXTRA + HALO * m + e : n * EXTRA + HALO * m + e + 1]
                        for m in range(2 * STENCILS)
                    ]
                    fill(at, cut[:STENCILS], cut[STENCILS:], edge_high, edge_low)
                    at += 32


def stencil_matrix(where, tables, halos, columns, after):
    rows = tables.shape[1]
    count_r = halos[2].shape[0] // HALO - EXTRA // HALO
    points = jax.ShapeDtypeStruct((count_r * rows, columns), BF16)
    edges = jax.ShapeDtypeStruct((2 * HALO * (rows + count_r), columns), BF16)
    return pl.pallas_call(
        stencil_kernel,
        in_specs=[SMEM, *[VMEM] * 5, ANY],
        out_specs=[VMEM] * 4,
        out_shape=[points, points, edges, edges],
        scratch_shapes=[pltpu.VMEM((LANES, LANES), F32)],
        compiler_params=pltpu.CompilerParams(vmem_limit_bytes=16 * MIB),
        cost_estimate=pl.CostEstimate(flops=15_000_000, bytes_accessed=6 * MIB, transcendentals=0),
        name="stencil_matrix",
    )(where, tables, *halos, after)


def last_kernel(
    where, one, packet, potential, tables, up, down, left, right, high, low,
    stencil_high, stencil_low, edge_high, edge_low, own_table, other_table,
    earlier, latest, field, prev, pot, done, sides, split_high, split_low, table, source, sems,
):
    count_r, rows, width = packet.shape
    steps = count_r // LAST
    is_product = where[PRODUCT] == 1
    quarter = own_table.shape[1]
    half = quarter // 2
    chips = own_table.shape[0]
    size = LAST * rows
    parts = pieces(count_r, LAST)

    def field_part(n):
        return field.at[pl.ds(HALO + n * LAST, LAST)]

    ones, highs, lows, prevs, pots = [], [], [], [], []
    for n, part in enumerate(parts):
        cut = pl.ds(n * size, size)
        ones.append(pltpu.make_async_copy(one.at[part], field_part(n), sems.at[0, n]))
        highs.append(pltpu.make_async_copy(stencil_high.at[cut], split_high.at[cut], sems.at[1, n]))
        lows.append(pltpu.make_async_copy(stencil_low.at[cut], split_low.at[cut], sems.at[2, n]))
        prevs.append(pltpu.make_async_copy(packet.at[part], prev.at[part], sems.at[3, n]))
        pots.append(pltpu.make_async_copy(potential.at[part], pot.at[part], sems.at[4, n]))
    earliers = [pltpu.make_async_copy(field_part(n), earlier.at[part], sems.at[5, n]) for n, part in enumerate(parts)]
    latests = [pltpu.make_async_copy(done.at[part], latest.at[part], sems.at[6, n]) for n, part in enumerate(parts)]

    def put_ends(up_value, down_value):
        for k in range(HALO):
            field[k] = up_value[k * rows : (k + 1) * rows]
            field[HALO + count_r + k] = down_value[k * rows : (k + 1) * rows]

    @pl.when(is_product)
    def _():
        for n in range(steps):
            ones[n].start()
            highs[n].start()
            lows[n].start()
        for n in range(steps):
            prevs[n].start()
            pots[n].start()
        for side, ref in enumerate((own_table, other_table)):
            for k in range(chips):
                at = (side * chips + k) * half
                for band in range(2):
                    upper, lower = halves(ref[k, band * half : (band + 1) * half])
                    table[2 * band, at : at + half] = upper
                    table[2 * band + 1, at : at + half] = lower
        source[...] = product((edge_high[...], edge_low[...]), table[0], table[1])
        edges = HALO * rows
        columns = HALO * count_r
        put_ends(up[...] + source[:edges], down[...] + source[edges : 2 * edges])
        put_sides(
            sides, left, right, count_r,
            source.at[pl.ds(2 * edges, columns)], source.at[pl.ds(2 * edges + columns, columns)],
        )
        for n in range(steps):
            ones[n].wait()
            highs[n].wait()
            lows[n].wait()
            cut = pl.ds(n * size, size)
            weights = (split_high[cut], split_low[cut])
            here = pl.ds(HALO + n * LAST, LAST)
            field[here] = field[here] + product(weights, table[0], table[1]).reshape(LAST, rows, width)
            done[parts[n]] = product(weights, table[2], table[3]).reshape(LAST, rows, width)
            earliers[n].start()

    @pl.when(jnp.logical_not(is_product))
    def _():
        for n in range(steps):
            ones[n].start()
            prevs[n].start()
            pots[n].start()
        put_ends(up, down)
        put_sides(sides, left, right, count_r)
        done[...] = jnp.zeros_like(done)
        for n in range(steps):
            ones[n].wait()
            earliers[n].start()

    def put(k, lanes, value):
        done[k, :, lanes] += value

    for n in range(steps):
        prevs[n].wait()
        pots[n].wait()
        advance(n, LAST, field, sides, prev, pot, tables, high, low, put)
        latests[n].start()
    for copy in earliers + latests:
        copy.wait()


def last_iteration(where, one, packet, potential, tables, halos, high, low, matrices, band_tables):
    count_r, rows, width = packet.shape
    steps = count_r // LAST
    columns = matrices[0].shape[1]
    return pl.pallas_call(
        last_kernel,
        in_specs=[SMEM, ANY, ANY, ANY, *[VMEM] * 7, ANY, ANY, *[VMEM] * 4],
        out_specs=[ANY, ANY],
        out_shape=[jax.ShapeDtypeStruct(packet.shape, F32)] * 2,
        scratch_shapes=[
            pltpu.VMEM((count_r + 2 * HALO, rows, width), F32),
            pltpu.VMEM(packet.shape, F32),
            pltpu.VMEM(packet.shape, F32),
            pltpu.VMEM(packet.shape, F32),
            pltpu.VMEM((count_r, 8, width), F32),
            pltpu.VMEM((count_r * rows, columns), BF16),
            pltpu.VMEM((count_r * rows, columns), BF16),
            pltpu.VMEM((4, columns, width), BF16),
            pltpu.VMEM((2 * HALO * (rows + count_r), width), F32),
            pltpu.SemaphoreType.DMA((7, steps)),
        ],
        compiler_params=pltpu.CompilerParams(vmem_limit_bytes=56 * MIB),
        cost_estimate=pl.CostEstimate(flops=20_000_000_000, bytes_accessed=36 * MIB, transcendentals=0),
        name="last_iteration",
    )(where, one, packet, potential, tables, *halos, high, low, *matrices, *band_tables)


def neighbours(axis, upward, downward):
    count = lax.axis_size(axis)
    return (
        lax.ppermute(upward, axis, [(i, i + 1) for i in range(count - 1)]),
        lax.ppermute(downward, axis, [(i + 1, i) for i in range(count - 1)]),
    )


def exchange(top, bottom, first, last):
    left, right = neighbours("row", last, first)
    up, down = neighbours("rr", bottom, top)
    return up, down, left, right


def local(packet, previous, potential, rotation, angular, damping, absorber, stencil_index, stencil_weight):
    packet, previous, potential = packet[0], previous[0], potential[0]
    rotation, angular, damping, absorber = rotation[0], angular[0], damping[0], absorber[0]
    count_r, rows, width = packet.shape
    sect = lax.axis_index("sect")
    rr = lax.axis_index("rr")
    row = lax.axis_index("row")
    count_rr, count_row = (lax.axis_size(name) for name in ("rr", "row"))
    chips = count_row // CORES
    where = jnp.stack(
        [((sect == 0) & (rr == count_rr - 1)).astype(jnp.int32), sect, row % CORES, row // CORES]
    ).astype(jnp.int32)

    firsts, lasts = band_slabs(where, rotation, damping, absorber, packet, previous, potential)
    axes = ("sect", "rr", "row")
    sources = (count_rr - 1) * count_row
    band_left = lax.ppermute(lasts, axes, [(sources + i, sources + i + 1) for i in range(count_row - 1)])
    band_right = lax.ppermute(firsts, axes, [(sources + i + 1, sources + i) for i in range(count_row - 1)])

    top, bottom, first, last, tables, high, low = prepare(
        packet, rotation, damping, absorber, stencil_index, stencil_weight, angular, firsts
    )
    table = bands(where, packet, previous, potential, tables, band_left, band_right, high, low)
    halos = exchange(top, bottom, first, last)

    plane = ("sect", "rr")
    half = count_rr // FAR
    start = count_rr - 1
    entries = [count_rr + (k + 1) * half - 1 for k in range(FAR)]
    piece = sum(lax.ppermute(table, plane, [(start, entry)]) for entry in entries)
    spread = piece
    for shift in (1, half - 1, 2):
        spread = spread + lax.ppermute(
            piece, plane, [(entry, entry - (half - 1) + (half - 1 + shift) % half) for entry in entries]
        )
    line = ("sect", "row")

    def around(shift):
        pairs = []
        for chip in range(chips):
            for core in range(CORES):
                pairs.append(
                    (count_row + chip * CORES + core, count_row + ((chip + shift) % chips) * CORES + core)
                )
        return lax.ppermute(spread, line, pairs)

    own = jnp.stack([spread, around(1), around(2), around(3)], axis=0)
    other = lax.ppermute(
        own, line, [(count_row + i, count_row + i + 1 - 2 * (i % CORES)) for i in range(count_row)]
    )

    one, *edges = first_iteration(packet, previous, potential, tables, halos, high, low, table)
    matrices = stencil_matrix(where, tables, halos, count_row * rows * BAND, piece)
    later = exchange(*edges)
    earlier, latest = last_iteration(
        where, one, packet, potential, tables, later, high, low, matrices, (own, other)
    )
    return latest[None], earlier[None]


def solution(mesh):
    in_specs = (
        P("sect", "rr", "row", None),
        P("sect", "rr", "row", None),
        P("sect", "rr", "row", None),
        P("sect", "rr", "row"),
        P("sect", None, None),
        P("sect", "rr", "row"),
        P("sect", "rr", "row"),
        P(None, "rr", "row"),
        P(None, "rr", "row"),
    )
    out_specs = (P("sect", "rr", "row", None), P("sect", "rr", "row", None))
    return jax.shard_map(local, mesh=mesh, in_specs=in_specs, out_specs=out_specs, check_vma=False)
```

```python
import functools

import jax
import jax.numpy as jnp
from jax import lax
from jax.experimental import pallas as pl
from jax.experimental.pallas import tpu as pltpu
from jax.sharding import PartitionSpec as P

BAND = 2
STENCILS = 4
HALO = 2
LANES = 128
CHUNK = 16
LAST = 16
CORES = 2
FAR = 2
ROT, RET, INDEX, WEIGHT, TABLES = 0, 1, 2, 6, 10
EXTRA = 2 * STENCILS * HALO
AXES = ("sect", "rr", "row")
MIB = 1 << 20
F32 = jnp.float32
BF16 = jnp.bfloat16
ANY = pl.BlockSpec(memory_space=pl.ANY)
HBM = pl.BlockSpec(memory_space=pltpu.HBM)
VMEM = pl.BlockSpec(memory_space=pltpu.VMEM)

SIDE1 = -16.0 / 96.0
SIDE2 = 1.0 / 96.0
MIDDLE = 2.0 * 30.0 / 96.0 - 7.5 / 4.0


def halves(value):
    high = value.astype(BF16)
    low = (value - high.astype(F32)).astype(BF16)
    return high, low


def product(left, right_high, right_low):
    high, low = left
    total = jnp.dot(high, right_high, preferred_element_type=F32)
    total += jnp.dot(low, right_high, preferred_element_type=F32)
    return total + jnp.dot(high, right_low, preferred_element_type=F32)


def doubled_hamilton(field, index, start, count, lanes, turned, potential, rotation):
    def at(shift_r, shift_v):
        return field[index + shift_r, pl.ds(start + shift_v, count), lanes]

    middle = at(0, 0)
    near = at(-1, 0) + at(1, 0) + (at(0, -1) + at(0, 1))
    far = at(-2, 0) + at(2, 0) + (at(0, -2) + at(0, 2))
    return (
        SIDE1 * near
        + SIDE2 * far
        + (0.25 * potential + MIDDLE) * middle
        + (0.25 * rotation) * turned
    )


def in_hbm(value):
    return pltpu.with_memory_space_constraint(value, pltpu.HBM)


def holds_bands():
    return (lax.axis_index("sect") == 0) & (lax.axis_index("rr") == lax.axis_size("rr") - 1)


def in_product():
    return lax.axis_index("sect") == 1


def retained_of(damping, absorber):
    return 1.0 - absorber.astype(F32) * (1.0 - damping)


def band_slab_kernel(rotation, damping, absorber, packet, previous, potential, firsts, lasts, held, factors, masks, sems):
    count_r, rows, width = packet.shape

    @pl.when(holds_bands())
    def _():
        copies = [
            pltpu.make_async_copy(ref.at[pl.ds(count_r - 4, 4)], held.at[n], sems.at[n])
            for n, ref in enumerate((packet, previous, potential))
        ]
        copies += [
            pltpu.make_async_copy(rotation, factors.at[0], sems.at[3]),
            pltpu.make_async_copy(damping, factors.at[1], sems.at[4]),
            pltpu.make_async_copy(absorber, masks, sems.at[5]),
        ]
        for copy in copies:
            copy.start()
        for copy in copies:
            copy.wait()
        retained = retained_of(factors[1], masks[...])
        rotated = factors[0]
        for out, far, near in ((firsts, 0, 0), (lasts, rows - 4, rows - 2)):
            for k in range(4):
                out[4 * k : 4 * k + 4] = held[0, k, far : far + 4]
            for k in range(BAND):
                at = count_r - BAND + k
                out[16 + 2 * k : 18 + 2 * k] = held[1, 2 + k, near : near + 2]
                out[20 + 2 * k : 22 + 2 * k] = held[2, 2 + k, near : near + 2]
                out[24 + 2 * k : 26 + 2 * k] = jnp.broadcast_to(rotated[near : near + 2, at : at + 1], (2, width))
                out[28 + 2 * k : 30 + 2 * k] = jnp.broadcast_to(retained[near : near + 2, at : at + 1], (2, width))


def band_slabs(rotation, damping, absorber, packet, previous, potential):
    count_r, rows, width = packet.shape
    return pl.pallas_call(
        band_slab_kernel,
        in_specs=[ANY, ANY, ANY, HBM, HBM, HBM],
        out_specs=[VMEM, VMEM],
        out_shape=[jax.ShapeDtypeStruct((32, width), F32)] * 2,
        scratch_shapes=[
            pltpu.VMEM((3, 4, rows, width), F32),
            pltpu.VMEM((2, rows, count_r), F32),
            pltpu.VMEM((rows, count_r), jnp.int32),
            pltpu.SemaphoreType.DMA((6,)),
        ],
        compiler_params=pltpu.CompilerParams(vmem_limit_bytes=8 * MIB),
        name="band_slabs",
    )(rotation, damping, absorber, packet, previous, potential)


def band_kernel(
    packet, previous, potential, tables, left, right, high, low, out, field, later, turned, held, sems
):
    count_r, rows, width = packet.shape
    base = 16
    wide = rows + 16

    @pl.when(holds_bands())
    def _():
        copies = [
            pltpu.make_async_copy(packet.at[pl.ds(count_r - 6, 6)], field.at[pl.ds(2, 6), pl.ds(base, rows)], sems.at[0]),
            pltpu.make_async_copy(previous.at[pl.ds(count_r - 4, 4)], held.at[0], sems.at[1]),
            pltpu.make_async_copy(potential.at[pl.ds(count_r - 4, 4)], held.at[1], sems.at[2]),
        ]
        later[...] = jnp.zeros_like(later)
        field[0:2] = jnp.zeros_like(field[0:2])
        field[8:10] = jnp.zeros_like(field[8:10])
        for k in range(2, 8):
            field[k, 0:base] = jnp.zeros((base, width), F32)
            field[k, base + rows :] = jnp.zeros((base, width), F32)
        for copy in copies:
            copy.start()
        for k in range(4):
            field[4 + k, base - 4 : base] = left[4 * k : 4 * k + 4]
            field[4 + k, base + rows : base + rows + 4] = right[4 * k : 4 * k + 4]
        columns = [
            (tables[ROT, :, count_r - 4 + k : count_r - 3 + k], tables[RET, :, count_r - 4 + k : count_r - 3 + k])
            for k in range(4)
        ]
        columns = [tuple(jnp.broadcast_to(c, (rows, LANES)) for c in pair) for pair in columns]
        for copy in copies:
            copy.wait()
        window = field[4:8, base - 8 : base + rows + 8].reshape(4 * wide, width)
        turned[...] = product(halves(window), high[...], low[...])
        for k in range(4):
            rotation, retained = columns[k]
            for at in range(0, width, LANES):
                lanes = slice(at, at + LANES)
                update = doubled_hamilton(
                    field, 4 + k, base, rows, lanes,
                    turned[k * wide + 8 : k * wide + 8 + rows, lanes], held[1, k, :, lanes], rotation,
                ) - retained * held[0, k, :, lanes]
                later[k, base : base + rows, lanes] = retained * update
                if k >= 2:
                    out[(k - 2) * rows : (k - 1) * rows, lanes] = (1.0 - retained) * update
        for k in range(2, 4):
            for slab, place, inside in ((left, base - 8, 6), (right, base + rows, 0)):
                at = 16 + 2 * (k - 2)
                prev, pot, rot, ret = (slab[at + 4 * n : at + 4 * n + 2] for n in range(4))
                update = doubled_hamilton(
                    field, 4 + k, place + inside, 2, slice(None),
                    turned[k * wide + place - base + 8 + inside : k * wide + place - base + 10 + inside], pot, rot,
                ) - ret * prev
                later[k, place + inside : place + inside + 2] = ret * update
        window = later[2:4, base : base + rows].reshape(2 * rows, width)
        turned[0 : 2 * rows] = product(halves(window), high[...], low[...])
        for k in range(2, 4):
            rotation, retained = columns[k]
            for at in range(0, width, LANES):
                lanes = slice(at, at + LANES)
                update = doubled_hamilton(
                    later, k, base, rows, lanes,
                    turned[(k - 2) * rows : (k - 1) * rows, lanes], held[1, k, :, lanes], rotation,
                ) - retained * field[4 + k, base : base + rows, lanes]
                out[k * rows : (k + 1) * rows, lanes] = (1.0 - retained) * update


def bands(packet, previous, potential, tables, left, right, high, low):
    _, rows, width = packet.shape
    return pl.pallas_call(
        band_kernel,
        in_specs=[HBM, HBM, HBM, VMEM, VMEM, VMEM, VMEM, VMEM],
        out_specs=VMEM,
        out_shape=jax.ShapeDtypeStruct((2 * BAND * rows, width), F32),
        scratch_shapes=[
            pltpu.VMEM((10, rows + 32, width), F32),
            pltpu.VMEM((6, rows + 32, width), F32),
            pltpu.VMEM((4 * (rows + 16), width), F32),
            pltpu.VMEM((2, 4, rows, width), F32),
            pltpu.SemaphoreType.DMA((3,)),
        ],
        compiler_params=pltpu.CompilerParams(vmem_limit_bytes=16 * MIB),
        cost_estimate=pl.CostEstimate(flops=400_000_000, bytes_accessed=4 * MIB, transcendentals=0),
        name="both_bands",
    )(packet, previous, potential, tables, left, right, high, low)


def prepare_kernel(
    packet, rotation, damping, absorber, index, weight, angular, after,
    top, bottom, first, last, tables, high, low, ends, sides, sems,
):
    count_r, rows, width = packet.shape
    copies = [
        pltpu.make_async_copy(packet.at[pl.ds(0, HALO)], ends.at[0], sems.at[0]),
        pltpu.make_async_copy(packet.at[pl.ds(count_r - HALO, HALO)], ends.at[1], sems.at[1]),
        pltpu.make_async_copy(packet.at[:, pl.ds(0, 8)], sides.at[0], sems.at[2]),
        pltpu.make_async_copy(packet.at[:, pl.ds(rows - 8, 8)], sides.at[1], sems.at[3]),
    ]
    for copy in copies:
        copy.start()
    values = [rotation[...], retained_of(damping[...], absorber[...])]
    values += [index[n].astype(F32) for n in range(STENCILS)]
    values += [weight[n] for n in range(STENCILS)]
    for n, value in enumerate(values):
        tables[n] = jnp.concatenate([value, jnp.zeros((rows, LANES - count_r), F32)], axis=1)
    edges = HALO * rows
    columns = HALO * count_r
    lane = lax.broadcasted_iota(jnp.int32, (rows, LANES), 1)
    upper = jnp.zeros((rows, LANES), F32)
    lower = jnp.zeros((rows, LANES), F32)
    for n in range(2 * STENCILS):
        value = tables[INDEX + n]
        at = n * HALO
        here = (lane >= at) & (lane < at + HALO)
        upper = jnp.where(here, pltpu.roll(value, at, 1), upper)
        lower = jnp.where(here, pltpu.roll(value, (at + LANES - (count_r - HALO)) % LANES, 1), lower)
        first[columns + at : columns + at + HALO, 0:LANES] = value[0:HALO]
        last[columns + at : columns + at + HALO, 0:LANES] = value[rows - HALO : rows]
    top[edges : edges + rows, 0:LANES] = upper
    bottom[edges : edges + rows, 0:LANES] = lower
    high[...], low[...] = halves(angular[...])
    for copy in copies:
        copy.wait()
    for out, n in ((top, 0), (bottom, 1)):
        for k in range(HALO):
            out[k * rows : (k + 1) * rows] = ends[n, k]
    for out, n, near in ((first, 0, 0), (last, 1, 8 - HALO)):
        for k in range(count_r):
            for r in range(HALO):
                out[r * count_r + k : r * count_r + k + 1] = sides[n, k, near + r : near + r + 1]


def prepare(packet, rotation, damping, absorber, index, weight, angular, after):
    count_r, rows, width = packet.shape
    ends = jax.ShapeDtypeStruct((HALO * rows + rows, width), F32)
    sides = jax.ShapeDtypeStruct((HALO * count_r + EXTRA, width), F32)
    part = jax.ShapeDtypeStruct(angular.shape, BF16)
    return pl.pallas_call(
        prepare_kernel,
        in_specs=[HBM, VMEM, VMEM, VMEM, VMEM, VMEM, VMEM, ANY],
        out_specs=[VMEM] * 7,
        out_shape=[ends, ends, sides, sides, jax.ShapeDtypeStruct((TABLES, rows, LANES), F32), part, part],
        scratch_shapes=[
            pltpu.VMEM((2, HALO, rows, width), F32),
            pltpu.VMEM((2, count_r, 8, width), F32),
            pltpu.SemaphoreType.DMA((4,)),
        ],
        compiler_params=pltpu.CompilerParams(vmem_limit_bytes=16 * MIB),
        cost_estimate=pl.CostEstimate(flops=1_000_000, bytes_accessed=6 * MIB, transcendentals=0),
        name="prepare",
    )(packet, rotation, damping, absorber, index, weight, angular, after)


def put_sides(sides, left, right, count_r, left_more=None, right_more=None):
    def body(k, carry):
        for r in range(HALO):
            at = pl.ds(r * count_r + k, 1)
            before, behind = left[at], right[at]
            if left_more is not None:
                before, behind = before + left_more[at], behind + right_more[at]
            sides[k, r : r + 1] = behind
            sides[k, 8 - HALO + r : 8 - HALO + r + 1] = before
        return carry

    lax.fori_loop(0, count_r, body, 0, unroll=8)


def advance(step, chunk, field, sides, previous, potential, tables, high, low, put):
    rows = previous.shape[1]
    width = previous.shape[2]
    here = step * chunk
    shift = lax.rem(LANES - here, LANES)
    columns = [pltpu.roll(tables[n], shift, 1) for n in (ROT, RET)]
    window = field[pl.ds(HALO + here, chunk)].reshape(chunk * rows, width)
    split = halves(window)
    wide = 2 * LANES
    for tile in range(0, width, wide):
        turned = product(split, high[:, tile : tile + wide], low[:, tile : tile + wide])
        for k in range(chunk):
            rotation = jnp.broadcast_to(0.25 * columns[0][:, k : k + 1], (rows, LANES))
            retained = jnp.broadcast_to(columns[1][:, k : k + 1], (rows, LANES))
            for at in range(tile, tile + wide, LANES):
                lanes = slice(at, at + LANES)

                def row(shift):
                    return field[HALO + here + k + shift, :, lanes]

                middle = row(0)
                ring = jnp.concatenate([middle, sides[here + k, :, lanes]], axis=0)
                around = [pltpu.roll(ring, s, 0)[:rows] for s in (1, rows + 7, 2, rows + 6)]
                near = row(-1) + row(1) + (around[0] + around[1])
                far = row(-2) + row(2) + (around[2] + around[3])
                update = (
                    SIDE1 * near
                    + SIDE2 * far
                    + (0.25 * potential[here + k, :, lanes] + MIDDLE) * middle
                    + rotation * turned[k * rows : (k + 1) * rows, at - tile : at - tile + LANES]
                    - retained * previous[here + k, :, lanes]
                )
                put(here + k, lanes, retained * update)


def first_kernel(
    packet, previous, potential, tables, up, down, left, right, high, low, after,
    done, top, bottom, first, last, field, prev, pot, sides, sems,
):
    count_r, rows, width = packet.shape
    steps = count_r // CHUNK

    def copies(n):
        part = pl.ds(n * CHUNK, CHUNK)
        return (
            pltpu.make_async_copy(packet.at[part], field.at[pl.ds(HALO + n * CHUNK, CHUNK)], sems.at[0, n]),
            pltpu.make_async_copy(previous.at[part], prev.at[part], sems.at[1, n]),
            pltpu.make_async_copy(potential.at[part], pot.at[part], sems.at[2, n]),
        )

    for n in range(steps):
        for copy in copies(n):
            copy.start()
    for k in range(HALO):
        field[k] = up[k * rows : (k + 1) * rows]
        field[HALO + count_r + k] = down[k * rows : (k + 1) * rows]
    put_sides(sides, left, right, count_r)
    copies(0)[0].wait()

    def put(k, lanes, value):
        done[k, :, lanes] = value

    def body(n, carry):
        @pl.when(n + 1 < steps)
        def _():
            copies(n + 1)[0].wait()

        copies(n)[1].wait()
        copies(n)[2].wait()
        advance(n, CHUNK, field, sides, prev, pot, tables, high, low, put)
        for k in range(CHUNK):
            for r in range(HALO):
                at = pl.ds(r * count_r + n * CHUNK + k, 1)
                first[at] = done[n * CHUNK + k, r : r + 1]
                last[at] = done[n * CHUNK + k, rows - HALO + r : rows - HALO + r + 1]
        return carry

    lax.fori_loop(0, steps, body, 0)
    for k in range(HALO):
        top[k * rows : (k + 1) * rows] = done[k]
        bottom[k * rows : (k + 1) * rows] = done[count_r - HALO + k]


def first_iteration(packet, previous, potential, tables, halos, high, low, after):
    count_r, rows, width = packet.shape
    ends = jax.ShapeDtypeStruct((HALO * rows, width), F32)
    sides = jax.ShapeDtypeStruct((HALO * count_r, width), F32)
    return pl.pallas_call(
        first_kernel,
        in_specs=[HBM, HBM, HBM, *[VMEM] * 7, ANY],
        out_specs=[VMEM] * 5,
        out_shape=[jax.ShapeDtypeStruct(packet.shape, F32), ends, ends, sides, sides],
        scratch_shapes=[
            pltpu.VMEM((count_r + 2 * HALO, rows, width), F32),
            pltpu.VMEM(packet.shape, F32),
            pltpu.VMEM(packet.shape, F32),
            pltpu.VMEM((count_r, 8, width), F32),
            pltpu.SemaphoreType.DMA((3, count_r // CHUNK)),
        ],
        compiler_params=pltpu.CompilerParams(vmem_limit_bytes=28 * MIB),
        cost_estimate=pl.CostEstimate(flops=7_000_000_000, bytes_accessed=20 * MIB, transcendentals=0),
        name="first_iteration",
    )(packet, previous, potential, tables, *halos, high, low, after)


def stencil_kernel(tables, up, down, left, right, after, high, low, edge_high, edge_low, square):
    _, rows, _ = tables.shape
    count_r = left.shape[0] // HALO - EXTRA // HALO
    width = high.shape[1]
    per = rows * BAND
    shift_owner = per.bit_length() - 1
    chips = width // per // CORES

    def place(value):
        index = value.astype(jnp.int32)
        owner = index >> shift_owner
        inside = index & (per - 1)
        core = (owner & 1) ^ (lax.axis_index("row") & 1)
        chip = ((lax.axis_index("row") >> 1) - (owner >> 1)) & (chips - 1)
        slot = ((core * chips + chip) << shift_owner) + (inside & 1) * rows + (inside >> 1)
        return slot.astype(F32)

    column = lax.broadcasted_iota(jnp.int32, (32, LANES), 1).astype(F32)

    def fill(at, places, weights, high_out, low_out):
        places = [jnp.broadcast_to(p, (32, LANES)) for p in places]
        weights = [jnp.broadcast_to(w, (32, LANES)) for w in weights]
        for tile in range(0, width, LANES):
            here = column + float(tile)
            total = jnp.where(here == places[0], weights[0], 0.0)
            for n in range(1, STENCILS):
                total += jnp.where(here == places[n], weights[n], 0.0)
            upper, lower = halves(total)
            high_out[pl.ds(at, 32), tile : tile + LANES] = upper
            low_out[pl.ds(at, 32), tile : tile + LANES] = lower

    @pl.when(in_product())
    def _():
        places = [place(tables[INDEX + n]) for n in range(STENCILS)]
        weights = [tables[WEIGHT + n] for n in range(STENCILS)]
        group = 8

        def body(step, carry):
            shift = lax.rem(LANES - step * group, LANES)
            moved = [pltpu.roll(value, shift, 1) for value in places + weights]
            for k in range(group):
                cut = [value[:, k : k + 1] for value in moved]
                at = pl.multiple_of((step * group + k) * rows, rows)
                fill(at, cut[:STENCILS], cut[STENCILS:], high, low)
            return carry

        lax.fori_loop(0, count_r // group, body, 0)

        edges = HALO * rows
        at = 0
        for side in (up, down):
            value = side[edges : edges + rows, 0:LANES]
            slots = place(value)
            for e in range(HALO):
                cut = [(slots if m < STENCILS else value)[:, HALO * m + e : HALO * m + e + 1] for m in range(2 * STENCILS)]
                fill(at, cut[:STENCILS], cut[STENCILS:], edge_high, edge_low)
                at += rows
        square[...] = jnp.zeros_like(square)
        for n, side in enumerate((left, right)):
            begin = HALO * count_r
            square[n * EXTRA : n * EXTRA + EXTRA // 2] = place(side[begin : begin + EXTRA // 2, 0:LANES])
            square[n * EXTRA + EXTRA // 2 : (n + 1) * EXTRA] = side[begin + EXTRA // 2 : begin + EXTRA, 0:LANES]
        turned = square[...].T
        for n in range(2):
            for e in range(HALO):
                for begin in range(0, count_r, rows):
                    cut = [
                        turned[begin : begin + rows, n * EXTRA + HALO * m + e : n * EXTRA + HALO * m + e + 1]
                        for m in range(2 * STENCILS)
                    ]
                    fill(at, cut[:STENCILS], cut[STENCILS:], edge_high, edge_low)
                    at += rows


def stencil_matrix(tables, halos, columns, after):
    rows = tables.shape[1]
    count_r = halos[2].shape[0] // HALO - EXTRA // HALO
    points = jax.ShapeDtypeStruct((count_r * rows, columns), BF16)
    edges = jax.ShapeDtypeStruct((2 * HALO * (rows + count_r), columns), BF16)
    return pl.pallas_call(
        stencil_kernel,
        in_specs=[*[VMEM] * 5, ANY],
        out_specs=[VMEM] * 4,
        out_shape=[points, points, edges, edges],
        scratch_shapes=[pltpu.VMEM((LANES, LANES), F32)],
        compiler_params=pltpu.CompilerParams(vmem_limit_bytes=16 * MIB),
        cost_estimate=pl.CostEstimate(flops=15_000_000, bytes_accessed=6 * MIB, transcendentals=0),
        name="stencil_matrix",
    )(tables, *halos, after)


def last_kernel(
    one, packet, potential, tables, up, down, left, right, high, low,
    split_high, split_low, edge_high, edge_low, own_table, other_table,
    earlier, latest, field, prev, pot, done, sides, table, source, sems,
):
    count_r, rows, width = packet.shape
    steps = count_r // LAST
    is_product = in_product()
    quarter = own_table.shape[1]
    half = quarter // 2
    chips = own_table.shape[0]
    size = LAST * rows

    def field_part(n):
        return field.at[pl.ds(HALO + n * LAST, LAST)]

    def part(n):
        return pl.ds(n * LAST, LAST)

    def cut(n):
        return pl.ds(pl.multiple_of(n * size, size), size)

    def locals_of(n):
        return (
            pltpu.make_async_copy(packet.at[part(n)], prev.at[part(n)], sems.at[0, n]),
            pltpu.make_async_copy(potential.at[part(n)], pot.at[part(n)], sems.at[1, n]),
        )

    def earliers(n):
        return pltpu.make_async_copy(field_part(n), earlier.at[part(n)], sems.at[2, n])

    def latests(n):
        return pltpu.make_async_copy(done.at[part(n)], latest.at[part(n)], sems.at[3, n])

    def put_ends(up_value, down_value):
        for k in range(HALO):
            field[k] = up_value[k * rows : (k + 1) * rows]
            field[HALO + count_r + k] = down_value[k * rows : (k + 1) * rows]

    for n in range(steps):
        for copy in locals_of(n):
            copy.start()

    @pl.when(is_product)
    def _():
        for side, ref in enumerate((own_table, other_table)):
            for k in range(chips):
                at = (side * chips + k) * half
                for band in range(2):
                    upper, lower = halves(ref[k, band * half : (band + 1) * half])
                    table[2 * band, at : at + half] = upper
                    table[2 * band + 1, at : at + half] = lower
        source[...] = product((edge_high[...], edge_low[...]), table[0], table[1])
        edges = HALO * rows
        columns = HALO * count_r
        put_ends(up[...] + source[:edges], down[...] + source[edges : 2 * edges])
        put_sides(
            sides, left, right, count_r,
            source.at[pl.ds(2 * edges, columns)], source.at[pl.ds(2 * edges + columns, columns)],
        )

        def body(n, carry):
            matrix = (split_high[cut(n)], split_low[cut(n)])
            here = pl.ds(HALO + n * LAST, LAST)
            field[here] = one[part(n)] + product(matrix, table[0], table[1]).reshape(LAST, rows, width)
            done[part(n)] = product(matrix, table[2], table[3]).reshape(LAST, rows, width)
            earliers(n).start()
            return carry

        lax.fori_loop(0, steps, body, 0)

    @pl.when(jnp.logical_not(is_product))
    def _():
        put_ends(up, down)
        put_sides(sides, left, right, count_r)
        done[...] = jnp.zeros_like(done)
        for n in range(steps):
            here = pl.ds(HALO + n * LAST, LAST)
            field[here] = one[part(n)]
            earliers(n).start()

    def put(k, lanes, value):
        done[k, :, lanes] += value

    def body(n, carry):
        for copy in locals_of(n):
            copy.wait()
        advance(n, LAST, field, sides, prev, pot, tables, high, low, put)
        latests(n).start()
        return carry

    lax.fori_loop(0, steps, body, 0)
    for n in range(steps):
        earliers(n).wait()
        latests(n).wait()


def last_iteration(one, packet, potential, tables, halos, high, low, matrices, band_tables):
    count_r, rows, width = packet.shape
    steps = count_r // LAST
    columns = matrices[0].shape[1]
    return pl.pallas_call(
        last_kernel,
        in_specs=[VMEM, HBM, HBM, *[VMEM] * 13],
        out_specs=[HBM, HBM],
        out_shape=[jax.ShapeDtypeStruct(packet.shape, F32)] * 2,
        scratch_shapes=[
            pltpu.VMEM((count_r + 2 * HALO, rows, width), F32),
            pltpu.VMEM(packet.shape, F32),
            pltpu.VMEM(packet.shape, F32),
            pltpu.VMEM(packet.shape, F32),
            pltpu.VMEM((count_r, 8, width), F32),
            pltpu.VMEM((4, columns, width), BF16),
            pltpu.VMEM((2 * HALO * (rows + count_r), width), F32),
            pltpu.SemaphoreType.DMA((4, steps)),
        ],
        compiler_params=pltpu.CompilerParams(vmem_limit_bytes=40 * MIB),
        cost_estimate=pl.CostEstimate(flops=20_000_000_000, bytes_accessed=36 * MIB, transcendentals=0),
        name="last_iteration",
    )(one, packet, potential, tables, *halos, high, low, *matrices, *band_tables)


def neighbours(axis, upward, downward):
    count = lax.axis_size(axis)
    return (
        lax.ppermute(upward, axis, [(i, i + 1) for i in range(count - 1)]),
        lax.ppermute(downward, axis, [(i + 1, i) for i in range(count - 1)]),
    )


def exchange(top, bottom, first, last):
    left, right = neighbours("row", last, first)
    up, down = neighbours("rr", bottom, top)
    return up, down, left, right


def local(packet, previous, potential, rotation, angular, damping, absorber, stencil_index, stencil_weight):
    packet, previous, potential = packet[0], previous[0], potential[0]
    rotation, angular, damping, absorber = rotation[0], angular[0], damping[0], absorber[0]
    count_r, rows, width = packet.shape
    count_rr, count_row = (lax.axis_size(name) for name in ("rr", "row"))
    chips = count_row // CORES
    packet, previous, potential = (in_hbm(value) for value in (packet, previous, potential))
    rotation, damping, absorber = (jnp.swapaxes(value, 0, 1) for value in (rotation, damping, absorber))
    stencil_index, stencil_weight = (jnp.swapaxes(value, 1, 2) for value in (stencil_index, stencil_weight))

    firsts, lasts = band_slabs(rotation, damping, absorber, packet, previous, potential)
    sources = (count_rr - 1) * count_row
    band_left = lax.ppermute(lasts, AXES, [(sources + i, sources + i + 1) for i in range(count_row - 1)])
    band_right = lax.ppermute(firsts, AXES, [(sources + i + 1, sources + i) for i in range(count_row - 1)])

    top, bottom, first, last, tables, high, low = prepare(
        packet, rotation, damping, absorber, stencil_index, stencil_weight, angular, firsts
    )
    table = bands(packet, previous, potential, tables, band_left, band_right, high, low)
    top, bottom, first, last, table = lax.optimization_barrier((top, bottom, first, last, table))
    halos = exchange(top, bottom, first, last)

    one, *edges = first_iteration(packet, previous, potential, tables, halos, high, low, table)

    plane = ("sect", "rr")
    half = count_rr // FAR
    start = count_rr - 1
    entries = [count_rr + (k + 1) * half - 1 for k in range(FAR)]
    crossed = [lax.ppermute(table, plane, [(start, entry)]) for entry in entries]
    *crossed, one = lax.optimization_barrier((*crossed, one))
    piece = sum(crossed)
    arrived = []
    for shift in (1, half - 1, 2):
        pairs = [(entry, entry - (half - 1) + (half - 1 + shift) % half) for entry in entries]
        arrived.append(lax.ppermute(piece, plane, pairs))
    matrices = stencil_matrix(tables, halos, count_row * rows * BAND, piece)
    *arrived, matrices = lax.optimization_barrier((*arrived, matrices))
    spread = piece + sum(arrived)
    line = ("sect", "row")

    def around(shift):
        pairs = []
        for chip in range(chips):
            for core in range(CORES):
                pairs.append(
                    (count_row + chip * CORES + core, count_row + ((chip + shift) % chips) * CORES + core)
                )
        return lax.ppermute(spread, line, pairs)

    rest = [around(1), around(2), around(3)]
    later = exchange(*edges)
    *rest, later = lax.optimization_barrier((*rest, later))
    own = jnp.stack([spread, *rest], axis=0)
    other = lax.ppermute(
        own, line, [(count_row + i, count_row + i + 1 - 2 * (i % CORES)) for i in range(count_row)]
    )
    earlier, latest = last_iteration(
        one, packet, potential, tables, later, high, low, matrices, (own, other)
    )
    return latest[None], earlier[None]


def solution(mesh):
    in_specs = (
        P("sect", "rr", "row", None),
        P("sect", "rr", "row", None),
        P("sect", "rr", "row", None),
        P("sect", "rr", "row"),
        P("sect", None, None),
        P("sect", "rr", "row"),
        P("sect", "rr", "row"),
        P(None, "rr", "row"),
        P(None, "rr", "row"),
    )
    out_specs = (P("sect", "rr", "row", None), P("sect", "rr", "row", None))
    return jax.shard_map(local, mesh=mesh, in_specs=in_specs, out_specs=out_specs, check_vma=False)
```

```python
import functools

import jax
import jax.numpy as jnp
from jax import lax
from jax.experimental import pallas as pl
from jax.experimental.pallas import tpu as pltpu
from jax.sharding import PartitionSpec as P

BAND = 2
STENCILS = 4
HALO = 2
LANES = 128
CHUNK = 16
LAST = 16
CORES = 2
FAR = 2
ROT, RET, INDEX, WEIGHT, TABLES = 0, 1, 2, 6, 10
EXTRA = 2 * STENCILS * HALO
OFBAND = 32
MIB = 1 << 20
F32 = jnp.float32
BF16 = jnp.bfloat16
ANY = pl.BlockSpec(memory_space=pl.ANY)
HBM = pl.BlockSpec(memory_space=pltpu.HBM)
VMEM = pl.BlockSpec(memory_space=pltpu.VMEM)

SIDE1 = -16.0 / 96.0
SIDE2 = 1.0 / 96.0
MIDDLE = 2.0 * 30.0 / 96.0 - 7.5 / 4.0


def halves(value):
    high = value.astype(BF16)
    low = (value - high.astype(F32)).astype(BF16)
    return high, low


def product(left, right_high, right_low):
    high, low = left
    total = jnp.dot(high, right_high, preferred_element_type=F32)
    total += jnp.dot(low, right_high, preferred_element_type=F32)
    return total + jnp.dot(high, right_low, preferred_element_type=F32)


def doubled_hamilton(field, index, start, count, lanes, turned, potential, rotation):
    def at(shift_r, shift_v):
        return field[index + shift_r, pl.ds(start + shift_v, count), lanes]

    middle = at(0, 0)
    near = at(-1, 0) + at(1, 0) + (at(0, -1) + at(0, 1))
    far = at(-2, 0) + at(2, 0) + (at(0, -2) + at(0, 2))
    return (
        SIDE1 * near
        + SIDE2 * far
        + (0.25 * potential + MIDDLE) * middle
        + (0.25 * rotation) * turned
    )


def in_hbm(value):
    return pltpu.with_memory_space_constraint(value, pltpu.HBM)


def holds_bands():
    return (lax.axis_index("sect") == 0) & (lax.axis_index("rr") == lax.axis_size("rr") - 1)


def in_product():
    return lax.axis_index("sect") == 1


def retained_of(damping, absorber):
    return 1.0 - absorber.astype(F32) * (1.0 - damping)


def band_kernel(
    packet, previous, potential, tables, left, right, high, low, out, field, later, turned, held, sems
):
    count_r, rows, width = packet.shape
    base = 16
    wide = rows + 16
    begin = left.shape[0] - OFBAND

    @pl.when(holds_bands())
    def _():
        copies = [
            pltpu.make_async_copy(packet.at[pl.ds(count_r - 6, 6)], field.at[pl.ds(2, 6), pl.ds(base, rows)], sems.at[0]),
            pltpu.make_async_copy(previous.at[pl.ds(count_r - 4, 4)], held.at[0], sems.at[1]),
            pltpu.make_async_copy(potential.at[pl.ds(count_r - 4, 4)], held.at[1], sems.at[2]),
        ]
        later[...] = jnp.zeros_like(later)
        field[0:2] = jnp.zeros_like(field[0:2])
        field[8:10] = jnp.zeros_like(field[8:10])
        for k in range(2, 8):
            field[k, 0:base] = jnp.zeros((base, width), F32)
            field[k, base + rows :] = jnp.zeros((base, width), F32)
        for copy in copies:
            copy.start()
        for k in range(4):
            at = begin + 4 * k
            field[4 + k, base - 4 : base] = left[at : at + 4]
            field[4 + k, base + rows : base + rows + 4] = right[at : at + 4]
        columns = [
            (tables[ROT, :, count_r - 4 + k : count_r - 3 + k], tables[RET, :, count_r - 4 + k : count_r - 3 + k])
            for k in range(4)
        ]
        columns = [tuple(jnp.broadcast_to(c, (rows, LANES)) for c in pair) for pair in columns]
        for copy in copies:
            copy.wait()
        window = field[4:8, base - 8 : base + rows + 8].reshape(4 * wide, width)
        turned[...] = product(halves(window), high[...], low[...])
        for k in range(4):
            rotation, retained = columns[k]
            for at in range(0, width, LANES):
                lanes = slice(at, at + LANES)
                update = doubled_hamilton(
                    field, 4 + k, base, rows, lanes,
                    turned[k * wide + 8 : k * wide + 8 + rows, lanes], held[1, k, :, lanes], rotation,
                ) - retained * held[0, k, :, lanes]
                later[k, base : base + rows, lanes] = retained * update
                if k >= 2:
                    out[(k - 2) * rows : (k - 1) * rows, lanes] = (1.0 - retained) * update
        for k in range(2, 4):
            for slab, place, inside in ((left, base - 8, 6), (right, base + rows, 0)):
                at = begin + 16 + 2 * (k - 2)
                prev, pot, rot, ret = (slab[at + 4 * n : at + 4 * n + 2] for n in range(4))
                update = doubled_hamilton(
                    field, 4 + k, place + inside, 2, slice(None),
                    turned[k * wide + place - base + 8 + inside : k * wide + place - base + 10 + inside], pot, rot,
                ) - ret * prev
                later[k, place + inside : place + inside + 2] = ret * update
        window = later[2:4, base : base + rows].reshape(2 * rows, width)
        turned[0 : 2 * rows] = product(halves(window), high[...], low[...])
        for k in range(2, 4):
            rotation, retained = columns[k]
            for at in range(0, width, LANES):
                lanes = slice(at, at + LANES)
                update = doubled_hamilton(
                    later, k, base, rows, lanes,
                    turned[(k - 2) * rows : (k - 1) * rows, lanes], held[1, k, :, lanes], rotation,
                ) - retained * field[4 + k, base : base + rows, lanes]
                out[k * rows : (k + 1) * rows, lanes] = (1.0 - retained) * update


def bands(packet, previous, potential, tables, left, right, high, low):
    _, rows, width = packet.shape
    return pl.pallas_call(
        band_kernel,
        in_specs=[HBM, HBM, HBM, VMEM, VMEM, VMEM, VMEM, VMEM],
        out_specs=VMEM,
        out_shape=jax.ShapeDtypeStruct((2 * BAND * rows, width), F32),
        scratch_shapes=[
            pltpu.VMEM((10, rows + 32, width), F32),
            pltpu.VMEM((6, rows + 32, width), F32),
            pltpu.VMEM((4 * (rows + 16), width), F32),
            pltpu.VMEM((2, 4, rows, width), F32),
            pltpu.SemaphoreType.DMA((3,)),
        ],
        compiler_params=pltpu.CompilerParams(vmem_limit_bytes=16 * MIB),
        cost_estimate=pl.CostEstimate(flops=400_000_000, bytes_accessed=4 * MIB, transcendentals=0),
        name="both_bands",
    )(packet, previous, potential, tables, left, right, high, low)


def prepare_kernel(
    packet, previous, potential, rotation, damping, absorber, index, weight, angular,
    top, bottom, first, last, tables, high, low,
    ends, sides, others, factors, masks, indices, weights, matrix, sems,
):
    count_r, rows, width = packet.shape
    small = [
        pltpu.make_async_copy(rotation, factors.at[0], sems.at[0]),
        pltpu.make_async_copy(damping, factors.at[1], sems.at[1]),
        pltpu.make_async_copy(absorber, masks, sems.at[2]),
        pltpu.make_async_copy(index, indices, sems.at[3]),
        pltpu.make_async_copy(weight, weights, sems.at[4]),
    ]
    copies = [
        pltpu.make_async_copy(packet.at[:, pl.ds(0, 8)], sides.at[0], sems.at[5]),
        pltpu.make_async_copy(packet.at[:, pl.ds(rows - 8, 8)], sides.at[1], sems.at[6]),
        pltpu.make_async_copy(packet.at[pl.ds(0, HALO)], ends.at[0], sems.at[7]),
        pltpu.make_async_copy(packet.at[pl.ds(count_r - HALO, HALO)], ends.at[1], sems.at[8]),
        pltpu.make_async_copy(previous.at[pl.ds(count_r - BAND, BAND)], others.at[0], sems.at[9]),
        pltpu.make_async_copy(potential.at[pl.ds(count_r - BAND, BAND)], others.at[1], sems.at[10]),
        pltpu.make_async_copy(angular, matrix, sems.at[11]),
    ]
    for copy in small + copies:
        copy.start()
    for copy in small:
        copy.wait()
    values = [factors[0], retained_of(factors[1], masks[...])]
    values += [indices[n].astype(F32) for n in range(STENCILS)]
    values += [weights[n] for n in range(STENCILS)]
    for n, value in enumerate(values):
        tables[n] = jnp.concatenate([value, jnp.zeros((rows, LANES - count_r), F32)], axis=1)
    edges = HALO * rows
    columns = HALO * count_r
    lane = lax.broadcasted_iota(jnp.int32, (rows, LANES), 1)
    upper = jnp.zeros((rows, LANES), F32)
    lower = jnp.zeros((rows, LANES), F32)
    for n in range(2 * STENCILS):
        value = tables[INDEX + n]
        at = n * HALO
        here = (lane >= at) & (lane < at + HALO)
        upper = jnp.where(here, pltpu.roll(value, at, 1), upper)
        lower = jnp.where(here, pltpu.roll(value, (at + LANES - (count_r - HALO)) % LANES, 1), lower)
        first[columns + at : columns + at + HALO, 0:LANES] = value[0:HALO]
        last[columns + at : columns + at + HALO, 0:LANES] = value[rows - HALO : rows]
    top[edges : edges + rows, 0:LANES] = upper
    bottom[edges : edges + rows, 0:LANES] = lower
    begin = columns + EXTRA
    for copy in copies:
        copy.wait()
    for out, n, far, near in ((first, 0, 0, 0), (last, 1, 4, rows - 2)):
        for k in range(4):
            out[begin + 4 * k : begin + 4 * k + 4] = sides[n, count_r - 4 + k, far : far + 4]
        for k in range(BAND):
            at = begin + 16 + 2 * k
            column = count_r - BAND + k
            out[at : at + 2] = others[0, k, near : near + 2]
            out[at + 4 : at + 6] = others[1, k, near : near + 2]
            for m in (ROT, RET):
                value = tables[m, near : near + 2, column : column + 1]
                out[at + 8 + 4 * m : at + 10 + 4 * m] = jnp.broadcast_to(value, (2, width))
    for out, n, near in ((first, 0, 0), (last, 1, 8 - HALO)):
        for k in range(count_r):
            for r in range(HALO):
                out[r * count_r + k : r * count_r + k + 1] = sides[n, k, near + r : near + r + 1]
    for out, n in ((top, 0), (bottom, 1)):
        for k in range(HALO):
            out[k * rows : (k + 1) * rows] = ends[n, k]
    high[...], low[...] = halves(matrix[...])


def prepare(packet, previous, potential, rotation, damping, absorber, index, weight, angular):
    count_r, rows, width = packet.shape
    ends = jax.ShapeDtypeStruct((HALO * rows + rows, width), F32)
    sides = jax.ShapeDtypeStruct((HALO * count_r + EXTRA + OFBAND, width), F32)
    part = jax.ShapeDtypeStruct(angular.shape, BF16)
    return pl.pallas_call(
        prepare_kernel,
        in_specs=[HBM] * 9,
        out_specs=[VMEM] * 7,
        out_shape=[ends, ends, sides, sides, jax.ShapeDtypeStruct((TABLES, rows, LANES), F32), part, part],
        scratch_shapes=[
            pltpu.VMEM((2, HALO, rows, width), F32),
            pltpu.VMEM((2, count_r, 8, width), F32),
            pltpu.VMEM((2, BAND, rows, width), F32),
            pltpu.VMEM((2, rows, count_r), F32),
            pltpu.VMEM((rows, count_r), jnp.int32),
            pltpu.VMEM((STENCILS, rows, count_r), jnp.int32),
            pltpu.VMEM((STENCILS, rows, count_r), F32),
            pltpu.VMEM(angular.shape, F32),
            pltpu.SemaphoreType.DMA((12,)),
        ],
        compiler_params=pltpu.CompilerParams(vmem_limit_bytes=16 * MIB),
        cost_estimate=pl.CostEstimate(flops=1_000_000, bytes_accessed=6 * MIB, transcendentals=0),
        name="prepare",
    )(packet, previous, potential, rotation, damping, absorber, index, weight, angular)


def put_sides(sides, left, right, count_r, left_more=None, right_more=None):
    def body(k, carry):
        for r in range(HALO):
            at = pl.ds(r * count_r + k, 1)
            before, behind = left[at], right[at]
            if left_more is not None:
                before, behind = before + left_more[at], behind + right_more[at]
            sides[k, r : r + 1] = behind
            sides[k, 8 - HALO + r : 8 - HALO + r + 1] = before
        return carry

    lax.fori_loop(0, count_r, body, 0, unroll=8)


def advance(step, chunk, field, sides, previous, potential, tables, high, low, put):
    rows = previous.shape[1]
    width = previous.shape[2]
    here = step * chunk
    shift = lax.rem(LANES - here, LANES)
    columns = [pltpu.roll(tables[n], shift, 1) for n in (ROT, RET)]
    window = field[pl.ds(HALO + here, chunk)].reshape(chunk * rows, width)
    split = halves(window)
    wide = 2 * LANES
    for tile in range(0, width, wide):
        turned = product(split, high[:, tile : tile + wide], low[:, tile : tile + wide])
        for k in range(chunk):
            rotation = jnp.broadcast_to(0.25 * columns[0][:, k : k + 1], (rows, LANES))
            retained = jnp.broadcast_to(columns[1][:, k : k + 1], (rows, LANES))
            for at in range(tile, tile + wide, LANES):
                lanes = slice(at, at + LANES)

                def row(shift):
                    return field[HALO + here + k + shift, :, lanes]

                middle = row(0)
                ring = jnp.concatenate([middle, sides[here + k, :, lanes]], axis=0)
                around = [pltpu.roll(ring, s, 0)[:rows] for s in (1, rows + 7, 2, rows + 6)]
                near = row(-1) + row(1) + (around[0] + around[1])
                far = row(-2) + row(2) + (around[2] + around[3])
                update = (
                    SIDE1 * near
                    + SIDE2 * far
                    + (0.25 * potential[here + k, :, lanes] + MIDDLE) * middle
                    + rotation * turned[k * rows : (k + 1) * rows, at - tile : at - tile + LANES]
                    - retained * previous[here + k, :, lanes]
                )
                put(here + k, lanes, retained * update)


def first_kernel(
    packet, previous, potential, tables, up, down, left, right, high, low, after,
    done, top, bottom, first, last, field, prev, pot, sides, sems,
):
    count_r, rows, width = packet.shape
    steps = count_r // CHUNK

    def copies(n):
        part = pl.ds(n * CHUNK, CHUNK)
        return (
            pltpu.make_async_copy(packet.at[part], field.at[pl.ds(HALO + n * CHUNK, CHUNK)], sems.at[0, n]),
            pltpu.make_async_copy(previous.at[part], prev.at[part], sems.at[1, n]),
            pltpu.make_async_copy(potential.at[part], pot.at[part], sems.at[2, n]),
        )

    for n in range(steps):
        for copy in copies(n):
            copy.start()
    for k in range(HALO):
        field[k] = up[k * rows : (k + 1) * rows]
        field[HALO + count_r + k] = down[k * rows : (k + 1) * rows]
    put_sides(sides, left, right, count_r)
    copies(0)[0].wait()

    def put(k, lanes, value):
        done[k, :, lanes] = value

    def body(n, carry):
        @pl.when(n + 1 < steps)
        def _():
            copies(n + 1)[0].wait()

        copies(n)[1].wait()
        copies(n)[2].wait()
        advance(n, CHUNK, field, sides, prev, pot, tables, high, low, put)
        for k in range(CHUNK):
            for r in range(HALO):
                at = pl.ds(r * count_r + n * CHUNK + k, 1)
                first[at] = done[n * CHUNK + k, r : r + 1]
                last[at] = done[n * CHUNK + k, rows - HALO + r : rows - HALO + r + 1]
        return carry

    lax.fori_loop(0, steps, body, 0)
    for k in range(HALO):
        top[k * rows : (k + 1) * rows] = done[k]
        bottom[k * rows : (k + 1) * rows] = done[count_r - HALO + k]


def first_iteration(packet, previous, potential, tables, halos, high, low, after):
    count_r, rows, width = packet.shape
    ends = jax.ShapeDtypeStruct((HALO * rows, width), F32)
    sides = jax.ShapeDtypeStruct((HALO * count_r, width), F32)
    return pl.pallas_call(
        first_kernel,
        in_specs=[HBM, HBM, HBM, *[VMEM] * 7, ANY],
        out_specs=[VMEM] * 5,
        out_shape=[jax.ShapeDtypeStruct(packet.shape, F32), ends, ends, sides, sides],
        scratch_shapes=[
            pltpu.VMEM((count_r + 2 * HALO, rows, width), F32),
            pltpu.VMEM(packet.shape, F32),
            pltpu.VMEM(packet.shape, F32),
            pltpu.VMEM((count_r, 8, width), F32),
            pltpu.SemaphoreType.DMA((3, count_r // CHUNK)),
        ],
        compiler_params=pltpu.CompilerParams(vmem_limit_bytes=28 * MIB),
        cost_estimate=pl.CostEstimate(flops=7_000_000_000, bytes_accessed=20 * MIB, transcendentals=0),
        name="first_iteration",
    )(packet, previous, potential, tables, *halos, high, low, after)


def stencil_kernel(tables, up, down, left, right, after, high, low, edge_high, edge_low, square):
    _, rows, _ = tables.shape
    count_r = high.shape[0] // rows
    width = high.shape[1]
    per = rows * BAND
    shift_owner = per.bit_length() - 1
    chips = width // per // CORES

    def place(value):
        index = value.astype(jnp.int32)
        owner = index >> shift_owner
        inside = index & (per - 1)
        core = (owner & 1) ^ (lax.axis_index("row") & 1)
        chip = ((lax.axis_index("row") >> 1) - (owner >> 1)) & (chips - 1)
        slot = ((core * chips + chip) << shift_owner) + (inside & 1) * rows + (inside >> 1)
        return slot.astype(F32)

    column = lax.broadcasted_iota(jnp.int32, (32, LANES), 1).astype(F32)

    def fill(at, places, weights, high_out, low_out):
        places = [jnp.broadcast_to(p, (32, LANES)) for p in places]
        weights = [jnp.broadcast_to(w, (32, LANES)) for w in weights]
        for tile in range(0, width, LANES):
            here = column + float(tile)
            total = jnp.where(here == places[0], weights[0], 0.0)
            for n in range(1, STENCILS):
                total += jnp.where(here == places[n], weights[n], 0.0)
            upper, lower = halves(total)
            high_out[pl.ds(at, 32), tile : tile + LANES] = upper
            low_out[pl.ds(at, 32), tile : tile + LANES] = lower

    @pl.when(in_product())
    def _():
        places = [place(tables[INDEX + n]) for n in range(STENCILS)]
        weights = [tables[WEIGHT + n] for n in range(STENCILS)]
        group = 8

        def body(step, carry):
            shift = lax.rem(LANES - step * group, LANES)
            moved = [pltpu.roll(value, shift, 1) for value in places + weights]
            for k in range(group):
                cut = [value[:, k : k + 1] for value in moved]
                at = pl.multiple_of((step * group + k) * rows, rows)
                fill(at, cut[:STENCILS], cut[STENCILS:], high, low)
            return carry

        lax.fori_loop(0, count_r // group, body, 0)

        edges = HALO * rows
        at = 0
        for side in (up, down):
            value = side[edges : edges + rows, 0:LANES]
            slots = place(value)
            for e in range(HALO):
                cut = [(slots if m < STENCILS else value)[:, HALO * m + e : HALO * m + e + 1] for m in range(2 * STENCILS)]
                fill(at, cut[:STENCILS], cut[STENCILS:], edge_high, edge_low)
                at += rows
        square[...] = jnp.zeros_like(square)
        for n, side in enumerate((left, right)):
            begin = HALO * count_r
            square[n * EXTRA : n * EXTRA + EXTRA // 2] = place(side[begin : begin + EXTRA // 2, 0:LANES])
            square[n * EXTRA + EXTRA // 2 : (n + 1) * EXTRA] = side[begin + EXTRA // 2 : begin + EXTRA, 0:LANES]
        turned = square[...].T
        for n in range(2):
            for e in range(HALO):
                for begin in range(0, count_r, rows):
                    cut = [
                        turned[begin : begin + rows, n * EXTRA + HALO * m + e : n * EXTRA + HALO * m + e + 1]
                        for m in range(2 * STENCILS)
                    ]
                    fill(at, cut[:STENCILS], cut[STENCILS:], edge_high, edge_low)
                    at += rows


def stencil_matrix(tables, halos, count_r, columns, after):
    rows = tables.shape[1]
    points = jax.ShapeDtypeStruct((count_r * rows, columns), BF16)
    edges = jax.ShapeDtypeStruct((2 * HALO * (rows + count_r), columns), BF16)
    return pl.pallas_call(
        stencil_kernel,
        in_specs=[*[VMEM] * 5, ANY],
        out_specs=[VMEM] * 4,
        out_shape=[points, points, edges, edges],
        scratch_shapes=[pltpu.VMEM((LANES, LANES), F32)],
        compiler_params=pltpu.CompilerParams(vmem_limit_bytes=16 * MIB),
        cost_estimate=pl.CostEstimate(flops=15_000_000, bytes_accessed=6 * MIB, transcendentals=0),
        name="stencil_matrix",
    )(tables, *halos, after)


def last_kernel(
    one, packet, potential, tables, up, down, left, right, high, low,
    split_high, split_low, edge_high, edge_low, own_table, other_table,
    earlier, latest, field, prev, pot, done, sides, table, source, sems,
):
    count_r, rows, width = packet.shape
    steps = count_r // LAST
    is_product = in_product()
    quarter = own_table.shape[1]
    half = quarter // 2
    chips = own_table.shape[0]
    size = LAST * rows

    def field_part(n):
        return field.at[pl.ds(HALO + n * LAST, LAST)]

    def part(n):
        return pl.ds(n * LAST, LAST)

    def cut(n):
        return pl.ds(pl.multiple_of(n * size, size), size)

    def locals_of(n):
        return (
            pltpu.make_async_copy(packet.at[part(n)], prev.at[part(n)], sems.at[0, n]),
            pltpu.make_async_copy(potential.at[part(n)], pot.at[part(n)], sems.at[1, n]),
        )

    def earliers(n):
        return pltpu.make_async_copy(field_part(n), earlier.at[part(n)], sems.at[2, n])

    def latests(n):
        return pltpu.make_async_copy(done.at[part(n)], latest.at[part(n)], sems.at[3, n])

    def put_ends(up_value, down_value):
        for k in range(HALO):
            field[k] = up_value[k * rows : (k + 1) * rows]
            field[HALO + count_r + k] = down_value[k * rows : (k + 1) * rows]

    for n in range(steps):
        for copy in locals_of(n):
            copy.start()

    @pl.when(is_product)
    def _():
        for side, ref in enumerate((own_table, other_table)):
            for k in range(chips):
                at = (side * chips + k) * half
                for band in range(2):
                    upper, lower = halves(ref[k, band * half : (band + 1) * half])
                    table[2 * band, at : at + half] = upper
                    table[2 * band + 1, at : at + half] = lower
        source[...] = product((edge_high[...], edge_low[...]), table[0], table[1])
        edges = HALO * rows
        columns = HALO * count_r
        put_ends(up[...] + source[:edges], down[...] + source[edges : 2 * edges])
        put_sides(
            sides, left, right, count_r,
            source.at[pl.ds(2 * edges, columns)], source.at[pl.ds(2 * edges + columns, columns)],
        )

        def body(n, carry):
            matrix = (split_high[cut(n)], split_low[cut(n)])
            here = pl.ds(HALO + n * LAST, LAST)
            field[here] = one[part(n)] + product(matrix, table[0], table[1]).reshape(LAST, rows, width)
            done[part(n)] = product(matrix, table[2], table[3]).reshape(LAST, rows, width)
            earliers(n).start()
            return carry

        lax.fori_loop(0, steps, body, 0)

    @pl.when(jnp.logical_not(is_product))
    def _():
        put_ends(up, down)
        put_sides(sides, left, right, count_r)
        done[...] = jnp.zeros_like(done)
        for n in range(steps):
            here = pl.ds(HALO + n * LAST, LAST)
            field[here] = one[part(n)]
            earliers(n).start()

    def put(k, lanes, value):
        done[k, :, lanes] += value

    def body(n, carry):
        for copy in locals_of(n):
            copy.wait()
        advance(n, LAST, field, sides, prev, pot, tables, high, low, put)
        latests(n).start()
        return carry

    lax.fori_loop(0, steps, body, 0)
    for n in range(steps):
        earliers(n).wait()
        latests(n).wait()


def last_iteration(one, packet, potential, tables, halos, high, low, matrices, band_tables):
    count_r, rows, width = packet.shape
    steps = count_r // LAST
    columns = matrices[0].shape[1]
    return pl.pallas_call(
        last_kernel,
        in_specs=[VMEM, HBM, HBM, *[VMEM] * 13],
        out_specs=[HBM, HBM],
        out_shape=[jax.ShapeDtypeStruct(packet.shape, F32)] * 2,
        scratch_shapes=[
            pltpu.VMEM((count_r + 2 * HALO, rows, width), F32),
            pltpu.VMEM(packet.shape, F32),
            pltpu.VMEM(packet.shape, F32),
            pltpu.VMEM(packet.shape, F32),
            pltpu.VMEM((count_r, 8, width), F32),
            pltpu.VMEM((4, columns, width), BF16),
            pltpu.VMEM((2 * HALO * (rows + count_r), width), F32),
            pltpu.SemaphoreType.DMA((4, steps)),
        ],
        compiler_params=pltpu.CompilerParams(vmem_limit_bytes=40 * MIB),
        cost_estimate=pl.CostEstimate(flops=20_000_000_000, bytes_accessed=36 * MIB, transcendentals=0),
        name="last_iteration",
    )(one, packet, potential, tables, *halos, high, low, *matrices, *band_tables)


def neighbours(axis, upward, downward):
    count = lax.axis_size(axis)
    return (
        lax.ppermute(upward, axis, [(i, i + 1) for i in range(count - 1)]),
        lax.ppermute(downward, axis, [(i + 1, i) for i in range(count - 1)]),
    )


def exchange(top, bottom, first, last):
    left, right = neighbours("row", last, first)
    up, down = neighbours("rr", bottom, top)
    return up, down, left, right


def local(packet, previous, potential, rotation, angular, damping, absorber, stencil_index, stencil_weight):
    packet, previous, potential = packet[0], previous[0], potential[0]
    rotation, angular, damping, absorber = rotation[0], angular[0], damping[0], absorber[0]
    count_r, rows, width = packet.shape
    count_rr, count_row = (lax.axis_size(name) for name in ("rr", "row"))
    chips = count_row // CORES
    rotation, damping, absorber = (jnp.swapaxes(value, 0, 1) for value in (rotation, damping, absorber))
    stencil_index, stencil_weight = (jnp.swapaxes(value, 1, 2) for value in (stencil_index, stencil_weight))
    packet, previous, potential, rotation, damping, absorber, stencil_index, stencil_weight, angular = (
        in_hbm(value)
        for value in (
            packet, previous, potential, rotation, damping, absorber, stencil_index, stencil_weight, angular
        )
    )

    top, bottom, first, last, tables, high, low = prepare(
        packet, previous, potential, rotation, damping, absorber, stencil_index, stencil_weight, angular
    )
    halos = exchange(top, bottom, first, last)
    table = bands(packet, previous, potential, tables, *halos[2:], high, low)
    one, *edges = first_iteration(packet, previous, potential, tables, halos, high, low, table)

    plane = ("sect", "rr")
    half = count_rr // FAR
    start = count_rr - 1
    entries = [count_rr + (k + 1) * half - 1 for k in range(FAR)]
    crossed = [lax.ppermute(table, plane, [(start, entry)]) for entry in entries]
    *crossed, one = lax.optimization_barrier((*crossed, one))
    piece = sum(crossed)
    arrived = []
    for shift in (1, half - 1, 2):
        pairs = [(entry, entry - (half - 1) + (half - 1 + shift) % half) for entry in entries]
        arrived.append(lax.ppermute(piece, plane, pairs))
    spread = piece + sum(arrived)
    line = ("sect", "row")

    def around(shift):
        pairs = []
        for chip in range(chips):
            for core in range(CORES):
                pairs.append(
                    (count_row + chip * CORES + core, count_row + ((chip + shift) % chips) * CORES + core)
                )
        return lax.ppermute(spread, line, pairs)

    rest = [around(1), around(2), around(3)]
    later = exchange(*edges)
    matrices = stencil_matrix(tables, halos, count_r, count_row * rows * BAND, spread)
    *rest, later, matrices = lax.optimization_barrier((*rest, later, matrices))
    own = jnp.stack([spread, *rest], axis=0)
    other = lax.ppermute(
        own, line, [(count_row + i, count_row + i + 1 - 2 * (i % CORES)) for i in range(count_row)]
    )
    earlier, latest = last_iteration(
        one, packet, potential, tables, later, high, low, matrices, (own, other)
    )
    return latest[None], earlier[None]


def solution(mesh):
    in_specs = (
        P("sect", "rr", "row", None),
        P("sect", "rr", "row", None),
        P("sect", "rr", "row", None),
        P("sect", "rr", "row"),
        P("sect", None, None),
        P("sect", "rr", "row"),
        P("sect", "rr", "row"),
        P(None, "rr", "row"),
        P(None, "rr", "row"),
    )
    out_specs = (P("sect", "rr", "row", None), P("sect", "rr", "row", None))
    return jax.shard_map(local, mesh=mesh, in_specs=in_specs, out_specs=out_specs, check_vma=False)
```

```python
import functools

import jax
import jax.numpy as jnp
from jax import lax
from jax.experimental import pallas as pl
from jax.experimental.pallas import tpu as pltpu
from jax.sharding import PartitionSpec as P

BAND = 2
STENCILS = 4
HALO = 2
LANES = 128
CHUNK = 16
LAST = 16
CORES = 2
FAR = 2
ROT, RET, INDEX, WEIGHT, TABLES = 0, 1, 2, 6, 10
EXTRA = 2 * STENCILS * HALO
OFBAND = 32
MIB = 1 << 20
F32 = jnp.float32
BF16 = jnp.bfloat16
ANY = pl.BlockSpec(memory_space=pl.ANY)
HBM = pl.BlockSpec(memory_space=pltpu.HBM)
VMEM = pl.BlockSpec(memory_space=pltpu.VMEM)

SIDE1 = -16.0 / 96.0
SIDE2 = 1.0 / 96.0
MIDDLE = 2.0 * 30.0 / 96.0 - 7.5 / 4.0


def halves(value):
    high = value.astype(BF16)
    low = (value - high.astype(F32)).astype(BF16)
    return high, low


def product(left, right_high, right_low):
    high, low = left
    total = jnp.dot(high, right_high, preferred_element_type=F32)
    total += jnp.dot(low, right_high, preferred_element_type=F32)
    return total + jnp.dot(high, right_low, preferred_element_type=F32)


def doubled_hamilton(field, index, start, count, lanes, turned, potential, rotation):
    def at(shift_r, shift_v):
        return field[index + shift_r, pl.ds(start + shift_v, count), lanes]

    middle = at(0, 0)
    near = at(-1, 0) + at(1, 0) + (at(0, -1) + at(0, 1))
    far = at(-2, 0) + at(2, 0) + (at(0, -2) + at(0, 2))
    return (
        SIDE1 * near
        + SIDE2 * far
        + (0.25 * potential + MIDDLE) * middle
        + (0.25 * rotation) * turned
    )


def in_hbm(value):
    return pltpu.with_memory_space_constraint(value, pltpu.HBM)


def holds_bands():
    return (lax.axis_index("sect") == 0) & (lax.axis_index("rr") == lax.axis_size("rr") - 1)


def in_product():
    return lax.axis_index("sect") == 1


def retained_of(damping, absorber):
    return 1.0 - absorber.astype(F32) * (1.0 - damping)


def band_kernel(
    packet, previous, potential, tables, left, right, high, low, out, field, later, turned, held, sems
):
    count_r, rows, width = packet.shape
    base = 16
    wide = rows + 16
    begin = left.shape[0] - OFBAND

    @pl.when(holds_bands())
    def _():
        copies = [
            pltpu.make_async_copy(packet.at[pl.ds(count_r - 6, 6)], field.at[pl.ds(2, 6), pl.ds(base, rows)], sems.at[0]),
            pltpu.make_async_copy(previous.at[pl.ds(count_r - 4, 4)], held.at[0], sems.at[1]),
            pltpu.make_async_copy(potential.at[pl.ds(count_r - 4, 4)], held.at[1], sems.at[2]),
        ]
        later[...] = jnp.zeros_like(later)
        field[0:2] = jnp.zeros_like(field[0:2])
        field[8:10] = jnp.zeros_like(field[8:10])
        for k in range(2, 8):
            field[k, 0:base] = jnp.zeros((base, width), F32)
            field[k, base + rows :] = jnp.zeros((base, width), F32)
        for copy in copies:
            copy.start()
        for k in range(4):
            at = begin + 4 * k
            field[4 + k, base - 4 : base] = left[at : at + 4]
            field[4 + k, base + rows : base + rows + 4] = right[at : at + 4]
        columns = [
            (tables[ROT, :, count_r - 4 + k : count_r - 3 + k], tables[RET, :, count_r - 4 + k : count_r - 3 + k])
            for k in range(4)
        ]
        columns = [tuple(jnp.broadcast_to(c, (rows, LANES)) for c in pair) for pair in columns]
        for copy in copies:
            copy.wait()
        window = field[4:8, base - 8 : base + rows + 8].reshape(4 * wide, width)
        turned[...] = product(halves(window), high[...], low[...])
        for k in range(4):
            rotation, retained = columns[k]
            for at in range(0, width, LANES):
                lanes = slice(at, at + LANES)
                update = doubled_hamilton(
                    field, 4 + k, base, rows, lanes,
                    turned[k * wide + 8 : k * wide + 8 + rows, lanes], held[1, k, :, lanes], rotation,
                ) - retained * held[0, k, :, lanes]
                later[k, base : base + rows, lanes] = retained * update
                if k >= 2:
                    out[(k - 2) * rows : (k - 1) * rows, lanes] = (1.0 - retained) * update
        for k in range(2, 4):
            for slab, place, inside in ((left, base - 8, 6), (right, base + rows, 0)):
                at = begin + 16 + 2 * (k - 2)
                prev, pot, rot, ret = (slab[at + 4 * n : at + 4 * n + 2] for n in range(4))
                update = doubled_hamilton(
                    field, 4 + k, place + inside, 2, slice(None),
                    turned[k * wide + place - base + 8 + inside : k * wide + place - base + 10 + inside], pot, rot,
                ) - ret * prev
                later[k, place + inside : place + inside + 2] = ret * update
        window = later[2:4, base : base + rows].reshape(2 * rows, width)
        turned[0 : 2 * rows] = product(halves(window), high[...], low[...])
        for k in range(2, 4):
            rotation, retained = columns[k]
            for at in range(0, width, LANES):
                lanes = slice(at, at + LANES)
                update = doubled_hamilton(
                    later, k, base, rows, lanes,
                    turned[(k - 2) * rows : (k - 1) * rows, lanes], held[1, k, :, lanes], rotation,
                ) - retained * field[4 + k, base : base + rows, lanes]
                out[k * rows : (k + 1) * rows, lanes] = (1.0 - retained) * update


def bands(packet, previous, potential, tables, left, right, high, low):
    _, rows, width = packet.shape
    return pl.pallas_call(
        band_kernel,
        in_specs=[HBM, HBM, HBM, VMEM, VMEM, VMEM, VMEM, VMEM],
        out_specs=VMEM,
        out_shape=jax.ShapeDtypeStruct((2 * BAND * rows, width), F32),
        scratch_shapes=[
            pltpu.VMEM((10, rows + 32, width), F32),
            pltpu.VMEM((6, rows + 32, width), F32),
            pltpu.VMEM((4 * (rows + 16), width), F32),
            pltpu.VMEM((2, 4, rows, width), F32),
            pltpu.SemaphoreType.DMA((3,)),
        ],
        compiler_params=pltpu.CompilerParams(vmem_limit_bytes=16 * MIB),
        cost_estimate=pl.CostEstimate(flops=400_000_000, bytes_accessed=4 * MIB, transcendentals=0),
        name="both_bands",
    )(packet, previous, potential, tables, left, right, high, low)


def prepare_kernel(
    packet, previous, potential, rotation, damping, absorber, index, weight, angular,
    top, bottom, first, last, tables, high, low,
    ends, sides, others, factors, masks, indices, weights, matrix, sems,
):
    count_r, rows, width = packet.shape
    small = [
        pltpu.make_async_copy(rotation, factors.at[0], sems.at[0]),
        pltpu.make_async_copy(damping, factors.at[1], sems.at[1]),
        pltpu.make_async_copy(absorber, masks, sems.at[2]),
        pltpu.make_async_copy(index, indices, sems.at[3]),
        pltpu.make_async_copy(weight, weights, sems.at[4]),
    ]
    copies = [
        pltpu.make_async_copy(packet.at[:, pl.ds(0, 8)], sides.at[0], sems.at[5]),
        pltpu.make_async_copy(packet.at[:, pl.ds(rows - 8, 8)], sides.at[1], sems.at[6]),
        pltpu.make_async_copy(packet.at[pl.ds(0, HALO)], ends.at[0], sems.at[7]),
        pltpu.make_async_copy(packet.at[pl.ds(count_r - HALO, HALO)], ends.at[1], sems.at[8]),
        pltpu.make_async_copy(previous.at[pl.ds(count_r - BAND, BAND)], others.at[0], sems.at[9]),
        pltpu.make_async_copy(potential.at[pl.ds(count_r - BAND, BAND)], others.at[1], sems.at[10]),
        pltpu.make_async_copy(angular, matrix, sems.at[11]),
    ]
    for copy in small + copies:
        copy.start()
    for copy in small:
        copy.wait()
    values = [factors[0], retained_of(factors[1], masks[...])]
    values += [indices[n].astype(F32) for n in range(STENCILS)]
    values += [weights[n] for n in range(STENCILS)]
    for n, value in enumerate(values):
        tables[n] = jnp.concatenate([value, jnp.zeros((rows, LANES - count_r), F32)], axis=1)
    edges = HALO * rows
    columns = HALO * count_r
    lane = lax.broadcasted_iota(jnp.int32, (rows, LANES), 1)
    upper = jnp.zeros((rows, LANES), F32)
    lower = jnp.zeros((rows, LANES), F32)
    for n in range(2 * STENCILS):
        value = tables[INDEX + n]
        at = n * HALO
        here = (lane >= at) & (lane < at + HALO)
        upper = jnp.where(here, pltpu.roll(value, at, 1), upper)
        lower = jnp.where(here, pltpu.roll(value, (at + LANES - (count_r - HALO)) % LANES, 1), lower)
        first[columns + at : columns + at + HALO, 0:LANES] = value[0:HALO]
        last[columns + at : columns + at + HALO, 0:LANES] = value[rows - HALO : rows]
    top[edges : edges + rows, 0:LANES] = upper
    bottom[edges : edges + rows, 0:LANES] = lower
    begin = columns + EXTRA
    for copy in copies:
        copy.wait()
    for out, n, far, near in ((first, 0, 0, 0), (last, 1, 4, rows - 2)):
        for k in range(4):
            out[begin + 4 * k : begin + 4 * k + 4] = sides[n, count_r - 4 + k, far : far + 4]
        for k in range(BAND):
            at = begin + 16 + 2 * k
            column = count_r - BAND + k
            out[at : at + 2] = others[0, k, near : near + 2]
            out[at + 4 : at + 6] = others[1, k, near : near + 2]
            for m in (ROT, RET):
                value = tables[m, near : near + 2, column : column + 1]
                out[at + 8 + 4 * m : at + 10 + 4 * m] = jnp.broadcast_to(value, (2, width))
    for out, n, near in ((first, 0, 0), (last, 1, 8 - HALO)):
        for k in range(count_r):
            for r in range(HALO):
                out[r * count_r + k : r * count_r + k + 1] = sides[n, k, near + r : near + r + 1]
    for out, n in ((top, 0), (bottom, 1)):
        for k in range(HALO):
            out[k * rows : (k + 1) * rows] = ends[n, k]
    high[...], low[...] = halves(matrix[...])


def prepare(packet, previous, potential, rotation, damping, absorber, index, weight, angular):
    count_r, rows, width = packet.shape
    ends = jax.ShapeDtypeStruct((HALO * rows + rows, width), F32)
    sides = jax.ShapeDtypeStruct((HALO * count_r + EXTRA + OFBAND, width), F32)
    part = jax.ShapeDtypeStruct(angular.shape, BF16)
    return pl.pallas_call(
        prepare_kernel,
        in_specs=[HBM] * 9,
        out_specs=[VMEM] * 7,
        out_shape=[ends, ends, sides, sides, jax.ShapeDtypeStruct((TABLES, rows, LANES), F32), part, part],
        scratch_shapes=[
            pltpu.VMEM((2, HALO, rows, width), F32),
            pltpu.VMEM((2, count_r, 8, width), F32),
            pltpu.VMEM((2, BAND, rows, width), F32),
            pltpu.VMEM((2, rows, count_r), F32),
            pltpu.VMEM((rows, count_r), jnp.int32),
            pltpu.VMEM((STENCILS, rows, count_r), jnp.int32),
            pltpu.VMEM((STENCILS, rows, count_r), F32),
            pltpu.VMEM(angular.shape, F32),
            pltpu.SemaphoreType.DMA((12,)),
        ],
        compiler_params=pltpu.CompilerParams(vmem_limit_bytes=16 * MIB),
        cost_estimate=pl.CostEstimate(flops=1_000_000, bytes_accessed=6 * MIB, transcendentals=0),
        name="prepare",
    )(packet, previous, potential, rotation, damping, absorber, index, weight, angular)


def put_sides(sides, left, right, count_r, left_more=None, right_more=None):
    def body(k, carry):
        for r in range(HALO):
            at = pl.ds(r * count_r + k, 1)
            before, behind = left[at], right[at]
            if left_more is not None:
                before, behind = before + left_more[at], behind + right_more[at]
            sides[k, r : r + 1] = behind
            sides[k, 8 - HALO + r : 8 - HALO + r + 1] = before
        return carry

    lax.fori_loop(0, count_r, body, 0, unroll=8)


def advance(step, chunk, field, sides, previous, potential, tables, high, low, put):
    rows = previous.shape[1]
    width = previous.shape[2]
    here = step * chunk
    shift = lax.rem(LANES - here, LANES)
    columns = [pltpu.roll(tables[n], shift, 1) for n in (ROT, RET)]
    window = field[pl.ds(HALO + here, chunk)].reshape(chunk * rows, width)
    split = halves(window)
    wide = 2 * LANES
    for tile in range(0, width, wide):
        turned = product(split, high[:, tile : tile + wide], low[:, tile : tile + wide])
        for k in range(chunk):
            rotation = jnp.broadcast_to(0.25 * columns[0][:, k : k + 1], (rows, LANES))
            retained = jnp.broadcast_to(columns[1][:, k : k + 1], (rows, LANES))
            for at in range(tile, tile + wide, LANES):
                lanes = slice(at, at + LANES)

                def row(shift):
                    return field[HALO + here + k + shift, :, lanes]

                middle = row(0)
                ring = jnp.concatenate([middle, sides[here + k, :, lanes]], axis=0)
                around = [pltpu.roll(ring, s, 0)[:rows] for s in (1, rows + 7, 2, rows + 6)]
                near = row(-1) + row(1) + (around[0] + around[1])
                far = row(-2) + row(2) + (around[2] + around[3])
                update = (
                    SIDE1 * near
                    + SIDE2 * far
                    + (0.25 * potential[here + k, :, lanes] + MIDDLE) * middle
                    + rotation * turned[k * rows : (k + 1) * rows, at - tile : at - tile + LANES]
                    - retained * previous[here + k, :, lanes]
                )
                put(here + k, lanes, retained * update)


def first_kernel(
    packet, previous, potential, tables, up, down, left, right, high, low, after,
    done, top, bottom, first, last, field, prev, pot, sides, sems,
):
    count_r, rows, width = packet.shape
    steps = count_r // CHUNK

    def copies(n):
        part = pl.ds(n * CHUNK, CHUNK)
        return (
            pltpu.make_async_copy(packet.at[part], field.at[pl.ds(HALO + n * CHUNK, CHUNK)], sems.at[0, n]),
            pltpu.make_async_copy(previous.at[part], prev.at[part], sems.at[1, n]),
            pltpu.make_async_copy(potential.at[part], pot.at[part], sems.at[2, n]),
        )

    for n in range(steps):
        for copy in copies(n):
            copy.start()
    for k in range(HALO):
        field[k] = up[k * rows : (k + 1) * rows]
        field[HALO + count_r + k] = down[k * rows : (k + 1) * rows]
    put_sides(sides, left, right, count_r)
    copies(0)[0].wait()

    def put(k, lanes, value):
        done[k, :, lanes] = value

    def body(n, carry):
        @pl.when(n + 1 < steps)
        def _():
            copies(n + 1)[0].wait()

        copies(n)[1].wait()
        copies(n)[2].wait()
        advance(n, CHUNK, field, sides, prev, pot, tables, high, low, put)
        for k in range(CHUNK):
            for r in range(HALO):
                at = pl.ds(r * count_r + n * CHUNK + k, 1)
                first[at] = done[n * CHUNK + k, r : r + 1]
                last[at] = done[n * CHUNK + k, rows - HALO + r : rows - HALO + r + 1]
        return carry

    lax.fori_loop(0, steps, body, 0)
    for k in range(HALO):
        top[k * rows : (k + 1) * rows] = done[k]
        bottom[k * rows : (k + 1) * rows] = done[count_r - HALO + k]


def first_iteration(packet, previous, potential, tables, halos, high, low, after):
    count_r, rows, width = packet.shape
    ends = jax.ShapeDtypeStruct((HALO * rows, width), F32)
    sides = jax.ShapeDtypeStruct((HALO * count_r, width), F32)
    return pl.pallas_call(
        first_kernel,
        in_specs=[HBM, HBM, HBM, *[VMEM] * 7, ANY],
        out_specs=[VMEM] * 5,
        out_shape=[jax.ShapeDtypeStruct(packet.shape, F32), ends, ends, sides, sides],
        scratch_shapes=[
            pltpu.VMEM((count_r + 2 * HALO, rows, width), F32),
            pltpu.VMEM(packet.shape, F32),
            pltpu.VMEM(packet.shape, F32),
            pltpu.VMEM((count_r, 8, width), F32),
            pltpu.SemaphoreType.DMA((3, count_r // CHUNK)),
        ],
        compiler_params=pltpu.CompilerParams(vmem_limit_bytes=28 * MIB),
        cost_estimate=pl.CostEstimate(flops=7_000_000_000, bytes_accessed=20 * MIB, transcendentals=0),
        name="first_iteration",
    )(packet, previous, potential, tables, *halos, high, low, after)


def slot_of(value, rows, width):
    per = rows * BAND
    shift_owner = per.bit_length() - 1
    chips = width // per // CORES
    row = lax.axis_index("row")
    index = value.astype(jnp.int32)
    owner = index >> shift_owner
    inside = index & (per - 1)
    core = (owner & 1) ^ (row & 1)
    chip = ((row >> 1) - (owner >> 1)) & (chips - 1)
    slot = ((core * chips + chip) << shift_owner) + (inside & 1) * rows + (inside >> 1)
    return slot.astype(F32)


def fill_rows(at, cut, rows, high, low):
    column = lax.broadcasted_iota(jnp.int32, (rows, LANES), 1).astype(F32)
    cut = [jnp.broadcast_to(value, (rows, LANES)) for value in cut]
    for tile in range(0, high.shape[1], LANES):
        here = column + float(tile)
        total = jnp.where(here == cut[0], cut[STENCILS], 0.0)
        for n in range(1, STENCILS):
            total += jnp.where(here == cut[n], cut[STENCILS + n], 0.0)
        upper, lower = halves(total)
        high[pl.ds(at, rows), tile : tile + LANES] = upper
        low[pl.ds(at, rows), tile : tile + LANES] = lower


def stencil_kernel(tables, after, high, low):
    _, rows, _ = tables.shape
    count_r = high.shape[0] // rows
    group = 8

    @pl.when(in_product())
    def _():
        values = [slot_of(tables[INDEX + n], rows, high.shape[1]) for n in range(STENCILS)]
        values += [tables[WEIGHT + n] for n in range(STENCILS)]

        def body(step, carry):
            shift = lax.rem(LANES - step * group, LANES)
            moved = [pltpu.roll(value, shift, 1) for value in values]
            for k in range(group):
                at = pl.multiple_of((step * group + k) * rows, rows)
                fill_rows(at, [value[:, k : k + 1] for value in moved], rows, high, low)
            return carry

        lax.fori_loop(0, count_r // group, body, 0)


def stencil_matrix(tables, count_r, columns, after):
    rows = tables.shape[1]
    points = jax.ShapeDtypeStruct((count_r * rows, columns), BF16)
    return pl.pallas_call(
        stencil_kernel,
        in_specs=[VMEM, ANY],
        out_specs=[VMEM] * 2,
        out_shape=[points, points],
        compiler_params=pltpu.CompilerParams(vmem_limit_bytes=16 * MIB),
        cost_estimate=pl.CostEstimate(flops=15_000_000, bytes_accessed=6 * MIB, transcendentals=0),
        name="stencil_matrix",
    )(tables, after)


def stencil_edge_kernel(up, down, left, right, after, high, low, square, *, rows, count_r):
    @pl.when(in_product())
    def _():
        edges = HALO * rows
        at = 0
        for side in (up, down):
            value = side[edges : edges + rows, 0:LANES]
            slots = slot_of(value, rows, high.shape[1])
            for e in range(HALO):
                cut = [
                    (slots if m < STENCILS else value)[:, HALO * m + e : HALO * m + e + 1]
                    for m in range(2 * STENCILS)
                ]
                fill_rows(at, cut, rows, high, low)
                at += rows
        square[...] = jnp.zeros_like(square)
        part = EXTRA // 2
        for n, side in enumerate((left, right)):
            begin = HALO * count_r
            square[n * EXTRA : n * EXTRA + part] = slot_of(side[begin : begin + part, 0:LANES], rows, high.shape[1])
            square[n * EXTRA + part : (n + 1) * EXTRA] = side[begin + part : begin + EXTRA, 0:LANES]
        turned = square[...].T
        for n in range(2):
            for e in range(HALO):
                for begin in range(0, count_r, rows):
                    cut = [
                        turned[begin : begin + rows, n * EXTRA + HALO * m + e : n * EXTRA + HALO * m + e + 1]
                        for m in range(2 * STENCILS)
                    ]
                    fill_rows(at, cut, rows, high, low)
                    at += rows


def stencil_edges(halos, rows, count_r, columns, after):
    points = jax.ShapeDtypeStruct((2 * HALO * (rows + count_r), columns), BF16)
    return pl.pallas_call(
        functools.partial(stencil_edge_kernel, rows=rows, count_r=count_r),
        in_specs=[*[VMEM] * 4, ANY],
        out_specs=[VMEM] * 2,
        out_shape=[points, points],
        scratch_shapes=[pltpu.VMEM((LANES, LANES), F32)],
        compiler_params=pltpu.CompilerParams(vmem_limit_bytes=16 * MIB),
        cost_estimate=pl.CostEstimate(flops=2_000_000, bytes_accessed=2 * MIB, transcendentals=0),
        name="stencil_edges",
    )(*halos, after)


def last_kernel(
    one, packet, potential, tables, up, down, left, right, high, low,
    split_high, split_low, edge_high, edge_low, own_table, other_table,
    earlier, latest, field, prev, pot, done, sides, table, source, sems,
):
    count_r, rows, width = packet.shape
    steps = count_r // LAST
    is_product = in_product()
    quarter = own_table.shape[1]
    half = quarter // 2
    chips = own_table.shape[0]
    size = LAST * rows

    def field_part(n):
        return field.at[pl.ds(HALO + n * LAST, LAST)]

    def part(n):
        return pl.ds(n * LAST, LAST)

    def cut(n):
        return pl.ds(pl.multiple_of(n * size, size), size)

    def locals_of(n):
        return (
            pltpu.make_async_copy(packet.at[part(n)], prev.at[part(n)], sems.at[0, n]),
            pltpu.make_async_copy(potential.at[part(n)], pot.at[part(n)], sems.at[1, n]),
        )

    def earliers(n):
        return pltpu.make_async_copy(field_part(n), earlier.at[part(n)], sems.at[2, n])

    def latests(n):
        return pltpu.make_async_copy(done.at[part(n)], latest.at[part(n)], sems.at[3, n])

    def put_ends(up_value, down_value):
        for k in range(HALO):
            field[k] = up_value[k * rows : (k + 1) * rows]
            field[HALO + count_r + k] = down_value[k * rows : (k + 1) * rows]

    for n in range(steps):
        for copy in locals_of(n):
            copy.start()

    @pl.when(is_product)
    def _():
        for side, ref in enumerate((own_table, other_table)):
            for k in range(chips):
                at = (side * chips + k) * half
                for band in range(2):
                    upper, lower = halves(ref[k, band * half : (band + 1) * half])
                    table[2 * band, at : at + half] = upper
                    table[2 * band + 1, at : at + half] = lower
        source[...] = product((edge_high[...], edge_low[...]), table[0], table[1])
        edges = HALO * rows
        columns = HALO * count_r
        put_ends(up[...] + source[:edges], down[...] + source[edges : 2 * edges])
        put_sides(
            sides, left, right, count_r,
            source.at[pl.ds(2 * edges, columns)], source.at[pl.ds(2 * edges + columns, columns)],
        )

        def body(n, carry):
            matrix = (split_high[cut(n)], split_low[cut(n)])
            here = pl.ds(HALO + n * LAST, LAST)
            field[here] = one[part(n)] + product(matrix, table[0], table[1]).reshape(LAST, rows, width)
            done[part(n)] = product(matrix, table[2], table[3]).reshape(LAST, rows, width)
            earliers(n).start()
            return carry

        lax.fori_loop(0, steps, body, 0)

    @pl.when(jnp.logical_not(is_product))
    def _():
        put_ends(up, down)
        put_sides(sides, left, right, count_r)
        done[...] = jnp.zeros_like(done)
        for n in range(steps):
            here = pl.ds(HALO + n * LAST, LAST)
            field[here] = one[part(n)]
            earliers(n).start()

    def put(k, lanes, value):
        done[k, :, lanes] += value

    def body(n, carry):
        for copy in locals_of(n):
            copy.wait()
        advance(n, LAST, field, sides, prev, pot, tables, high, low, put)
        latests(n).start()
        return carry

    lax.fori_loop(0, steps, body, 0)
    for n in range(steps):
        earliers(n).wait()
        latests(n).wait()


def last_iteration(one, packet, potential, tables, halos, high, low, matrices, band_tables):
    count_r, rows, width = packet.shape
    steps = count_r // LAST
    columns = matrices[0].shape[1]
    return pl.pallas_call(
        last_kernel,
        in_specs=[VMEM, HBM, HBM, *[VMEM] * 13],
        out_specs=[HBM, HBM],
        out_shape=[jax.ShapeDtypeStruct(packet.shape, F32)] * 2,
        scratch_shapes=[
            pltpu.VMEM((count_r + 2 * HALO, rows, width), F32),
            pltpu.VMEM(packet.shape, F32),
            pltpu.VMEM(packet.shape, F32),
            pltpu.VMEM(packet.shape, F32),
            pltpu.VMEM((count_r, 8, width), F32),
            pltpu.VMEM((4, columns, width), BF16),
            pltpu.VMEM((2 * HALO * (rows + count_r), width), F32),
            pltpu.SemaphoreType.DMA((4, steps)),
        ],
        compiler_params=pltpu.CompilerParams(vmem_limit_bytes=40 * MIB),
        cost_estimate=pl.CostEstimate(flops=20_000_000_000, bytes_accessed=36 * MIB, transcendentals=0),
        name="last_iteration",
    )(one, packet, potential, tables, *halos, high, low, *matrices, *band_tables)


def neighbours(axis, upward, downward):
    count = lax.axis_size(axis)
    return (
        lax.ppermute(upward, axis, [(i, i + 1) for i in range(count - 1)]),
        lax.ppermute(downward, axis, [(i + 1, i) for i in range(count - 1)]),
    )


def exchange(top, bottom, first, last):
    left, right = neighbours("row", last, first)
    up, down = neighbours("rr", bottom, top)
    return up, down, left, right


def local(packet, previous, potential, rotation, angular, damping, absorber, stencil_index, stencil_weight):
    packet, previous, potential = packet[0], previous[0], potential[0]
    rotation, angular, damping, absorber = rotation[0], angular[0], damping[0], absorber[0]
    count_r, rows, width = packet.shape
    count_rr, count_row = (lax.axis_size(name) for name in ("rr", "row"))
    chips = count_row // CORES
    rotation, damping, absorber = (jnp.swapaxes(value, 0, 1) for value in (rotation, damping, absorber))
    stencil_index, stencil_weight = (jnp.swapaxes(value, 1, 2) for value in (stencil_index, stencil_weight))
    packet, previous, potential, rotation, damping, absorber, stencil_index, stencil_weight, angular = (
        in_hbm(value)
        for value in (
            packet, previous, potential, rotation, damping, absorber, stencil_index, stencil_weight, angular
        )
    )

    top, bottom, first, last, tables, high, low = prepare(
        packet, previous, potential, rotation, damping, absorber, stencil_index, stencil_weight, angular
    )
    halos = exchange(top, bottom, first, last)
    table = bands(packet, previous, potential, tables, *halos[2:], high, low)

    columns = count_row * rows * BAND
    plane = ("sect", "rr")
    half = count_rr // FAR
    start = count_rr - 1
    entries = [count_rr + (k + 1) * half - 1 for k in range(FAR)]
    crossed = [lax.ppermute(table, plane, [(start, entry)]) for entry in entries]
    matrix = stencil_matrix(tables, count_r, columns, table)
    *crossed, matrix = lax.optimization_barrier((*crossed, matrix))
    piece = sum(crossed)
    arrived = []
    for shift in (1, half - 1, 2):
        pairs = [(entry, entry - (half - 1) + (half - 1 + shift) % half) for entry in entries]
        arrived.append(lax.ppermute(piece, plane, pairs))
    one, *edges = first_iteration(packet, previous, potential, tables, halos, high, low, piece)
    *arrived, one, edges = lax.optimization_barrier((*arrived, one, edges))
    spread = piece + sum(arrived)
    line = ("sect", "row")

    def around(shift):
        pairs = []
        for chip in range(chips):
            for core in range(CORES):
                pairs.append(
                    (count_row + chip * CORES + core, count_row + ((chip + shift) % chips) * CORES + core)
                )
        return lax.ppermute(spread, line, pairs)

    rest = [around(1), around(2), around(3)]
    edge_matrix = stencil_edges(halos, rows, count_r, columns, spread)
    rest[-1], edge_matrix, edges = lax.optimization_barrier((rest[-1], edge_matrix, edges))
    later = exchange(*edges)
    *rest, later = lax.optimization_barrier((*rest, later))
    own = jnp.stack([spread, *rest], axis=0)
    other = lax.ppermute(
        own, line, [(count_row + i, count_row + i + 1 - 2 * (i % CORES)) for i in range(count_row)]
    )
    earlier, latest = last_iteration(
        one, packet, potential, tables, later, high, low, (*matrix, *edge_matrix), (own, other)
    )
    return latest[None], earlier[None]


def solution(mesh):
    in_specs = (
        P("sect", "rr", "row", None),
        P("sect", "rr", "row", None),
        P("sect", "rr", "row", None),
        P("sect", "rr", "row"),
        P("sect", None, None),
        P("sect", "rr", "row"),
        P("sect", "rr", "row"),
        P(None, "rr", "row"),
        P(None, "rr", "row"),
    )
    out_specs = (P("sect", "rr", "row", None), P("sect", "rr", "row", None))
    return jax.shard_map(local, mesh=mesh, in_specs=in_specs, out_specs=out_specs, check_vma=False)
```

```python
import functools

import jax
import jax.numpy as jnp
from jax import lax
from jax.experimental import pallas as pl
from jax.experimental.pallas import tpu as pltpu
from jax.sharding import PartitionSpec as P

BAND = 2
STENCILS = 4
HALO = 2
LANES = 128
CHUNK = 16
LAST = 16
CORES = 2
FAR = 2
ROT, RET, INDEX, WEIGHT, TABLES = 0, 1, 2, 6, 10
EXTRA = 2 * STENCILS * HALO
OFBAND = 32
MIB = 1 << 20
F32 = jnp.float32
BF16 = jnp.bfloat16
ANY = pl.BlockSpec(memory_space=pl.ANY)
HBM = pl.BlockSpec(memory_space=pltpu.HBM)
VMEM = pl.BlockSpec(memory_space=pltpu.VMEM)

SIDE1 = -16.0 / 96.0
SIDE2 = 1.0 / 96.0
MIDDLE = 2.0 * 30.0 / 96.0 - 7.5 / 4.0


def halves(value):
    high = value.astype(BF16)
    low = (value - high.astype(F32)).astype(BF16)
    return high, low


def product(left, right_high, right_low):
    high, low = left
    total = jnp.dot(high, right_high, preferred_element_type=F32)
    total += jnp.dot(low, right_high, preferred_element_type=F32)
    return total + jnp.dot(high, right_low, preferred_element_type=F32)


def doubled_hamilton(field, index, start, count, lanes, turned, potential, rotation):
    def at(shift_r, shift_v):
        return field[index + shift_r, pl.ds(start + shift_v, count), lanes]

    middle = at(0, 0)
    near = at(-1, 0) + at(1, 0) + (at(0, -1) + at(0, 1))
    far = at(-2, 0) + at(2, 0) + (at(0, -2) + at(0, 2))
    return (
        SIDE1 * near
        + SIDE2 * far
        + (0.25 * potential + MIDDLE) * middle
        + (0.25 * rotation) * turned
    )


def in_hbm(value):
    return pltpu.with_memory_space_constraint(value, pltpu.HBM)


def holds_bands():
    return (lax.axis_index("sect") == 0) & (lax.axis_index("rr") == lax.axis_size("rr") - 1)


def in_product():
    return lax.axis_index("sect") == 1


def retained_of(damping, absorber):
    return 1.0 - absorber.astype(F32) * (1.0 - damping)


def band_kernel(
    packet, previous, potential, tables, left, right, high, low, out, field, later, turned, held, sems
):
    count_r, rows, width = packet.shape
    base = 16
    wide = rows + 16
    begin = left.shape[0] - OFBAND

    @pl.when(holds_bands())
    def _():
        copies = [
            pltpu.make_async_copy(packet.at[pl.ds(count_r - 6, 6)], field.at[pl.ds(2, 6), pl.ds(base, rows)], sems.at[0]),
            pltpu.make_async_copy(previous.at[pl.ds(count_r - 4, 4)], held.at[0], sems.at[1]),
            pltpu.make_async_copy(potential.at[pl.ds(count_r - 4, 4)], held.at[1], sems.at[2]),
        ]
        later[...] = jnp.zeros_like(later)
        field[0:2] = jnp.zeros_like(field[0:2])
        field[8:10] = jnp.zeros_like(field[8:10])
        for k in range(2, 8):
            field[k, 0:base] = jnp.zeros((base, width), F32)
            field[k, base + rows :] = jnp.zeros((base, width), F32)
        for copy in copies:
            copy.start()
        for k in range(4):
            at = begin + 4 * k
            field[4 + k, base - 4 : base] = left[at : at + 4]
            field[4 + k, base + rows : base + rows + 4] = right[at : at + 4]
        columns = [
            (tables[ROT, :, count_r - 4 + k : count_r - 3 + k], tables[RET, :, count_r - 4 + k : count_r - 3 + k])
            for k in range(4)
        ]
        columns = [tuple(jnp.broadcast_to(c, (rows, LANES)) for c in pair) for pair in columns]
        for copy in copies:
            copy.wait()
        window = field[4:8, base - 8 : base + rows + 8].reshape(4 * wide, width)
        turned[...] = product(halves(window), high[...], low[...])
        for k in range(4):
            rotation, retained = columns[k]
            for at in range(0, width, LANES):
                lanes = slice(at, at + LANES)
                update = doubled_hamilton(
                    field, 4 + k, base, rows, lanes,
                    turned[k * wide + 8 : k * wide + 8 + rows, lanes], held[1, k, :, lanes], rotation,
                ) - retained * held[0, k, :, lanes]
                later[k, base : base + rows, lanes] = retained * update
                if k >= 2:
                    out[(k - 2) * rows : (k - 1) * rows, lanes] = (1.0 - retained) * update
        for k in range(2, 4):
            for slab, place, inside in ((left, base - 8, 6), (right, base + rows, 0)):
                at = begin + 16 + 2 * (k - 2)
                prev, pot, rot, ret = (slab[at + 4 * n : at + 4 * n + 2] for n in range(4))
                update = doubled_hamilton(
                    field, 4 + k, place + inside, 2, slice(None),
                    turned[k * wide + place - base + 8 + inside : k * wide + place - base + 10 + inside], pot, rot,
                ) - ret * prev
                later[k, place + inside : place + inside + 2] = ret * update
        window = later[2:4, base : base + rows].reshape(2 * rows, width)
        turned[0 : 2 * rows] = product(halves(window), high[...], low[...])
        for k in range(2, 4):
            rotation, retained = columns[k]
            for at in range(0, width, LANES):
                lanes = slice(at, at + LANES)
                update = doubled_hamilton(
                    later, k, base, rows, lanes,
                    turned[(k - 2) * rows : (k - 1) * rows, lanes], held[1, k, :, lanes], rotation,
                ) - retained * field[4 + k, base : base + rows, lanes]
                out[k * rows : (k + 1) * rows, lanes] = (1.0 - retained) * update


def bands(packet, previous, potential, tables, left, right, high, low):
    _, rows, width = packet.shape
    return pl.pallas_call(
        band_kernel,
        in_specs=[HBM, HBM, HBM, VMEM, VMEM, VMEM, VMEM, VMEM],
        out_specs=VMEM,
        out_shape=jax.ShapeDtypeStruct((2 * BAND * rows, width), F32),
        scratch_shapes=[
            pltpu.VMEM((10, rows + 32, width), F32),
            pltpu.VMEM((6, rows + 32, width), F32),
            pltpu.VMEM((4 * (rows + 16), width), F32),
            pltpu.VMEM((2, 4, rows, width), F32),
            pltpu.SemaphoreType.DMA((3,)),
        ],
        compiler_params=pltpu.CompilerParams(vmem_limit_bytes=16 * MIB),
        cost_estimate=pl.CostEstimate(flops=400_000_000, bytes_accessed=4 * MIB, transcendentals=0),
        name="both_bands",
    )(packet, previous, potential, tables, left, right, high, low)


def prepare_kernel(
    packet, previous, potential, rotation, damping, absorber, index, weight, angular,
    top, bottom, first, last, tables, high, low,
    ends, sides, others, factors, masks, indices, weights, matrix, sems,
):
    count_r, rows, width = packet.shape
    small = [
        pltpu.make_async_copy(rotation, factors.at[0], sems.at[0]),
        pltpu.make_async_copy(damping, factors.at[1], sems.at[1]),
        pltpu.make_async_copy(absorber, masks, sems.at[2]),
        pltpu.make_async_copy(index, indices, sems.at[3]),
        pltpu.make_async_copy(weight, weights, sems.at[4]),
    ]
    copies = [
        pltpu.make_async_copy(packet.at[:, pl.ds(0, 8)], sides.at[0], sems.at[5]),
        pltpu.make_async_copy(packet.at[:, pl.ds(rows - 8, 8)], sides.at[1], sems.at[6]),
        pltpu.make_async_copy(packet.at[pl.ds(0, HALO)], ends.at[0], sems.at[7]),
        pltpu.make_async_copy(packet.at[pl.ds(count_r - HALO, HALO)], ends.at[1], sems.at[8]),
        pltpu.make_async_copy(previous.at[pl.ds(count_r - BAND, BAND)], others.at[0], sems.at[9]),
        pltpu.make_async_copy(potential.at[pl.ds(count_r - BAND, BAND)], others.at[1], sems.at[10]),
        pltpu.make_async_copy(angular, matrix, sems.at[11]),
    ]
    for copy in small + copies:
        copy.start()
    for copy in small:
        copy.wait()
    values = [factors[0], retained_of(factors[1], masks[...])]
    values += [indices[n].astype(F32) for n in range(STENCILS)]
    values += [weights[n] for n in range(STENCILS)]
    for n, value in enumerate(values):
        tables[n] = jnp.concatenate([value, jnp.zeros((rows, LANES - count_r), F32)], axis=1)
    edges = HALO * rows
    columns = HALO * count_r
    lane = lax.broadcasted_iota(jnp.int32, (rows, LANES), 1)
    upper = jnp.zeros((rows, LANES), F32)
    lower = jnp.zeros((rows, LANES), F32)
    for n in range(2 * STENCILS):
        value = tables[INDEX + n]
        at = n * HALO
        here = (lane >= at) & (lane < at + HALO)
        upper = jnp.where(here, pltpu.roll(value, at, 1), upper)
        lower = jnp.where(here, pltpu.roll(value, (at + LANES - (count_r - HALO)) % LANES, 1), lower)
        first[columns + at : columns + at + HALO, 0:LANES] = value[0:HALO]
        last[columns + at : columns + at + HALO, 0:LANES] = value[rows - HALO : rows]
    top[edges : edges + rows, 0:LANES] = upper
    bottom[edges : edges + rows, 0:LANES] = lower
    begin = columns + EXTRA
    for copy in copies:
        copy.wait()
    for out, n, far, near in ((first, 0, 0, 0), (last, 1, 4, rows - 2)):
        for k in range(4):
            out[begin + 4 * k : begin + 4 * k + 4] = sides[n, count_r - 4 + k, far : far + 4]
        for k in range(BAND):
            at = begin + 16 + 2 * k
            column = count_r - BAND + k
            out[at : at + 2] = others[0, k, near : near + 2]
            out[at + 4 : at + 6] = others[1, k, near : near + 2]
            for m in (ROT, RET):
                value = tables[m, near : near + 2, column : column + 1]
                out[at + 8 + 4 * m : at + 10 + 4 * m] = jnp.broadcast_to(value, (2, width))
    for out, n, near in ((first, 0, 0), (last, 1, 8 - HALO)):
        for k in range(count_r):
            for r in range(HALO):
                out[r * count_r + k : r * count_r + k + 1] = sides[n, k, near + r : near + r + 1]
    for out, n in ((top, 0), (bottom, 1)):
        for k in range(HALO):
            out[k * rows : (k + 1) * rows] = ends[n, k]
    high[...], low[...] = halves(matrix[...])


def prepare(packet, previous, potential, rotation, damping, absorber, index, weight, angular):
    count_r, rows, width = packet.shape
    ends = jax.ShapeDtypeStruct((HALO * rows + rows, width), F32)
    sides = jax.ShapeDtypeStruct((HALO * count_r + EXTRA + OFBAND, width), F32)
    part = jax.ShapeDtypeStruct(angular.shape, BF16)
    return pl.pallas_call(
        prepare_kernel,
        in_specs=[HBM] * 9,
        out_specs=[VMEM] * 7,
        out_shape=[ends, ends, sides, sides, jax.ShapeDtypeStruct((TABLES, rows, LANES), F32), part, part],
        scratch_shapes=[
            pltpu.VMEM((2, HALO, rows, width), F32),
            pltpu.VMEM((2, count_r, 8, width), F32),
            pltpu.VMEM((2, BAND, rows, width), F32),
            pltpu.VMEM((2, rows, count_r), F32),
            pltpu.VMEM((rows, count_r), jnp.int32),
            pltpu.VMEM((STENCILS, rows, count_r), jnp.int32),
            pltpu.VMEM((STENCILS, rows, count_r), F32),
            pltpu.VMEM(angular.shape, F32),
            pltpu.SemaphoreType.DMA((12,)),
        ],
        compiler_params=pltpu.CompilerParams(vmem_limit_bytes=16 * MIB),
        cost_estimate=pl.CostEstimate(flops=1_000_000, bytes_accessed=6 * MIB, transcendentals=0),
        name="prepare",
    )(packet, previous, potential, rotation, damping, absorber, index, weight, angular)


def put_sides(sides, left, right, count_r, left_more=None, right_more=None):
    def body(k, carry):
        for r in range(HALO):
            at = pl.ds(r * count_r + k, 1)
            before, behind = left[at], right[at]
            if left_more is not None:
                before, behind = before + left_more[at], behind + right_more[at]
            sides[k, r : r + 1] = behind
            sides[k, 8 - HALO + r : 8 - HALO + r + 1] = before
        return carry

    lax.fori_loop(0, count_r, body, 0, unroll=8)


def advance(step, chunk, field, sides, previous, potential, tables, high, low, put):
    rows = previous.shape[1]
    width = previous.shape[2]
    here = step * chunk
    shift = lax.rem(LANES - here, LANES)
    columns = [pltpu.roll(tables[n], shift, 1) for n in (ROT, RET)]
    window = field[pl.ds(HALO + here, chunk)].reshape(chunk * rows, width)
    split = halves(window)
    wide = 2 * LANES
    for tile in range(0, width, wide):
        turned = product(split, high[:, tile : tile + wide], low[:, tile : tile + wide])
        for k in range(chunk):
            rotation = jnp.broadcast_to(0.25 * columns[0][:, k : k + 1], (rows, LANES))
            retained = jnp.broadcast_to(columns[1][:, k : k + 1], (rows, LANES))
            for at in range(tile, tile + wide, LANES):
                lanes = slice(at, at + LANES)

                def row(shift):
                    return field[HALO + here + k + shift, :, lanes]

                middle = row(0)
                ring = jnp.concatenate([middle, sides[here + k, :, lanes]], axis=0)
                around = [pltpu.roll(ring, s, 0)[:rows] for s in (1, rows + 7, 2, rows + 6)]
                near = row(-1) + row(1) + (around[0] + around[1])
                far = row(-2) + row(2) + (around[2] + around[3])
                update = (
                    SIDE1 * near
                    + SIDE2 * far
                    + (0.25 * potential[here + k, :, lanes] + MIDDLE) * middle
                    + rotation * turned[k * rows : (k + 1) * rows, at - tile : at - tile + LANES]
                    - retained * previous[here + k, :, lanes]
                )
                put(here + k, lanes, retained * update)


def first_kernel(
    packet, previous, potential, tables, up, down, left, right, high, low, after,
    done, top, bottom, first, last, field, prev, pot, sides, sems,
):
    count_r, rows, width = packet.shape
    steps = count_r // CHUNK

    def copies(n):
        part = pl.ds(n * CHUNK, CHUNK)
        return (
            pltpu.make_async_copy(packet.at[part], field.at[pl.ds(HALO + n * CHUNK, CHUNK)], sems.at[0, n]),
            pltpu.make_async_copy(previous.at[part], prev.at[part], sems.at[1, n]),
            pltpu.make_async_copy(potential.at[part], pot.at[part], sems.at[2, n]),
        )

    for n in range(steps):
        for copy in copies(n):
            copy.start()
    for k in range(HALO):
        field[k] = up[k * rows : (k + 1) * rows]
        field[HALO + count_r + k] = down[k * rows : (k + 1) * rows]
    put_sides(sides, left, right, count_r)
    copies(0)[0].wait()

    def put(k, lanes, value):
        done[k, :, lanes] = value

    def body(n, carry):
        @pl.when(n + 1 < steps)
        def _():
            copies(n + 1)[0].wait()

        copies(n)[1].wait()
        copies(n)[2].wait()
        advance(n, CHUNK, field, sides, prev, pot, tables, high, low, put)
        for k in range(CHUNK):
            for r in range(HALO):
                at = pl.ds(r * count_r + n * CHUNK + k, 1)
                first[at] = done[n * CHUNK + k, r : r + 1]
                last[at] = done[n * CHUNK + k, rows - HALO + r : rows - HALO + r + 1]
        return carry

    lax.fori_loop(0, steps, body, 0)
    for k in range(HALO):
        top[k * rows : (k + 1) * rows] = done[k]
        bottom[k * rows : (k + 1) * rows] = done[count_r - HALO + k]


def first_iteration(packet, previous, potential, tables, halos, high, low, after):
    count_r, rows, width = packet.shape
    ends = jax.ShapeDtypeStruct((HALO * rows, width), F32)
    sides = jax.ShapeDtypeStruct((HALO * count_r, width), F32)
    return pl.pallas_call(
        first_kernel,
        in_specs=[HBM, HBM, HBM, *[VMEM] * 7, ANY],
        out_specs=[VMEM] * 5,
        out_shape=[jax.ShapeDtypeStruct(packet.shape, F32), ends, ends, sides, sides],
        scratch_shapes=[
            pltpu.VMEM((count_r + 2 * HALO, rows, width), F32),
            pltpu.VMEM(packet.shape, F32),
            pltpu.VMEM(packet.shape, F32),
            pltpu.VMEM((count_r, 8, width), F32),
            pltpu.SemaphoreType.DMA((3, count_r // CHUNK)),
        ],
        compiler_params=pltpu.CompilerParams(vmem_limit_bytes=28 * MIB),
        cost_estimate=pl.CostEstimate(flops=7_000_000_000, bytes_accessed=20 * MIB, transcendentals=0),
        name="first_iteration",
    )(packet, previous, potential, tables, *halos, high, low, after)


def slot_of(value, rows, width):
    per = rows * BAND
    shift_owner = per.bit_length() - 1
    chips = width // per // CORES
    row = lax.axis_index("row")
    index = value.astype(jnp.int32)
    owner = index >> shift_owner
    inside = index & (per - 1)
    core = (owner & 1) ^ (row & 1)
    chip = ((row >> 1) - (owner >> 1)) & (chips - 1)
    slot = ((core * chips + chip) << shift_owner) + (inside & 1) * rows + (inside >> 1)
    return slot.astype(F32)


def fill_rows(at, cut, rows, high, low):
    column = lax.broadcasted_iota(jnp.int32, (rows, LANES), 1).astype(F32)
    cut = [jnp.broadcast_to(value, (rows, LANES)) for value in cut]
    for tile in range(0, high.shape[1], LANES):
        here = column + float(tile)
        total = jnp.where(here == cut[0], cut[STENCILS], 0.0)
        for n in range(1, STENCILS):
            total += jnp.where(here == cut[n], cut[STENCILS + n], 0.0)
        upper, lower = halves(total)
        high[pl.ds(at, rows), tile : tile + LANES] = upper
        low[pl.ds(at, rows), tile : tile + LANES] = lower


def stencil_kernel(tables, high, low):
    _, rows, _ = tables.shape
    count_r = high.shape[0] // rows
    group = 8

    @pl.when(in_product())
    def _():
        values = [slot_of(tables[INDEX + n], rows, high.shape[1]) for n in range(STENCILS)]
        values += [tables[WEIGHT + n] for n in range(STENCILS)]

        def body(step, carry):
            shift = lax.rem(LANES - step * group, LANES)
            moved = [pltpu.roll(value, shift, 1) for value in values]
            for k in range(group):
                at = pl.multiple_of((step * group + k) * rows, rows)
                fill_rows(at, [value[:, k : k + 1] for value in moved], rows, high, low)
            return carry

        lax.fori_loop(0, count_r // group, body, 0)


def stencil_matrix(tables, count_r, columns):
    rows = tables.shape[1]
    points = jax.ShapeDtypeStruct((count_r * rows, columns), BF16)
    return pl.pallas_call(
        stencil_kernel,
        in_specs=[VMEM],
        out_specs=[VMEM] * 2,
        out_shape=[points, points],
        compiler_params=pltpu.CompilerParams(vmem_limit_bytes=16 * MIB),
        cost_estimate=pl.CostEstimate(flops=15_000_000, bytes_accessed=6 * MIB, transcendentals=0),
        name="stencil_matrix",
    )(tables)


def stencil_edge_kernel(up, down, left, right, after, high, low, square, *, rows, count_r):
    @pl.when(in_product())
    def _():
        edges = HALO * rows
        at = 0
        for side in (up, down):
            value = side[edges : edges + rows, 0:LANES]
            slots = slot_of(value, rows, high.shape[1])
            for e in range(HALO):
                cut = [
                    (slots if m < STENCILS else value)[:, HALO * m + e : HALO * m + e + 1]
                    for m in range(2 * STENCILS)
                ]
                fill_rows(at, cut, rows, high, low)
                at += rows
        square[...] = jnp.zeros_like(square)
        part = EXTRA // 2
        for n, side in enumerate((left, right)):
            begin = HALO * count_r
            square[n * EXTRA : n * EXTRA + part] = slot_of(side[begin : begin + part, 0:LANES], rows, high.shape[1])
            square[n * EXTRA + part : (n + 1) * EXTRA] = side[begin + part : begin + EXTRA, 0:LANES]
        turned = square[...].T
        for n in range(2):
            for e in range(HALO):
                for begin in range(0, count_r, rows):
                    cut = [
                        turned[begin : begin + rows, n * EXTRA + HALO * m + e : n * EXTRA + HALO * m + e + 1]
                        for m in range(2 * STENCILS)
                    ]
                    fill_rows(at, cut, rows, high, low)
                    at += rows


def stencil_edges(halos, rows, count_r, columns, after):
    points = jax.ShapeDtypeStruct((2 * HALO * (rows + count_r), columns), BF16)
    return pl.pallas_call(
        functools.partial(stencil_edge_kernel, rows=rows, count_r=count_r),
        in_specs=[*[VMEM] * 4, ANY],
        out_specs=[VMEM] * 2,
        out_shape=[points, points],
        scratch_shapes=[pltpu.VMEM((LANES, LANES), F32)],
        compiler_params=pltpu.CompilerParams(vmem_limit_bytes=16 * MIB),
        cost_estimate=pl.CostEstimate(flops=2_000_000, bytes_accessed=2 * MIB, transcendentals=0),
        name="stencil_edges",
    )(*halos, after)


def last_kernel(
    one, packet, potential, tables, up, down, left, right, high, low,
    split_high, split_low, edge_high, edge_low, own_table, other_table,
    earlier, latest, field, prev, pot, done, sides, table, source, sems,
):
    count_r, rows, width = packet.shape
    steps = count_r // LAST
    is_product = in_product()
    quarter = own_table.shape[1]
    half = quarter // 2
    chips = own_table.shape[0]
    size = LAST * rows

    def field_part(n):
        return field.at[pl.ds(HALO + n * LAST, LAST)]

    def part(n):
        return pl.ds(n * LAST, LAST)

    def cut(n):
        return pl.ds(pl.multiple_of(n * size, size), size)

    def locals_of(n):
        return (
            pltpu.make_async_copy(packet.at[part(n)], prev.at[part(n)], sems.at[0, n]),
            pltpu.make_async_copy(potential.at[part(n)], pot.at[part(n)], sems.at[1, n]),
        )

    def earliers(n):
        return pltpu.make_async_copy(field_part(n), earlier.at[part(n)], sems.at[2, n])

    def latests(n):
        return pltpu.make_async_copy(done.at[part(n)], latest.at[part(n)], sems.at[3, n])

    def put_ends(up_value, down_value):
        for k in range(HALO):
            field[k] = up_value[k * rows : (k + 1) * rows]
            field[HALO + count_r + k] = down_value[k * rows : (k + 1) * rows]

    for n in range(steps):
        for copy in locals_of(n):
            copy.start()

    @pl.when(is_product)
    def _():
        for side, ref in enumerate((own_table, other_table)):
            for k in range(chips):
                at = (side * chips + k) * half
                for band in range(2):
                    upper, lower = halves(ref[k, band * half : (band + 1) * half])
                    table[2 * band, at : at + half] = upper
                    table[2 * band + 1, at : at + half] = lower
        source[...] = product((edge_high[...], edge_low[...]), table[0], table[1])
        edges = HALO * rows
        columns = HALO * count_r
        put_ends(up[...] + source[:edges], down[...] + source[edges : 2 * edges])
        put_sides(
            sides, left, right, count_r,
            source.at[pl.ds(2 * edges, columns)], source.at[pl.ds(2 * edges + columns, columns)],
        )

        def body(n, carry):
            matrix = (split_high[cut(n)], split_low[cut(n)])
            here = pl.ds(HALO + n * LAST, LAST)
            field[here] = one[part(n)] + product(matrix, table[0], table[1]).reshape(LAST, rows, width)
            done[part(n)] = product(matrix, table[2], table[3]).reshape(LAST, rows, width)
            earliers(n).start()
            return carry

        lax.fori_loop(0, steps, body, 0)

    @pl.when(jnp.logical_not(is_product))
    def _():
        put_ends(up, down)
        put_sides(sides, left, right, count_r)
        done[...] = jnp.zeros_like(done)
        for n in range(steps):
            here = pl.ds(HALO + n * LAST, LAST)
            field[here] = one[part(n)]
            earliers(n).start()

    def put(k, lanes, value):
        done[k, :, lanes] += value

    def body(n, carry):
        for copy in locals_of(n):
            copy.wait()
        advance(n, LAST, field, sides, prev, pot, tables, high, low, put)
        latests(n).start()
        return carry

    lax.fori_loop(0, steps, body, 0)
    for n in range(steps):
        earliers(n).wait()
        latests(n).wait()


def last_iteration(one, packet, potential, tables, halos, high, low, matrices, band_tables):
    count_r, rows, width = packet.shape
    steps = count_r // LAST
    columns = matrices[0].shape[1]
    return pl.pallas_call(
        last_kernel,
        in_specs=[VMEM, HBM, HBM, *[VMEM] * 13],
        out_specs=[HBM, HBM],
        out_shape=[jax.ShapeDtypeStruct(packet.shape, F32)] * 2,
        scratch_shapes=[
            pltpu.VMEM((count_r + 2 * HALO, rows, width), F32),
            pltpu.VMEM(packet.shape, F32),
            pltpu.VMEM(packet.shape, F32),
            pltpu.VMEM(packet.shape, F32),
            pltpu.VMEM((count_r, 8, width), F32),
            pltpu.VMEM((4, columns, width), BF16),
            pltpu.VMEM((2 * HALO * (rows + count_r), width), F32),
            pltpu.SemaphoreType.DMA((4, steps)),
        ],
        compiler_params=pltpu.CompilerParams(vmem_limit_bytes=40 * MIB),
        cost_estimate=pl.CostEstimate(flops=20_000_000_000, bytes_accessed=36 * MIB, transcendentals=0),
        name="last_iteration",
    )(one, packet, potential, tables, *halos, high, low, *matrices, *band_tables)


def neighbours(axis, upward, downward):
    count = lax.axis_size(axis)
    return (
        lax.ppermute(upward, axis, [(i, i + 1) for i in range(count - 1)]),
        lax.ppermute(downward, axis, [(i + 1, i) for i in range(count - 1)]),
    )


def local(packet, previous, potential, rotation, angular, damping, absorber, stencil_index, stencil_weight):
    packet, previous, potential = packet[0], previous[0], potential[0]
    rotation, angular, damping, absorber = rotation[0], angular[0], damping[0], absorber[0]
    count_r, rows, width = packet.shape
    count_rr, count_row = (lax.axis_size(name) for name in ("rr", "row"))
    chips = count_row // CORES
    rotation, damping, absorber = (jnp.swapaxes(value, 0, 1) for value in (rotation, damping, absorber))
    stencil_index, stencil_weight = (jnp.swapaxes(value, 1, 2) for value in (stencil_index, stencil_weight))
    packet, previous, potential, rotation, damping, absorber, stencil_index, stencil_weight, angular = (
        in_hbm(value)
        for value in (
            packet, previous, potential, rotation, damping, absorber, stencil_index, stencil_weight, angular
        )
    )

    top, bottom, first, last, tables, high, low = prepare(
        packet, previous, potential, rotation, damping, absorber, stencil_index, stencil_weight, angular
    )
    columns = count_row * rows * BAND
    left, right = neighbours("row", last, first)
    matrix = stencil_matrix(tables, count_r, columns)
    left, right, matrix = lax.optimization_barrier((left, right, matrix))
    table = bands(packet, previous, potential, tables, left, right, high, low)
    up, down = neighbours("rr", bottom, top)

    plane = ("sect", "rr")
    half = count_rr // FAR
    start = count_rr - 1
    entries = [count_rr + (k + 1) * half - 1 for k in range(FAR)]
    crossed = [lax.ppermute(table, plane, [(start, entry)]) for entry in entries]
    *crossed, up, down = lax.optimization_barrier((*crossed, up, down))
    halos = (up, down, left, right)
    piece = sum(crossed)
    arrived = []
    for shift in (1, half - 1, 2):
        pairs = [(entry, entry - (half - 1) + (half - 1 + shift) % half) for entry in entries]
        arrived.append(lax.ppermute(piece, plane, pairs))
    spread = piece + sum(arrived)
    line = ("sect", "row")

    def around(shift):
        pairs = []
        for chip in range(chips):
            for core in range(CORES):
                pairs.append(
                    (count_row + chip * CORES + core, count_row + ((chip + shift) % chips) * CORES + core)
                )
        return lax.ppermute(spread, line, pairs)

    rest = [around(1), around(2), around(3)]
    one, *edges = first_iteration(packet, previous, potential, tables, halos, high, low, spread)
    edge_matrix = stencil_edges(halos, rows, count_r, columns, one)
    top, bottom, first, last = edges
    left, right = neighbours("row", last, first)
    *rest, edge_matrix, left, right = lax.optimization_barrier((*rest, edge_matrix, left, right))
    up, down = neighbours("rr", bottom, top)
    later = (up, down, left, right)
    own = jnp.stack([spread, *rest], axis=0)
    other = lax.ppermute(
        own, line, [(count_row + i, count_row + i + 1 - 2 * (i % CORES)) for i in range(count_row)]
    )
    earlier, latest = last_iteration(
        one, packet, potential, tables, later, high, low, (*matrix, *edge_matrix), (own, other)
    )
    return latest[None], earlier[None]


def solution(mesh):
    in_specs = (
        P("sect", "rr", "row", None),
        P("sect", "rr", "row", None),
        P("sect", "rr", "row", None),
        P("sect", "rr", "row"),
        P("sect", None, None),
        P("sect", "rr", "row"),
        P("sect", "rr", "row"),
        P(None, "rr", "row"),
        P(None, "rr", "row"),
    )
    out_specs = (P("sect", "rr", "row", None), P("sect", "rr", "row", None))
    return jax.shard_map(local, mesh=mesh, in_specs=in_specs, out_specs=out_specs, check_vma=False)
```

```python
import functools

import jax
import jax.numpy as jnp
from jax import lax
from jax.experimental import pallas as pl
from jax.experimental.pallas import tpu as pltpu
from jax.sharding import PartitionSpec as P

BAND = 2
STENCILS = 4
HALO = 2
LANES = 128
CHUNK = 16
LAST = 16
CORES = 2
FAR = 2
ROT, RET, INDEX, WEIGHT, TABLES = 0, 1, 2, 6, 10
EXTRA = 2 * STENCILS * HALO
OFBAND = 32
MIB = 1 << 20
F32 = jnp.float32
BF16 = jnp.bfloat16
ANY = pl.BlockSpec(memory_space=pl.ANY)
HBM = pl.BlockSpec(memory_space=pltpu.HBM)
VMEM = pl.BlockSpec(memory_space=pltpu.VMEM)

SIDE1 = -16.0 / 96.0
SIDE2 = 1.0 / 96.0
MIDDLE = 2.0 * 30.0 / 96.0 - 7.5 / 4.0


def halves(value):
    high = value.astype(BF16)
    low = (value - high.astype(F32)).astype(BF16)
    return high, low


def product(left, right_high, right_low):
    high, low = left
    total = jnp.dot(high, right_high, preferred_element_type=F32)
    total += jnp.dot(low, right_high, preferred_element_type=F32)
    return total + jnp.dot(high, right_low, preferred_element_type=F32)


def doubled_hamilton(field, index, start, count, lanes, turned, potential, rotation):
    def at(shift_r, shift_v):
        return field[index + shift_r, pl.ds(start + shift_v, count), lanes]

    middle = at(0, 0)
    near = at(-1, 0) + at(1, 0) + (at(0, -1) + at(0, 1))
    far = at(-2, 0) + at(2, 0) + (at(0, -2) + at(0, 2))
    return (
        SIDE1 * near
        + SIDE2 * far
        + (0.25 * potential + MIDDLE) * middle
        + (0.25 * rotation) * turned
    )


def in_hbm(value):
    return pltpu.with_memory_space_constraint(value, pltpu.HBM)


def holds_bands():
    return (lax.axis_index("sect") == 0) & (lax.axis_index("rr") == lax.axis_size("rr") - 1)


def in_product():
    return lax.axis_index("sect") == 1


def retained_of(damping, absorber):
    return 1.0 - absorber.astype(F32) * (1.0 - damping)


def band_kernel(
    packet, previous, potential, tables, left, right, high, low, out, field, later, turned, held, sems
):
    count_r, rows, width = packet.shape
    base = 16
    wide = rows + 16
    begin = left.shape[0] - OFBAND

    @pl.when(holds_bands())
    def _():
        copies = [
            pltpu.make_async_copy(packet.at[pl.ds(count_r - 6, 6)], field.at[pl.ds(2, 6), pl.ds(base, rows)], sems.at[0]),
            pltpu.make_async_copy(previous.at[pl.ds(count_r - 4, 4)], held.at[0], sems.at[1]),
            pltpu.make_async_copy(potential.at[pl.ds(count_r - 4, 4)], held.at[1], sems.at[2]),
        ]
        later[...] = jnp.zeros_like(later)
        field[0:2] = jnp.zeros_like(field[0:2])
        field[8:10] = jnp.zeros_like(field[8:10])
        for k in range(2, 8):
            field[k, 0:base] = jnp.zeros((base, width), F32)
            field[k, base + rows :] = jnp.zeros((base, width), F32)
        for copy in copies:
            copy.start()
        for k in range(4):
            at = begin + 4 * k
            field[4 + k, base - 4 : base] = left[at : at + 4]
            field[4 + k, base + rows : base + rows + 4] = right[at : at + 4]
        columns = [
            (tables[ROT, :, count_r - 4 + k : count_r - 3 + k], tables[RET, :, count_r - 4 + k : count_r - 3 + k])
            for k in range(4)
        ]
        columns = [tuple(jnp.broadcast_to(c, (rows, LANES)) for c in pair) for pair in columns]
        for copy in copies:
            copy.wait()
        window = field[4:8, base - 8 : base + rows + 8].reshape(4 * wide, width)
        turned[...] = product(halves(window), high[...], low[...])
        for k in range(4):
            rotation, retained = columns[k]
            for at in range(0, width, LANES):
                lanes = slice(at, at + LANES)
                update = doubled_hamilton(
                    field, 4 + k, base, rows, lanes,
                    turned[k * wide + 8 : k * wide + 8 + rows, lanes], held[1, k, :, lanes], rotation,
                ) - retained * held[0, k, :, lanes]
                later[k, base : base + rows, lanes] = retained * update
                if k >= 2:
                    out[(k - 2) * rows : (k - 1) * rows, lanes] = (1.0 - retained) * update
        for k in range(2, 4):
            for slab, place, inside in ((left, base - 8, 6), (right, base + rows, 0)):
                at = begin + 16 + 2 * (k - 2)
                prev, pot, rot, ret = (slab[at + 4 * n : at + 4 * n + 2] for n in range(4))
                update = doubled_hamilton(
                    field, 4 + k, place + inside, 2, slice(None),
                    turned[k * wide + place - base + 8 + inside : k * wide + place - base + 10 + inside], pot, rot,
                ) - ret * prev
                later[k, place + inside : place + inside + 2] = ret * update
        window = later[2:4, base : base + rows].reshape(2 * rows, width)
        turned[0 : 2 * rows] = product(halves(window), high[...], low[...])
        for k in range(2, 4):
            rotation, retained = columns[k]
            for at in range(0, width, LANES):
                lanes = slice(at, at + LANES)
                update = doubled_hamilton(
                    later, k, base, rows, lanes,
                    turned[(k - 2) * rows : (k - 1) * rows, lanes], held[1, k, :, lanes], rotation,
                ) - retained * field[4 + k, base : base + rows, lanes]
                out[k * rows : (k + 1) * rows, lanes] = (1.0 - retained) * update


def bands(packet, previous, potential, tables, left, right, high, low):
    _, rows, width = packet.shape
    return pl.pallas_call(
        band_kernel,
        in_specs=[HBM, HBM, HBM, VMEM, VMEM, VMEM, VMEM, VMEM],
        out_specs=VMEM,
        out_shape=jax.ShapeDtypeStruct((2 * BAND * rows, width), F32),
        scratch_shapes=[
            pltpu.VMEM((10, rows + 32, width), F32),
            pltpu.VMEM((6, rows + 32, width), F32),
            pltpu.VMEM((4 * (rows + 16), width), F32),
            pltpu.VMEM((2, 4, rows, width), F32),
            pltpu.SemaphoreType.DMA((3,)),
        ],
        compiler_params=pltpu.CompilerParams(vmem_limit_bytes=16 * MIB),
        cost_estimate=pl.CostEstimate(flops=400_000_000, bytes_accessed=4 * MIB, transcendentals=0),
        name="both_bands",
    )(packet, previous, potential, tables, left, right, high, low)


def prepare_kernel(
    packet, previous, potential, rotation, damping, absorber, index, weight, angular,
    top, bottom, first, last, tables, high, low,
    ends, sides, others, factors, masks, indices, weights, matrix, sems,
):
    count_r, rows, width = packet.shape
    small = [
        pltpu.make_async_copy(rotation, factors.at[0], sems.at[0]),
        pltpu.make_async_copy(damping, factors.at[1], sems.at[1]),
        pltpu.make_async_copy(absorber, masks, sems.at[2]),
        pltpu.make_async_copy(index, indices, sems.at[3]),
        pltpu.make_async_copy(weight, weights, sems.at[4]),
    ]
    copies = [
        pltpu.make_async_copy(packet.at[:, pl.ds(0, 8)], sides.at[0], sems.at[5]),
        pltpu.make_async_copy(packet.at[:, pl.ds(rows - 8, 8)], sides.at[1], sems.at[6]),
        pltpu.make_async_copy(packet.at[pl.ds(0, HALO)], ends.at[0], sems.at[7]),
        pltpu.make_async_copy(packet.at[pl.ds(count_r - HALO, HALO)], ends.at[1], sems.at[8]),
        pltpu.make_async_copy(previous.at[pl.ds(count_r - BAND, BAND)], others.at[0], sems.at[9]),
        pltpu.make_async_copy(potential.at[pl.ds(count_r - BAND, BAND)], others.at[1], sems.at[10]),
        pltpu.make_async_copy(angular, matrix, sems.at[11]),
    ]
    for copy in small + copies:
        copy.start()
    for copy in small:
        copy.wait()
    values = [factors[0], retained_of(factors[1], masks[...])]
    values += [indices[n].astype(F32) for n in range(STENCILS)]
    values += [weights[n] for n in range(STENCILS)]
    for n, value in enumerate(values):
        tables[n] = jnp.concatenate([value, jnp.zeros((rows, LANES - count_r), F32)], axis=1)
    edges = HALO * rows
    columns = HALO * count_r
    lane = lax.broadcasted_iota(jnp.int32, (rows, LANES), 1)
    upper = jnp.zeros((rows, LANES), F32)
    lower = jnp.zeros((rows, LANES), F32)
    for n in range(2 * STENCILS):
        value = tables[INDEX + n]
        at = n * HALO
        here = (lane >= at) & (lane < at + HALO)
        upper = jnp.where(here, pltpu.roll(value, at, 1), upper)
        lower = jnp.where(here, pltpu.roll(value, (at + LANES - (count_r - HALO)) % LANES, 1), lower)
        first[columns + at : columns + at + HALO, 0:LANES] = value[0:HALO]
        last[columns + at : columns + at + HALO, 0:LANES] = value[rows - HALO : rows]
    top[edges : edges + rows, 0:LANES] = upper
    bottom[edges : edges + rows, 0:LANES] = lower
    begin = columns + EXTRA
    for copy in copies:
        copy.wait()
    for out, n, far, near in ((first, 0, 0, 0), (last, 1, 4, rows - 2)):
        for k in range(4):
            out[begin + 4 * k : begin + 4 * k + 4] = sides[n, count_r - 4 + k, far : far + 4]
        for k in range(BAND):
            at = begin + 16 + 2 * k
            column = count_r - BAND + k
            out[at : at + 2] = others[0, k, near : near + 2]
            out[at + 4 : at + 6] = others[1, k, near : near + 2]
            for m in (ROT, RET):
                value = tables[m, near : near + 2, column : column + 1]
                out[at + 8 + 4 * m : at + 10 + 4 * m] = jnp.broadcast_to(value, (2, width))
    for out, n, near in ((first, 0, 0), (last, 1, 8 - HALO)):
        for k in range(count_r):
            for r in range(HALO):
                out[r * count_r + k : r * count_r + k + 1] = sides[n, k, near + r : near + r + 1]
    for out, n in ((top, 0), (bottom, 1)):
        for k in range(HALO):
            out[k * rows : (k + 1) * rows] = ends[n, k]
    high[...], low[...] = halves(matrix[...])


def prepare(packet, previous, potential, rotation, damping, absorber, index, weight, angular):
    count_r, rows, width = packet.shape
    ends = jax.ShapeDtypeStruct((HALO * rows + rows, width), F32)
    sides = jax.ShapeDtypeStruct((HALO * count_r + EXTRA + OFBAND, width), F32)
    part = jax.ShapeDtypeStruct(angular.shape, BF16)
    return pl.pallas_call(
        prepare_kernel,
        in_specs=[HBM] * 9,
        out_specs=[VMEM] * 7,
        out_shape=[ends, ends, sides, sides, jax.ShapeDtypeStruct((TABLES, rows, LANES), F32), part, part],
        scratch_shapes=[
            pltpu.VMEM((2, HALO, rows, width), F32),
            pltpu.VMEM((2, count_r, 8, width), F32),
            pltpu.VMEM((2, BAND, rows, width), F32),
            pltpu.VMEM((2, rows, count_r), F32),
            pltpu.VMEM((rows, count_r), jnp.int32),
            pltpu.VMEM((STENCILS, rows, count_r), jnp.int32),
            pltpu.VMEM((STENCILS, rows, count_r), F32),
            pltpu.VMEM(angular.shape, F32),
            pltpu.SemaphoreType.DMA((12,)),
        ],
        compiler_params=pltpu.CompilerParams(vmem_limit_bytes=16 * MIB),
        cost_estimate=pl.CostEstimate(flops=1_000_000, bytes_accessed=6 * MIB, transcendentals=0),
        name="prepare",
    )(packet, previous, potential, rotation, damping, absorber, index, weight, angular)


def put_sides(sides, left, right, count_r, left_more=None, right_more=None):
    def body(k, carry):
        for r in range(HALO):
            at = pl.ds(r * count_r + k, 1)
            before, behind = left[at], right[at]
            if left_more is not None:
                before, behind = before + left_more[at], behind + right_more[at]
            sides[k, r : r + 1] = behind
            sides[k, 8 - HALO + r : 8 - HALO + r + 1] = before
        return carry

    lax.fori_loop(0, count_r, body, 0, unroll=8)


def advance(step, chunk, field, sides, previous, potential, tables, high, low, put, more=None):
    rows = previous.shape[1]
    width = previous.shape[2]
    here = step * chunk
    shift = lax.rem(LANES - here, LANES)
    columns = [pltpu.roll(tables[n], shift, 1) for n in (ROT, RET)]
    window = field[pl.ds(HALO + here, chunk)].reshape(chunk * rows, width)
    split = halves(window)
    wide = 2 * LANES
    for tile in range(0, width, wide):
        turned = product(split, high[:, tile : tile + wide], low[:, tile : tile + wide])
        source = None if more is None else more(slice(tile, tile + wide))
        for k in range(chunk):
            rotation = jnp.broadcast_to(0.25 * columns[0][:, k : k + 1], (rows, LANES))
            retained = jnp.broadcast_to(columns[1][:, k : k + 1], (rows, LANES))
            for at in range(tile, tile + wide, LANES):
                lanes = slice(at, at + LANES)

                def row(shift):
                    return field[HALO + here + k + shift, :, lanes]

                middle = row(0)
                ring = jnp.concatenate([middle, sides[here + k, :, lanes]], axis=0)
                around = [pltpu.roll(ring, s, 0)[:rows] for s in (1, rows + 7, 2, rows + 6)]
                near = row(-1) + row(1) + (around[0] + around[1])
                far = row(-2) + row(2) + (around[2] + around[3])
                update = (
                    SIDE1 * near
                    + SIDE2 * far
                    + (0.25 * potential[here + k, :, lanes] + MIDDLE) * middle
                    + rotation * turned[k * rows : (k + 1) * rows, at - tile : at - tile + LANES]
                    - retained * previous[here + k, :, lanes]
                )
                value = retained * update
                if source is not None:
                    value += source[k * rows : (k + 1) * rows, at - tile : at - tile + LANES]
                put(here + k, lanes, value)


def first_kernel(
    packet, previous, potential, tables, up, down, left, right, high, low, after,
    done, top, bottom, first, last, field, prev, pot, sides, sems,
):
    count_r, rows, width = packet.shape
    steps = count_r // CHUNK

    def copies(n):
        part = pl.ds(n * CHUNK, CHUNK)
        return (
            pltpu.make_async_copy(packet.at[part], field.at[pl.ds(HALO + n * CHUNK, CHUNK)], sems.at[0, n]),
            pltpu.make_async_copy(previous.at[part], prev.at[part], sems.at[1, n]),
            pltpu.make_async_copy(potential.at[part], pot.at[part], sems.at[2, n]),
        )

    for n in range(steps):
        for copy in copies(n):
            copy.start()
    for k in range(HALO):
        field[k] = up[k * rows : (k + 1) * rows]
        field[HALO + count_r + k] = down[k * rows : (k + 1) * rows]
    put_sides(sides, left, right, count_r)
    copies(0)[0].wait()

    def put(k, lanes, value):
        done[k, :, lanes] = value

    def body(n, carry):
        @pl.when(n + 1 < steps)
        def _():
            copies(n + 1)[0].wait()

        copies(n)[1].wait()
        copies(n)[2].wait()
        advance(n, CHUNK, field, sides, prev, pot, tables, high, low, put)
        for k in range(CHUNK):
            for r in range(HALO):
                at = pl.ds(r * count_r + n * CHUNK + k, 1)
                first[at] = done[n * CHUNK + k, r : r + 1]
                last[at] = done[n * CHUNK + k, rows - HALO + r : rows - HALO + r + 1]
        return carry

    lax.fori_loop(0, steps, body, 0)
    for k in range(HALO):
        top[k * rows : (k + 1) * rows] = done[k]
        bottom[k * rows : (k + 1) * rows] = done[count_r - HALO + k]


def first_iteration(packet, previous, potential, tables, halos, high, low, after):
    count_r, rows, width = packet.shape
    ends = jax.ShapeDtypeStruct((HALO * rows, width), F32)
    sides = jax.ShapeDtypeStruct((HALO * count_r, width), F32)
    return pl.pallas_call(
        first_kernel,
        in_specs=[HBM, HBM, HBM, *[VMEM] * 7, ANY],
        out_specs=[VMEM] * 5,
        out_shape=[jax.ShapeDtypeStruct(packet.shape, F32), ends, ends, sides, sides],
        scratch_shapes=[
            pltpu.VMEM((count_r + 2 * HALO, rows, width), F32),
            pltpu.VMEM(packet.shape, F32),
            pltpu.VMEM(packet.shape, F32),
            pltpu.VMEM((count_r, 8, width), F32),
            pltpu.SemaphoreType.DMA((3, count_r // CHUNK)),
        ],
        compiler_params=pltpu.CompilerParams(vmem_limit_bytes=28 * MIB),
        cost_estimate=pl.CostEstimate(flops=7_000_000_000, bytes_accessed=20 * MIB, transcendentals=0),
        name="first_iteration",
    )(packet, previous, potential, tables, *halos, high, low, after)


def slot_of(value, rows, width):
    per = rows * BAND
    shift_owner = per.bit_length() - 1
    chips = width // per // CORES
    row = lax.axis_index("row")
    index = value.astype(jnp.int32)
    owner = index >> shift_owner
    inside = index & (per - 1)
    core = (owner & 1) ^ (row & 1)
    chip = ((row >> 1) - (owner >> 1)) & (chips - 1)
    slot = ((core * chips + chip) << shift_owner) + (inside & 1) * rows + (inside >> 1)
    return slot.astype(F32)


def fill_rows(at, cut, rows, high, low):
    column = lax.broadcasted_iota(jnp.int32, (rows, LANES), 1).astype(F32)
    cut = [jnp.broadcast_to(value, (rows, LANES)) for value in cut]
    for tile in range(0, high.shape[1], LANES):
        here = column + float(tile)
        total = jnp.where(here == cut[0], cut[STENCILS], 0.0)
        for n in range(1, STENCILS):
            total += jnp.where(here == cut[n], cut[STENCILS + n], 0.0)
        upper, lower = halves(total)
        high[pl.ds(at, rows), tile : tile + LANES] = upper
        low[pl.ds(at, rows), tile : tile + LANES] = lower


def stencil_kernel(tables, high, low):
    _, rows, _ = tables.shape
    count_r = high.shape[0] // rows
    group = 8

    @pl.when(in_product())
    def _():
        values = [slot_of(tables[INDEX + n], rows, high.shape[1]) for n in range(STENCILS)]
        values += [tables[WEIGHT + n] for n in range(STENCILS)]

        def body(step, carry):
            shift = lax.rem(LANES - step * group, LANES)
            moved = [pltpu.roll(value, shift, 1) for value in values]
            for k in range(group):
                at = pl.multiple_of((step * group + k) * rows, rows)
                fill_rows(at, [value[:, k : k + 1] for value in moved], rows, high, low)
            return carry

        lax.fori_loop(0, count_r // group, body, 0)


def stencil_matrix(tables, count_r, columns):
    rows = tables.shape[1]
    points = jax.ShapeDtypeStruct((count_r * rows, columns), BF16)
    return pl.pallas_call(
        stencil_kernel,
        in_specs=[VMEM],
        out_specs=[VMEM] * 2,
        out_shape=[points, points],
        compiler_params=pltpu.CompilerParams(vmem_limit_bytes=16 * MIB),
        cost_estimate=pl.CostEstimate(flops=15_000_000, bytes_accessed=6 * MIB, transcendentals=0),
        name="stencil_matrix",
    )(tables)


def stencil_edge_kernel(up, down, left, right, after, high, low, square, *, rows, count_r):
    @pl.when(in_product())
    def _():
        edges = HALO * rows
        at = 0
        for side in (up, down):
            value = side[edges : edges + rows, 0:LANES]
            slots = slot_of(value, rows, high.shape[1])
            for e in range(HALO):
                cut = [
                    (slots if m < STENCILS else value)[:, HALO * m + e : HALO * m + e + 1]
                    for m in range(2 * STENCILS)
                ]
                fill_rows(at, cut, rows, high, low)
                at += rows
        square[...] = jnp.zeros_like(square)
        part = EXTRA // 2
        for n, side in enumerate((left, right)):
            begin = HALO * count_r
            square[n * EXTRA : n * EXTRA + part] = slot_of(side[begin : begin + part, 0:LANES], rows, high.shape[1])
            square[n * EXTRA + part : (n + 1) * EXTRA] = side[begin + part : begin + EXTRA, 0:LANES]
        turned = square[...].T
        for n in range(2):
            for e in range(HALO):
                for begin in range(0, count_r, rows):
                    cut = [
                        turned[begin : begin + rows, n * EXTRA + HALO * m + e : n * EXTRA + HALO * m + e + 1]
                        for m in range(2 * STENCILS)
                    ]
                    fill_rows(at, cut, rows, high, low)
                    at += rows


def stencil_edges(halos, rows, count_r, columns, after):
    points = jax.ShapeDtypeStruct((2 * HALO * (rows + count_r), columns), BF16)
    return pl.pallas_call(
        functools.partial(stencil_edge_kernel, rows=rows, count_r=count_r),
        in_specs=[*[VMEM] * 4, ANY],
        out_specs=[VMEM] * 2,
        out_shape=[points, points],
        scratch_shapes=[pltpu.VMEM((LANES, LANES), F32)],
        compiler_params=pltpu.CompilerParams(vmem_limit_bytes=16 * MIB),
        cost_estimate=pl.CostEstimate(flops=2_000_000, bytes_accessed=2 * MIB, transcendentals=0),
        name="stencil_edges",
    )(*halos, after)


def split_table(pieces, table):
    half = pieces.shape[1] // 2
    for k in range(pieces.shape[0]):
        for band in range(2):
            upper, lower = halves(pieces[k, band * half : (band + 1) * half])
            table[2 * band, k * half : (k + 1) * half] = upper
            table[2 * band + 1, k * half : (k + 1) * half] = lower


def own_source_kernel(one, stencil_high, stencil_low, edge_high, edge_low, own, sum_one, source, edge_source, table):
    count_r, rows, width = one.shape
    columns = table.shape[1]
    size = LAST * rows

    @pl.when(in_product())
    def _():
        split_table(own, table)

        def body(n, carry):
            cut = pl.ds(pl.multiple_of(n * size, size), size)
            part = pl.ds(n * LAST, LAST)
            weights = (stencil_high[cut, 0:columns], stencil_low[cut, 0:columns])
            sum_one[part] = one[part] + product(weights, table[0], table[1]).reshape(LAST, rows, width)
            source[cut] = product(weights, table[2], table[3])
            return carry

        lax.fori_loop(0, count_r // LAST, body, 0)
        edge_source[...] = product((edge_high[:, 0:columns], edge_low[:, 0:columns]), table[0], table[1])

    @pl.when(jnp.logical_not(in_product()))
    def _():
        sum_one[...] = one[...]


def own_source(one, matrices, own):
    count_r, rows, width = one.shape
    points = count_r * rows
    return pl.pallas_call(
        own_source_kernel,
        in_specs=[VMEM] * 6,
        out_specs=[VMEM] * 3,
        out_shape=[
            jax.ShapeDtypeStruct(one.shape, F32),
            jax.ShapeDtypeStruct((points, width), F32),
            jax.ShapeDtypeStruct((matrices[2].shape[0], width), F32),
        ],
        scratch_shapes=[pltpu.VMEM((4, own.shape[0] * own.shape[1] // 2, width), BF16)],
        compiler_params=pltpu.CompilerParams(vmem_limit_bytes=16 * MIB),
        cost_estimate=pl.CostEstimate(flops=7_000_000_000, bytes_accessed=20 * MIB, transcendentals=0),
        name="own_source",
    )(one, *matrices, own)


def last_kernel(
    one, source, edge_source, packet, potential, tables, up, down, left, right, high, low,
    stencil_high, stencil_low, edge_high, edge_low, other,
    earlier, latest, field, prev, pot, done, sides, table, ends, sems,
):
    count_r, rows, width = packet.shape
    steps = count_r // LAST
    size = LAST * rows
    columns = table.shape[1]
    is_product = in_product()

    def part(n):
        return pl.ds(n * LAST, LAST)

    def cut(n):
        return pl.ds(pl.multiple_of(n * size, size), size)

    def locals_of(n):
        return (
            pltpu.make_async_copy(packet.at[part(n)], prev.at[part(n)], sems.at[0, n]),
            pltpu.make_async_copy(potential.at[part(n)], pot.at[part(n)], sems.at[1, n]),
        )

    def earliers(n):
        return pltpu.make_async_copy(field.at[pl.ds(HALO + n * LAST, LAST)], earlier.at[part(n)], sems.at[2, n])

    def latests(n):
        return pltpu.make_async_copy(done.at[part(n)], latest.at[part(n)], sems.at[3, n])

    def put_ends(up_value, down_value):
        for k in range(HALO):
            field[k] = up_value[k * rows : (k + 1) * rows]
            field[HALO + count_r + k] = down_value[k * rows : (k + 1) * rows]

    def put(k, lanes, value):
        done[k, :, lanes] = value

    for n in range(steps):
        for copy in locals_of(n):
            copy.start()

    @pl.when(is_product)
    def _():
        split_table(other, table)
        ends[...] = edge_source[...] + product(
            (edge_high[:, columns : 2 * columns], edge_low[:, columns : 2 * columns]), table[0], table[1]
        )
        edges = HALO * rows
        long = HALO * count_r
        put_ends(up[...] + ends[:edges], down[...] + ends[edges : 2 * edges])
        put_sides(
            sides, left, right, count_r, ends.at[pl.ds(2 * edges, long)], ends.at[pl.ds(2 * edges + long, long)]
        )

        def weights(n):
            return stencil_high[cut(n), columns : 2 * columns], stencil_low[cut(n), columns : 2 * columns]

        def add(n, carry):
            more = product(weights(n), table[0], table[1]).reshape(LAST, rows, width)
            field[pl.ds(HALO + n * LAST, LAST)] = one[part(n)] + more
            earliers(n).start()
            return carry

        lax.fori_loop(0, steps, add, 0)

        def body(n, carry):
            for copy in locals_of(n):
                copy.wait()
            matrix = weights(n)

            def more(lanes):
                return source[cut(n), lanes] + product(matrix, table[2, :, lanes], table[3, :, lanes])

            advance(n, LAST, field, sides, prev, pot, tables, high, low, put, more)
            latests(n).start()
            return carry

        lax.fori_loop(0, steps, body, 0)

    @pl.when(jnp.logical_not(is_product))
    def _():
        put_ends(up, down)
        put_sides(sides, left, right, count_r)
        for n in range(steps):
            field[pl.ds(HALO + n * LAST, LAST)] = one[part(n)]
            earliers(n).start()

        def body(n, carry):
            for copy in locals_of(n):
                copy.wait()
            advance(n, LAST, field, sides, prev, pot, tables, high, low, put)
            latests(n).start()
            return carry

        lax.fori_loop(0, steps, body, 0)

    for n in range(steps):
        earliers(n).wait()
        latests(n).wait()


def last_iteration(own_sums, packet, potential, tables, halos, high, low, matrices, other):
    count_r, rows, width = packet.shape
    steps = count_r // LAST
    return pl.pallas_call(
        last_kernel,
        in_specs=[VMEM, VMEM, VMEM, HBM, HBM, *[VMEM] * 12],
        out_specs=[HBM, HBM],
        out_shape=[jax.ShapeDtypeStruct(packet.shape, F32)] * 2,
        scratch_shapes=[
            pltpu.VMEM((count_r + 2 * HALO, rows, width), F32),
            pltpu.VMEM(packet.shape, F32),
            pltpu.VMEM(packet.shape, F32),
            pltpu.VMEM(packet.shape, F32),
            pltpu.VMEM((count_r, 8, width), F32),
            pltpu.VMEM((4, other.shape[0] * other.shape[1] // 2, width), BF16),
            pltpu.VMEM((2 * HALO * (rows + count_r), width), F32),
            pltpu.SemaphoreType.DMA((4, steps)),
        ],
        compiler_params=pltpu.CompilerParams(vmem_limit_bytes=32 * MIB),
        cost_estimate=pl.CostEstimate(flops=14_000_000_000, bytes_accessed=36 * MIB, transcendentals=0),
        name="last_iteration",
    )(*own_sums, packet, potential, tables, *halos, high, low, *matrices, other)


def neighbours(axis, upward, downward):
    count = lax.axis_size(axis)
    return (
        lax.ppermute(upward, axis, [(i, i + 1) for i in range(count - 1)]),
        lax.ppermute(downward, axis, [(i + 1, i) for i in range(count - 1)]),
    )


def exchange(top, bottom, first, last):
    up, down = neighbours("rr", bottom, top)
    left, right = neighbours("row", last, first)
    return up, down, left, right


def local(packet, previous, potential, rotation, angular, damping, absorber, stencil_index, stencil_weight):
    packet, previous, potential = packet[0], previous[0], potential[0]
    rotation, angular, damping, absorber = rotation[0], angular[0], damping[0], absorber[0]
    count_r, rows, width = packet.shape
    count_rr, count_row = (lax.axis_size(name) for name in ("rr", "row"))
    chips = count_row // CORES
    rotation, damping, absorber = (jnp.swapaxes(value, 0, 1) for value in (rotation, damping, absorber))
    stencil_index, stencil_weight = (jnp.swapaxes(value, 1, 2) for value in (stencil_index, stencil_weight))
    packet, previous, potential, rotation, damping, absorber, stencil_index, stencil_weight, angular = (
        in_hbm(value)
        for value in (
            packet, previous, potential, rotation, damping, absorber, stencil_index, stencil_weight, angular
        )
    )

    top, bottom, first, last, tables, high, low = prepare(
        packet, previous, potential, rotation, damping, absorber, stencil_index, stencil_weight, angular
    )
    columns = count_row * rows * BAND
    left, right = neighbours("row", last, first)
    matrix = stencil_matrix(tables, count_r, columns)
    left, right, matrix = lax.optimization_barrier((left, right, matrix))
    table = bands(packet, previous, potential, tables, left, right, high, low)
    up, down = neighbours("rr", bottom, top)

    plane = ("sect", "rr")
    half = count_rr // FAR
    start = count_rr - 1
    entries = [count_rr + (k + 1) * half - 1 for k in range(FAR)]
    crossed = [lax.ppermute(table, plane, [(start, entry)]) for entry in entries]
    halos = (up, down, left, right)
    piece = sum(crossed)
    arrived = []
    for shift in (1, half - 1, 2):
        pairs = [(entry, entry - (half - 1) + (half - 1 + shift) % half) for entry in entries]
        arrived.append(lax.ppermute(piece, plane, pairs))
    one, *edges = first_iteration(packet, previous, potential, tables, halos, high, low, piece)
    *arrived, one, edges = lax.optimization_barrier((*arrived, one, edges))
    spread = piece + sum(arrived)
    line = ("sect", "row")

    def around(shift):
        pairs = []
        for chip in range(chips):
            for core in range(CORES):
                pairs.append(
                    (count_row + chip * CORES + core, count_row + ((chip + shift) % chips) * CORES + core)
                )
        return lax.ppermute(spread, line, pairs)

    rest = [around(1), around(3), around(2)]
    edge_matrix = stencil_edges(halos, rows, count_r, columns, spread)
    rest[1], edge_matrix, edges = lax.optimization_barrier((rest[1], edge_matrix, edges))
    later = exchange(*edges)
    *rest, later = lax.optimization_barrier((*rest, later))
    own = jnp.stack([spread, rest[0], rest[2], rest[1]], axis=0)
    other = lax.ppermute(
        own, line, [(count_row + i, count_row + i + 1 - 2 * (i % CORES)) for i in range(count_row)]
    )
    matrices = (*matrix, *edge_matrix)
    own_sums = own_source(one, matrices, own)
    other, own_sums = lax.optimization_barrier((other, own_sums))
    earlier, latest = last_iteration(own_sums, packet, potential, tables, later, high, low, matrices, other)
    return latest[None], earlier[None]


def solution(mesh):
    in_specs = (
        P("sect", "rr", "row", None),
        P("sect", "rr", "row", None),
        P("sect", "rr", "row", None),
        P("sect", "rr", "row"),
        P("sect", None, None),
        P("sect", "rr", "row"),
        P("sect", "rr", "row"),
        P(None, "rr", "row"),
        P(None, "rr", "row"),
    )
    out_specs = (P("sect", "rr", "row", None), P("sect", "rr", "row", None))
    return jax.shard_map(local, mesh=mesh, in_specs=in_specs, out_specs=out_specs, check_vma=False)
```

```python
import functools

import jax
import jax.numpy as jnp
from jax import lax
from jax.experimental import pallas as pl
from jax.experimental.pallas import tpu as pltpu
from jax.sharding import PartitionSpec as P

BAND = 2
STENCILS = 4
HALO = 2
LANES = 128
CHUNK = 16
LAST = 16
CORES = 2
PLANES = 2
ROT, RET, INDEX, WEIGHT, TABLES = 0, 1, 2, 6, 10
EXTRA = 2 * STENCILS * HALO
OFBAND = 32
MIB = 1 << 20
F32 = jnp.float32
BF16 = jnp.bfloat16
ANY = pl.BlockSpec(memory_space=pl.ANY)
HBM = pl.BlockSpec(memory_space=pltpu.HBM)
VMEM = pl.BlockSpec(memory_space=pltpu.VMEM)

SIDE1 = -16.0 / 96.0
SIDE2 = 1.0 / 96.0
MIDDLE = 2.0 * 30.0 / 96.0 - 7.5 / 4.0


def halves(value):
    high = value.astype(BF16)
    low = (value - high.astype(F32)).astype(BF16)
    return high, low


def product(left, right_high, right_low):
    high, low = left
    total = jnp.dot(high, right_high, preferred_element_type=F32)
    total += jnp.dot(low, right_high, preferred_element_type=F32)
    return total + jnp.dot(high, right_low, preferred_element_type=F32)


def doubled_hamilton(field, index, start, count, lanes, turned, potential, rotation):
    def at(shift_r, shift_v):
        return field[index + shift_r, pl.ds(start + shift_v, count), lanes]

    middle = at(0, 0)
    near = at(-1, 0) + at(1, 0) + (at(0, -1) + at(0, 1))
    far = at(-2, 0) + at(2, 0) + (at(0, -2) + at(0, 2))
    return (
        SIDE1 * near
        + SIDE2 * far
        + (0.25 * potential + MIDDLE) * middle
        + (0.25 * rotation) * turned
    )


def in_hbm(value):
    return pltpu.with_memory_space_constraint(value, pltpu.HBM)


def holds_bands():
    return (lax.axis_index("sect") == 0) & (lax.axis_index("rr") == lax.axis_size("rr") - 1)


def in_product():
    return lax.axis_index("sect") == 1


def retained_of(damping, absorber):
    return 1.0 - absorber.astype(F32) * (1.0 - damping)


def band_kernel(
    packet, previous, potential, tables, left, right, high, low, out, field, later, turned, held, sems
):
    count_r, rows, width = packet.shape
    base = 16
    wide = rows + 16
    begin = left.shape[0] - OFBAND

    @pl.when(holds_bands())
    def _():
        copies = [
            pltpu.make_async_copy(packet.at[pl.ds(count_r - 6, 6)], field.at[pl.ds(2, 6), pl.ds(base, rows)], sems.at[0]),
            pltpu.make_async_copy(previous.at[pl.ds(count_r - 4, 4)], held.at[0], sems.at[1]),
            pltpu.make_async_copy(potential.at[pl.ds(count_r - 4, 4)], held.at[1], sems.at[2]),
        ]
        later[...] = jnp.zeros_like(later)
        field[0:2] = jnp.zeros_like(field[0:2])
        field[8:10] = jnp.zeros_like(field[8:10])
        for k in range(2, 8):
            field[k, 0:base] = jnp.zeros((base, width), F32)
            field[k, base + rows :] = jnp.zeros((base, width), F32)
        for copy in copies:
            copy.start()
        for k in range(4):
            at = begin + 4 * k
            field[4 + k, base - 4 : base] = left[at : at + 4]
            field[4 + k, base + rows : base + rows + 4] = right[at : at + 4]
        columns = [
            (tables[ROT, :, count_r - 4 + k : count_r - 3 + k], tables[RET, :, count_r - 4 + k : count_r - 3 + k])
            for k in range(4)
        ]
        columns = [tuple(jnp.broadcast_to(c, (rows, LANES)) for c in pair) for pair in columns]
        for copy in copies:
            copy.wait()
        window = field[4:8, base - 8 : base + rows + 8].reshape(4 * wide, width)
        turned[...] = product(halves(window), high[...], low[...])
        for k in range(4):
            rotation, retained = columns[k]
            for at in range(0, width, LANES):
                lanes = slice(at, at + LANES)
                update = doubled_hamilton(
                    field, 4 + k, base, rows, lanes,
                    turned[k * wide + 8 : k * wide + 8 + rows, lanes], held[1, k, :, lanes], rotation,
                ) - retained * held[0, k, :, lanes]
                later[k, base : base + rows, lanes] = retained * update
                if k >= 2:
                    out[(k - 2) * rows : (k - 1) * rows, lanes] = (1.0 - retained) * update
        for k in range(2, 4):
            for slab, place, inside in ((left, base - 8, 6), (right, base + rows, 0)):
                at = begin + 16 + 2 * (k - 2)
                prev, pot, rot, ret = (slab[at + 4 * n : at + 4 * n + 2] for n in range(4))
                update = doubled_hamilton(
                    field, 4 + k, place + inside, 2, slice(None),
                    turned[k * wide + place - base + 8 + inside : k * wide + place - base + 10 + inside], pot, rot,
                ) - ret * prev
                later[k, place + inside : place + inside + 2] = ret * update
        window = later[2:4, base : base + rows].reshape(2 * rows, width)
        turned[0 : 2 * rows] = product(halves(window), high[...], low[...])
        for k in range(2, 4):
            rotation, retained = columns[k]
            for at in range(0, width, LANES):
                lanes = slice(at, at + LANES)
                update = doubled_hamilton(
                    later, k, base, rows, lanes,
                    turned[(k - 2) * rows : (k - 1) * rows, lanes], held[1, k, :, lanes], rotation,
                ) - retained * field[4 + k, base : base + rows, lanes]
                out[k * rows : (k + 1) * rows, lanes] = (1.0 - retained) * update


def bands(packet, previous, potential, tables, left, right, high, low):
    _, rows, width = packet.shape
    return pl.pallas_call(
        band_kernel,
        in_specs=[HBM, HBM, HBM, VMEM, VMEM, VMEM, VMEM, VMEM],
        out_specs=VMEM,
        out_shape=jax.ShapeDtypeStruct((2 * BAND * rows, width), F32),
        scratch_shapes=[
            pltpu.VMEM((10, rows + 32, width), F32),
            pltpu.VMEM((6, rows + 32, width), F32),
            pltpu.VMEM((4 * (rows + 16), width), F32),
            pltpu.VMEM((2, 4, rows, width), F32),
            pltpu.SemaphoreType.DMA((3,)),
        ],
        compiler_params=pltpu.CompilerParams(vmem_limit_bytes=16 * MIB),
        cost_estimate=pl.CostEstimate(flops=400_000_000, bytes_accessed=4 * MIB, transcendentals=0),
        name="both_bands",
    )(packet, previous, potential, tables, left, right, high, low)


def prepare_kernel(
    packet, previous, potential, rotation, damping, absorber, index, weight, angular,
    top, bottom, first, last, tables, high, low,
    ends, sides, others, factors, masks, indices, weights, matrix, sems,
):
    count_r, rows, width = packet.shape
    small = [
        pltpu.make_async_copy(rotation, factors.at[0], sems.at[0]),
        pltpu.make_async_copy(damping, factors.at[1], sems.at[1]),
        pltpu.make_async_copy(absorber, masks, sems.at[2]),
        pltpu.make_async_copy(index, indices, sems.at[3]),
        pltpu.make_async_copy(weight, weights, sems.at[4]),
    ]
    copies = [
        pltpu.make_async_copy(packet.at[:, pl.ds(0, 8)], sides.at[0], sems.at[5]),
        pltpu.make_async_copy(packet.at[:, pl.ds(rows - 8, 8)], sides.at[1], sems.at[6]),
        pltpu.make_async_copy(packet.at[pl.ds(0, HALO)], ends.at[0], sems.at[7]),
        pltpu.make_async_copy(packet.at[pl.ds(count_r - HALO, HALO)], ends.at[1], sems.at[8]),
        pltpu.make_async_copy(previous.at[pl.ds(count_r - BAND, BAND)], others.at[0], sems.at[9]),
        pltpu.make_async_copy(potential.at[pl.ds(count_r - BAND, BAND)], others.at[1], sems.at[10]),
        pltpu.make_async_copy(angular, matrix, sems.at[11]),
    ]
    for copy in small + copies:
        copy.start()
    for copy in small:
        copy.wait()
    values = [factors[0], retained_of(factors[1], masks[...])]
    values += [indices[n].astype(F32) for n in range(STENCILS)]
    values += [weights[n] for n in range(STENCILS)]
    for n, value in enumerate(values):
        tables[n] = jnp.concatenate([value, jnp.zeros((rows, LANES - count_r), F32)], axis=1)
    edges = HALO * rows
    columns = HALO * count_r
    lane = lax.broadcasted_iota(jnp.int32, (rows, LANES), 1)
    upper = jnp.zeros((rows, LANES), F32)
    lower = jnp.zeros((rows, LANES), F32)
    for n in range(2 * STENCILS):
        value = tables[INDEX + n]
        at = n * HALO
        here = (lane >= at) & (lane < at + HALO)
        upper = jnp.where(here, pltpu.roll(value, at, 1), upper)
        lower = jnp.where(here, pltpu.roll(value, (at + LANES - (count_r - HALO)) % LANES, 1), lower)
        first[columns + at : columns + at + HALO, 0:LANES] = value[0:HALO]
        last[columns + at : columns + at + HALO, 0:LANES] = value[rows - HALO : rows]
    top[edges : edges + rows, 0:LANES] = upper
    bottom[edges : edges + rows, 0:LANES] = lower
    begin = columns + EXTRA
    for copy in copies:
        copy.wait()
    for out, n, far, near in ((first, 0, 0, 0), (last, 1, 4, rows - 2)):
        for k in range(4):
            out[begin + 4 * k : begin + 4 * k + 4] = sides[n, count_r - 4 + k, far : far + 4]
        for k in range(BAND):
            at = begin + 16 + 2 * k
            column = count_r - BAND + k
            out[at : at + 2] = others[0, k, near : near + 2]
            out[at + 4 : at + 6] = others[1, k, near : near + 2]
            for m in (ROT, RET):
                value = tables[m, near : near + 2, column : column + 1]
                out[at + 8 + 4 * m : at + 10 + 4 * m] = jnp.broadcast_to(value, (2, width))
    for out, n, near in ((first, 0, 0), (last, 1, 8 - HALO)):
        for k in range(count_r):
            for r in range(HALO):
                out[r * count_r + k : r * count_r + k + 1] = sides[n, k, near + r : near + r + 1]
    for out, n in ((top, 0), (bottom, 1)):
        for k in range(HALO):
            out[k * rows : (k + 1) * rows] = ends[n, k]
    high[...], low[...] = halves(matrix[...])


def prepare(packet, previous, potential, rotation, damping, absorber, index, weight, angular):
    count_r, rows, width = packet.shape
    ends = jax.ShapeDtypeStruct((HALO * rows + rows, width), F32)
    sides = jax.ShapeDtypeStruct((HALO * count_r + EXTRA + OFBAND, width), F32)
    part = jax.ShapeDtypeStruct(angular.shape, BF16)
    return pl.pallas_call(
        prepare_kernel,
        in_specs=[HBM] * 9,
        out_specs=[VMEM] * 7,
        out_shape=[ends, ends, sides, sides, jax.ShapeDtypeStruct((TABLES, rows, LANES), F32), part, part],
        scratch_shapes=[
            pltpu.VMEM((2, HALO, rows, width), F32),
            pltpu.VMEM((2, count_r, 8, width), F32),
            pltpu.VMEM((2, BAND, rows, width), F32),
            pltpu.VMEM((2, rows, count_r), F32),
            pltpu.VMEM((rows, count_r), jnp.int32),
            pltpu.VMEM((STENCILS, rows, count_r), jnp.int32),
            pltpu.VMEM((STENCILS, rows, count_r), F32),
            pltpu.VMEM(angular.shape, F32),
            pltpu.SemaphoreType.DMA((12,)),
        ],
        compiler_params=pltpu.CompilerParams(vmem_limit_bytes=16 * MIB),
        cost_estimate=pl.CostEstimate(flops=1_000_000, bytes_accessed=6 * MIB, transcendentals=0),
        name="prepare",
    )(packet, previous, potential, rotation, damping, absorber, index, weight, angular)


def put_sides(sides, left, right, count_r, left_more=None, right_more=None):
    def body(k, carry):
        for r in range(HALO):
            at = pl.ds(r * count_r + k, 1)
            before, behind = left[at], right[at]
            if left_more is not None:
                before, behind = before + left_more[at], behind + right_more[at]
            sides[k, r : r + 1] = behind
            sides[k, 8 - HALO + r : 8 - HALO + r + 1] = before
        return carry

    lax.fori_loop(0, count_r, body, 0, unroll=8)


def advance(step, chunk, field, sides, previous, potential, tables, high, low, put, more=None):
    rows = previous.shape[1]
    width = previous.shape[2]
    here = step * chunk
    shift = lax.rem(LANES - here, LANES)
    columns = [pltpu.roll(tables[n], shift, 1) for n in (ROT, RET)]
    window = field[pl.ds(HALO + here, chunk)].reshape(chunk * rows, width)
    split = halves(window)
    wide = 2 * LANES
    for tile in range(0, width, wide):
        turned = product(split, high[:, tile : tile + wide], low[:, tile : tile + wide])
        source = None if more is None else more(slice(tile, tile + wide))
        for k in range(chunk):
            rotation = jnp.broadcast_to(0.25 * columns[0][:, k : k + 1], (rows, LANES))
            retained = jnp.broadcast_to(columns[1][:, k : k + 1], (rows, LANES))
            for at in range(tile, tile + wide, LANES):
                lanes = slice(at, at + LANES)

                def row(shift):
                    return field[HALO + here + k + shift, :, lanes]

                middle = row(0)
                ring = jnp.concatenate([middle, sides[here + k, :, lanes]], axis=0)
                around = [pltpu.roll(ring, s, 0)[:rows] for s in (1, rows + 7, 2, rows + 6)]
                near = row(-1) + row(1) + (around[0] + around[1])
                far = row(-2) + row(2) + (around[2] + around[3])
                update = (
                    SIDE1 * near
                    + SIDE2 * far
                    + (0.25 * potential[here + k, :, lanes] + MIDDLE) * middle
                    + rotation * turned[k * rows : (k + 1) * rows, at - tile : at - tile + LANES]
                    - retained * previous[here + k, :, lanes]
                )
                value = retained * update
                if source is not None:
                    value += source[k * rows : (k + 1) * rows, at - tile : at - tile + LANES]
                put(here + k, lanes, value)


def first_kernel(
    packet, previous, potential, tables, left, right, high, low, after,
    done, top, bottom, first, last, field, prev, pot, sides, sems,
):
    count_r, rows, width = packet.shape
    steps = count_r // CHUNK

    def copies(n):
        part = pl.ds(n * CHUNK, CHUNK)
        return (
            pltpu.make_async_copy(packet.at[part], field.at[pl.ds(HALO + n * CHUNK, CHUNK)], sems.at[0, n]),
            pltpu.make_async_copy(previous.at[part], prev.at[part], sems.at[1, n]),
            pltpu.make_async_copy(potential.at[part], pot.at[part], sems.at[2, n]),
        )

    for n in range(steps):
        for copy in copies(n):
            copy.start()
    field[0:HALO] = jnp.zeros((HALO, rows, width), F32)
    field[HALO + count_r :] = jnp.zeros((HALO, rows, width), F32)
    put_sides(sides, left, right, count_r)
    copies(0)[0].wait()

    def put(k, lanes, value):
        done[k, :, lanes] = value

    def body(n, carry):
        @pl.when(n + 1 < steps)
        def _():
            copies(n + 1)[0].wait()

        copies(n)[1].wait()
        copies(n)[2].wait()
        advance(n, CHUNK, field, sides, prev, pot, tables, high, low, put)
        for k in range(CHUNK):
            for r in range(HALO):
                at = pl.ds(r * count_r + n * CHUNK + k, 1)
                first[at] = done[n * CHUNK + k, r : r + 1]
                last[at] = done[n * CHUNK + k, rows - HALO + r : rows - HALO + r + 1]
        return carry

    lax.fori_loop(0, steps, body, 0)
    for k in range(HALO):
        top[k * rows : (k + 1) * rows] = done[k]
        bottom[k * rows : (k + 1) * rows] = done[count_r - HALO + k]


def first_iteration(packet, previous, potential, tables, left, right, high, low, after):
    count_r, rows, width = packet.shape
    ends = jax.ShapeDtypeStruct((HALO * rows, width), F32)
    sides = jax.ShapeDtypeStruct((HALO * count_r, width), F32)
    return pl.pallas_call(
        first_kernel,
        in_specs=[HBM, HBM, HBM, *[VMEM] * 5, ANY],
        out_specs=[VMEM] * 5,
        out_shape=[jax.ShapeDtypeStruct(packet.shape, F32), ends, ends, sides, sides],
        scratch_shapes=[
            pltpu.VMEM((count_r + 2 * HALO, rows, width), F32),
            pltpu.VMEM(packet.shape, F32),
            pltpu.VMEM(packet.shape, F32),
            pltpu.VMEM((count_r, 8, width), F32),
            pltpu.SemaphoreType.DMA((3, count_r // CHUNK)),
        ],
        compiler_params=pltpu.CompilerParams(vmem_limit_bytes=28 * MIB),
        cost_estimate=pl.CostEstimate(flops=7_000_000_000, bytes_accessed=20 * MIB, transcendentals=0),
        name="first_iteration",
    )(packet, previous, potential, tables, left, right, high, low, after)


def slot_of(value, rows, width):
    per = rows * BAND
    shift_owner = per.bit_length() - 1
    chips = width // per // CORES
    row = lax.axis_index("row")
    index = value.astype(jnp.int32)
    owner = index >> shift_owner
    inside = index & (per - 1)
    core = (owner & 1) ^ (row & 1)
    chip = ((row >> 1) - (owner >> 1)) & (chips - 1)
    slot = ((core * chips + chip) << shift_owner) + (inside & 1) * rows + (inside >> 1)
    return slot.astype(F32)


def fill_rows(at, cut, rows, high, low, begin=0):
    column = lax.broadcasted_iota(jnp.int32, (rows, LANES), 1).astype(F32)
    cut = [jnp.broadcast_to(value, (rows, LANES)) for value in cut]
    for tile in range(0, high.shape[1], LANES):
        here = column + float(begin + tile)
        total = jnp.where(here == cut[0], cut[STENCILS], 0.0)
        for n in range(1, STENCILS):
            total += jnp.where(here == cut[n], cut[STENCILS + n], 0.0)
        upper, lower = halves(total)
        high[pl.ds(at, rows), tile : tile + LANES] = upper
        low[pl.ds(at, rows), tile : tile + LANES] = lower


def stencil_kernel(tables, after, high, low, *, side):
    _, rows, _ = tables.shape
    count_r = high.shape[0] // rows
    group = 8
    half = high.shape[1]

    @pl.when(in_product())
    def _():
        values = [slot_of(tables[INDEX + n], rows, CORES * half) for n in range(STENCILS)]
        values += [tables[WEIGHT + n] for n in range(STENCILS)]

        def body(step, carry):
            shift = lax.rem(LANES - step * group, LANES)
            moved = [pltpu.roll(value, shift, 1) for value in values]
            for k in range(group):
                at = pl.multiple_of((step * group + k) * rows, rows)
                fill_rows(at, [value[:, k : k + 1] for value in moved], rows, high, low, side * half)
            return carry

        lax.fori_loop(0, count_r // group, body, 0)


def stencil_matrix(tables, count_r, columns, side, after):
    rows = tables.shape[1]
    points = jax.ShapeDtypeStruct((count_r * rows, columns // CORES), BF16)
    return pl.pallas_call(
        functools.partial(stencil_kernel, side=side),
        in_specs=[VMEM, ANY],
        out_specs=[VMEM] * 2,
        out_shape=[points, points],
        compiler_params=pltpu.CompilerParams(vmem_limit_bytes=16 * MIB),
        cost_estimate=pl.CostEstimate(flops=8_000_000, bytes_accessed=6 * MIB, transcendentals=0),
        name="stencil_matrix",
    )(tables, after)


def edge_kernel(
    up, down, left, right, tables, top, bottom, first, last, after,
    high, low, new_top, new_bottom, new_first, new_last, added, square, *, rows, count_r,
):
    width = up.shape[1]
    edges = HALO * rows

    def retained(k):
        return jnp.broadcast_to(tables[RET, :, k : k + 1], (rows, width))

    added[0] = retained(0) * (SIDE1 * up[rows:edges] + SIDE2 * up[0:rows])
    added[1] = retained(1) * (SIDE2 * up[rows:edges])
    added[2] = retained(count_r - 2) * (SIDE2 * down[0:rows])
    added[3] = retained(count_r - 1) * (SIDE1 * down[0:rows] + SIDE2 * down[rows:edges])
    new_first[...] = first[...]
    new_last[...] = last[...]
    for k in range(HALO):
        here = slice(k * rows, (k + 1) * rows)
        new_top[here] = top[here] + added[k]
        new_bottom[here] = bottom[here] + added[HALO + k]
        for n, r_row in ((k, k), (HALO + k, count_r - HALO + k)):
            for r in range(HALO):
                at = r * count_r + r_row
                new_first[at : at + 1] = first[at : at + 1] + added[n, r : r + 1]
                new_last[at : at + 1] = last[at : at + 1] + added[n, rows - HALO + r : rows - HALO + r + 1]

    @pl.when(in_product())
    def _():
        at = 0
        for side in (up, down):
            value = side[edges : edges + rows, 0:LANES]
            slots = slot_of(value, rows, high.shape[1])
            for e in range(HALO):
                cut = [
                    (slots if m < STENCILS else value)[:, HALO * m + e : HALO * m + e + 1]
                    for m in range(2 * STENCILS)
                ]
                fill_rows(at, cut, rows, high, low)
                at += rows
        square[...] = jnp.zeros_like(square)
        part = EXTRA // 2
        for n, side in enumerate((left, right)):
            begin = HALO * count_r
            square[n * EXTRA : n * EXTRA + part] = slot_of(side[begin : begin + part, 0:LANES], rows, high.shape[1])
            square[n * EXTRA + part : (n + 1) * EXTRA] = side[begin + part : begin + EXTRA, 0:LANES]
        turned = square[...].T
        for n in range(2):
            for e in range(HALO):
                for begin in range(0, count_r, rows):
                    cut = [
                        turned[begin : begin + rows, n * EXTRA + HALO * m + e : n * EXTRA + HALO * m + e + 1]
                        for m in range(2 * STENCILS)
                    ]
                    fill_rows(at, cut, rows, high, low)
                    at += rows


def finish_edges(halos, tables, edges, rows, count_r, columns, after):
    points = jax.ShapeDtypeStruct((2 * HALO * (rows + count_r), columns), BF16)
    width = edges[0].shape[1]
    return pl.pallas_call(
        functools.partial(edge_kernel, rows=rows, count_r=count_r),
        in_specs=[*[VMEM] * 9, ANY],
        out_specs=[VMEM] * 7,
        out_shape=[
            points, points,
            *[jax.ShapeDtypeStruct(edge.shape, F32) for edge in edges],
            jax.ShapeDtypeStruct((2 * HALO, rows, width), F32),
        ],
        scratch_shapes=[pltpu.VMEM((LANES, LANES), F32)],
        compiler_params=pltpu.CompilerParams(vmem_limit_bytes=16 * MIB),
        cost_estimate=pl.CostEstimate(flops=2_000_000, bytes_accessed=3 * MIB, transcendentals=0),
        name="finish_edges",
    )(*halos, tables, *edges, after)


def split_table(pieces, table):
    half = pieces.shape[1] // 2
    for k in range(pieces.shape[0]):
        for band in range(2):
            upper, lower = halves(pieces[k, band * half : (band + 1) * half])
            table[2 * band, k * half : (k + 1) * half] = upper
            table[2 * band + 1, k * half : (k + 1) * half] = lower


def own_source_kernel(
    one, added, stencil_high, stencil_low, edge_high, edge_low, own, sum_one, source, edge_source, table
):
    count_r, rows, width = one.shape
    columns = table.shape[1]
    size = LAST * rows

    @pl.when(in_product())
    def _():
        split_table(own, table)

        def body(n, carry):
            cut = pl.ds(pl.multiple_of(n * size, size), size)
            part = pl.ds(n * LAST, LAST)
            weights = (stencil_high[cut], stencil_low[cut])
            sum_one[part] = one[part] + product(weights, table[0], table[1]).reshape(LAST, rows, width)
            source[cut] = product(weights, table[2], table[3])
            return carry

        lax.fori_loop(0, count_r // LAST, body, 0)
        edge_source[...] = product((edge_high[:, 0:columns], edge_low[:, 0:columns]), table[0], table[1])

    @pl.when(jnp.logical_not(in_product()))
    def _():
        sum_one[...] = one[...]

    for k in range(HALO):
        sum_one[k] += added[k]
        sum_one[count_r - HALO + k] += added[HALO + k]


def own_source(one, added, matrices, own):
    count_r, rows, width = one.shape
    points = count_r * rows
    return pl.pallas_call(
        own_source_kernel,
        in_specs=[VMEM] * 7,
        out_specs=[VMEM] * 3,
        out_shape=[
            jax.ShapeDtypeStruct(one.shape, F32),
            jax.ShapeDtypeStruct((points, width), F32),
            jax.ShapeDtypeStruct((matrices[2].shape[0], width), F32),
        ],
        scratch_shapes=[pltpu.VMEM((4, own.shape[0] * own.shape[1] // 2, width), BF16)],
        compiler_params=pltpu.CompilerParams(vmem_limit_bytes=16 * MIB),
        cost_estimate=pl.CostEstimate(flops=7_000_000_000, bytes_accessed=20 * MIB, transcendentals=0),
        name="own_source",
    )(one, added, *matrices, own)


def last_kernel(
    one, source, edge_source, packet, potential, tables, up, down, left, right, high, low,
    stencil_high, stencil_low, edge_high, edge_low, other,
    earlier, latest, field, prev, pot, done, sides, table, ends, sems,
):
    count_r, rows, width = packet.shape
    steps = count_r // LAST
    size = LAST * rows
    columns = table.shape[1]
    is_product = in_product()

    def part(n):
        return pl.ds(n * LAST, LAST)

    def cut(n):
        return pl.ds(pl.multiple_of(n * size, size), size)

    def locals_of(n):
        return (
            pltpu.make_async_copy(packet.at[part(n)], prev.at[part(n)], sems.at[0, n]),
            pltpu.make_async_copy(potential.at[part(n)], pot.at[part(n)], sems.at[1, n]),
        )

    def earliers(n):
        return pltpu.make_async_copy(field.at[pl.ds(HALO + n * LAST, LAST)], earlier.at[part(n)], sems.at[2, n])

    def latests(n):
        return pltpu.make_async_copy(done.at[part(n)], latest.at[part(n)], sems.at[3, n])

    def put_ends(up_value, down_value):
        for k in range(HALO):
            field[k] = up_value[k * rows : (k + 1) * rows]
            field[HALO + count_r + k] = down_value[k * rows : (k + 1) * rows]

    def put(k, lanes, value):
        done[k, :, lanes] = value

    for n in range(steps):
        for copy in locals_of(n):
            copy.start()

    @pl.when(is_product)
    def _():
        split_table(other, table)
        ends[...] = edge_source[...] + product(
            (edge_high[:, columns : 2 * columns], edge_low[:, columns : 2 * columns]), table[0], table[1]
        )
        edges = HALO * rows
        long = HALO * count_r
        put_ends(up[...] + ends[:edges], down[...] + ends[edges : 2 * edges])
        put_sides(
            sides, left, right, count_r, ends.at[pl.ds(2 * edges, long)], ends.at[pl.ds(2 * edges + long, long)]
        )

        def weights(n):
            return stencil_high[cut(n)], stencil_low[cut(n)]

        def add(n, carry):
            more = product(weights(n), table[0], table[1]).reshape(LAST, rows, width)
            field[pl.ds(HALO + n * LAST, LAST)] = one[part(n)] + more
            earliers(n).start()
            return carry

        lax.fori_loop(0, steps, add, 0)

        def body(n, carry):
            for copy in locals_of(n):
                copy.wait()
            matrix = weights(n)

            def more(lanes):
                return source[cut(n), lanes] + product(matrix, table[2, :, lanes], table[3, :, lanes])

            advance(n, LAST, field, sides, prev, pot, tables, high, low, put, more)
            latests(n).start()
            return carry

        lax.fori_loop(0, steps, body, 0)

    @pl.when(jnp.logical_not(is_product))
    def _():
        put_ends(up, down)
        put_sides(sides, left, right, count_r)
        for n in range(steps):
            field[pl.ds(HALO + n * LAST, LAST)] = one[part(n)]
            earliers(n).start()

        def body(n, carry):
            for copy in locals_of(n):
                copy.wait()
            advance(n, LAST, field, sides, prev, pot, tables, high, low, put)
            latests(n).start()
            return carry

        lax.fori_loop(0, steps, body, 0)

    for n in range(steps):
        earliers(n).wait()
        latests(n).wait()


def last_iteration(own_sums, packet, potential, tables, halos, high, low, matrices, other):
    count_r, rows, width = packet.shape
    steps = count_r // LAST
    return pl.pallas_call(
        last_kernel,
        in_specs=[VMEM, VMEM, VMEM, HBM, HBM, *[VMEM] * 12],
        out_specs=[HBM, HBM],
        out_shape=[jax.ShapeDtypeStruct(packet.shape, F32)] * 2,
        scratch_shapes=[
            pltpu.VMEM((count_r + 2 * HALO, rows, width), F32),
            pltpu.VMEM(packet.shape, F32),
            pltpu.VMEM(packet.shape, F32),
            pltpu.VMEM(packet.shape, F32),
            pltpu.VMEM((count_r, 8, width), F32),
            pltpu.VMEM((4, other.shape[0] * other.shape[1] // 2, width), BF16),
            pltpu.VMEM((2 * HALO * (rows + count_r), width), F32),
            pltpu.SemaphoreType.DMA((4, steps)),
        ],
        compiler_params=pltpu.CompilerParams(vmem_limit_bytes=32 * MIB),
        cost_estimate=pl.CostEstimate(flops=14_000_000_000, bytes_accessed=36 * MIB, transcendentals=0),
        name="last_iteration",
    )(*own_sums, packet, potential, tables, *halos, high, low, *matrices, other)


def neighbours(axis, upward, downward):
    count = lax.axis_size(axis)
    return (
        lax.ppermute(upward, axis, [(i, i + 1) for i in range(count - 1)]),
        lax.ppermute(downward, axis, [(i + 1, i) for i in range(count - 1)]),
    )


def local(packet, previous, potential, rotation, angular, damping, absorber, stencil_index, stencil_weight):
    packet, previous, potential = packet[0], previous[0], potential[0]
    rotation, angular, damping, absorber = rotation[0], angular[0], damping[0], absorber[0]
    count_r, rows, width = packet.shape
    count_rr, count_row = (lax.axis_size(name) for name in ("rr", "row"))
    chips = count_row // CORES
    rotation, damping, absorber = (jnp.swapaxes(value, 0, 1) for value in (rotation, damping, absorber))
    stencil_index, stencil_weight = (jnp.swapaxes(value, 1, 2) for value in (stencil_index, stencil_weight))
    packet, previous, potential, rotation, damping, absorber, stencil_index, stencil_weight, angular = (
        in_hbm(value)
        for value in (
            packet, previous, potential, rotation, damping, absorber, stencil_index, stencil_weight, angular
        )
    )

    top, bottom, first, last, tables, high, low = prepare(
        packet, previous, potential, rotation, damping, absorber, stencil_index, stencil_weight, angular
    )
    columns = count_row * rows * BAND
    left, right = neighbours("row", last, first)
    own_matrix = stencil_matrix(tables, count_r, columns, 0, first)
    left, right, own_matrix = lax.optimization_barrier((left, right, own_matrix))
    table = bands(packet, previous, potential, tables, left, right, high, low)

    half = count_rr // PLANES
    start = count_rr - 1
    plane = ("sect", "rr")
    low_side, high_side = start - half + 1, start - 1
    relays = [low_side, high_side, count_rr + half - 1, count_rr + start]
    crossed = [lax.ppermute(table, plane, [(start, relay)]) for relay in relays]
    one, *edges = first_iteration(packet, previous, potential, tables, left, right, high, low, table)
    *crossed, one, edges = lax.optimization_barrier((*crossed, one, edges))
    piece = sum(crossed)
    near = [(low_side, count_rr), (high_side, count_rr + half - 2)]
    near += [(count_rr + half - 1, count_rr + half - 3), (count_rr + start, count_rr + start - 2)]
    opposite = [(low_side, count_rr + low_side), (high_side, count_rr + high_side)]
    arrived = [lax.ppermute(piece, plane, near), lax.ppermute(piece, plane, opposite)]
    top, bottom, piece = lax.optimization_barrier((top, bottom, piece))
    up, down = neighbours("rr", bottom, top)
    other_matrix = stencil_matrix(tables, count_r, columns, 1, piece)
    *arrived, other_matrix, up, down = lax.optimization_barrier((*arrived, other_matrix, up, down))
    halos = (up, down, left, right)
    spread = piece + sum(arrived)
    line = ("sect", "row")

    def around(shift):
        pairs = []
        for chip in range(chips):
            for core in range(CORES):
                pairs.append(
                    (count_row + chip * CORES + core, count_row + ((chip + shift) % chips) * CORES + core)
                )
        return lax.ppermute(spread, line, pairs)

    rest = [around(1), around(3), around(2)]
    *edge_matrix, top, bottom, first, last, added = finish_edges(halos, tables, edges, rows, count_r, columns, spread)
    rest[0], edge_matrix, top, bottom = lax.optimization_barrier((rest[0], edge_matrix, top, bottom))
    up, down = neighbours("rr", bottom, top)
    rest[0], rest[1], first, last = lax.optimization_barrier((rest[0], rest[1], first, last))
    left, right = neighbours("row", last, first)
    *rest, up, down, left, right = lax.optimization_barrier((*rest, up, down, left, right))
    own = jnp.stack([spread, rest[0], rest[2], rest[1]], axis=0)
    other = lax.ppermute(
        own, line, [(count_row + i, count_row + i + 1 - 2 * (i % CORES)) for i in range(count_row)]
    )
    own_sums = own_source(one, added, (*own_matrix, *edge_matrix), own)
    other, own_sums = lax.optimization_barrier((other, own_sums))
    earlier, latest = last_iteration(
        own_sums, packet, potential, tables, (up, down, left, right), high, low, (*other_matrix, *edge_matrix), other
    )
    return latest[None], earlier[None]


def solution(mesh):
    in_specs = (
        P("sect", "rr", "row", None),
        P("sect", "rr", "row", None),
        P("sect", "rr", "row", None),
        P("sect", "rr", "row"),
        P("sect", None, None),
        P("sect", "rr", "row"),
        P("sect", "rr", "row"),
        P(None, "rr", "row"),
        P(None, "rr", "row"),
    )
    out_specs = (P("sect", "rr", "row", None), P("sect", "rr", "row", None))
    return jax.shard_map(local, mesh=mesh, in_specs=in_specs, out_specs=out_specs, check_vma=False)
```

```python
import functools

import jax
import jax.numpy as jnp
from jax import lax
from jax.experimental import pallas as pl
from jax.experimental.pallas import tpu as pltpu
from jax.sharding import PartitionSpec as P

BAND = 2
STENCILS = 4
HALO = 2
LANES = 128
CHUNK = 16
LAST = 16
CORES = 2
PLANES = 2
ROT, RET, INDEX, WEIGHT, TABLES = 0, 1, 2, 6, 10
EXTRA = 2 * STENCILS * HALO
OFBAND = 32
MIB = 1 << 20
F32 = jnp.float32
BF16 = jnp.bfloat16
ANY = pl.BlockSpec(memory_space=pl.ANY)
HBM = pl.BlockSpec(memory_space=pltpu.HBM)
VMEM = pl.BlockSpec(memory_space=pltpu.VMEM)

SIDE1 = -16.0 / 96.0
SIDE2 = 1.0 / 96.0
MIDDLE = 2.0 * 30.0 / 96.0 - 7.5 / 4.0


def halves(value):
    high = value.astype(BF16)
    low = (value - high.astype(F32)).astype(BF16)
    return high, low


def product(left, right_high, right_low):
    high, low = left
    total = jnp.dot(high, right_high, preferred_element_type=F32)
    total += jnp.dot(low, right_high, preferred_element_type=F32)
    return total + jnp.dot(high, right_low, preferred_element_type=F32)


def doubled_hamilton(field, index, start, count, lanes, turned, potential, rotation):
    def at(shift_r, shift_v):
        return field[index + shift_r, pl.ds(start + shift_v, count), lanes]

    middle = at(0, 0)
    near = at(-1, 0) + at(1, 0) + (at(0, -1) + at(0, 1))
    far = at(-2, 0) + at(2, 0) + (at(0, -2) + at(0, 2))
    return (
        SIDE1 * near
        + SIDE2 * far
        + (0.25 * potential + MIDDLE) * middle
        + (0.25 * rotation) * turned
    )


def in_hbm(value):
    return pltpu.with_memory_space_constraint(value, pltpu.HBM)


def holds_bands():
    return (lax.axis_index("sect") == 0) & (lax.axis_index("rr") == lax.axis_size("rr") - 1)


def in_product():
    return lax.axis_index("sect") == 1


def retained_of(damping, absorber):
    return 1.0 - absorber.astype(F32) * (1.0 - damping)


def band_kernel(
    packet, previous, potential, tables, left, right, high, low, out, field, later, turned, held, sems
):
    count_r, rows, width = packet.shape
    base = 16
    wide = rows + 16
    begin = left.shape[0] - OFBAND

    @pl.when(holds_bands())
    def _():
        copies = [
            pltpu.make_async_copy(packet.at[pl.ds(count_r - 6, 6)], field.at[pl.ds(2, 6), pl.ds(base, rows)], sems.at[0]),
            pltpu.make_async_copy(previous.at[pl.ds(count_r - 4, 4)], held.at[0], sems.at[1]),
            pltpu.make_async_copy(potential.at[pl.ds(count_r - 4, 4)], held.at[1], sems.at[2]),
        ]
        later[...] = jnp.zeros_like(later)
        field[0:2] = jnp.zeros_like(field[0:2])
        field[8:10] = jnp.zeros_like(field[8:10])
        for k in range(2, 8):
            field[k, 0:base] = jnp.zeros((base, width), F32)
            field[k, base + rows :] = jnp.zeros((base, width), F32)
        for copy in copies:
            copy.start()
        for k in range(4):
            at = begin + 4 * k
            field[4 + k, base - 4 : base] = left[at : at + 4]
            field[4 + k, base + rows : base + rows + 4] = right[at : at + 4]
        columns = [
            (tables[ROT, :, count_r - 4 + k : count_r - 3 + k], tables[RET, :, count_r - 4 + k : count_r - 3 + k])
            for k in range(4)
        ]
        columns = [tuple(jnp.broadcast_to(c, (rows, LANES)) for c in pair) for pair in columns]
        for copy in copies:
            copy.wait()
        window = field[4:8, base - 8 : base + rows + 8].reshape(4 * wide, width)
        turned[...] = product(halves(window), high[...], low[...])
        for k in range(4):
            rotation, retained = columns[k]
            for at in range(0, width, LANES):
                lanes = slice(at, at + LANES)
                update = doubled_hamilton(
                    field, 4 + k, base, rows, lanes,
                    turned[k * wide + 8 : k * wide + 8 + rows, lanes], held[1, k, :, lanes], rotation,
                ) - retained * held[0, k, :, lanes]
                later[k, base : base + rows, lanes] = retained * update
                if k >= 2:
                    out[(k - 2) * rows : (k - 1) * rows, lanes] = (1.0 - retained) * update
        for k in range(2, 4):
            for slab, place, inside in ((left, base - 8, 6), (right, base + rows, 0)):
                at = begin + 16 + 2 * (k - 2)
                prev, pot, rot, ret = (slab[at + 4 * n : at + 4 * n + 2] for n in range(4))
                update = doubled_hamilton(
                    field, 4 + k, place + inside, 2, slice(None),
                    turned[k * wide + place - base + 8 + inside : k * wide + place - base + 10 + inside], pot, rot,
                ) - ret * prev
                later[k, place + inside : place + inside + 2] = ret * update
        window = later[2:4, base : base + rows].reshape(2 * rows, width)
        turned[0 : 2 * rows] = product(halves(window), high[...], low[...])
        for k in range(2, 4):
            rotation, retained = columns[k]
            for at in range(0, width, LANES):
                lanes = slice(at, at + LANES)
                update = doubled_hamilton(
                    later, k, base, rows, lanes,
                    turned[(k - 2) * rows : (k - 1) * rows, lanes], held[1, k, :, lanes], rotation,
                ) - retained * field[4 + k, base : base + rows, lanes]
                out[k * rows : (k + 1) * rows, lanes] = (1.0 - retained) * update


def bands(packet, previous, potential, tables, left, right, high, low):
    _, rows, width = packet.shape
    return pl.pallas_call(
        band_kernel,
        in_specs=[HBM, HBM, HBM, VMEM, VMEM, VMEM, VMEM, VMEM],
        out_specs=VMEM,
        out_shape=jax.ShapeDtypeStruct((2 * BAND * rows, width), F32),
        scratch_shapes=[
            pltpu.VMEM((10, rows + 32, width), F32),
            pltpu.VMEM((6, rows + 32, width), F32),
            pltpu.VMEM((4 * (rows + 16), width), F32),
            pltpu.VMEM((2, 4, rows, width), F32),
            pltpu.SemaphoreType.DMA((3,)),
        ],
        compiler_params=pltpu.CompilerParams(vmem_limit_bytes=16 * MIB),
        cost_estimate=pl.CostEstimate(flops=400_000_000, bytes_accessed=4 * MIB, transcendentals=0),
        name="both_bands",
    )(packet, previous, potential, tables, left, right, high, low)


def prepare_kernel(
    packet, previous, potential, rotation, damping, absorber, index, weight, angular,
    upper, lower, first, last, tables, high, low,
    sides, others, factors, masks, indices, weights, matrix, sems,
):
    count_r, rows, width = packet.shape
    small = [
        pltpu.make_async_copy(rotation, factors.at[0], sems.at[0]),
        pltpu.make_async_copy(damping, factors.at[1], sems.at[1]),
        pltpu.make_async_copy(absorber, masks, sems.at[2]),
        pltpu.make_async_copy(index, indices, sems.at[3]),
        pltpu.make_async_copy(weight, weights, sems.at[4]),
    ]
    copies = [
        pltpu.make_async_copy(packet.at[:, pl.ds(0, 8)], sides.at[0], sems.at[5]),
        pltpu.make_async_copy(packet.at[:, pl.ds(rows - 8, 8)], sides.at[1], sems.at[6]),
        pltpu.make_async_copy(previous.at[pl.ds(count_r - BAND, BAND)], others.at[0], sems.at[7]),
        pltpu.make_async_copy(potential.at[pl.ds(count_r - BAND, BAND)], others.at[1], sems.at[8]),
        pltpu.make_async_copy(angular, matrix, sems.at[9]),
    ]
    for copy in small + copies:
        copy.start()
    for copy in small:
        copy.wait()
    values = [factors[0], retained_of(factors[1], masks[...])]
    values += [indices[n].astype(F32) for n in range(STENCILS)]
    values += [weights[n] for n in range(STENCILS)]
    for n, value in enumerate(values):
        tables[n] = jnp.concatenate([value, jnp.zeros((rows, LANES - count_r), F32)], axis=1)
    columns = HALO * count_r
    lane = lax.broadcasted_iota(jnp.int32, (rows, LANES), 1)
    at_top = jnp.zeros((rows, LANES), F32)
    at_bottom = jnp.zeros((rows, LANES), F32)
    for n, table in enumerate([*range(INDEX, TABLES), RET]):
        value = tables[table]
        at = n * HALO
        here = (lane >= at) & (lane < at + HALO)
        at_top = jnp.where(here, pltpu.roll(value, at, 1), at_top)
        at_bottom = jnp.where(here, pltpu.roll(value, (at + LANES - (count_r - HALO)) % LANES, 1), at_bottom)
        if table != RET:
            first[columns + at : columns + at + HALO, 0:LANES] = value[0:HALO]
            last[columns + at : columns + at + HALO, 0:LANES] = value[rows - HALO : rows]
    upper[...] = at_top
    lower[...] = at_bottom
    begin = columns + EXTRA
    for copy in copies:
        copy.wait()
    for out, n, far, near in ((first, 0, 0, 0), (last, 1, 4, rows - 2)):
        for k in range(4):
            out[begin + 4 * k : begin + 4 * k + 4] = sides[n, count_r - 4 + k, far : far + 4]
        for k in range(BAND):
            at = begin + 16 + 2 * k
            column = count_r - BAND + k
            out[at : at + 2] = others[0, k, near : near + 2]
            out[at + 4 : at + 6] = others[1, k, near : near + 2]
            for m in (ROT, RET):
                value = tables[m, near : near + 2, column : column + 1]
                out[at + 8 + 4 * m : at + 10 + 4 * m] = jnp.broadcast_to(value, (2, width))
    for out, n, near in ((first, 0, 0), (last, 1, 8 - HALO)):
        for k in range(count_r):
            for r in range(HALO):
                out[r * count_r + k : r * count_r + k + 1] = sides[n, k, near + r : near + r + 1]
    high[...], low[...] = halves(matrix[...])


def prepare(packet, previous, potential, rotation, damping, absorber, index, weight, angular):
    count_r, rows, width = packet.shape
    ends = jax.ShapeDtypeStruct((rows, LANES), F32)
    sides = jax.ShapeDtypeStruct((HALO * count_r + EXTRA + OFBAND, width), F32)
    part = jax.ShapeDtypeStruct(angular.shape, BF16)
    return pl.pallas_call(
        prepare_kernel,
        in_specs=[HBM] * 9,
        out_specs=[VMEM] * 7,
        out_shape=[ends, ends, sides, sides, jax.ShapeDtypeStruct((TABLES, rows, LANES), F32), part, part],
        scratch_shapes=[
            pltpu.VMEM((2, count_r, 8, width), F32),
            pltpu.VMEM((2, BAND, rows, width), F32),
            pltpu.VMEM((2, rows, count_r), F32),
            pltpu.VMEM((rows, count_r), jnp.int32),
            pltpu.VMEM((STENCILS, rows, count_r), jnp.int32),
            pltpu.VMEM((STENCILS, rows, count_r), F32),
            pltpu.VMEM(angular.shape, F32),
            pltpu.SemaphoreType.DMA((10,)),
        ],
        compiler_params=pltpu.CompilerParams(vmem_limit_bytes=16 * MIB),
        cost_estimate=pl.CostEstimate(flops=1_000_000, bytes_accessed=6 * MIB, transcendentals=0),
        name="prepare",
    )(packet, previous, potential, rotation, damping, absorber, index, weight, angular)


def put_sides(sides, left, right, count_r, left_more=None, right_more=None):
    def body(k, carry):
        for r in range(HALO):
            at = pl.ds(r * count_r + k, 1)
            before, behind = left[at], right[at]
            if left_more is not None:
                before, behind = before + left_more[at], behind + right_more[at]
            sides[k, r : r + 1] = behind
            sides[k, 8 - HALO + r : 8 - HALO + r + 1] = before
        return carry

    lax.fori_loop(0, count_r, body, 0, unroll=8)


def advance(step, chunk, field, sides, previous, potential, tables, high, low, put, more=None):
    rows = previous.shape[1]
    width = previous.shape[2]
    here = step * chunk
    shift = lax.rem(LANES - here, LANES)
    columns = [pltpu.roll(tables[n], shift, 1) for n in (ROT, RET)]
    window = field[pl.ds(HALO + here, chunk)].reshape(chunk * rows, width)
    split = halves(window)
    wide = 2 * LANES
    for tile in range(0, width, wide):
        turned = product(split, high[:, tile : tile + wide], low[:, tile : tile + wide])
        source = None if more is None else more(slice(tile, tile + wide))
        for k in range(chunk):
            rotation = jnp.broadcast_to(0.25 * columns[0][:, k : k + 1], (rows, LANES))
            retained = jnp.broadcast_to(columns[1][:, k : k + 1], (rows, LANES))
            for at in range(tile, tile + wide, LANES):
                lanes = slice(at, at + LANES)

                def row(shift):
                    return field[HALO + here + k + shift, :, lanes]

                middle = row(0)
                ring = jnp.concatenate([middle, sides[here + k, :, lanes]], axis=0)
                around = [pltpu.roll(ring, s, 0)[:rows] for s in (1, rows + 7, 2, rows + 6)]
                near = row(-1) + row(1) + (around[0] + around[1])
                far = row(-2) + row(2) + (around[2] + around[3])
                update = (
                    SIDE1 * near
                    + SIDE2 * far
                    + (0.25 * potential[here + k, :, lanes] + MIDDLE) * middle
                    + rotation * turned[k * rows : (k + 1) * rows, at - tile : at - tile + LANES]
                    - retained * previous[here + k, :, lanes]
                )
                value = retained * update
                if source is not None:
                    value += source[k * rows : (k + 1) * rows, at - tile : at - tile + LANES]
                put(here + k, lanes, value)


def first_kernel(
    packet, previous, potential, tables, upper, lower, left, right, high, low, after,
    done, top, bottom, first, last, field, prev, pot, sides, sems,
):
    count_r, rows, width = packet.shape
    steps = count_r // CHUNK

    def copies(n):
        part = pl.ds(n * CHUNK, CHUNK)
        return (
            pltpu.make_async_copy(packet.at[part], field.at[pl.ds(HALO + n * CHUNK, CHUNK)], sems.at[0, n]),
            pltpu.make_async_copy(previous.at[part], prev.at[part], sems.at[1, n]),
            pltpu.make_async_copy(potential.at[part], pot.at[part], sems.at[2, n]),
        )

    for n in range(steps):
        for copy in copies(n):
            copy.start()
    field[0:HALO] = jnp.zeros((HALO, rows, width), F32)
    field[HALO + count_r :] = jnp.zeros((HALO, rows, width), F32)
    put_sides(sides, left, right, count_r)
    copies(0)[0].wait()

    def put(k, lanes, value):
        done[k, :, lanes] = value

    def body(n, carry):
        @pl.when(n + 1 < steps)
        def _():
            copies(n + 1)[0].wait()

        copies(n)[1].wait()
        copies(n)[2].wait()
        advance(n, CHUNK, field, sides, prev, pot, tables, high, low, put)
        for k in range(CHUNK):
            for r in range(HALO):
                at = pl.ds(r * count_r + n * CHUNK + k, 1)
                first[at] = done[n * CHUNK + k, r : r + 1]
                last[at] = done[n * CHUNK + k, rows - HALO + r : rows - HALO + r + 1]
        return carry

    lax.fori_loop(0, steps, body, 0)
    edges = HALO * rows
    for k in range(HALO):
        here = slice(k * rows, (k + 1) * rows)
        beside = slice(edges + k * rows, edges + (k + 1) * rows)
        top[here] = done[k]
        bottom[here] = done[count_r - HALO + k]
        top[beside] = field[HALO + k]
        bottom[beside] = field[count_r + k]
    top[2 * edges : 2 * edges + rows, 0:LANES] = upper[...]
    bottom[2 * edges : 2 * edges + rows, 0:LANES] = lower[...]


def first_iteration(packet, previous, potential, tables, upper, lower, left, right, high, low, after):
    count_r, rows, width = packet.shape
    ends = jax.ShapeDtypeStruct((2 * HALO * rows + rows, width), F32)
    sides = jax.ShapeDtypeStruct((HALO * count_r, width), F32)
    return pl.pallas_call(
        first_kernel,
        in_specs=[HBM, HBM, HBM, *[VMEM] * 7, ANY],
        out_specs=[VMEM] * 5,
        out_shape=[jax.ShapeDtypeStruct(packet.shape, F32), ends, ends, sides, sides],
        scratch_shapes=[
            pltpu.VMEM((count_r + 2 * HALO, rows, width), F32),
            pltpu.VMEM(packet.shape, F32),
            pltpu.VMEM(packet.shape, F32),
            pltpu.VMEM((count_r, 8, width), F32),
            pltpu.SemaphoreType.DMA((3, count_r // CHUNK)),
        ],
        compiler_params=pltpu.CompilerParams(vmem_limit_bytes=28 * MIB),
        cost_estimate=pl.CostEstimate(flops=7_000_000_000, bytes_accessed=20 * MIB, transcendentals=0),
        name="first_iteration",
    )(packet, previous, potential, tables, upper, lower, left, right, high, low, after)


def slot_of(value, rows, width):
    per = rows * BAND
    shift_owner = per.bit_length() - 1
    chips = width // per // CORES
    row = lax.axis_index("row")
    index = value.astype(jnp.int32)
    owner = index >> shift_owner
    inside = index & (per - 1)
    core = (owner & 1) ^ (row & 1)
    chip = ((row >> 1) - (owner >> 1)) & (chips - 1)
    slot = ((core * chips + chip) << shift_owner) + (inside & 1) * rows + (inside >> 1)
    return slot.astype(F32)


def fill_rows(at, cut, rows, high, low, begin=0):
    column = lax.broadcasted_iota(jnp.int32, (rows, LANES), 1).astype(F32)
    cut = [jnp.broadcast_to(value, (rows, LANES)) for value in cut]
    for tile in range(0, high.shape[1], LANES):
        here = column + float(begin + tile)
        total = jnp.where(here == cut[0], cut[STENCILS], 0.0)
        for n in range(1, STENCILS):
            total += jnp.where(here == cut[n], cut[STENCILS + n], 0.0)
        upper, lower = halves(total)
        high[pl.ds(at, rows), tile : tile + LANES] = upper
        low[pl.ds(at, rows), tile : tile + LANES] = lower


def stencil_kernel(tables, after, high, low, other_high, other_low):
    _, rows, _ = tables.shape
    count_r = high.shape[0] // rows
    group = 8
    half = high.shape[1]

    @pl.when(in_product())
    def _():
        values = [slot_of(tables[INDEX + n], rows, CORES * half) for n in range(STENCILS)]
        values += [tables[WEIGHT + n] for n in range(STENCILS)]

        def body(step, carry):
            shift = lax.rem(LANES - step * group, LANES)
            moved = [pltpu.roll(value, shift, 1) for value in values]
            for k in range(group):
                at = pl.multiple_of((step * group + k) * rows, rows)
                cut = [jnp.broadcast_to(value[:, k : k + 1], (rows, LANES)) for value in moved]
                fill_rows(at, cut, rows, high, low)
                fill_rows(at, cut, rows, other_high, other_low, half)
            return carry

        lax.fori_loop(0, count_r // group, body, 0)


def stencil_matrix(tables, count_r, columns, after):
    rows = tables.shape[1]
    points = jax.ShapeDtypeStruct((count_r * rows, columns // CORES), BF16)
    return pl.pallas_call(
        stencil_kernel,
        in_specs=[VMEM, ANY],
        out_specs=[VMEM] * 4,
        out_shape=[points] * 4,
        compiler_params=pltpu.CompilerParams(vmem_limit_bytes=16 * MIB),
        cost_estimate=pl.CostEstimate(flops=15_000_000, bytes_accessed=6 * MIB, transcendentals=0),
        name="stencil_matrix",
    )(tables, after)


def edge_kernel(
    up, down, left, right, tables, top, bottom, first, last, after,
    high, low, whole_up, whole_down, new_first, new_last, added, square, *, rows, count_r,
):
    width = up.shape[1]
    edges = HALO * rows

    def retained(k):
        return jnp.broadcast_to(tables[RET, :, k : k + 1], (rows, width))

    def there(side, k):
        at = 2 * STENCILS * HALO + k
        return jnp.broadcast_to(side[2 * edges : 2 * edges + rows, at : at + 1], (rows, width))

    def packet_row(slab, k):
        return slab[edges + k * rows : edges + (k + 1) * rows]

    added[0] = retained(0) * (SIDE1 * packet_row(up, 1) + SIDE2 * packet_row(up, 0))
    added[1] = retained(1) * (SIDE2 * packet_row(up, 1))
    added[2] = retained(count_r - 2) * (SIDE2 * packet_row(down, 0))
    added[3] = retained(count_r - 1) * (SIDE1 * packet_row(down, 0) + SIDE2 * packet_row(down, 1))
    whole_up[0:rows] = up[0:rows] + there(up, 0) * (SIDE2 * packet_row(top, 0))
    whole_up[rows:edges] = up[rows:edges] + there(up, 1) * (SIDE1 * packet_row(top, 0) + SIDE2 * packet_row(top, 1))
    whole_down[0:rows] = down[0:rows] + there(down, 0) * (SIDE1 * packet_row(bottom, 1) + SIDE2 * packet_row(bottom, 0))
    whole_down[rows:edges] = down[rows:edges] + there(down, 1) * (SIDE2 * packet_row(bottom, 1))
    new_first[...] = first[...]
    new_last[...] = last[...]
    for k in range(HALO):
        for n, r_row in ((k, k), (HALO + k, count_r - HALO + k)):
            for r in range(HALO):
                at = r * count_r + r_row
                new_first[at : at + 1] = first[at : at + 1] + added[n, r : r + 1]
                new_last[at : at + 1] = last[at : at + 1] + added[n, rows - HALO + r : rows - HALO + r + 1]

    @pl.when(in_product())
    def _():
        at = 0
        for side in (up, down):
            value = side[2 * edges : 2 * edges + rows, 0:LANES]
            slots = slot_of(value, rows, high.shape[1])
            for e in range(HALO):
                cut = [
                    (slots if m < STENCILS else value)[:, HALO * m + e : HALO * m + e + 1]
                    for m in range(2 * STENCILS)
                ]
                fill_rows(at, cut, rows, high, low)
                at += rows
        square[...] = jnp.zeros_like(square)
        part = EXTRA // 2
        for n, side in enumerate((left, right)):
            begin = HALO * count_r
            square[n * EXTRA : n * EXTRA + part] = slot_of(side[begin : begin + part, 0:LANES], rows, high.shape[1])
            square[n * EXTRA + part : (n + 1) * EXTRA] = side[begin + part : begin + EXTRA, 0:LANES]
        turned = square[...].T
        for n in range(2):
            for e in range(HALO):
                for begin in range(0, count_r, rows):
                    cut = [
                        turned[begin : begin + rows, n * EXTRA + HALO * m + e : n * EXTRA + HALO * m + e + 1]
                        for m in range(2 * STENCILS)
                    ]
                    fill_rows(at, cut, rows, high, low)
                    at += rows


def finish_edges(halos, tables, edges, rows, count_r, columns, after):
    points = jax.ShapeDtypeStruct((2 * HALO * (rows + count_r), columns), BF16)
    width = edges[0].shape[1]
    return pl.pallas_call(
        functools.partial(edge_kernel, rows=rows, count_r=count_r),
        in_specs=[*[VMEM] * 9, ANY],
        out_specs=[VMEM] * 7,
        out_shape=[
            points, points,
            *[jax.ShapeDtypeStruct((HALO * length, width), F32) for length in (rows, rows, count_r, count_r)],
            jax.ShapeDtypeStruct((2 * HALO, rows, width), F32),
        ],
        scratch_shapes=[pltpu.VMEM((LANES, LANES), F32)],
        compiler_params=pltpu.CompilerParams(vmem_limit_bytes=16 * MIB),
        cost_estimate=pl.CostEstimate(flops=2_000_000, bytes_accessed=3 * MIB, transcendentals=0),
        name="finish_edges",
    )(*halos, tables, *edges, after)


def split_table(pieces, table):
    half = pieces.shape[1] // 2
    for k in range(pieces.shape[0]):
        for band in range(2):
            upper, lower = halves(pieces[k, band * half : (band + 1) * half])
            table[2 * band, k * half : (k + 1) * half] = upper
            table[2 * band + 1, k * half : (k + 1) * half] = lower


def own_source_kernel(
    one, added, stencil_high, stencil_low, edge_high, edge_low, own, sum_one, source, edge_source, table
):
    count_r, rows, width = one.shape
    columns = table.shape[1]
    size = LAST * rows

    @pl.when(in_product())
    def _():
        split_table(own, table)

        def body(n, carry):
            cut = pl.ds(pl.multiple_of(n * size, size), size)
            part = pl.ds(n * LAST, LAST)
            weights = (stencil_high[cut], stencil_low[cut])
            sum_one[part] = one[part] + product(weights, table[0], table[1]).reshape(LAST, rows, width)
            source[cut] = product(weights, table[2], table[3])
            return carry

        lax.fori_loop(0, count_r // LAST, body, 0)
        edge_source[...] = product((edge_high[:, 0:columns], edge_low[:, 0:columns]), table[0], table[1])

    @pl.when(jnp.logical_not(in_product()))
    def _():
        sum_one[...] = one[...]

    for k in range(HALO):
        sum_one[k] += added[k]
        sum_one[count_r - HALO + k] += added[HALO + k]


def own_source(one, added, matrices, own):
    count_r, rows, width = one.shape
    points = count_r * rows
    return pl.pallas_call(
        own_source_kernel,
        in_specs=[VMEM] * 7,
        out_specs=[VMEM] * 3,
        out_shape=[
            jax.ShapeDtypeStruct(one.shape, F32),
            jax.ShapeDtypeStruct((points, width), F32),
            jax.ShapeDtypeStruct((matrices[2].shape[0], width), F32),
        ],
        scratch_shapes=[pltpu.VMEM((4, own.shape[0] * own.shape[1] // 2, width), BF16)],
        compiler_params=pltpu.CompilerParams(vmem_limit_bytes=16 * MIB),
        cost_estimate=pl.CostEstimate(flops=7_000_000_000, bytes_accessed=20 * MIB, transcendentals=0),
        name="own_source",
    )(one, added, *matrices, own)


def last_kernel(
    one, source, edge_source, packet, potential, tables, up, down, left, right, high, low,
    stencil_high, stencil_low, edge_high, edge_low, other,
    earlier, latest, field, prev, pot, done, sides, table, ends, sems,
):
    count_r, rows, width = packet.shape
    steps = count_r // LAST
    size = LAST * rows
    columns = table.shape[1]
    is_product = in_product()

    def part(n):
        return pl.ds(n * LAST, LAST)

    def cut(n):
        return pl.ds(pl.multiple_of(n * size, size), size)

    def locals_of(n):
        return (
            pltpu.make_async_copy(packet.at[part(n)], prev.at[part(n)], sems.at[0, n]),
            pltpu.make_async_copy(potential.at[part(n)], pot.at[part(n)], sems.at[1, n]),
        )

    def earliers(n):
        return pltpu.make_async_copy(field.at[pl.ds(HALO + n * LAST, LAST)], earlier.at[part(n)], sems.at[2, n])

    def latests(n):
        return pltpu.make_async_copy(done.at[part(n)], latest.at[part(n)], sems.at[3, n])

    def put_ends(up_value, down_value):
        for k in range(HALO):
            field[k] = up_value[k * rows : (k + 1) * rows]
            field[HALO + count_r + k] = down_value[k * rows : (k + 1) * rows]

    def put(k, lanes, value):
        done[k, :, lanes] = value

    for n in range(steps):
        for copy in locals_of(n):
            copy.start()

    @pl.when(is_product)
    def _():
        split_table(other, table)
        ends[...] = edge_source[...] + product(
            (edge_high[:, columns : 2 * columns], edge_low[:, columns : 2 * columns]), table[0], table[1]
        )
        edges = HALO * rows
        long = HALO * count_r
        put_ends(up[...] + ends[:edges], down[...] + ends[edges : 2 * edges])
        put_sides(
            sides, left, right, count_r, ends.at[pl.ds(2 * edges, long)], ends.at[pl.ds(2 * edges + long, long)]
        )

        def weights(n):
            return stencil_high[cut(n)], stencil_low[cut(n)]

        def add(n, carry):
            more = product(weights(n), table[0], table[1]).reshape(LAST, rows, width)
            field[pl.ds(HALO + n * LAST, LAST)] = one[part(n)] + more
            earliers(n).start()
            return carry

        lax.fori_loop(0, steps, add, 0)

        def body(n, carry):
            for copy in locals_of(n):
                copy.wait()
            matrix = weights(n)

            def more(lanes):
                return source[cut(n), lanes] + product(matrix, table[2, :, lanes], table[3, :, lanes])

            advance(n, LAST, field, sides, prev, pot, tables, high, low, put, more)
            latests(n).start()
            return carry

        lax.fori_loop(0, steps, body, 0)

    @pl.when(jnp.logical_not(is_product))
    def _():
        put_ends(up, down)
        put_sides(sides, left, right, count_r)
        for n in range(steps):
            field[pl.ds(HALO + n * LAST, LAST)] = one[part(n)]
            earliers(n).start()

        def body(n, carry):
            for copy in locals_of(n):
                copy.wait()
            advance(n, LAST, field, sides, prev, pot, tables, high, low, put)
            latests(n).start()
            return carry

        lax.fori_loop(0, steps, body, 0)

    for n in range(steps):
        earliers(n).wait()
        latests(n).wait()


def last_iteration(own_sums, packet, potential, tables, halos, high, low, matrices, other):
    count_r, rows, width = packet.shape
    steps = count_r // LAST
    return pl.pallas_call(
        last_kernel,
        in_specs=[VMEM, VMEM, VMEM, HBM, HBM, *[VMEM] * 12],
        out_specs=[HBM, HBM],
        out_shape=[jax.ShapeDtypeStruct(packet.shape, F32)] * 2,
        scratch_shapes=[
            pltpu.VMEM((count_r + 2 * HALO, rows, width), F32),
            pltpu.VMEM(packet.shape, F32),
            pltpu.VMEM(packet.shape, F32),
            pltpu.VMEM(packet.shape, F32),
            pltpu.VMEM((count_r, 8, width), F32),
            pltpu.VMEM((4, other.shape[0] * other.shape[1] // 2, width), BF16),
            pltpu.VMEM((2 * HALO * (rows + count_r), width), F32),
            pltpu.SemaphoreType.DMA((4, steps)),
        ],
        compiler_params=pltpu.CompilerParams(vmem_limit_bytes=32 * MIB),
        cost_estimate=pl.CostEstimate(flops=14_000_000_000, bytes_accessed=36 * MIB, transcendentals=0),
        name="last_iteration",
    )(*own_sums, packet, potential, tables, *halos, high, low, *matrices, other)


def neighbours(axis, upward, downward):
    count = lax.axis_size(axis)
    return (
        lax.ppermute(upward, axis, [(i, i + 1) for i in range(count - 1)]),
        lax.ppermute(downward, axis, [(i + 1, i) for i in range(count - 1)]),
    )


def local(packet, previous, potential, rotation, angular, damping, absorber, stencil_index, stencil_weight):
    packet, previous, potential = packet[0], previous[0], potential[0]
    rotation, angular, damping, absorber = rotation[0], angular[0], damping[0], absorber[0]
    count_r, rows, width = packet.shape
    count_rr, count_row = (lax.axis_size(name) for name in ("rr", "row"))
    chips = count_row // CORES
    rotation, damping, absorber = (jnp.swapaxes(value, 0, 1) for value in (rotation, damping, absorber))
    stencil_index, stencil_weight = (jnp.swapaxes(value, 1, 2) for value in (stencil_index, stencil_weight))
    packet, previous, potential, rotation, damping, absorber, stencil_index, stencil_weight, angular = (
        in_hbm(value)
        for value in (
            packet, previous, potential, rotation, damping, absorber, stencil_index, stencil_weight, angular
        )
    )

    upper, lower, first, last, tables, high, low = prepare(
        packet, previous, potential, rotation, damping, absorber, stencil_index, stencil_weight, angular
    )
    columns = count_row * rows * BAND
    left, right = neighbours("row", last, first)
    matrix = stencil_matrix(tables, count_r, columns, first)
    left, right, matrix = lax.optimization_barrier((left, right, matrix))
    table = bands(packet, previous, potential, tables, left, right, high, low)

    half = count_rr // PLANES
    start = count_rr - 1
    plane = ("sect", "rr")
    low_side, high_side = start - half + 1, start - 1
    relays = [low_side, high_side, count_rr + half - 1, count_rr + start]
    crossed = [lax.ppermute(table, plane, [(start, relay)]) for relay in relays]
    one, *edges = first_iteration(
        packet, previous, potential, tables, upper, lower, left, right, high, low, table
    )
    *crossed, one, edges = lax.optimization_barrier((*crossed, one, edges))
    piece = sum(crossed)
    near = [(low_side, count_rr), (high_side, count_rr + half - 2)]
    near += [(count_rr + half - 1, count_rr + half - 3), (count_rr + start, count_rr + start - 2)]
    opposite = [(low_side, count_rr + low_side), (high_side, count_rr + high_side)]
    arrived = [lax.ppermute(piece, plane, near), lax.ppermute(piece, plane, opposite)]
    top, bottom, first, last = edges
    top, bottom, piece = lax.optimization_barrier((top, bottom, piece))
    up, down = neighbours("rr", bottom, top)
    spread = piece + sum(arrived)
    line = ("sect", "row")

    def around(shift):
        pairs = []
        for chip in range(chips):
            for core in range(CORES):
                pairs.append(
                    (count_row + chip * CORES + core, count_row + ((chip + shift) % chips) * CORES + core)
                )
        return lax.ppermute(spread, line, pairs)

    rest = [around(1), around(3), around(2)]
    edge_matrix_and_ends = finish_edges(
        (up, down, left, right), tables, (top, bottom, first, last), rows, count_r, columns, spread
    )
    *edge_matrix, up, down, first, last, added = edge_matrix_and_ends
    rest[1], edge_matrix, first, last = lax.optimization_barrier((rest[1], edge_matrix, first, last))
    left, right = neighbours("row", last, first)
    *rest, left, right = lax.optimization_barrier((*rest, left, right))
    own = jnp.stack([spread, rest[0], rest[2], rest[1]], axis=0)
    other = lax.ppermute(
        own, line, [(count_row + i, count_row + i + 1 - 2 * (i % CORES)) for i in range(count_row)]
    )
    own_sums = own_source(one, added, (*matrix[:2], *edge_matrix), own)
    other, own_sums = lax.optimization_barrier((other, own_sums))
    earlier, latest = last_iteration(
        own_sums, packet, potential, tables, (up, down, left, right), high, low, (*matrix[2:], *edge_matrix), other
    )
    return latest[None], earlier[None]


def solution(mesh):
    in_specs = (
        P("sect", "rr", "row", None),
        P("sect", "rr", "row", None),
        P("sect", "rr", "row", None),
        P("sect", "rr", "row"),
        P("sect", None, None),
        P("sect", "rr", "row"),
        P("sect", "rr", "row"),
        P(None, "rr", "row"),
        P(None, "rr", "row"),
    )
    out_specs = (P("sect", "rr", "row", None), P("sect", "rr", "row", None))
    return jax.shard_map(local, mesh=mesh, in_specs=in_specs, out_specs=out_specs, check_vma=False)
```

```python
import functools

import jax
import jax.numpy as jnp
from jax import lax
from jax.experimental import pallas as pl
from jax.experimental.pallas import tpu as pltpu
from jax.sharding import PartitionSpec as P

BAND = 2
STENCILS = 4
HALO = 2
LANES = 128
CHUNK = 16
LAST = 16
CORES = 2
PLANES = 2
ROT, RET, INDEX, WEIGHT, TABLES = 0, 1, 2, 6, 10
EXTRA = 2 * STENCILS * HALO
OFBAND = 32
MIB = 1 << 20
F32 = jnp.float32
BF16 = jnp.bfloat16
ANY = pl.BlockSpec(memory_space=pl.ANY)
HBM = pl.BlockSpec(memory_space=pltpu.HBM)
VMEM = pl.BlockSpec(memory_space=pltpu.VMEM)

SIDE1 = -16.0 / 96.0
SIDE2 = 1.0 / 96.0
MIDDLE = 2.0 * 30.0 / 96.0 - 7.5 / 4.0


def halves(value):
    high = value.astype(BF16)
    low = (value - high.astype(F32)).astype(BF16)
    return high, low


def product(left, right_high, right_low):
    high, low = left
    total = jnp.dot(high, right_high, preferred_element_type=F32)
    total += jnp.dot(low, right_high, preferred_element_type=F32)
    return total + jnp.dot(high, right_low, preferred_element_type=F32)


def doubled_hamilton(field, index, start, count, lanes, turned, potential, rotation):
    def at(shift_r, shift_v):
        return field[index + shift_r, pl.ds(start + shift_v, count), lanes]

    middle = at(0, 0)
    near = at(-1, 0) + at(1, 0) + (at(0, -1) + at(0, 1))
    far = at(-2, 0) + at(2, 0) + (at(0, -2) + at(0, 2))
    return (
        SIDE1 * near
        + SIDE2 * far
        + (0.25 * potential + MIDDLE) * middle
        + (0.25 * rotation) * turned
    )


def in_hbm(value):
    return pltpu.with_memory_space_constraint(value, pltpu.HBM)


def holds_bands():
    return (lax.axis_index("sect") == 0) & (lax.axis_index("rr") == lax.axis_size("rr") - 1)


def in_product():
    return lax.axis_index("sect") == 1


def retained_of(damping, absorber):
    return 1.0 - absorber.astype(F32) * (1.0 - damping)


def band_kernel(
    packet, previous, potential, tables, left, right, high, low, out, field, later, turned, held, sems
):
    count_r, rows, width = packet.shape
    base = 16
    wide = rows + 16
    begin = left.shape[0] - OFBAND

    @pl.when(holds_bands())
    def _():
        copies = [
            pltpu.make_async_copy(packet.at[pl.ds(count_r - 6, 6)], field.at[pl.ds(2, 6), pl.ds(base, rows)], sems.at[0]),
            pltpu.make_async_copy(previous.at[pl.ds(count_r - 4, 4)], held.at[0], sems.at[1]),
            pltpu.make_async_copy(potential.at[pl.ds(count_r - 4, 4)], held.at[1], sems.at[2]),
        ]
        later[...] = jnp.zeros_like(later)
        field[0:2] = jnp.zeros_like(field[0:2])
        field[8:10] = jnp.zeros_like(field[8:10])
        for k in range(2, 8):
            field[k, 0:base] = jnp.zeros((base, width), F32)
            field[k, base + rows :] = jnp.zeros((base, width), F32)
        for copy in copies:
            copy.start()
        for k in range(4):
            at = begin + 4 * k
            field[4 + k, base - 4 : base] = left[at : at + 4]
            field[4 + k, base + rows : base + rows + 4] = right[at : at + 4]
        columns = [
            (tables[ROT, :, count_r - 4 + k : count_r - 3 + k], tables[RET, :, count_r - 4 + k : count_r - 3 + k])
            for k in range(4)
        ]
        columns = [tuple(jnp.broadcast_to(c, (rows, LANES)) for c in pair) for pair in columns]
        for copy in copies:
            copy.wait()
        window = field[4:8, base - 8 : base + rows + 8].reshape(4 * wide, width)
        turned[...] = product(halves(window), high[...], low[...])
        for k in range(4):
            rotation, retained = columns[k]
            for at in range(0, width, LANES):
                lanes = slice(at, at + LANES)
                update = doubled_hamilton(
                    field, 4 + k, base, rows, lanes,
                    turned[k * wide + 8 : k * wide + 8 + rows, lanes], held[1, k, :, lanes], rotation,
                ) - retained * held[0, k, :, lanes]
                later[k, base : base + rows, lanes] = retained * update
                if k >= 2:
                    out[(k - 2) * rows : (k - 1) * rows, lanes] = (1.0 - retained) * update
        for k in range(2, 4):
            for slab, place, inside in ((left, base - 8, 6), (right, base + rows, 0)):
                at = begin + 16 + 2 * (k - 2)
                prev, pot, rot, ret = (slab[at + 4 * n : at + 4 * n + 2] for n in range(4))
                update = doubled_hamilton(
                    field, 4 + k, place + inside, 2, slice(None),
                    turned[k * wide + place - base + 8 + inside : k * wide + place - base + 10 + inside], pot, rot,
                ) - ret * prev
                later[k, place + inside : place + inside + 2] = ret * update
        window = later[2:4, base : base + rows].reshape(2 * rows, width)
        turned[0 : 2 * rows] = product(halves(window), high[...], low[...])
        for k in range(2, 4):
            rotation, retained = columns[k]
            for at in range(0, width, LANES):
                lanes = slice(at, at + LANES)
                update = doubled_hamilton(
                    later, k, base, rows, lanes,
                    turned[(k - 2) * rows : (k - 1) * rows, lanes], held[1, k, :, lanes], rotation,
                ) - retained * field[4 + k, base : base + rows, lanes]
                out[k * rows : (k + 1) * rows, lanes] = (1.0 - retained) * update


def bands(packet, previous, potential, tables, left, right, high, low):
    _, rows, width = packet.shape
    return pl.pallas_call(
        band_kernel,
        in_specs=[HBM, HBM, HBM, VMEM, VMEM, VMEM, VMEM, VMEM],
        out_specs=VMEM,
        out_shape=jax.ShapeDtypeStruct((2 * BAND * rows, width), F32),
        scratch_shapes=[
            pltpu.VMEM((10, rows + 32, width), F32),
            pltpu.VMEM((6, rows + 32, width), F32),
            pltpu.VMEM((4 * (rows + 16), width), F32),
            pltpu.VMEM((2, 4, rows, width), F32),
            pltpu.SemaphoreType.DMA((3,)),
        ],
        compiler_params=pltpu.CompilerParams(vmem_limit_bytes=16 * MIB),
        cost_estimate=pl.CostEstimate(flops=400_000_000, bytes_accessed=4 * MIB, transcendentals=0),
        name="both_bands",
    )(packet, previous, potential, tables, left, right, high, low)


def prepare_kernel(
    packet, previous, potential, rotation, damping, absorber, index, weight, angular,
    upper, lower, first, last, tables, high, low,
    sides, others, factors, masks, indices, weights, matrix, sems,
):
    count_r, rows, width = packet.shape
    small = [
        pltpu.make_async_copy(rotation, factors.at[0], sems.at[0]),
        pltpu.make_async_copy(damping, factors.at[1], sems.at[1]),
        pltpu.make_async_copy(absorber, masks, sems.at[2]),
        pltpu.make_async_copy(index, indices, sems.at[3]),
        pltpu.make_async_copy(weight, weights, sems.at[4]),
    ]
    copies = [
        pltpu.make_async_copy(packet.at[:, pl.ds(0, 8)], sides.at[0], sems.at[5]),
        pltpu.make_async_copy(packet.at[:, pl.ds(rows - 8, 8)], sides.at[1], sems.at[6]),
        pltpu.make_async_copy(previous.at[pl.ds(count_r - BAND, BAND)], others.at[0], sems.at[7]),
        pltpu.make_async_copy(potential.at[pl.ds(count_r - BAND, BAND)], others.at[1], sems.at[8]),
        pltpu.make_async_copy(angular, matrix, sems.at[9]),
    ]
    for copy in small + copies:
        copy.start()
    for copy in small:
        copy.wait()
    values = [factors[0], retained_of(factors[1], masks[...])]
    values += [indices[n].astype(F32) for n in range(STENCILS)]
    values += [weights[n] for n in range(STENCILS)]
    for n, value in enumerate(values):
        tables[n] = jnp.concatenate([value, jnp.zeros((rows, LANES - count_r), F32)], axis=1)
    columns = HALO * count_r
    lane = lax.broadcasted_iota(jnp.int32, (rows, LANES), 1)
    at_top = jnp.zeros((rows, LANES), F32)
    at_bottom = jnp.zeros((rows, LANES), F32)
    for n, table in enumerate([*range(INDEX, TABLES), RET]):
        value = tables[table]
        at = n * HALO
        here = (lane >= at) & (lane < at + HALO)
        at_top = jnp.where(here, pltpu.roll(value, at, 1), at_top)
        at_bottom = jnp.where(here, pltpu.roll(value, (at + LANES - (count_r - HALO)) % LANES, 1), at_bottom)
        if table != RET:
            first[columns + at : columns + at + HALO, 0:LANES] = value[0:HALO]
            last[columns + at : columns + at + HALO, 0:LANES] = value[rows - HALO : rows]
    upper[...] = at_top
    lower[...] = at_bottom
    begin = columns + EXTRA
    for copy in copies:
        copy.wait()
    for out, n, far, near in ((first, 0, 0, 0), (last, 1, 4, rows - 2)):
        for k in range(4):
            out[begin + 4 * k : begin + 4 * k + 4] = sides[n, count_r - 4 + k, far : far + 4]
        for k in range(BAND):
            at = begin + 16 + 2 * k
            column = count_r - BAND + k
            out[at : at + 2] = others[0, k, near : near + 2]
            out[at + 4 : at + 6] = others[1, k, near : near + 2]
            for m in (ROT, RET):
                value = tables[m, near : near + 2, column : column + 1]
                out[at + 8 + 4 * m : at + 10 + 4 * m] = jnp.broadcast_to(value, (2, width))
    for out, n, near in ((first, 0, 0), (last, 1, 8 - HALO)):
        for k in range(count_r):
            for r in range(HALO):
                out[r * count_r + k : r * count_r + k + 1] = sides[n, k, near + r : near + r + 1]
    high[...], low[...] = halves(matrix[...])


def prepare(packet, previous, potential, rotation, damping, absorber, index, weight, angular):
    count_r, rows, width = packet.shape
    ends = jax.ShapeDtypeStruct((rows, LANES), F32)
    sides = jax.ShapeDtypeStruct((HALO * count_r + EXTRA + OFBAND, width), F32)
    part = jax.ShapeDtypeStruct(angular.shape, BF16)
    return pl.pallas_call(
        prepare_kernel,
        in_specs=[HBM] * 9,
        out_specs=[VMEM] * 7,
        out_shape=[ends, ends, sides, sides, jax.ShapeDtypeStruct((TABLES, rows, LANES), F32), part, part],
        scratch_shapes=[
            pltpu.VMEM((2, count_r, 8, width), F32),
            pltpu.VMEM((2, BAND, rows, width), F32),
            pltpu.VMEM((2, rows, count_r), F32),
            pltpu.VMEM((rows, count_r), jnp.int32),
            pltpu.VMEM((STENCILS, rows, count_r), jnp.int32),
            pltpu.VMEM((STENCILS, rows, count_r), F32),
            pltpu.VMEM(angular.shape, F32),
            pltpu.SemaphoreType.DMA((10,)),
        ],
        compiler_params=pltpu.CompilerParams(vmem_limit_bytes=16 * MIB),
        cost_estimate=pl.CostEstimate(flops=1_000_000, bytes_accessed=6 * MIB, transcendentals=0),
        name="prepare",
    )(packet, previous, potential, rotation, damping, absorber, index, weight, angular)


def put_sides(sides, left, right, count_r, left_more=None, right_more=None):
    def body(k, carry):
        for r in range(HALO):
            at = pl.ds(r * count_r + k, 1)
            before, behind = left[at], right[at]
            if left_more is not None:
                before, behind = before + left_more[at], behind + right_more[at]
            sides[k, r : r + 1] = behind
            sides[k, 8 - HALO + r : 8 - HALO + r + 1] = before
        return carry

    lax.fori_loop(0, count_r, body, 0, unroll=8)


def advance(step, chunk, field, sides, previous, potential, tables, high, low, put, more=None):
    rows = previous.shape[1]
    width = previous.shape[2]
    here = step * chunk
    shift = lax.rem(LANES - here, LANES)
    columns = [pltpu.roll(tables[n], shift, 1) for n in (ROT, RET)]
    window = field[pl.ds(HALO + here, chunk)].reshape(chunk * rows, width)
    split = halves(window)
    wide = 2 * LANES
    for tile in range(0, width, wide):
        turned = product(split, high[:, tile : tile + wide], low[:, tile : tile + wide])
        source = None if more is None else more(slice(tile, tile + wide))
        for k in range(chunk):
            rotation = jnp.broadcast_to(0.25 * columns[0][:, k : k + 1], (rows, LANES))
            retained = jnp.broadcast_to(columns[1][:, k : k + 1], (rows, LANES))
            for at in range(tile, tile + wide, LANES):
                lanes = slice(at, at + LANES)

                def row(shift):
                    return field[HALO + here + k + shift, :, lanes]

                middle = row(0)
                ring = jnp.concatenate([middle, sides[here + k, :, lanes]], axis=0)
                around = [pltpu.roll(ring, s, 0)[:rows] for s in (1, rows + 7, 2, rows + 6)]
                near = row(-1) + row(1) + (around[0] + around[1])
                far = row(-2) + row(2) + (around[2] + around[3])
                update = (
                    SIDE1 * near
                    + SIDE2 * far
                    + (0.25 * potential[here + k, :, lanes] + MIDDLE) * middle
                    + rotation * turned[k * rows : (k + 1) * rows, at - tile : at - tile + LANES]
                    - retained * previous[here + k, :, lanes]
                )
                value = retained * update
                if source is not None:
                    value += source[k * rows : (k + 1) * rows, at - tile : at - tile + LANES]
                put(here + k, lanes, value)


def first_kernel(
    packet, previous, potential, tables, upper, lower, left, right, high, low, after,
    done, top, bottom, first, last, field, sides, sems,
):
    count_r, rows, width = packet.shape
    steps = count_r // CHUNK

    def copies(n):
        part = pl.ds(n * CHUNK, CHUNK)
        return pltpu.make_async_copy(packet.at[part], field.at[pl.ds(HALO + n * CHUNK, CHUNK)], sems.at[n])

    for n in range(steps):
        copies(n).start()
    field[0:HALO] = jnp.zeros((HALO, rows, width), F32)
    field[HALO + count_r :] = jnp.zeros((HALO, rows, width), F32)
    put_sides(sides, left, right, count_r)
    copies(0).wait()

    def put(k, lanes, value):
        done[k, :, lanes] = value

    def body(n, carry):
        @pl.when(n + 1 < steps)
        def _():
            copies(n + 1).wait()

        advance(n, CHUNK, field, sides, previous, potential, tables, high, low, put)
        for k in range(CHUNK):
            for r in range(HALO):
                at = pl.ds(r * count_r + n * CHUNK + k, 1)
                first[at] = done[n * CHUNK + k, r : r + 1]
                last[at] = done[n * CHUNK + k, rows - HALO + r : rows - HALO + r + 1]
        return carry

    lax.fori_loop(0, steps, body, 0)
    edges = HALO * rows
    for k in range(HALO):
        here = slice(k * rows, (k + 1) * rows)
        beside = slice(edges + k * rows, edges + (k + 1) * rows)
        top[here] = done[k]
        bottom[here] = done[count_r - HALO + k]
        top[beside] = field[HALO + k]
        bottom[beside] = field[count_r + k]
    top[2 * edges : 2 * edges + rows, 0:LANES] = upper[...]
    bottom[2 * edges : 2 * edges + rows, 0:LANES] = lower[...]


def first_iteration(packet, previous, potential, tables, upper, lower, left, right, high, low, after):
    count_r, rows, width = packet.shape
    ends = jax.ShapeDtypeStruct((2 * HALO * rows + rows, width), F32)
    sides = jax.ShapeDtypeStruct((HALO * count_r, width), F32)
    return pl.pallas_call(
        first_kernel,
        in_specs=[HBM, *[VMEM] * 9, ANY],
        out_specs=[VMEM] * 5,
        out_shape=[jax.ShapeDtypeStruct(packet.shape, F32), ends, ends, sides, sides],
        scratch_shapes=[
            pltpu.VMEM((count_r + 2 * HALO, rows, width), F32),
            pltpu.VMEM((count_r, 8, width), F32),
            pltpu.SemaphoreType.DMA((count_r // CHUNK,)),
        ],
        compiler_params=pltpu.CompilerParams(vmem_limit_bytes=14 * MIB),
        cost_estimate=pl.CostEstimate(flops=7_000_000_000, bytes_accessed=20 * MIB, transcendentals=0),
        name="first_iteration",
    )(packet, previous, potential, tables, upper, lower, left, right, high, low, after)


def slot_of(value, rows, width):
    per = rows * BAND
    shift_owner = per.bit_length() - 1
    chips = width // per // CORES
    row = lax.axis_index("row")
    index = value.astype(jnp.int32)
    owner = index >> shift_owner
    inside = index & (per - 1)
    core = (owner & 1) ^ (row & 1)
    chip = ((row >> 1) - (owner >> 1)) & (chips - 1)
    slot = ((core * chips + chip) << shift_owner) + (inside & 1) * rows + (inside >> 1)
    return slot.astype(F32)


def fill_rows(at, cut, rows, high, low, begin=0):
    column = lax.broadcasted_iota(jnp.int32, (rows, LANES), 1).astype(F32)
    cut = [jnp.broadcast_to(value, (rows, LANES)) for value in cut]
    for tile in range(0, high.shape[1], LANES):
        here = column + float(begin + tile)
        total = jnp.where(here == cut[0], cut[STENCILS], 0.0)
        for n in range(1, STENCILS):
            total += jnp.where(here == cut[n], cut[STENCILS + n], 0.0)
        upper, lower = halves(total)
        high[pl.ds(at, rows), tile : tile + LANES] = upper
        low[pl.ds(at, rows), tile : tile + LANES] = lower


def stencil_kernel(tables, after, high, low, other_high, other_low):
    _, rows, _ = tables.shape
    count_r = high.shape[0] // rows
    group = 8
    half = high.shape[1]

    @pl.when(in_product())
    def _():
        values = [slot_of(tables[INDEX + n], rows, CORES * half) for n in range(STENCILS)]
        values += [tables[WEIGHT + n] for n in range(STENCILS)]

        def body(step, carry):
            shift = lax.rem(LANES - step * group, LANES)
            moved = [pltpu.roll(value, shift, 1) for value in values]
            for k in range(group):
                at = pl.multiple_of((step * group + k) * rows, rows)
                cut = [jnp.broadcast_to(value[:, k : k + 1], (rows, LANES)) for value in moved]
                fill_rows(at, cut, rows, high, low)
                fill_rows(at, cut, rows, other_high, other_low, half)
            return carry

        lax.fori_loop(0, count_r // group, body, 0)


def stencil_matrix(tables, count_r, columns, after):
    rows = tables.shape[1]
    points = jax.ShapeDtypeStruct((count_r * rows, columns // CORES), BF16)
    return pl.pallas_call(
        stencil_kernel,
        in_specs=[VMEM, ANY],
        out_specs=[VMEM] * 4,
        out_shape=[points] * 4,
        compiler_params=pltpu.CompilerParams(vmem_limit_bytes=16 * MIB),
        cost_estimate=pl.CostEstimate(flops=15_000_000, bytes_accessed=6 * MIB, transcendentals=0),
        name="stencil_matrix",
    )(tables, after)


def edge_kernel(
    up, down, left, right, tables, top, bottom, first, last, after,
    high, low, whole_up, whole_down, new_first, new_last, added, square, *, rows, count_r,
):
    width = up.shape[1]
    edges = HALO * rows

    def retained(k):
        return jnp.broadcast_to(tables[RET, :, k : k + 1], (rows, width))

    def there(side, k):
        at = 2 * STENCILS * HALO + k
        return jnp.broadcast_to(side[2 * edges : 2 * edges + rows, at : at + 1], (rows, width))

    def packet_row(slab, k):
        return slab[edges + k * rows : edges + (k + 1) * rows]

    added[0] = retained(0) * (SIDE1 * packet_row(up, 1) + SIDE2 * packet_row(up, 0))
    added[1] = retained(1) * (SIDE2 * packet_row(up, 1))
    added[2] = retained(count_r - 2) * (SIDE2 * packet_row(down, 0))
    added[3] = retained(count_r - 1) * (SIDE1 * packet_row(down, 0) + SIDE2 * packet_row(down, 1))
    whole_up[0:rows] = up[0:rows] + there(up, 0) * (SIDE2 * packet_row(top, 0))
    whole_up[rows:edges] = up[rows:edges] + there(up, 1) * (SIDE1 * packet_row(top, 0) + SIDE2 * packet_row(top, 1))
    whole_down[0:rows] = down[0:rows] + there(down, 0) * (SIDE1 * packet_row(bottom, 1) + SIDE2 * packet_row(bottom, 0))
    whole_down[rows:edges] = down[rows:edges] + there(down, 1) * (SIDE2 * packet_row(bottom, 1))
    new_first[...] = first[...]
    new_last[...] = last[...]
    for k in range(HALO):
        for n, r_row in ((k, k), (HALO + k, count_r - HALO + k)):
            for r in range(HALO):
                at = r * count_r + r_row
                new_first[at : at + 1] = first[at : at + 1] + added[n, r : r + 1]
                new_last[at : at + 1] = last[at : at + 1] + added[n, rows - HALO + r : rows - HALO + r + 1]

    @pl.when(in_product())
    def _():
        at = 0
        for side in (up, down):
            value = side[2 * edges : 2 * edges + rows, 0:LANES]
            slots = slot_of(value, rows, high.shape[1])
            for e in range(HALO):
                cut = [
                    (slots if m < STENCILS else value)[:, HALO * m + e : HALO * m + e + 1]
                    for m in range(2 * STENCILS)
                ]
                fill_rows(at, cut, rows, high, low)
                at += rows
        square[...] = jnp.zeros_like(square)
        part = EXTRA // 2
        for n, side in enumerate((left, right)):
            begin = HALO * count_r
            square[n * EXTRA : n * EXTRA + part] = slot_of(side[begin : begin + part, 0:LANES], rows, high.shape[1])
            square[n * EXTRA + part : (n + 1) * EXTRA] = side[begin + part : begin + EXTRA, 0:LANES]
        turned = square[...].T
        for n in range(2):
            for e in range(HALO):
                for begin in range(0, count_r, rows):
                    cut = [
                        turned[begin : begin + rows, n * EXTRA + HALO * m + e : n * EXTRA + HALO * m + e + 1]
                        for m in range(2 * STENCILS)
                    ]
                    fill_rows(at, cut, rows, high, low)
                    at += rows


def finish_edges(halos, tables, edges, rows, count_r, columns, after):
    points = jax.ShapeDtypeStruct((2 * HALO * (rows + count_r), columns), BF16)
    width = edges[0].shape[1]
    return pl.pallas_call(
        functools.partial(edge_kernel, rows=rows, count_r=count_r),
        in_specs=[*[VMEM] * 9, ANY],
        out_specs=[VMEM] * 7,
        out_shape=[
            points, points,
            *[jax.ShapeDtypeStruct((HALO * length, width), F32) for length in (rows, rows, count_r, count_r)],
            jax.ShapeDtypeStruct((2 * HALO, rows, width), F32),
        ],
        scratch_shapes=[pltpu.VMEM((LANES, LANES), F32)],
        compiler_params=pltpu.CompilerParams(vmem_limit_bytes=16 * MIB),
        cost_estimate=pl.CostEstimate(flops=2_000_000, bytes_accessed=3 * MIB, transcendentals=0),
        name="finish_edges",
    )(*halos, tables, *edges, after)


def split_table(pieces, table):
    half = pieces.shape[1] // 2
    for k in range(pieces.shape[0]):
        for band in range(2):
            upper, lower = halves(pieces[k, band * half : (band + 1) * half])
            table[2 * band, k * half : (k + 1) * half] = upper
            table[2 * band + 1, k * half : (k + 1) * half] = lower


def own_source_kernel(
    one, added, stencil_high, stencil_low, edge_high, edge_low, own, sum_one, source, edge_source, table
):
    count_r, rows, width = one.shape
    columns = table.shape[1]
    size = LAST * rows

    @pl.when(in_product())
    def _():
        split_table(own, table)

        def body(n, carry):
            cut = pl.ds(pl.multiple_of(n * size, size), size)
            part = pl.ds(n * LAST, LAST)
            weights = (stencil_high[cut], stencil_low[cut])
            sum_one[part] = one[part] + product(weights, table[0], table[1]).reshape(LAST, rows, width)
            source[cut] = product(weights, table[2], table[3])
            return carry

        lax.fori_loop(0, count_r // LAST, body, 0)
        edge_source[...] = product((edge_high[:, 0:columns], edge_low[:, 0:columns]), table[0], table[1])

    @pl.when(jnp.logical_not(in_product()))
    def _():
        sum_one[...] = one[...]

    for k in range(HALO):
        sum_one[k] += added[k]
        sum_one[count_r - HALO + k] += added[HALO + k]


def own_source(one, added, matrices, own):
    count_r, rows, width = one.shape
    points = count_r * rows
    return pl.pallas_call(
        own_source_kernel,
        in_specs=[VMEM] * 7,
        out_specs=[VMEM] * 3,
        out_shape=[
            jax.ShapeDtypeStruct(one.shape, F32),
            jax.ShapeDtypeStruct((points, width), F32),
            jax.ShapeDtypeStruct((matrices[2].shape[0], width), F32),
        ],
        scratch_shapes=[pltpu.VMEM((4, own.shape[0] * own.shape[1] // 2, width), BF16)],
        compiler_params=pltpu.CompilerParams(vmem_limit_bytes=16 * MIB),
        cost_estimate=pl.CostEstimate(flops=7_000_000_000, bytes_accessed=20 * MIB, transcendentals=0),
        name="own_source",
    )(one, added, *matrices, own)


def last_kernel(
    one, source, edge_source, packet, potential, tables, up, down, left, right, high, low,
    stencil_high, stencil_low, edge_high, edge_low, other,
    earlier, latest, field, done, sides, table, ends, sems,
):
    count_r, rows, width = packet.shape
    steps = count_r // LAST
    size = LAST * rows
    columns = table.shape[1]
    is_product = in_product()

    def part(n):
        return pl.ds(n * LAST, LAST)

    def cut(n):
        return pl.ds(pl.multiple_of(n * size, size), size)

    def earliers(n):
        return pltpu.make_async_copy(field.at[pl.ds(HALO + n * LAST, LAST)], earlier.at[part(n)], sems.at[0, n])

    def latests(n):
        return pltpu.make_async_copy(done.at[part(n)], latest.at[part(n)], sems.at[1, n])

    def put_ends(up_value, down_value):
        for k in range(HALO):
            field[k] = up_value[k * rows : (k + 1) * rows]
            field[HALO + count_r + k] = down_value[k * rows : (k + 1) * rows]

    def put(k, lanes, value):
        done[k, :, lanes] = value

    @pl.when(is_product)
    def _():
        split_table(other, table)
        ends[...] = edge_source[...] + product(
            (edge_high[:, columns : 2 * columns], edge_low[:, columns : 2 * columns]), table[0], table[1]
        )
        edges = HALO * rows
        long = HALO * count_r
        put_ends(up[...] + ends[:edges], down[...] + ends[edges : 2 * edges])
        put_sides(
            sides, left, right, count_r, ends.at[pl.ds(2 * edges, long)], ends.at[pl.ds(2 * edges + long, long)]
        )

        def weights(n):
            return stencil_high[cut(n)], stencil_low[cut(n)]

        def add(n, carry):
            more = product(weights(n), table[0], table[1]).reshape(LAST, rows, width)
            field[pl.ds(HALO + n * LAST, LAST)] = one[part(n)] + more
            earliers(n).start()
            return carry

        lax.fori_loop(0, steps, add, 0)

        def body(n, carry):
            matrix = weights(n)

            def more(lanes):
                return source[cut(n), lanes] + product(matrix, table[2, :, lanes], table[3, :, lanes])

            advance(n, LAST, field, sides, packet, potential, tables, high, low, put, more)
            latests(n).start()
            return carry

        lax.fori_loop(0, steps, body, 0)

    @pl.when(jnp.logical_not(is_product))
    def _():
        put_ends(up, down)
        put_sides(sides, left, right, count_r)
        for n in range(steps):
            field[pl.ds(HALO + n * LAST, LAST)] = one[part(n)]
            earliers(n).start()

        def body(n, carry):
            advance(n, LAST, field, sides, packet, potential, tables, high, low, put)
            latests(n).start()
            return carry

        lax.fori_loop(0, steps, body, 0)

    for n in range(steps):
        earliers(n).wait()
        latests(n).wait()


def last_iteration(own_sums, packet, potential, tables, halos, high, low, matrices, other):
    count_r, rows, width = packet.shape
    steps = count_r // LAST
    return pl.pallas_call(
        last_kernel,
        in_specs=[VMEM] * 17,
        out_specs=[HBM, HBM],
        out_shape=[jax.ShapeDtypeStruct(packet.shape, F32)] * 2,
        scratch_shapes=[
            pltpu.VMEM((count_r + 2 * HALO, rows, width), F32),
            pltpu.VMEM(packet.shape, F32),
            pltpu.VMEM((count_r, 8, width), F32),
            pltpu.VMEM((4, other.shape[0] * other.shape[1] // 2, width), BF16),
            pltpu.VMEM((2 * HALO * (rows + count_r), width), F32),
            pltpu.SemaphoreType.DMA((2, steps)),
        ],
        compiler_params=pltpu.CompilerParams(vmem_limit_bytes=20 * MIB),
        cost_estimate=pl.CostEstimate(flops=14_000_000_000, bytes_accessed=36 * MIB, transcendentals=0),
        name="last_iteration",
    )(*own_sums, packet, potential, tables, *halos, high, low, *matrices, other)


def neighbours(axis, upward, downward):
    count = lax.axis_size(axis)
    return (
        lax.ppermute(upward, axis, [(i, i + 1) for i in range(count - 1)]),
        lax.ppermute(downward, axis, [(i + 1, i) for i in range(count - 1)]),
    )


def local(packet, previous, potential, rotation, angular, damping, absorber, stencil_index, stencil_weight):
    packet, previous, potential = packet[0], previous[0], potential[0]
    rotation, angular, damping, absorber = rotation[0], angular[0], damping[0], absorber[0]
    count_r, rows, width = packet.shape
    count_rr, count_row = (lax.axis_size(name) for name in ("rr", "row"))
    chips = count_row // CORES
    rotation, damping, absorber = (jnp.swapaxes(value, 0, 1) for value in (rotation, damping, absorber))
    stencil_index, stencil_weight = (jnp.swapaxes(value, 1, 2) for value in (stencil_index, stencil_weight))
    near_packet, near_previous, near_potential = packet, previous, potential
    packet, previous, potential, rotation, damping, absorber, stencil_index, stencil_weight, angular = (
        in_hbm(value)
        for value in (
            packet, previous, potential, rotation, damping, absorber, stencil_index, stencil_weight, angular
        )
    )

    upper, lower, first, last, tables, high, low = prepare(
        packet, previous, potential, rotation, damping, absorber, stencil_index, stencil_weight, angular
    )
    columns = count_row * rows * BAND
    left, right = neighbours("row", last, first)
    matrix = stencil_matrix(tables, count_r, columns, first)
    left, right, matrix = lax.optimization_barrier((left, right, matrix))
    table = bands(packet, previous, potential, tables, left, right, high, low)

    half = count_rr // PLANES
    start = count_rr - 1
    plane = ("sect", "rr")
    low_side, high_side = start - half + 1, start - 1
    relays = [count_rr + half - 1, count_rr + start, high_side, low_side]
    crossed = [lax.ppermute(table, plane, [(start, relay)]) for relay in relays]
    one, *edges = first_iteration(
        packet, near_previous, near_potential, tables, upper, lower, left, right, high, low, table
    )
    *crossed, one, edges = lax.optimization_barrier((*crossed, one, edges))
    piece = sum(crossed)
    near = [(low_side, count_rr), (high_side, count_rr + half - 2)]
    near += [(count_rr + half - 1, count_rr + half - 3), (count_rr + start, count_rr + start - 2)]
    opposite = [(low_side, count_rr + low_side), (high_side, count_rr + high_side)]
    arrived = [lax.ppermute(piece, plane, near), lax.ppermute(piece, plane, opposite)]
    top, bottom, first, last = edges
    top, bottom, piece = lax.optimization_barrier((top, bottom, piece))
    up, down = neighbours("rr", bottom, top)
    spread = piece + sum(arrived)
    line = ("sect", "row")

    def around(shift):
        pairs = []
        for chip in range(chips):
            for core in range(CORES):
                pairs.append(
                    (count_row + chip * CORES + core, count_row + ((chip + shift) % chips) * CORES + core)
                )
        return lax.ppermute(spread, line, pairs)

    rest = [around(1), around(3), around(2)]
    edge_matrix_and_ends = finish_edges(
        (up, down, left, right), tables, (top, bottom, first, last), rows, count_r, columns, spread
    )
    *edge_matrix, up, down, first, last, added = edge_matrix_and_ends
    rest[1], edge_matrix, first, last = lax.optimization_barrier((rest[1], edge_matrix, first, last))
    left, right = neighbours("row", last, first)
    *rest, left, right = lax.optimization_barrier((*rest, left, right))
    own = jnp.stack([spread, rest[0], rest[2], rest[1]], axis=0)
    other = lax.ppermute(
        own, line, [(count_row + i, count_row + i + 1 - 2 * (i % CORES)) for i in range(count_row)]
    )
    own_sums = own_source(one, added, (*matrix[:2], *edge_matrix), own)
    other, own_sums = lax.optimization_barrier((other, own_sums))
    earlier, latest = last_iteration(
        own_sums, near_packet, near_potential, tables, (up, down, left, right), high, low, (*matrix[2:], *edge_matrix), other
    )
    return latest[None], earlier[None]


def solution(mesh):
    in_specs = (
        P("sect", "rr", "row", None),
        P("sect", "rr", "row", None),
        P("sect", "rr", "row", None),
        P("sect", "rr", "row"),
        P("sect", None, None),
        P("sect", "rr", "row"),
        P("sect", "rr", "row"),
        P(None, "rr", "row"),
        P(None, "rr", "row"),
    )
    out_specs = (P("sect", "rr", "row", None), P("sect", "rr", "row", None))
    return jax.shard_map(local, mesh=mesh, in_specs=in_specs, out_specs=out_specs, check_vma=False)
```

```python
import functools

import jax
import jax.numpy as jnp
from jax import lax
from jax.experimental import pallas as pl
from jax.experimental.pallas import tpu as pltpu
from jax.sharding import PartitionSpec as P

BAND = 2
STENCILS = 4
HALO = 2
LANES = 128
CHUNK = 16
LAST = 16
CORES = 2
PLANES = 2
ROT, RET, INDEX, WEIGHT, TABLES = 0, 1, 2, 6, 10
EXTRA = 2 * STENCILS * HALO
OFBAND = 32
MIB = 1 << 20
F32 = jnp.float32
BF16 = jnp.bfloat16
ANY = pl.BlockSpec(memory_space=pl.ANY)
HBM = pl.BlockSpec(memory_space=pltpu.HBM)
VMEM = pl.BlockSpec(memory_space=pltpu.VMEM)

SIDE1 = -16.0 / 96.0
SIDE2 = 1.0 / 96.0
MIDDLE = 2.0 * 30.0 / 96.0 - 7.5 / 4.0


def halves(value):
    high = value.astype(BF16)
    low = (value - high.astype(F32)).astype(BF16)
    return high, low


def product(left, right_high, right_low):
    high, low = left
    total = jnp.dot(high, right_high, preferred_element_type=F32)
    total += jnp.dot(low, right_high, preferred_element_type=F32)
    return total + jnp.dot(high, right_low, preferred_element_type=F32)


def doubled_hamilton(field, index, start, count, lanes, turned, potential, rotation):
    def at(shift_r, shift_v):
        return field[index + shift_r, pl.ds(start + shift_v, count), lanes]

    middle = at(0, 0)
    near = at(-1, 0) + at(1, 0) + (at(0, -1) + at(0, 1))
    far = at(-2, 0) + at(2, 0) + (at(0, -2) + at(0, 2))
    return (
        SIDE1 * near
        + SIDE2 * far
        + (0.25 * potential + MIDDLE) * middle
        + (0.25 * rotation) * turned
    )


def in_hbm(value):
    return pltpu.with_memory_space_constraint(value, pltpu.HBM)


def holds_bands():
    return (lax.axis_index("sect") == 0) & (lax.axis_index("rr") == lax.axis_size("rr") - 1)


def in_product():
    return lax.axis_index("sect") == 1


def retained_of(damping, absorber):
    return 1.0 - absorber.astype(F32) * (1.0 - damping)


def band_kernel(
    packet, previous, potential, tables, left, right, high, low, out, field, later, turned, held, sems
):
    count_r, rows, width = packet.shape
    base = 16
    wide = rows + 16
    begin = left.shape[0] - OFBAND

    @pl.when(holds_bands())
    def _():
        copies = [
            pltpu.make_async_copy(packet.at[pl.ds(count_r - 6, 6)], field.at[pl.ds(2, 6), pl.ds(base, rows)], sems.at[0]),
            pltpu.make_async_copy(previous.at[pl.ds(count_r - 4, 4)], held.at[0], sems.at[1]),
            pltpu.make_async_copy(potential.at[pl.ds(count_r - 4, 4)], held.at[1], sems.at[2]),
        ]
        later[...] = jnp.zeros_like(later)
        field[0:2] = jnp.zeros_like(field[0:2])
        field[8:10] = jnp.zeros_like(field[8:10])
        for k in range(2, 8):
            field[k, 0:base] = jnp.zeros((base, width), F32)
            field[k, base + rows :] = jnp.zeros((base, width), F32)
        for copy in copies:
            copy.start()
        for k in range(4):
            at = begin + 4 * k
            field[4 + k, base - 4 : base] = left[at : at + 4]
            field[4 + k, base + rows : base + rows + 4] = right[at : at + 4]
        columns = [
            (tables[ROT, :, count_r - 4 + k : count_r - 3 + k], tables[RET, :, count_r - 4 + k : count_r - 3 + k])
            for k in range(4)
        ]
        columns = [tuple(jnp.broadcast_to(c, (rows, LANES)) for c in pair) for pair in columns]
        for copy in copies:
            copy.wait()
        window = field[4:8, base - 8 : base + rows + 8].reshape(4 * wide, width)
        turned[...] = product(halves(window), high[...], low[...])
        for k in range(4):
            rotation, retained = columns[k]
            for at in range(0, width, LANES):
                lanes = slice(at, at + LANES)
                update = doubled_hamilton(
                    field, 4 + k, base, rows, lanes,
                    turned[k * wide + 8 : k * wide + 8 + rows, lanes], held[1, k, :, lanes], rotation,
                ) - retained * held[0, k, :, lanes]
                later[k, base : base + rows, lanes] = retained * update
                if k >= 2:
                    out[(k - 2) * rows : (k - 1) * rows, lanes] = (1.0 - retained) * update
        for k in range(2, 4):
            for slab, place, inside in ((left, base - 8, 6), (right, base + rows, 0)):
                at = begin + 16 + 2 * (k - 2)
                prev, pot, rot, ret = (slab[at + 4 * n : at + 4 * n + 2] for n in range(4))
                update = doubled_hamilton(
                    field, 4 + k, place + inside, 2, slice(None),
                    turned[k * wide + place - base + 8 + inside : k * wide + place - base + 10 + inside], pot, rot,
                ) - ret * prev
                later[k, place + inside : place + inside + 2] = ret * update
        window = later[2:4, base : base + rows].reshape(2 * rows, width)
        turned[0 : 2 * rows] = product(halves(window), high[...], low[...])
        for k in range(2, 4):
            rotation, retained = columns[k]
            for at in range(0, width, LANES):
                lanes = slice(at, at + LANES)
                update = doubled_hamilton(
                    later, k, base, rows, lanes,
                    turned[(k - 2) * rows : (k - 1) * rows, lanes], held[1, k, :, lanes], rotation,
                ) - retained * field[4 + k, base : base + rows, lanes]
                out[k * rows : (k + 1) * rows, lanes] = (1.0 - retained) * update


def bands(packet, previous, potential, tables, left, right, high, low):
    _, rows, width = packet.shape
    return pl.pallas_call(
        band_kernel,
        in_specs=[HBM, HBM, HBM, VMEM, VMEM, VMEM, VMEM, VMEM],
        out_specs=VMEM,
        out_shape=jax.ShapeDtypeStruct((2 * BAND * rows, width), F32),
        scratch_shapes=[
            pltpu.VMEM((10, rows + 32, width), F32),
            pltpu.VMEM((6, rows + 32, width), F32),
            pltpu.VMEM((4 * (rows + 16), width), F32),
            pltpu.VMEM((2, 4, rows, width), F32),
            pltpu.SemaphoreType.DMA((3,)),
        ],
        compiler_params=pltpu.CompilerParams(vmem_limit_bytes=16 * MIB),
        cost_estimate=pl.CostEstimate(flops=400_000_000, bytes_accessed=4 * MIB, transcendentals=0),
        name="both_bands",
    )(packet, previous, potential, tables, left, right, high, low)


def prepare_kernel(
    packet, previous, potential, rotation, damping, absorber, index, weight, angular,
    upper, lower, first, last, tables, high, low,
    sides, others, factors, masks, indices, weights, matrix, sems,
):
    count_r, rows, width = packet.shape
    small = [
        pltpu.make_async_copy(rotation, factors.at[0], sems.at[0]),
        pltpu.make_async_copy(damping, factors.at[1], sems.at[1]),
        pltpu.make_async_copy(absorber, masks, sems.at[2]),
        pltpu.make_async_copy(index, indices, sems.at[3]),
        pltpu.make_async_copy(weight, weights, sems.at[4]),
    ]
    copies = [
        pltpu.make_async_copy(packet.at[:, pl.ds(0, 8)], sides.at[0], sems.at[5]),
        pltpu.make_async_copy(packet.at[:, pl.ds(rows - 8, 8)], sides.at[1], sems.at[6]),
        pltpu.make_async_copy(previous.at[pl.ds(count_r - BAND, BAND)], others.at[0], sems.at[7]),
        pltpu.make_async_copy(potential.at[pl.ds(count_r - BAND, BAND)], others.at[1], sems.at[8]),
        pltpu.make_async_copy(angular, matrix, sems.at[9]),
    ]
    for copy in small + copies:
        copy.start()
    for copy in small:
        copy.wait()
    values = [factors[0], retained_of(factors[1], masks[...])]
    values += [indices[n].astype(F32) for n in range(STENCILS)]
    values += [weights[n] for n in range(STENCILS)]
    for n, value in enumerate(values):
        tables[n] = jnp.concatenate([value, jnp.zeros((rows, LANES - count_r), F32)], axis=1)
    columns = HALO * count_r
    lane = lax.broadcasted_iota(jnp.int32, (rows, LANES), 1)
    at_top = jnp.zeros((rows, LANES), F32)
    at_bottom = jnp.zeros((rows, LANES), F32)
    for n, table in enumerate([*range(INDEX, TABLES), RET]):
        value = tables[table]
        at = n * HALO
        here = (lane >= at) & (lane < at + HALO)
        at_top = jnp.where(here, pltpu.roll(value, at, 1), at_top)
        at_bottom = jnp.where(here, pltpu.roll(value, (at + LANES - (count_r - HALO)) % LANES, 1), at_bottom)
        if table != RET:
            first[columns + at : columns + at + HALO, 0:LANES] = value[0:HALO]
            last[columns + at : columns + at + HALO, 0:LANES] = value[rows - HALO : rows]
    upper[...] = at_top
    lower[...] = at_bottom
    begin = columns + EXTRA
    for copy in copies:
        copy.wait()
    for out, n, far, near in ((first, 0, 0, 0), (last, 1, 4, rows - 2)):
        for k in range(4):
            out[begin + 4 * k : begin + 4 * k + 4] = sides[n, count_r - 4 + k, far : far + 4]
        for k in range(BAND):
            at = begin + 16 + 2 * k
            column = count_r - BAND + k
            out[at : at + 2] = others[0, k, near : near + 2]
            out[at + 4 : at + 6] = others[1, k, near : near + 2]
            for m in (ROT, RET):
                value = tables[m, near : near + 2, column : column + 1]
                out[at + 8 + 4 * m : at + 10 + 4 * m] = jnp.broadcast_to(value, (2, width))
    for out, n, near in ((first, 0, 0), (last, 1, 8 - HALO)):
        for k in range(count_r):
            for r in range(HALO):
                out[r * count_r + k : r * count_r + k + 1] = sides[n, k, near + r : near + r + 1]
    high[...], low[...] = halves(matrix[...])


def prepare(packet, previous, potential, rotation, damping, absorber, index, weight, angular):
    count_r, rows, width = packet.shape
    ends = jax.ShapeDtypeStruct((rows, LANES), F32)
    sides = jax.ShapeDtypeStruct((HALO * count_r + EXTRA + OFBAND, width), F32)
    part = jax.ShapeDtypeStruct(angular.shape, BF16)
    return pl.pallas_call(
        prepare_kernel,
        in_specs=[HBM] * 9,
        out_specs=[VMEM] * 7,
        out_shape=[ends, ends, sides, sides, jax.ShapeDtypeStruct((TABLES, rows, LANES), F32), part, part],
        scratch_shapes=[
            pltpu.VMEM((2, count_r, 8, width), F32),
            pltpu.VMEM((2, BAND, rows, width), F32),
            pltpu.VMEM((2, rows, count_r), F32),
            pltpu.VMEM((rows, count_r), jnp.int32),
            pltpu.VMEM((STENCILS, rows, count_r), jnp.int32),
            pltpu.VMEM((STENCILS, rows, count_r), F32),
            pltpu.VMEM(angular.shape, F32),
            pltpu.SemaphoreType.DMA((10,)),
        ],
        compiler_params=pltpu.CompilerParams(vmem_limit_bytes=16 * MIB),
        cost_estimate=pl.CostEstimate(flops=1_000_000, bytes_accessed=6 * MIB, transcendentals=0),
        name="prepare",
    )(packet, previous, potential, rotation, damping, absorber, index, weight, angular)


def put_sides(sides, left, right, count_r, left_more=None, right_more=None):
    def body(k, carry):
        for r in range(HALO):
            at = pl.ds(r * count_r + k, 1)
            before, behind = left[at], right[at]
            if left_more is not None:
                before, behind = before + left_more[at], behind + right_more[at]
            sides[k, r : r + 1] = behind
            sides[k, 8 - HALO + r : 8 - HALO + r + 1] = before
        return carry

    lax.fori_loop(0, count_r, body, 0, unroll=8)


def advance(step, chunk, field, sides, previous, potential, tables, high, low, put, more=None):
    rows = previous.shape[1]
    width = previous.shape[2]
    here = step * chunk
    shift = lax.rem(LANES - here, LANES)
    columns = [pltpu.roll(tables[n], shift, 1) for n in (ROT, RET)]
    window = field[pl.ds(HALO + here, chunk)].reshape(chunk * rows, width)
    split = halves(window)
    wide = 2 * LANES
    for tile in range(0, width, wide):
        turned = product(split, high[:, tile : tile + wide], low[:, tile : tile + wide])
        source = None if more is None else more(slice(tile, tile + wide))
        for k in range(chunk):
            rotation = jnp.broadcast_to(0.25 * columns[0][:, k : k + 1], (rows, LANES))
            retained = jnp.broadcast_to(columns[1][:, k : k + 1], (rows, LANES))
            for at in range(tile, tile + wide, LANES):
                lanes = slice(at, at + LANES)

                def row(shift):
                    return field[HALO + here + k + shift, :, lanes]

                middle = row(0)
                ring = jnp.concatenate([middle, sides[here + k, :, lanes]], axis=0)
                around = [pltpu.roll(ring, s, 0)[:rows] for s in (1, rows + 7, 2, rows + 6)]
                near = row(-1) + row(1) + (around[0] + around[1])
                far = row(-2) + row(2) + (around[2] + around[3])
                update = (
                    SIDE1 * near
                    + SIDE2 * far
                    + (0.25 * potential[here + k, :, lanes] + MIDDLE) * middle
                    + rotation * turned[k * rows : (k + 1) * rows, at - tile : at - tile + LANES]
                    - retained * previous[here + k, :, lanes]
                )
                value = retained * update
                if source is not None:
                    value += source[k * rows : (k + 1) * rows, at - tile : at - tile + LANES]
                put(here + k, lanes, value)


def first_kernel(
    packet, previous, potential, tables, upper, lower, left, right, high, low, after,
    done, top, bottom, first, last, field, sides, sems,
):
    count_r, rows, width = packet.shape
    steps = count_r // CHUNK

    def copies(n):
        part = pl.ds(n * CHUNK, CHUNK)
        return pltpu.make_async_copy(packet.at[part], field.at[pl.ds(HALO + n * CHUNK, CHUNK)], sems.at[n])

    for n in range(steps):
        copies(n).start()
    field[0:HALO] = jnp.zeros((HALO, rows, width), F32)
    field[HALO + count_r :] = jnp.zeros((HALO, rows, width), F32)
    put_sides(sides, left, right, count_r)
    copies(0).wait()

    def put(k, lanes, value):
        done[k, :, lanes] = value

    def body(n, carry):
        @pl.when(n + 1 < steps)
        def _():
            copies(n + 1).wait()

        advance(n, CHUNK, field, sides, previous, potential, tables, high, low, put)
        for k in range(CHUNK):
            for r in range(HALO):
                at = pl.ds(r * count_r + n * CHUNK + k, 1)
                first[at] = done[n * CHUNK + k, r : r + 1]
                last[at] = done[n * CHUNK + k, rows - HALO + r : rows - HALO + r + 1]
        return carry

    lax.fori_loop(0, steps, body, 0)
    edges = HALO * rows
    for k in range(HALO):
        here = slice(k * rows, (k + 1) * rows)
        beside = slice(edges + k * rows, edges + (k + 1) * rows)
        top[here] = done[k]
        bottom[here] = done[count_r - HALO + k]
        top[beside] = field[HALO + k]
        bottom[beside] = field[count_r + k]
    top[2 * edges : 2 * edges + rows, 0:LANES] = upper[...]
    bottom[2 * edges : 2 * edges + rows, 0:LANES] = lower[...]


def first_iteration(packet, previous, potential, tables, upper, lower, left, right, high, low, after):
    count_r, rows, width = packet.shape
    ends = jax.ShapeDtypeStruct((2 * HALO * rows + rows, width), F32)
    sides = jax.ShapeDtypeStruct((HALO * count_r, width), F32)
    return pl.pallas_call(
        first_kernel,
        in_specs=[HBM, *[VMEM] * 9, ANY],
        out_specs=[VMEM] * 5,
        out_shape=[jax.ShapeDtypeStruct(packet.shape, F32), ends, ends, sides, sides],
        scratch_shapes=[
            pltpu.VMEM((count_r + 2 * HALO, rows, width), F32),
            pltpu.VMEM((count_r, 8, width), F32),
            pltpu.SemaphoreType.DMA((count_r // CHUNK,)),
        ],
        compiler_params=pltpu.CompilerParams(vmem_limit_bytes=14 * MIB),
        cost_estimate=pl.CostEstimate(flops=7_000_000_000, bytes_accessed=20 * MIB, transcendentals=0),
        name="first_iteration",
    )(packet, previous, potential, tables, upper, lower, left, right, high, low, after)


def slot_of(value, rows, width):
    per = rows * BAND
    shift_owner = per.bit_length() - 1
    chips = width // per // CORES
    row = lax.axis_index("row")
    index = value.astype(jnp.int32)
    owner = index >> shift_owner
    inside = index & (per - 1)
    core = (owner & 1) ^ (row & 1)
    chip = ((row >> 1) - (owner >> 1)) & (chips - 1)
    slot = ((core * chips + chip) << shift_owner) + (inside & 1) * rows + (inside >> 1)
    return slot.astype(F32)


def fill_rows(at, cut, rows, high, low, begin=0):
    column = lax.broadcasted_iota(jnp.int32, (rows, LANES), 1).astype(F32)
    cut = [jnp.broadcast_to(value, (rows, LANES)) for value in cut]
    for tile in range(0, high.shape[1], LANES):
        here = column + float(begin + tile)
        total = jnp.where(here == cut[0], cut[STENCILS], 0.0)
        for n in range(1, STENCILS):
            total += jnp.where(here == cut[n], cut[STENCILS + n], 0.0)
        upper, lower = halves(total)
        high[pl.ds(at, rows), tile : tile + LANES] = upper
        low[pl.ds(at, rows), tile : tile + LANES] = lower


def stencil_kernel(tables, after, high, low, other_high, other_low):
    _, rows, _ = tables.shape
    count_r = high.shape[0] // rows
    group = 8
    half = high.shape[1]

    @pl.when(in_product())
    def _():
        values = [slot_of(tables[INDEX + n], rows, CORES * half) for n in range(STENCILS)]
        values += [tables[WEIGHT + n] for n in range(STENCILS)]

        def body(step, carry):
            shift = lax.rem(LANES - step * group, LANES)
            moved = [pltpu.roll(value, shift, 1) for value in values]
            for k in range(group):
                at = pl.multiple_of((step * group + k) * rows, rows)
                cut = [jnp.broadcast_to(value[:, k : k + 1], (rows, LANES)) for value in moved]
                fill_rows(at, cut, rows, high, low)
                fill_rows(at, cut, rows, other_high, other_low, half)
            return carry

        lax.fori_loop(0, count_r // group, body, 0)


def stencil_matrix(tables, count_r, columns, after):
    rows = tables.shape[1]
    points = jax.ShapeDtypeStruct((count_r * rows, columns // CORES), BF16)
    return pl.pallas_call(
        stencil_kernel,
        in_specs=[VMEM, ANY],
        out_specs=[VMEM] * 4,
        out_shape=[points] * 4,
        compiler_params=pltpu.CompilerParams(vmem_limit_bytes=16 * MIB),
        cost_estimate=pl.CostEstimate(flops=15_000_000, bytes_accessed=6 * MIB, transcendentals=0),
        name="stencil_matrix",
    )(tables, after)


def edge_kernel(
    up, down, left, right, tables, top, bottom, first, last, after,
    high, low, whole_up, whole_down, new_first, new_last, added, square, *, rows, count_r,
):
    width = up.shape[1]
    edges = HALO * rows

    def retained(k):
        return jnp.broadcast_to(tables[RET, :, k : k + 1], (rows, width))

    def there(side, k):
        at = 2 * STENCILS * HALO + k
        return jnp.broadcast_to(side[2 * edges : 2 * edges + rows, at : at + 1], (rows, width))

    def packet_row(slab, k):
        return slab[edges + k * rows : edges + (k + 1) * rows]

    added[0] = retained(0) * (SIDE1 * packet_row(up, 1) + SIDE2 * packet_row(up, 0))
    added[1] = retained(1) * (SIDE2 * packet_row(up, 1))
    added[2] = retained(count_r - 2) * (SIDE2 * packet_row(down, 0))
    added[3] = retained(count_r - 1) * (SIDE1 * packet_row(down, 0) + SIDE2 * packet_row(down, 1))
    whole_up[0:rows] = up[0:rows] + there(up, 0) * (SIDE2 * packet_row(top, 0))
    whole_up[rows:edges] = up[rows:edges] + there(up, 1) * (SIDE1 * packet_row(top, 0) + SIDE2 * packet_row(top, 1))
    whole_down[0:rows] = down[0:rows] + there(down, 0) * (SIDE1 * packet_row(bottom, 1) + SIDE2 * packet_row(bottom, 0))
    whole_down[rows:edges] = down[rows:edges] + there(down, 1) * (SIDE2 * packet_row(bottom, 1))
    new_first[...] = first[...]
    new_last[...] = last[...]
    for k in range(HALO):
        for n, r_row in ((k, k), (HALO + k, count_r - HALO + k)):
            for r in range(HALO):
                at = r * count_r + r_row
                new_first[at : at + 1] = first[at : at + 1] + added[n, r : r + 1]
                new_last[at : at + 1] = last[at : at + 1] + added[n, rows - HALO + r : rows - HALO + r + 1]

    @pl.when(in_product())
    def _():
        at = 0
        for side in (up, down):
            value = side[2 * edges : 2 * edges + rows, 0:LANES]
            slots = slot_of(value, rows, high.shape[1])
            for e in range(HALO):
                cut = [
                    (slots if m < STENCILS else value)[:, HALO * m + e : HALO * m + e + 1]
                    for m in range(2 * STENCILS)
                ]
                fill_rows(at, cut, rows, high, low)
                at += rows
        square[...] = jnp.zeros_like(square)
        part = EXTRA // 2
        for n, side in enumerate((left, right)):
            begin = HALO * count_r
            square[n * EXTRA : n * EXTRA + part] = slot_of(side[begin : begin + part, 0:LANES], rows, high.shape[1])
            square[n * EXTRA + part : (n + 1) * EXTRA] = side[begin + part : begin + EXTRA, 0:LANES]
        turned = square[...].T
        for n in range(2):
            for e in range(HALO):
                for begin in range(0, count_r, rows):
                    cut = [
                        turned[begin : begin + rows, n * EXTRA + HALO * m + e : n * EXTRA + HALO * m + e + 1]
                        for m in range(2 * STENCILS)
                    ]
                    fill_rows(at, cut, rows, high, low)
                    at += rows


def finish_edges(halos, tables, edges, rows, count_r, columns, after):
    points = jax.ShapeDtypeStruct((2 * HALO * (rows + count_r), columns), BF16)
    width = edges[0].shape[1]
    return pl.pallas_call(
        functools.partial(edge_kernel, rows=rows, count_r=count_r),
        in_specs=[*[VMEM] * 9, ANY],
        out_specs=[VMEM] * 7,
        out_shape=[
            points, points,
            *[jax.ShapeDtypeStruct((HALO * length, width), F32) for length in (rows, rows, count_r, count_r)],
            jax.ShapeDtypeStruct((2 * HALO, rows, width), F32),
        ],
        scratch_shapes=[pltpu.VMEM((LANES, LANES), F32)],
        compiler_params=pltpu.CompilerParams(vmem_limit_bytes=16 * MIB),
        cost_estimate=pl.CostEstimate(flops=2_000_000, bytes_accessed=3 * MIB, transcendentals=0),
        name="finish_edges",
    )(*halos, tables, *edges, after)


def split_table(pieces, band, table, at):
    half = pieces.shape[1] // 2
    for k in range(pieces.shape[0]):
        upper, lower = halves(pieces[k, band * half : (band + 1) * half])
        table[at, k * half : (k + 1) * half] = upper
        table[at + 1, k * half : (k + 1) * half] = lower


def own_source_kernel(
    one, added, stencil_high, stencil_low, edge_high, edge_low, own, sum_one, edge_source, table
):
    count_r, rows, width = one.shape
    columns = table.shape[1]
    size = LAST * rows

    @pl.when(in_product())
    def _():
        split_table(own, 0, table, 0)

        def body(n, carry):
            cut = pl.ds(pl.multiple_of(n * size, size), size)
            part = pl.ds(n * LAST, LAST)
            weights = (stencil_high[cut], stencil_low[cut])
            sum_one[part] = one[part] + product(weights, table[0], table[1]).reshape(LAST, rows, width)
            return carry

        lax.fori_loop(0, count_r // LAST, body, 0)
        edge_source[...] = product((edge_high[:, 0:columns], edge_low[:, 0:columns]), table[0], table[1])

    @pl.when(jnp.logical_not(in_product()))
    def _():
        sum_one[...] = one[...]

    for k in range(HALO):
        sum_one[k] += added[k]
        sum_one[count_r - HALO + k] += added[HALO + k]


def own_source(one, added, matrices, own):
    width = one.shape[2]
    return pl.pallas_call(
        own_source_kernel,
        in_specs=[VMEM] * 7,
        out_specs=[VMEM] * 2,
        out_shape=[
            jax.ShapeDtypeStruct(one.shape, F32),
            jax.ShapeDtypeStruct((matrices[2].shape[0], width), F32),
        ],
        scratch_shapes=[pltpu.VMEM((2, own.shape[0] * own.shape[1] // 2, width), BF16)],
        compiler_params=pltpu.CompilerParams(vmem_limit_bytes=16 * MIB),
        cost_estimate=pl.CostEstimate(flops=100_000_000_000, bytes_accessed=200 * MIB, transcendentals=0),
        name="own_source",
    )(one, added, *matrices, own)


def last_kernel(
    one, edge_source, packet, potential, tables, up, down, left, right, high, low,
    own_high, own_low, stencil_high, stencil_low, edge_high, edge_low, own, other,
    earlier, latest, field, done, sides, table, ends, sems,
):
    count_r, rows, width = packet.shape
    steps = count_r // LAST
    size = LAST * rows
    columns = table.shape[1]
    is_product = in_product()

    def part(n):
        return pl.ds(n * LAST, LAST)

    def cut(n):
        return pl.ds(pl.multiple_of(n * size, size), size)

    def earliers(n):
        return pltpu.make_async_copy(field.at[pl.ds(HALO + n * LAST, LAST)], earlier.at[part(n)], sems.at[0, n])

    def latests(n):
        return pltpu.make_async_copy(done.at[part(n)], latest.at[part(n)], sems.at[1, n])

    def put_ends(up_value, down_value):
        for k in range(HALO):
            field[k] = up_value[k * rows : (k + 1) * rows]
            field[HALO + count_r + k] = down_value[k * rows : (k + 1) * rows]

    def put(k, lanes, value):
        done[k, :, lanes] = value

    @pl.when(is_product)
    def _():
        split_table(other, 0, table, 0)
        split_table(own, 1, table, 2)
        split_table(other, 1, table, 4)
        ends[...] = edge_source[...] + product(
            (edge_high[:, columns : 2 * columns], edge_low[:, columns : 2 * columns]), table[0], table[1]
        )
        edges = HALO * rows
        long = HALO * count_r
        put_ends(up[...] + ends[:edges], down[...] + ends[edges : 2 * edges])
        put_sides(
            sides, left, right, count_r, ends.at[pl.ds(2 * edges, long)], ends.at[pl.ds(2 * edges + long, long)]
        )

        def weights(n):
            return stencil_high[cut(n)], stencil_low[cut(n)]

        def add(n, carry):
            more = product(weights(n), table[0], table[1]).reshape(LAST, rows, width)
            field[pl.ds(HALO + n * LAST, LAST)] = one[part(n)] + more
            earliers(n).start()
            return carry

        lax.fori_loop(0, steps, add, 0)

        def body(n, carry):
            mine, theirs = (own_high[cut(n)], own_low[cut(n)]), weights(n)

            def more(lanes):
                return product(mine, table[2, :, lanes], table[3, :, lanes]) + product(
                    theirs, table[4, :, lanes], table[5, :, lanes]
                )

            advance(n, LAST, field, sides, packet, potential, tables, high, low, put, more)
            latests(n).start()
            return carry

        lax.fori_loop(0, steps, body, 0)

    @pl.when(jnp.logical_not(is_product))
    def _():
        put_ends(up, down)
        put_sides(sides, left, right, count_r)
        for n in range(steps):
            field[pl.ds(HALO + n * LAST, LAST)] = one[part(n)]
            earliers(n).start()

        def body(n, carry):
            advance(n, LAST, field, sides, packet, potential, tables, high, low, put)
            latests(n).start()
            return carry

        lax.fori_loop(0, steps, body, 0)

    for n in range(steps):
        earliers(n).wait()
        latests(n).wait()


def last_iteration(own_sums, packet, potential, tables, halos, high, low, matrices, pieces):
    count_r, rows, width = packet.shape
    steps = count_r // LAST
    return pl.pallas_call(
        last_kernel,
        in_specs=[VMEM] * 19,
        out_specs=[HBM, HBM],
        out_shape=[jax.ShapeDtypeStruct(packet.shape, F32)] * 2,
        scratch_shapes=[
            pltpu.VMEM((count_r + 2 * HALO, rows, width), F32),
            pltpu.VMEM(packet.shape, F32),
            pltpu.VMEM((count_r, 8, width), F32),
            pltpu.VMEM((6, pieces[0].shape[0] * pieces[0].shape[1] // 2, width), BF16),
            pltpu.VMEM((2 * HALO * (rows + count_r), width), F32),
            pltpu.SemaphoreType.DMA((2, steps)),
        ],
        compiler_params=pltpu.CompilerParams(vmem_limit_bytes=20 * MIB),
        cost_estimate=pl.CostEstimate(flops=14_000_000_000, bytes_accessed=36 * MIB, transcendentals=0),
        name="last_iteration",
    )(*own_sums, packet, potential, tables, *halos, high, low, *matrices, *pieces)


def neighbours(axis, upward, downward):
    count = lax.axis_size(axis)
    return (
        lax.ppermute(upward, axis, [(i, i + 1) for i in range(count - 1)]),
        lax.ppermute(downward, axis, [(i + 1, i) for i in range(count - 1)]),
    )


def local(packet, previous, potential, rotation, angular, damping, absorber, stencil_index, stencil_weight):
    packet, previous, potential = packet[0], previous[0], potential[0]
    rotation, angular, damping, absorber = rotation[0], angular[0], damping[0], absorber[0]
    count_r, rows, width = packet.shape
    count_rr, count_row = (lax.axis_size(name) for name in ("rr", "row"))
    chips = count_row // CORES
    rotation, damping, absorber = (jnp.swapaxes(value, 0, 1) for value in (rotation, damping, absorber))
    stencil_index, stencil_weight = (jnp.swapaxes(value, 1, 2) for value in (stencil_index, stencil_weight))
    near_packet, near_previous, near_potential = packet, previous, potential
    packet, previous, potential, rotation, damping, absorber, stencil_index, stencil_weight, angular = (
        in_hbm(value)
        for value in (
            packet, previous, potential, rotation, damping, absorber, stencil_index, stencil_weight, angular
        )
    )

    upper, lower, first, last, tables, high, low = prepare(
        packet, previous, potential, rotation, damping, absorber, stencil_index, stencil_weight, angular
    )
    columns = count_row * rows * BAND
    left, right = neighbours("row", last, first)
    matrix = stencil_matrix(tables, count_r, columns, first)
    left, right, matrix = lax.optimization_barrier((left, right, matrix))
    table = bands(packet, previous, potential, tables, left, right, high, low)

    half = count_rr // PLANES
    start = count_rr - 1
    plane = ("sect", "rr")
    low_side, high_side = start - half + 1, start - 1
    relays = [count_rr + half - 1, count_rr + start, high_side, low_side]
    crossed = [lax.ppermute(table, plane, [(start, relay)]) for relay in relays]
    one, *edges = first_iteration(
        packet, near_previous, near_potential, tables, upper, lower, left, right, high, low, table
    )
    *crossed, one, edges = lax.optimization_barrier((*crossed, one, edges))
    piece = sum(crossed)
    near = [(low_side, count_rr), (high_side, count_rr + half - 2)]
    near += [(count_rr + half - 1, count_rr + half - 3), (count_rr + start, count_rr + start - 2)]
    opposite = [(low_side, count_rr + low_side), (high_side, count_rr + high_side)]
    arrived = [lax.ppermute(piece, plane, near), lax.ppermute(piece, plane, opposite)]
    top, bottom, first, last = edges
    top, bottom, piece = lax.optimization_barrier((top, bottom, piece))
    up, down = neighbours("rr", bottom, top)
    spread = piece + sum(arrived)
    line = ("sect", "row")

    def around(shift):
        pairs = []
        for chip in range(chips):
            for core in range(CORES):
                pairs.append(
                    (count_row + chip * CORES + core, count_row + ((chip + shift) % chips) * CORES + core)
                )
        return lax.ppermute(spread, line, pairs)

    rest = [around(1), around(3), around(2)]
    edge_matrix_and_ends = finish_edges(
        (up, down, left, right), tables, (top, bottom, first, last), rows, count_r, columns, spread
    )
    *edge_matrix, up, down, first, last, added = edge_matrix_and_ends
    rest[1], edge_matrix, first, last = lax.optimization_barrier((rest[1], edge_matrix, first, last))
    left, right = neighbours("row", last, first)
    own = jnp.stack([spread, rest[0], rest[2], rest[1]], axis=0)
    other = lax.ppermute(
        own, line, [(count_row + i, count_row + i + 1 - 2 * (i % CORES)) for i in range(count_row)]
    )
    left, right, added = lax.optimization_barrier((left, right, added))
    own_sums = own_source(one, added, (*matrix[:2], *edge_matrix), own)
    other, own_sums = lax.optimization_barrier((other, own_sums))
    earlier, latest = last_iteration(
        own_sums, near_packet, near_potential, tables, (up, down, left, right), high, low, (*matrix, *edge_matrix), (own, other)
    )
    return latest[None], earlier[None]


def solution(mesh):
    in_specs = (
        P("sect", "rr", "row", None),
        P("sect", "rr", "row", None),
        P("sect", "rr", "row", None),
        P("sect", "rr", "row"),
        P("sect", None, None),
        P("sect", "rr", "row"),
        P("sect", "rr", "row"),
        P(None, "rr", "row"),
        P(None, "rr", "row"),
    )
    out_specs = (P("sect", "rr", "row", None), P("sect", "rr", "row", None))
    return jax.shard_map(local, mesh=mesh, in_specs=in_specs, out_specs=out_specs, check_vma=False)
```

```python
import functools

import jax
import jax.numpy as jnp
from jax import lax
from jax.experimental import pallas as pl
from jax.experimental.pallas import tpu as pltpu
from jax.sharding import PartitionSpec as P

BAND = 2
STENCILS = 4
HALO = 2
LANES = 128
CHUNK = 16
LAST = 16
CORES = 2
PLANES = 2
ROT, RET, INDEX, WEIGHT, TABLES = 0, 1, 2, 6, 10
EXTRA = 2 * STENCILS * HALO
OFBAND = 32
MIB = 1 << 20
F32 = jnp.float32
BF16 = jnp.bfloat16
ANY = pl.BlockSpec(memory_space=pl.ANY)
HBM = pl.BlockSpec(memory_space=pltpu.HBM)
VMEM = pl.BlockSpec(memory_space=pltpu.VMEM)

SIDE1 = -16.0 / 96.0
SIDE2 = 1.0 / 96.0
MIDDLE = 2.0 * 30.0 / 96.0 - 7.5 / 4.0


def halves(value):
    high = value.astype(BF16)
    low = (value - high.astype(F32)).astype(BF16)
    return high, low


def product(left, right_high, right_low):
    high, low = left
    total = jnp.dot(high, right_high, preferred_element_type=F32)
    total += jnp.dot(low, right_high, preferred_element_type=F32)
    return total + jnp.dot(high, right_low, preferred_element_type=F32)


def doubled_hamilton(field, index, start, count, lanes, turned, potential, rotation):
    def at(shift_r, shift_v):
        return field[index + shift_r, pl.ds(start + shift_v, count), lanes]

    middle = at(0, 0)
    near = at(-1, 0) + at(1, 0) + (at(0, -1) + at(0, 1))
    far = at(-2, 0) + at(2, 0) + (at(0, -2) + at(0, 2))
    return (
        SIDE1 * near
        + SIDE2 * far
        + (0.25 * potential + MIDDLE) * middle
        + (0.25 * rotation) * turned
    )


def in_hbm(value):
    return pltpu.with_memory_space_constraint(value, pltpu.HBM)


def holds_bands():
    return (lax.axis_index("sect") == 0) & (lax.axis_index("rr") == lax.axis_size("rr") - 1)


def in_product():
    return lax.axis_index("sect") == 1


def retained_of(damping, absorber):
    return 1.0 - absorber.astype(F32) * (1.0 - damping)


def band_kernel(
    packet, previous, potential, tables, left, right, high, low, out, field, later, turned, held, sems
):
    count_r, rows, width = packet.shape
    base = 16
    wide = rows + 16
    begin = left.shape[0] - OFBAND

    @pl.when(holds_bands())
    def _():
        copies = [
            pltpu.make_async_copy(packet.at[pl.ds(count_r - 6, 6)], field.at[pl.ds(2, 6), pl.ds(base, rows)], sems.at[0]),
            pltpu.make_async_copy(previous.at[pl.ds(count_r - 4, 4)], held.at[0], sems.at[1]),
            pltpu.make_async_copy(potential.at[pl.ds(count_r - 4, 4)], held.at[1], sems.at[2]),
        ]
        later[...] = jnp.zeros_like(later)
        field[0:2] = jnp.zeros_like(field[0:2])
        field[8:10] = jnp.zeros_like(field[8:10])
        for k in range(2, 8):
            field[k, 0:base] = jnp.zeros((base, width), F32)
            field[k, base + rows :] = jnp.zeros((base, width), F32)
        for copy in copies:
            copy.start()
        for k in range(4):
            at = begin + 4 * k
            field[4 + k, base - 4 : base] = left[at : at + 4]
            field[4 + k, base + rows : base + rows + 4] = right[at : at + 4]
        columns = [
            (tables[ROT, :, count_r - 4 + k : count_r - 3 + k], tables[RET, :, count_r - 4 + k : count_r - 3 + k])
            for k in range(4)
        ]
        columns = [tuple(jnp.broadcast_to(c, (rows, LANES)) for c in pair) for pair in columns]
        for copy in copies:
            copy.wait()
        window = field[4:8, base - 8 : base + rows + 8].reshape(4 * wide, width)
        turned[...] = product(halves(window), high[...], low[...])
        for k in range(4):
            rotation, retained = columns[k]
            for at in range(0, width, LANES):
                lanes = slice(at, at + LANES)
                update = doubled_hamilton(
                    field, 4 + k, base, rows, lanes,
                    turned[k * wide + 8 : k * wide + 8 + rows, lanes], held[1, k, :, lanes], rotation,
                ) - retained * held[0, k, :, lanes]
                later[k, base : base + rows, lanes] = retained * update
                if k >= 2:
                    out[(k - 2) * rows : (k - 1) * rows, lanes] = (1.0 - retained) * update
        for k in range(2, 4):
            for slab, place, inside in ((left, base - 8, 6), (right, base + rows, 0)):
                at = begin + 16 + 2 * (k - 2)
                prev, pot, rot, ret = (slab[at + 4 * n : at + 4 * n + 2] for n in range(4))
                update = doubled_hamilton(
                    field, 4 + k, place + inside, 2, slice(None),
                    turned[k * wide + place - base + 8 + inside : k * wide + place - base + 10 + inside], pot, rot,
                ) - ret * prev
                later[k, place + inside : place + inside + 2] = ret * update
        window = later[2:4, base : base + rows].reshape(2 * rows, width)
        turned[0 : 2 * rows] = product(halves(window), high[...], low[...])
        for k in range(2, 4):
            rotation, retained = columns[k]
            for at in range(0, width, LANES):
                lanes = slice(at, at + LANES)
                update = doubled_hamilton(
                    later, k, base, rows, lanes,
                    turned[(k - 2) * rows : (k - 1) * rows, lanes], held[1, k, :, lanes], rotation,
                ) - retained * field[4 + k, base : base + rows, lanes]
                out[k * rows : (k + 1) * rows, lanes] = (1.0 - retained) * update


def bands(packet, previous, potential, tables, left, right, high, low):
    _, rows, width = packet.shape
    return pl.pallas_call(
        band_kernel,
        in_specs=[HBM, HBM, HBM, VMEM, VMEM, VMEM, VMEM, VMEM],
        out_specs=VMEM,
        out_shape=jax.ShapeDtypeStruct((2 * BAND * rows, width), F32),
        scratch_shapes=[
            pltpu.VMEM((10, rows + 32, width), F32),
            pltpu.VMEM((6, rows + 32, width), F32),
            pltpu.VMEM((4 * (rows + 16), width), F32),
            pltpu.VMEM((2, 4, rows, width), F32),
            pltpu.SemaphoreType.DMA((3,)),
        ],
        compiler_params=pltpu.CompilerParams(vmem_limit_bytes=16 * MIB),
        cost_estimate=pl.CostEstimate(flops=400_000_000, bytes_accessed=4 * MIB, transcendentals=0),
        name="both_bands",
    )(packet, previous, potential, tables, left, right, high, low)


def prepare_kernel(
    packet, previous, potential, rotation, damping, absorber, index, weight,
    upper, lower, first, last, tables,
    sides, others, factors, masks, indices, weights, sems,
):
    count_r, rows, width = packet.shape
    small = [
        pltpu.make_async_copy(rotation, factors.at[0], sems.at[0]),
        pltpu.make_async_copy(damping, factors.at[1], sems.at[1]),
        pltpu.make_async_copy(absorber, masks, sems.at[2]),
        pltpu.make_async_copy(index, indices, sems.at[3]),
        pltpu.make_async_copy(weight, weights, sems.at[4]),
    ]
    copies = [
        pltpu.make_async_copy(packet.at[:, pl.ds(0, 8)], sides.at[0], sems.at[5]),
        pltpu.make_async_copy(packet.at[:, pl.ds(rows - 8, 8)], sides.at[1], sems.at[6]),
        pltpu.make_async_copy(previous.at[pl.ds(count_r - BAND, BAND)], others.at[0], sems.at[7]),
        pltpu.make_async_copy(potential.at[pl.ds(count_r - BAND, BAND)], others.at[1], sems.at[8]),
    ]
    for copy in small + copies:
        copy.start()
    for copy in small:
        copy.wait()
    values = [factors[0], retained_of(factors[1], masks[...])]
    values += [indices[n].astype(F32) for n in range(STENCILS)]
    values += [weights[n] for n in range(STENCILS)]
    for n, value in enumerate(values):
        tables[n] = jnp.concatenate([value, jnp.zeros((rows, LANES - count_r), F32)], axis=1)
    columns = HALO * count_r
    lane = lax.broadcasted_iota(jnp.int32, (rows, LANES), 1)
    at_top = jnp.zeros((rows, LANES), F32)
    at_bottom = jnp.zeros((rows, LANES), F32)
    for n, table in enumerate([*range(INDEX, TABLES), RET]):
        value = tables[table]
        at = n * HALO
        here = (lane >= at) & (lane < at + HALO)
        at_top = jnp.where(here, pltpu.roll(value, at, 1), at_top)
        at_bottom = jnp.where(here, pltpu.roll(value, (at + LANES - (count_r - HALO)) % LANES, 1), at_bottom)
        if table != RET:
            first[columns + at : columns + at + HALO, 0:LANES] = value[0:HALO]
            last[columns + at : columns + at + HALO, 0:LANES] = value[rows - HALO : rows]
    upper[...] = at_top
    lower[...] = at_bottom
    begin = columns + EXTRA
    for copy in copies:
        copy.wait()
    for out, n, far, near in ((first, 0, 0, 0), (last, 1, 4, rows - 2)):
        for k in range(4):
            out[begin + 4 * k : begin + 4 * k + 4] = sides[n, count_r - 4 + k, far : far + 4]
        for k in range(BAND):
            at = begin + 16 + 2 * k
            column = count_r - BAND + k
            out[at : at + 2] = others[0, k, near : near + 2]
            out[at + 4 : at + 6] = others[1, k, near : near + 2]
            for m in (ROT, RET):
                value = tables[m, near : near + 2, column : column + 1]
                out[at + 8 + 4 * m : at + 10 + 4 * m] = jnp.broadcast_to(value, (2, width))
    for out, n, near in ((first, 0, 0), (last, 1, 8 - HALO)):
        for k in range(count_r):
            for r in range(HALO):
                out[r * count_r + k : r * count_r + k + 1] = sides[n, k, near + r : near + r + 1]


def prepare(packet, previous, potential, rotation, damping, absorber, index, weight):
    count_r, rows, width = packet.shape
    ends = jax.ShapeDtypeStruct((rows, LANES), F32)
    sides = jax.ShapeDtypeStruct((HALO * count_r + EXTRA + OFBAND, width), F32)
    return pl.pallas_call(
        prepare_kernel,
        in_specs=[HBM] * 8,
        out_specs=[VMEM] * 5,
        out_shape=[ends, ends, sides, sides, jax.ShapeDtypeStruct((TABLES, rows, LANES), F32)],
        scratch_shapes=[
            pltpu.VMEM((2, count_r, 8, width), F32),
            pltpu.VMEM((2, BAND, rows, width), F32),
            pltpu.VMEM((2, rows, count_r), F32),
            pltpu.VMEM((rows, count_r), jnp.int32),
            pltpu.VMEM((STENCILS, rows, count_r), jnp.int32),
            pltpu.VMEM((STENCILS, rows, count_r), F32),
            pltpu.SemaphoreType.DMA((9,)),
        ],
        compiler_params=pltpu.CompilerParams(vmem_limit_bytes=16 * MIB),
        cost_estimate=pl.CostEstimate(flops=1_000_000, bytes_accessed=6 * MIB, transcendentals=0),
        name="prepare",
    )(packet, previous, potential, rotation, damping, absorber, index, weight)


def put_sides(sides, left, right, count_r, left_more=None, right_more=None):
    def body(k, carry):
        for r in range(HALO):
            at = pl.ds(r * count_r + k, 1)
            before, behind = left[at], right[at]
            if left_more is not None:
                before, behind = before + left_more[at], behind + right_more[at]
            sides[k, r : r + 1] = behind
            sides[k, 8 - HALO + r : 8 - HALO + r + 1] = before
        return carry

    lax.fori_loop(0, count_r, body, 0, unroll=8)


def advance(step, chunk, field, sides, previous, potential, tables, high, low, put, more=None):
    rows = previous.shape[1]
    width = previous.shape[2]
    here = step * chunk
    shift = lax.rem(LANES - here, LANES)
    columns = [pltpu.roll(tables[n], shift, 1) for n in (ROT, RET)]
    window = field[pl.ds(HALO + here, chunk)].reshape(chunk * rows, width)
    split = halves(window)
    wide = 2 * LANES
    for tile in range(0, width, wide):
        turned = product(split, high[:, tile : tile + wide], low[:, tile : tile + wide])
        source = None if more is None else more(slice(tile, tile + wide))
        for k in range(chunk):
            rotation = jnp.broadcast_to(0.25 * columns[0][:, k : k + 1], (rows, LANES))
            retained = jnp.broadcast_to(columns[1][:, k : k + 1], (rows, LANES))
            for at in range(tile, tile + wide, LANES):
                lanes = slice(at, at + LANES)

                def row(shift):
                    return field[HALO + here + k + shift, :, lanes]

                middle = row(0)
                ring = jnp.concatenate([middle, sides[here + k, :, lanes]], axis=0)
                around = [pltpu.roll(ring, s, 0)[:rows] for s in (1, rows + 7, 2, rows + 6)]
                near = row(-1) + row(1) + (around[0] + around[1])
                far = row(-2) + row(2) + (around[2] + around[3])
                update = (
                    SIDE1 * near
                    + SIDE2 * far
                    + (0.25 * potential[here + k, :, lanes] + MIDDLE) * middle
                    + rotation * turned[k * rows : (k + 1) * rows, at - tile : at - tile + LANES]
                    - retained * previous[here + k, :, lanes]
                )
                value = retained * update
                if source is not None:
                    value += source[k * rows : (k + 1) * rows, at - tile : at - tile + LANES]
                put(here + k, lanes, value)


def first_kernel(
    packet, previous, potential, tables, upper, lower, left, right, high, low, after,
    done, top, bottom, first, last, field, sides, sems,
):
    count_r, rows, width = packet.shape
    steps = count_r // CHUNK

    def copies(n):
        part = pl.ds(n * CHUNK, CHUNK)
        return pltpu.make_async_copy(packet.at[part], field.at[pl.ds(HALO + n * CHUNK, CHUNK)], sems.at[n])

    for n in range(steps):
        copies(n).start()
    field[0:HALO] = jnp.zeros((HALO, rows, width), F32)
    field[HALO + count_r :] = jnp.zeros((HALO, rows, width), F32)
    put_sides(sides, left, right, count_r)
    copies(0).wait()

    def put(k, lanes, value):
        done[k, :, lanes] = value

    def body(n, carry):
        @pl.when(n + 1 < steps)
        def _():
            copies(n + 1).wait()

        advance(n, CHUNK, field, sides, previous, potential, tables, high, low, put)
        for k in range(CHUNK):
            for r in range(HALO):
                at = pl.ds(r * count_r + n * CHUNK + k, 1)
                first[at] = done[n * CHUNK + k, r : r + 1]
                last[at] = done[n * CHUNK + k, rows - HALO + r : rows - HALO + r + 1]
        return carry

    lax.fori_loop(0, steps, body, 0)
    edges = HALO * rows
    for k in range(HALO):
        here = slice(k * rows, (k + 1) * rows)
        beside = slice(edges + k * rows, edges + (k + 1) * rows)
        top[here] = done[k]
        bottom[here] = done[count_r - HALO + k]
        top[beside] = field[HALO + k]
        bottom[beside] = field[count_r + k]
    top[2 * edges : 2 * edges + rows, 0:LANES] = upper[...]
    bottom[2 * edges : 2 * edges + rows, 0:LANES] = lower[...]


def first_iteration(packet, previous, potential, tables, upper, lower, left, right, high, low, after):
    count_r, rows, width = packet.shape
    ends = jax.ShapeDtypeStruct((2 * HALO * rows + rows, width), F32)
    sides = jax.ShapeDtypeStruct((HALO * count_r, width), F32)
    return pl.pallas_call(
        first_kernel,
        in_specs=[HBM, *[VMEM] * 9, ANY],
        out_specs=[VMEM] * 5,
        out_shape=[jax.ShapeDtypeStruct(packet.shape, F32), ends, ends, sides, sides],
        scratch_shapes=[
            pltpu.VMEM((count_r + 2 * HALO, rows, width), F32),
            pltpu.VMEM((count_r, 8, width), F32),
            pltpu.SemaphoreType.DMA((count_r // CHUNK,)),
        ],
        compiler_params=pltpu.CompilerParams(vmem_limit_bytes=14 * MIB),
        cost_estimate=pl.CostEstimate(flops=7_000_000_000, bytes_accessed=20 * MIB, transcendentals=0),
        name="first_iteration",
    )(packet, previous, potential, tables, upper, lower, left, right, high, low, after)


def slot_of(value, rows, width):
    per = rows * BAND
    shift_owner = per.bit_length() - 1
    chips = width // per // CORES
    row = lax.axis_index("row")
    index = value.astype(jnp.int32)
    owner = index >> shift_owner
    inside = index & (per - 1)
    core = (owner & 1) ^ (row & 1)
    chip = ((row >> 1) - (owner >> 1)) & (chips - 1)
    slot = ((core * chips + chip) << shift_owner) + (inside & 1) * rows + (inside >> 1)
    return slot.astype(F32)


def fill_rows(at, cut, rows, high, low, begin=0):
    column = lax.broadcasted_iota(jnp.int32, (rows, LANES), 1).astype(F32)
    cut = [jnp.broadcast_to(value, (rows, LANES)) for value in cut]
    for tile in range(0, high.shape[1], LANES):
        here = column + float(begin + tile)
        total = jnp.where(here == cut[0], cut[STENCILS], 0.0)
        for n in range(1, STENCILS):
            total += jnp.where(here == cut[n], cut[STENCILS + n], 0.0)
        upper, lower = halves(total)
        high[pl.ds(at, rows), tile : tile + LANES] = upper
        low[pl.ds(at, rows), tile : tile + LANES] = lower


def stencil_kernel(tables, angular, after, high, low, other_high, other_low, angular_high, angular_low):
    _, rows, _ = tables.shape
    count_r = high.shape[0] // rows
    group = 8
    half = high.shape[1]
    angular_high[...], angular_low[...] = halves(angular[...])

    @pl.when(in_product())
    def _():
        values = [slot_of(tables[INDEX + n], rows, CORES * half) for n in range(STENCILS)]
        values += [tables[WEIGHT + n] for n in range(STENCILS)]

        def body(step, carry):
            shift = lax.rem(LANES - step * group, LANES)
            moved = [pltpu.roll(value, shift, 1) for value in values]
            for k in range(group):
                at = pl.multiple_of((step * group + k) * rows, rows)
                cut = [jnp.broadcast_to(value[:, k : k + 1], (rows, LANES)) for value in moved]
                fill_rows(at, cut, rows, high, low)
                fill_rows(at, cut, rows, other_high, other_low, half)
            return carry

        lax.fori_loop(0, count_r // group, body, 0)


def matrices_of(tables, angular, count_r, columns, after):
    rows = tables.shape[1]
    points = jax.ShapeDtypeStruct((count_r * rows, columns // CORES), BF16)
    return pl.pallas_call(
        stencil_kernel,
        in_specs=[VMEM, VMEM, ANY],
        out_specs=[VMEM] * 6,
        out_shape=[points] * 4 + [jax.ShapeDtypeStruct(angular.shape, BF16)] * 2,
        compiler_params=pltpu.CompilerParams(vmem_limit_bytes=16 * MIB),
        cost_estimate=pl.CostEstimate(flops=15_000_000, bytes_accessed=6 * MIB, transcendentals=0),
        name="stencil_matrix",
    )(tables, angular, after)


def edge_kernel(
    up, down, left, right, tables, top, bottom, first, last, after,
    high, low, whole_up, whole_down, new_first, new_last, added, square, *, rows, count_r,
):
    width = up.shape[1]
    edges = HALO * rows

    def retained(k):
        return jnp.broadcast_to(tables[RET, :, k : k + 1], (rows, width))

    def there(side, k):
        at = 2 * STENCILS * HALO + k
        return jnp.broadcast_to(side[2 * edges : 2 * edges + rows, at : at + 1], (rows, width))

    def packet_row(slab, k):
        return slab[edges + k * rows : edges + (k + 1) * rows]

    added[0] = retained(0) * (SIDE1 * packet_row(up, 1) + SIDE2 * packet_row(up, 0))
    added[1] = retained(1) * (SIDE2 * packet_row(up, 1))
    added[2] = retained(count_r - 2) * (SIDE2 * packet_row(down, 0))
    added[3] = retained(count_r - 1) * (SIDE1 * packet_row(down, 0) + SIDE2 * packet_row(down, 1))
    whole_up[0:rows] = up[0:rows] + there(up, 0) * (SIDE2 * packet_row(top, 0))
    whole_up[rows:edges] = up[rows:edges] + there(up, 1) * (SIDE1 * packet_row(top, 0) + SIDE2 * packet_row(top, 1))
    whole_down[0:rows] = down[0:rows] + there(down, 0) * (SIDE1 * packet_row(bottom, 1) + SIDE2 * packet_row(bottom, 0))
    whole_down[rows:edges] = down[rows:edges] + there(down, 1) * (SIDE2 * packet_row(bottom, 1))
    new_first[...] = first[...]
    new_last[...] = last[...]
    for k in range(HALO):
        for n, r_row in ((k, k), (HALO + k, count_r - HALO + k)):
            for r in range(HALO):
                at = r * count_r + r_row
                new_first[at : at + 1] = first[at : at + 1] + added[n, r : r + 1]
                new_last[at : at + 1] = last[at : at + 1] + added[n, rows - HALO + r : rows - HALO + r + 1]

    @pl.when(in_product())
    def _():
        at = 0
        for side in (up, down):
            value = side[2 * edges : 2 * edges + rows, 0:LANES]
            slots = slot_of(value, rows, high.shape[1])
            for e in range(HALO):
                cut = [
                    (slots if m < STENCILS else value)[:, HALO * m + e : HALO * m + e + 1]
                    for m in range(2 * STENCILS)
                ]
                fill_rows(at, cut, rows, high, low)
                at += rows
        square[...] = jnp.zeros_like(square)
        part = EXTRA // 2
        for n, side in enumerate((left, right)):
            begin = HALO * count_r
            square[n * EXTRA : n * EXTRA + part] = slot_of(side[begin : begin + part, 0:LANES], rows, high.shape[1])
            square[n * EXTRA + part : (n + 1) * EXTRA] = side[begin + part : begin + EXTRA, 0:LANES]
        turned = square[...].T
        for n in range(2):
            for e in range(HALO):
                for begin in range(0, count_r, rows):
                    cut = [
                        turned[begin : begin + rows, n * EXTRA + HALO * m + e : n * EXTRA + HALO * m + e + 1]
                        for m in range(2 * STENCILS)
                    ]
                    fill_rows(at, cut, rows, high, low)
                    at += rows


def finish_edges(halos, tables, edges, rows, count_r, columns, after):
    points = jax.ShapeDtypeStruct((2 * HALO * (rows + count_r), columns), BF16)
    width = edges[0].shape[1]
    return pl.pallas_call(
        functools.partial(edge_kernel, rows=rows, count_r=count_r),
        in_specs=[*[VMEM] * 9, ANY],
        out_specs=[VMEM] * 7,
        out_shape=[
            points, points,
            *[jax.ShapeDtypeStruct((HALO * length, width), F32) for length in (rows, rows, count_r, count_r)],
            jax.ShapeDtypeStruct((2 * HALO, rows, width), F32),
        ],
        scratch_shapes=[pltpu.VMEM((LANES, LANES), F32)],
        compiler_params=pltpu.CompilerParams(vmem_limit_bytes=16 * MIB),
        cost_estimate=pl.CostEstimate(flops=2_000_000, bytes_accessed=3 * MIB, transcendentals=0),
        name="finish_edges",
    )(*halos, tables, *edges, after)


def split_table(pieces, band, table, at):
    half = pieces.shape[1] // 2
    for k in range(pieces.shape[0]):
        upper, lower = halves(pieces[k, band * half : (band + 1) * half])
        table[at, k * half : (k + 1) * half] = upper
        table[at + 1, k * half : (k + 1) * half] = lower


def own_source_kernel(
    one, added, stencil_high, stencil_low, edge_high, edge_low, own, sum_one, edge_source, table
):
    count_r, rows, width = one.shape
    columns = table.shape[1]
    size = LAST * rows

    @pl.when(in_product())
    def _():
        split_table(own, 0, table, 0)

        def body(n, carry):
            cut = pl.ds(pl.multiple_of(n * size, size), size)
            part = pl.ds(n * LAST, LAST)
            weights = (stencil_high[cut], stencil_low[cut])
            sum_one[part] = one[part] + product(weights, table[0], table[1]).reshape(LAST, rows, width)
            return carry

        lax.fori_loop(0, count_r // LAST, body, 0)
        edge_source[...] = product((edge_high[:, 0:columns], edge_low[:, 0:columns]), table[0], table[1])

    @pl.when(jnp.logical_not(in_product()))
    def _():
        sum_one[...] = one[...]

    for k in range(HALO):
        sum_one[k] += added[k]
        sum_one[count_r - HALO + k] += added[HALO + k]


def own_source(one, added, matrices, own):
    width = one.shape[2]
    return pl.pallas_call(
        own_source_kernel,
        in_specs=[VMEM] * 7,
        out_specs=[VMEM] * 2,
        out_shape=[
            jax.ShapeDtypeStruct(one.shape, F32),
            jax.ShapeDtypeStruct((matrices[2].shape[0], width), F32),
        ],
        scratch_shapes=[pltpu.VMEM((2, own.shape[0] * own.shape[1] // 2, width), BF16)],
        compiler_params=pltpu.CompilerParams(vmem_limit_bytes=16 * MIB),
        cost_estimate=pl.CostEstimate(flops=100_000_000_000, bytes_accessed=200 * MIB, transcendentals=0),
        name="own_source",
    )(one, added, *matrices, own)


def last_kernel(
    one, edge_source, packet, potential, tables, up, down, left, right, high, low,
    own_high, own_low, stencil_high, stencil_low, edge_high, edge_low, own, other,
    earlier, latest, field, done, sides, table, ends, sems,
):
    count_r, rows, width = packet.shape
    steps = count_r // LAST
    size = LAST * rows
    columns = table.shape[1]
    is_product = in_product()

    def part(n):
        return pl.ds(n * LAST, LAST)

    def cut(n):
        return pl.ds(pl.multiple_of(n * size, size), size)

    def earliers(n):
        return pltpu.make_async_copy(field.at[pl.ds(HALO + n * LAST, LAST)], earlier.at[part(n)], sems.at[0, n])

    def latests(n):
        return pltpu.make_async_copy(done.at[part(n)], latest.at[part(n)], sems.at[1, n])

    def put_ends(up_value, down_value):
        for k in range(HALO):
            field[k] = up_value[k * rows : (k + 1) * rows]
            field[HALO + count_r + k] = down_value[k * rows : (k + 1) * rows]

    def put(k, lanes, value):
        done[k, :, lanes] = value

    @pl.when(is_product)
    def _():
        split_table(other, 0, table, 0)
        split_table(own, 1, table, 2)
        split_table(other, 1, table, 4)
        ends[...] = edge_source[...] + product(
            (edge_high[:, columns : 2 * columns], edge_low[:, columns : 2 * columns]), table[0], table[1]
        )
        edges = HALO * rows
        long = HALO * count_r
        put_ends(up[...] + ends[:edges], down[...] + ends[edges : 2 * edges])
        put_sides(
            sides, left, right, count_r, ends.at[pl.ds(2 * edges, long)], ends.at[pl.ds(2 * edges + long, long)]
        )

        def weights(n):
            return stencil_high[cut(n)], stencil_low[cut(n)]

        def add(n, carry):
            more = product(weights(n), table[0], table[1]).reshape(LAST, rows, width)
            field[pl.ds(HALO + n * LAST, LAST)] = one[part(n)] + more
            earliers(n).start()
            return carry

        lax.fori_loop(0, steps, add, 0)

        def body(n, carry):
            mine, theirs = (own_high[cut(n)], own_low[cut(n)]), weights(n)

            def more(lanes):
                return product(mine, table[2, :, lanes], table[3, :, lanes]) + product(
                    theirs, table[4, :, lanes], table[5, :, lanes]
                )

            advance(n, LAST, field, sides, packet, potential, tables, high, low, put, more)
            latests(n).start()
            return carry

        lax.fori_loop(0, steps, body, 0)

    @pl.when(jnp.logical_not(is_product))
    def _():
        put_ends(up, down)
        put_sides(sides, left, right, count_r)
        for n in range(steps):
            field[pl.ds(HALO + n * LAST, LAST)] = one[part(n)]
            earliers(n).start()

        def body(n, carry):
            advance(n, LAST, field, sides, packet, potential, tables, high, low, put)
            latests(n).start()
            return carry

        lax.fori_loop(0, steps, body, 0)

    for n in range(steps):
        earliers(n).wait()
        latests(n).wait()


def last_iteration(own_sums, packet, potential, tables, halos, high, low, matrices, pieces):
    count_r, rows, width = packet.shape
    steps = count_r // LAST
    return pl.pallas_call(
        last_kernel,
        in_specs=[VMEM] * 19,
        out_specs=[HBM, HBM],
        out_shape=[jax.ShapeDtypeStruct(packet.shape, F32)] * 2,
        scratch_shapes=[
            pltpu.VMEM((count_r + 2 * HALO, rows, width), F32),
            pltpu.VMEM(packet.shape, F32),
            pltpu.VMEM((count_r, 8, width), F32),
            pltpu.VMEM((6, pieces[0].shape[0] * pieces[0].shape[1] // 2, width), BF16),
            pltpu.VMEM((2 * HALO * (rows + count_r), width), F32),
            pltpu.SemaphoreType.DMA((2, steps)),
        ],
        compiler_params=pltpu.CompilerParams(vmem_limit_bytes=20 * MIB),
        cost_estimate=pl.CostEstimate(flops=14_000_000_000, bytes_accessed=36 * MIB, transcendentals=0),
        name="last_iteration",
    )(*own_sums, packet, potential, tables, *halos, high, low, *matrices, *pieces)


def neighbours(axis, upward, downward):
    count = lax.axis_size(axis)
    return (
        lax.ppermute(upward, axis, [(i, i + 1) for i in range(count - 1)]),
        lax.ppermute(downward, axis, [(i + 1, i) for i in range(count - 1)]),
    )


def local(packet, previous, potential, rotation, angular, damping, absorber, stencil_index, stencil_weight):
    packet, previous, potential = packet[0], previous[0], potential[0]
    rotation, angular, damping, absorber = rotation[0], angular[0], damping[0], absorber[0]
    count_r, rows, width = packet.shape
    count_rr, count_row = (lax.axis_size(name) for name in ("rr", "row"))
    chips = count_row // CORES
    rotation, damping, absorber = (jnp.swapaxes(value, 0, 1) for value in (rotation, damping, absorber))
    stencil_index, stencil_weight = (jnp.swapaxes(value, 1, 2) for value in (stencil_index, stencil_weight))
    near_packet, near_previous, near_potential = packet, previous, potential
    packet, previous, potential, rotation, damping, absorber, stencil_index, stencil_weight = (
        in_hbm(value)
        for value in (
            packet, previous, potential, rotation, damping, absorber, stencil_index, stencil_weight
        )
    )

    upper, lower, first, last, tables = prepare(
        packet, previous, potential, rotation, damping, absorber, stencil_index, stencil_weight
    )
    columns = count_row * rows * BAND
    left, right = neighbours("row", last, first)
    *matrix, high, low = matrices_of(tables, angular, count_r, columns, first)
    left, right, matrix = lax.optimization_barrier((left, right, matrix))
    table = bands(packet, previous, potential, tables, left, right, high, low)

    half = count_rr // PLANES
    start = count_rr - 1
    plane = ("sect", "rr")
    low_side, high_side = start - half + 1, start - 1
    relays = [count_rr + half - 1, count_rr + start, high_side, low_side]
    crossed = [lax.ppermute(table, plane, [(start, relay)]) for relay in relays]
    one, *edges = first_iteration(
        packet, near_previous, near_potential, tables, upper, lower, left, right, high, low, table
    )
    *crossed, one, edges = lax.optimization_barrier((*crossed, one, edges))
    piece = sum(crossed)
    near = [(low_side, count_rr), (high_side, count_rr + half - 2)]
    near += [(count_rr + half - 1, count_rr + half - 3), (count_rr + start, count_rr + start - 2)]
    opposite = [(low_side, count_rr + low_side), (high_side, count_rr + high_side)]
    arrived = [lax.ppermute(piece, plane, opposite), lax.ppermute(piece, plane, near)]
    top, bottom, first, last = edges
    top, bottom, piece = lax.optimization_barrier((top, bottom, piece))
    up, down = neighbours("rr", bottom, top)
    spread = piece + sum(arrived)
    line = ("sect", "row")

    def around(shift):
        pairs = []
        for chip in range(chips):
            for core in range(CORES):
                pairs.append(
                    (count_row + chip * CORES + core, count_row + ((chip + shift) % chips) * CORES + core)
                )
        return lax.ppermute(spread, line, pairs)

    rest = [around(1), around(3), around(2)]
    edge_matrix_and_ends = finish_edges(
        (up, down, left, right), tables, (top, bottom, first, last), rows, count_r, columns, spread
    )
    *edge_matrix, up, down, first, last, added = edge_matrix_and_ends
    rest[2], edge_matrix, first, last = lax.optimization_barrier((rest[2], edge_matrix, first, last))
    left, right = neighbours("row", last, first)
    own = jnp.stack([spread, rest[0], rest[2], rest[1]], axis=0)
    other = lax.ppermute(
        own, line, [(count_row + i, count_row + i + 1 - 2 * (i % CORES)) for i in range(count_row)]
    )
    left, right, added = lax.optimization_barrier((left, right, added))
    own_sums = own_source(one, added, (*matrix[:2], *edge_matrix), own)
    other, own_sums = lax.optimization_barrier((other, own_sums))
    earlier, latest = last_iteration(
        own_sums, near_packet, near_potential, tables, (up, down, left, right), high, low, (*matrix, *edge_matrix), (own, other)
    )
    return latest[None], earlier[None]


def solution(mesh):
    in_specs = (
        P("sect", "rr", "row", None),
        P("sect", "rr", "row", None),
        P("sect", "rr", "row", None),
        P("sect", "rr", "row"),
        P("sect", None, None),
        P("sect", "rr", "row"),
        P("sect", "rr", "row"),
        P(None, "rr", "row"),
        P(None, "rr", "row"),
    )
    out_specs = (P("sect", "rr", "row", None), P("sect", "rr", "row", None))
    return jax.shard_map(local, mesh=mesh, in_specs=in_specs, out_specs=out_specs, check_vma=False)
```

```python
import functools

import jax
import jax.numpy as jnp
from jax import lax
from jax.experimental import pallas as pl
from jax.experimental.pallas import tpu as pltpu
from jax.sharding import PartitionSpec as P

BAND = 2
STENCILS = 4
HALO = 2
LANES = 128
CHUNK = 16
LAST = 16
CORES = 2
PLANES = 2
ROT, RET, INDEX, WEIGHT, TABLES = 0, 1, 2, 6, 10
EXTRA = 2 * STENCILS * HALO
OFBAND = 32
MIB = 1 << 20
F32 = jnp.float32
BF16 = jnp.bfloat16
ANY = pl.BlockSpec(memory_space=pl.ANY)
HBM = pl.BlockSpec(memory_space=pltpu.HBM)
VMEM = pl.BlockSpec(memory_space=pltpu.VMEM)

SIDE1 = -16.0 / 96.0
SIDE2 = 1.0 / 96.0
MIDDLE = 2.0 * 30.0 / 96.0 - 7.5 / 4.0


def halves(value):
    high = value.astype(BF16)
    low = (value - high.astype(F32)).astype(BF16)
    return high, low


def product(left, right_high, right_low):
    high, low = left
    total = jnp.dot(high, right_high, preferred_element_type=F32)
    total += jnp.dot(low, right_high, preferred_element_type=F32)
    return total + jnp.dot(high, right_low, preferred_element_type=F32)


def doubled_hamilton(field, index, start, count, lanes, turned, potential, rotation):
    def at(shift_r, shift_v):
        return field[index + shift_r, pl.ds(start + shift_v, count), lanes]

    middle = at(0, 0)
    near = at(-1, 0) + at(1, 0) + (at(0, -1) + at(0, 1))
    far = at(-2, 0) + at(2, 0) + (at(0, -2) + at(0, 2))
    return (
        SIDE1 * near
        + SIDE2 * far
        + (0.25 * potential + MIDDLE) * middle
        + (0.25 * rotation) * turned
    )


def in_hbm(value):
    return pltpu.with_memory_space_constraint(value, pltpu.HBM)


def holds_bands():
    return (lax.axis_index("sect") == 0) & (lax.axis_index("rr") == lax.axis_size("rr") - 1)


def in_product():
    return lax.axis_index("sect") == 1


def retained_of(damping, absorber):
    return 1.0 - absorber.astype(F32) * (1.0 - damping)


def band_kernel(
    packet, previous, potential, tables, left, right, high, low, out, field, later, turned, held, sems
):
    count_r, rows, width = packet.shape
    base = 16
    wide = rows + 16
    begin = left.shape[0] - OFBAND

    @pl.when(holds_bands())
    def _():
        copies = [
            pltpu.make_async_copy(packet.at[pl.ds(count_r - 6, 6)], field.at[pl.ds(2, 6), pl.ds(base, rows)], sems.at[0]),
            pltpu.make_async_copy(previous.at[pl.ds(count_r - 4, 4)], held.at[0], sems.at[1]),
            pltpu.make_async_copy(potential.at[pl.ds(count_r - 4, 4)], held.at[1], sems.at[2]),
        ]
        later[...] = jnp.zeros_like(later)
        field[0:2] = jnp.zeros_like(field[0:2])
        field[8:10] = jnp.zeros_like(field[8:10])
        for k in range(2, 8):
            field[k, 0:base] = jnp.zeros((base, width), F32)
            field[k, base + rows :] = jnp.zeros((base, width), F32)
        for copy in copies:
            copy.start()
        for k in range(4):
            at = begin + 4 * k
            field[4 + k, base - 4 : base] = left[at : at + 4]
            field[4 + k, base + rows : base + rows + 4] = right[at : at + 4]
        columns = [
            (tables[ROT, :, count_r - 4 + k : count_r - 3 + k], tables[RET, :, count_r - 4 + k : count_r - 3 + k])
            for k in range(4)
        ]
        columns = [tuple(jnp.broadcast_to(c, (rows, LANES)) for c in pair) for pair in columns]
        for copy in copies:
            copy.wait()
        window = field[4:8, base - 8 : base + rows + 8].reshape(4 * wide, width)
        turned[...] = product(halves(window), high[...], low[...])
        for k in range(4):
            rotation, retained = columns[k]
            for at in range(0, width, LANES):
                lanes = slice(at, at + LANES)
                update = doubled_hamilton(
                    field, 4 + k, base, rows, lanes,
                    turned[k * wide + 8 : k * wide + 8 + rows, lanes], held[1, k, :, lanes], rotation,
                ) - retained * held[0, k, :, lanes]
                later[k, base : base + rows, lanes] = retained * update
                if k >= 2:
                    out[(k - 2) * rows : (k - 1) * rows, lanes] = (1.0 - retained) * update
        for k in range(2, 4):
            for slab, place, inside in ((left, base - 8, 6), (right, base + rows, 0)):
                at = begin + 16 + 2 * (k - 2)
                prev, pot, rot, ret = (slab[at + 4 * n : at + 4 * n + 2] for n in range(4))
                update = doubled_hamilton(
                    field, 4 + k, place + inside, 2, slice(None),
                    turned[k * wide + place - base + 8 + inside : k * wide + place - base + 10 + inside], pot, rot,
                ) - ret * prev
                later[k, place + inside : place + inside + 2] = ret * update
        window = later[2:4, base : base + rows].reshape(2 * rows, width)
        turned[0 : 2 * rows] = product(halves(window), high[...], low[...])
        for k in range(2, 4):
            rotation, retained = columns[k]
            for at in range(0, width, LANES):
                lanes = slice(at, at + LANES)
                update = doubled_hamilton(
                    later, k, base, rows, lanes,
                    turned[(k - 2) * rows : (k - 1) * rows, lanes], held[1, k, :, lanes], rotation,
                ) - retained * field[4 + k, base : base + rows, lanes]
                out[k * rows : (k + 1) * rows, lanes] = (1.0 - retained) * update


def bands(packet, previous, potential, tables, left, right, high, low):
    _, rows, width = packet.shape
    return pl.pallas_call(
        band_kernel,
        in_specs=[HBM, HBM, HBM, VMEM, VMEM, VMEM, VMEM, VMEM],
        out_specs=VMEM,
        out_shape=jax.ShapeDtypeStruct((2 * BAND * rows, width), F32),
        scratch_shapes=[
            pltpu.VMEM((10, rows + 32, width), F32),
            pltpu.VMEM((6, rows + 32, width), F32),
            pltpu.VMEM((4 * (rows + 16), width), F32),
            pltpu.VMEM((2, 4, rows, width), F32),
            pltpu.SemaphoreType.DMA((3,)),
        ],
        compiler_params=pltpu.CompilerParams(vmem_limit_bytes=16 * MIB),
        cost_estimate=pl.CostEstimate(flops=400_000_000, bytes_accessed=4 * MIB, transcendentals=0),
        name="both_bands",
    )(packet, previous, potential, tables, left, right, high, low)


def prepare_kernel(
    packet, previous, potential, rotation, damping, absorber, index, weight,
    upper, lower, first, last, tables,
    sides, others, factors, masks, indices, weights, sems,
):
    count_r, rows, width = packet.shape
    small = [
        pltpu.make_async_copy(rotation, factors.at[0], sems.at[0]),
        pltpu.make_async_copy(damping, factors.at[1], sems.at[1]),
        pltpu.make_async_copy(absorber, masks, sems.at[2]),
        pltpu.make_async_copy(index, indices, sems.at[3]),
        pltpu.make_async_copy(weight, weights, sems.at[4]),
    ]
    copies = [
        pltpu.make_async_copy(packet.at[:, pl.ds(0, 8)], sides.at[0], sems.at[5]),
        pltpu.make_async_copy(packet.at[:, pl.ds(rows - 8, 8)], sides.at[1], sems.at[6]),
        pltpu.make_async_copy(previous.at[pl.ds(count_r - BAND, BAND)], others.at[0], sems.at[7]),
        pltpu.make_async_copy(potential.at[pl.ds(count_r - BAND, BAND)], others.at[1], sems.at[8]),
    ]
    for copy in small + copies:
        copy.start()
    for copy in small:
        copy.wait()
    values = [factors[0], retained_of(factors[1], masks[...])]
    values += [indices[n].astype(F32) for n in range(STENCILS)]
    values += [weights[n] for n in range(STENCILS)]
    for n, value in enumerate(values):
        tables[n] = jnp.concatenate([value, jnp.zeros((rows, LANES - count_r), F32)], axis=1)
    columns = HALO * count_r
    lane = lax.broadcasted_iota(jnp.int32, (rows, LANES), 1)
    at_top = jnp.zeros((rows, LANES), F32)
    at_bottom = jnp.zeros((rows, LANES), F32)
    for n, table in enumerate([*range(INDEX, TABLES), RET]):
        value = tables[table]
        at = n * HALO
        here = (lane >= at) & (lane < at + HALO)
        at_top = jnp.where(here, pltpu.roll(value, at, 1), at_top)
        at_bottom = jnp.where(here, pltpu.roll(value, (at + LANES - (count_r - HALO)) % LANES, 1), at_bottom)
        if table != RET:
            first[columns + at : columns + at + HALO, 0:LANES] = value[0:HALO]
            last[columns + at : columns + at + HALO, 0:LANES] = value[rows - HALO : rows]
    upper[...] = at_top
    lower[...] = at_bottom
    begin = columns + EXTRA
    for copy in copies:
        copy.wait()
    for out, n, far, near in ((first, 0, 0, 0), (last, 1, 4, rows - 2)):
        for k in range(4):
            out[begin + 4 * k : begin + 4 * k + 4] = sides[n, count_r - 4 + k, far : far + 4]
        for k in range(BAND):
            at = begin + 16 + 2 * k
            column = count_r - BAND + k
            out[at : at + 2] = others[0, k, near : near + 2]
            out[at + 4 : at + 6] = others[1, k, near : near + 2]
            for m in (ROT, RET):
                value = tables[m, near : near + 2, column : column + 1]
                out[at + 8 + 4 * m : at + 10 + 4 * m] = jnp.broadcast_to(value, (2, width))
    for out, n, near in ((first, 0, 0), (last, 1, 8 - HALO)):
        for k in range(count_r):
            for r in range(HALO):
                out[r * count_r + k : r * count_r + k + 1] = sides[n, k, near + r : near + r + 1]


def prepare(packet, previous, potential, rotation, damping, absorber, index, weight):
    count_r, rows, width = packet.shape
    ends = jax.ShapeDtypeStruct((rows, LANES), F32)
    sides = jax.ShapeDtypeStruct((HALO * count_r + EXTRA + OFBAND, width), F32)
    return pl.pallas_call(
        prepare_kernel,
        in_specs=[HBM] * 8,
        out_specs=[VMEM] * 5,
        out_shape=[ends, ends, sides, sides, jax.ShapeDtypeStruct((TABLES, rows, LANES), F32)],
        scratch_shapes=[
            pltpu.VMEM((2, count_r, 8, width), F32),
            pltpu.VMEM((2, BAND, rows, width), F32),
            pltpu.VMEM((2, rows, count_r), F32),
            pltpu.VMEM((rows, count_r), jnp.int32),
            pltpu.VMEM((STENCILS, rows, count_r), jnp.int32),
            pltpu.VMEM((STENCILS, rows, count_r), F32),
            pltpu.SemaphoreType.DMA((9,)),
        ],
        compiler_params=pltpu.CompilerParams(vmem_limit_bytes=16 * MIB),
        cost_estimate=pl.CostEstimate(flops=1_000_000, bytes_accessed=6 * MIB, transcendentals=0),
        name="prepare",
    )(packet, previous, potential, rotation, damping, absorber, index, weight)


def put_sides(sides, left, right, count_r, left_more=None, right_more=None):
    def body(k, carry):
        for r in range(HALO):
            at = pl.ds(r * count_r + k, 1)
            before, behind = left[at], right[at]
            if left_more is not None:
                before, behind = before + left_more[at], behind + right_more[at]
            sides[k, r : r + 1] = behind
            sides[k, 8 - HALO + r : 8 - HALO + r + 1] = before
        return carry

    lax.fori_loop(0, count_r, body, 0, unroll=8)


def advance(step, chunk, field, sides, previous, potential, tables, high, low, put, more=None):
    rows = previous.shape[1]
    width = previous.shape[2]
    here = step * chunk
    shift = lax.rem(LANES - here, LANES)
    columns = [pltpu.roll(tables[n], shift, 1) for n in (ROT, RET)]
    window = field[pl.ds(HALO + here, chunk)].reshape(chunk * rows, width)
    split = halves(window)
    wide = 2 * LANES
    for tile in range(0, width, wide):
        turned = product(split, high[:, tile : tile + wide], low[:, tile : tile + wide])
        source = None if more is None else more(slice(tile, tile + wide))
        for k in range(chunk):
            rotation = jnp.broadcast_to(0.25 * columns[0][:, k : k + 1], (rows, LANES))
            retained = jnp.broadcast_to(columns[1][:, k : k + 1], (rows, LANES))
            for at in range(tile, tile + wide, LANES):
                lanes = slice(at, at + LANES)

                def row(shift):
                    return field[HALO + here + k + shift, :, lanes]

                middle = row(0)
                ring = jnp.concatenate([middle, sides[here + k, :, lanes]], axis=0)
                around = [pltpu.roll(ring, s, 0)[:rows] for s in (1, rows + 7, 2, rows + 6)]
                near = row(-1) + row(1) + (around[0] + around[1])
                far = row(-2) + row(2) + (around[2] + around[3])
                update = (
                    SIDE1 * near
                    + SIDE2 * far
                    + (0.25 * potential[here + k, :, lanes] + MIDDLE) * middle
                    + rotation * turned[k * rows : (k + 1) * rows, at - tile : at - tile + LANES]
                    - retained * previous[here + k, :, lanes]
                )
                value = retained * update
                if source is not None:
                    value += source[k * rows : (k + 1) * rows, at - tile : at - tile + LANES]
                put(here + k, lanes, value)


def first_kernel(
    packet, previous, potential, tables, upper, lower, left, right, high, low, after,
    done, top, bottom, first, last, field, sides, sems,
):
    count_r, rows, width = packet.shape
    steps = count_r // CHUNK

    def copies(n):
        part = pl.ds(n * CHUNK, CHUNK)
        return pltpu.make_async_copy(packet.at[part], field.at[pl.ds(HALO + n * CHUNK, CHUNK)], sems.at[n])

    for n in range(steps):
        copies(n).start()
    field[0:HALO] = jnp.zeros((HALO, rows, width), F32)
    field[HALO + count_r :] = jnp.zeros((HALO, rows, width), F32)
    put_sides(sides, left, right, count_r)
    copies(0).wait()

    def put(k, lanes, value):
        done[k, :, lanes] = value

    def body(n, carry):
        @pl.when(n + 1 < steps)
        def _():
            copies(n + 1).wait()

        advance(n, CHUNK, field, sides, previous, potential, tables, high, low, put)
        for k in range(CHUNK):
            for r in range(HALO):
                at = pl.ds(r * count_r + n * CHUNK + k, 1)
                first[at] = done[n * CHUNK + k, r : r + 1]
                last[at] = done[n * CHUNK + k, rows - HALO + r : rows - HALO + r + 1]
        return carry

    lax.fori_loop(0, steps, body, 0)
    edges = HALO * rows
    for k in range(HALO):
        here = slice(k * rows, (k + 1) * rows)
        beside = slice(edges + k * rows, edges + (k + 1) * rows)
        top[here] = done[k]
        bottom[here] = done[count_r - HALO + k]
        top[beside] = field[HALO + k]
        bottom[beside] = field[count_r + k]
    top[2 * edges : 2 * edges + rows, 0:LANES] = upper[...]
    bottom[2 * edges : 2 * edges + rows, 0:LANES] = lower[...]


def first_iteration(packet, previous, potential, tables, upper, lower, left, right, high, low, after):
    count_r, rows, width = packet.shape
    ends = jax.ShapeDtypeStruct((2 * HALO * rows + rows, width), F32)
    sides = jax.ShapeDtypeStruct((HALO * count_r, width), F32)
    return pl.pallas_call(
        first_kernel,
        in_specs=[HBM, *[VMEM] * 9, ANY],
        out_specs=[VMEM] * 5,
        out_shape=[jax.ShapeDtypeStruct(packet.shape, F32), ends, ends, sides, sides],
        scratch_shapes=[
            pltpu.VMEM((count_r + 2 * HALO, rows, width), F32),
            pltpu.VMEM((count_r, 8, width), F32),
            pltpu.SemaphoreType.DMA((count_r // CHUNK,)),
        ],
        compiler_params=pltpu.CompilerParams(vmem_limit_bytes=14 * MIB),
        cost_estimate=pl.CostEstimate(flops=7_000_000_000, bytes_accessed=20 * MIB, transcendentals=0),
        name="first_iteration",
    )(packet, previous, potential, tables, upper, lower, left, right, high, low, after)


def slot_of(value, rows, width):
    per = rows * BAND
    shift_owner = per.bit_length() - 1
    chips = width // per // CORES
    row = lax.axis_index("row")
    index = value.astype(jnp.int32)
    owner = index >> shift_owner
    inside = index & (per - 1)
    core = (owner & 1) ^ (row & 1)
    chip = ((row >> 1) - (owner >> 1)) & (chips - 1)
    slot = ((core * chips + chip) << shift_owner) + (inside & 1) * rows + (inside >> 1)
    return slot.astype(F32)


def fill_rows(at, cut, rows, high, low, begin=0):
    column = lax.broadcasted_iota(jnp.int32, (rows, LANES), 1).astype(F32)
    cut = [jnp.broadcast_to(value, (rows, LANES)) for value in cut]
    for tile in range(0, high.shape[1], LANES):
        here = column + float(begin + tile)
        total = jnp.where(here == cut[0], cut[STENCILS], 0.0)
        for n in range(1, STENCILS):
            total += jnp.where(here == cut[n], cut[STENCILS + n], 0.0)
        upper, lower = halves(total)
        high[pl.ds(at, rows), tile : tile + LANES] = upper
        low[pl.ds(at, rows), tile : tile + LANES] = lower


def stencil_kernel(tables, angular, after, high, low, other_high, other_low, angular_high, angular_low):
    _, rows, _ = tables.shape
    count_r = high.shape[0] // rows
    group = 8
    half = high.shape[1]
    angular_high[...], angular_low[...] = halves(angular[...])

    @pl.when(in_product())
    def _():
        values = [slot_of(tables[INDEX + n], rows, CORES * half) for n in range(STENCILS)]
        values += [tables[WEIGHT + n] for n in range(STENCILS)]

        def body(step, carry):
            shift = lax.rem(LANES - step * group, LANES)
            moved = [pltpu.roll(value, shift, 1) for value in values]
            for k in range(group):
                at = pl.multiple_of((step * group + k) * rows, rows)
                cut = [jnp.broadcast_to(value[:, k : k + 1], (rows, LANES)) for value in moved]
                fill_rows(at, cut, rows, high, low)
                fill_rows(at, cut, rows, other_high, other_low, half)
            return carry

        lax.fori_loop(0, count_r // group, body, 0)


def matrices_of(tables, angular, count_r, columns, after):
    rows = tables.shape[1]
    points = jax.ShapeDtypeStruct((count_r * rows, columns // CORES), BF16)
    return pl.pallas_call(
        stencil_kernel,
        in_specs=[VMEM, VMEM, ANY],
        out_specs=[VMEM] * 6,
        out_shape=[points] * 4 + [jax.ShapeDtypeStruct(angular.shape, BF16)] * 2,
        compiler_params=pltpu.CompilerParams(vmem_limit_bytes=16 * MIB),
        cost_estimate=pl.CostEstimate(flops=15_000_000, bytes_accessed=6 * MIB, transcendentals=0),
        name="stencil_matrix",
    )(tables, angular, after)


def edge_kernel(
    up, down, left, right, tables, top, bottom, first, last, after,
    high, low, whole_up, whole_down, new_first, new_last, added, square, *, rows, count_r,
):
    width = up.shape[1]
    edges = HALO * rows

    def retained(k):
        return jnp.broadcast_to(tables[RET, :, k : k + 1], (rows, width))

    def there(side, k):
        at = 2 * STENCILS * HALO + k
        return jnp.broadcast_to(side[2 * edges : 2 * edges + rows, at : at + 1], (rows, width))

    def packet_row(slab, k):
        return slab[edges + k * rows : edges + (k + 1) * rows]

    added[0] = retained(0) * (SIDE1 * packet_row(up, 1) + SIDE2 * packet_row(up, 0))
    added[1] = retained(1) * (SIDE2 * packet_row(up, 1))
    added[2] = retained(count_r - 2) * (SIDE2 * packet_row(down, 0))
    added[3] = retained(count_r - 1) * (SIDE1 * packet_row(down, 0) + SIDE2 * packet_row(down, 1))
    whole_up[0:rows] = up[0:rows] + there(up, 0) * (SIDE2 * packet_row(top, 0))
    whole_up[rows:edges] = up[rows:edges] + there(up, 1) * (SIDE1 * packet_row(top, 0) + SIDE2 * packet_row(top, 1))
    whole_down[0:rows] = down[0:rows] + there(down, 0) * (SIDE1 * packet_row(bottom, 1) + SIDE2 * packet_row(bottom, 0))
    whole_down[rows:edges] = down[rows:edges] + there(down, 1) * (SIDE2 * packet_row(bottom, 1))
    new_first[...] = first[...]
    new_last[...] = last[...]
    for k in range(HALO):
        for n, r_row in ((k, k), (HALO + k, count_r - HALO + k)):
            for r in range(HALO):
                at = r * count_r + r_row
                new_first[at : at + 1] = first[at : at + 1] + added[n, r : r + 1]
                new_last[at : at + 1] = last[at : at + 1] + added[n, rows - HALO + r : rows - HALO + r + 1]

    @pl.when(in_product())
    def _():
        at = 0
        for side in (up, down):
            value = side[2 * edges : 2 * edges + rows, 0:LANES]
            slots = slot_of(value, rows, high.shape[1])
            for e in range(HALO):
                cut = [
                    (slots if m < STENCILS else value)[:, HALO * m + e : HALO * m + e + 1]
                    for m in range(2 * STENCILS)
                ]
                fill_rows(at, cut, rows, high, low)
                at += rows
        square[...] = jnp.zeros_like(square)
        part = EXTRA // 2
        for n, side in enumerate((left, right)):
            begin = HALO * count_r
            square[n * EXTRA : n * EXTRA + part] = slot_of(side[begin : begin + part, 0:LANES], rows, high.shape[1])
            square[n * EXTRA + part : (n + 1) * EXTRA] = side[begin + part : begin + EXTRA, 0:LANES]
        turned = square[...].T
        for n in range(2):
            for e in range(HALO):
                for begin in range(0, count_r, rows):
                    cut = [
                        turned[begin : begin + rows, n * EXTRA + HALO * m + e : n * EXTRA + HALO * m + e + 1]
                        for m in range(2 * STENCILS)
                    ]
                    fill_rows(at, cut, rows, high, low)
                    at += rows


def finish_edges(halos, tables, edges, rows, count_r, columns, after):
    points = jax.ShapeDtypeStruct((2 * HALO * (rows + count_r), columns), BF16)
    width = edges[0].shape[1]
    return pl.pallas_call(
        functools.partial(edge_kernel, rows=rows, count_r=count_r),
        in_specs=[*[VMEM] * 9, ANY],
        out_specs=[VMEM] * 7,
        out_shape=[
            points, points,
            *[jax.ShapeDtypeStruct((HALO * length, width), F32) for length in (rows, rows, count_r, count_r)],
            jax.ShapeDtypeStruct((2 * HALO, rows, width), F32),
        ],
        scratch_shapes=[pltpu.VMEM((LANES, LANES), F32)],
        compiler_params=pltpu.CompilerParams(vmem_limit_bytes=16 * MIB),
        cost_estimate=pl.CostEstimate(flops=2_000_000, bytes_accessed=3 * MIB, transcendentals=0),
        name="finish_edges",
    )(*halos, tables, *edges, after)


def split_table(pieces, band, table, at):
    half = pieces.shape[1] // 2
    for k in range(pieces.shape[0]):
        upper, lower = halves(pieces[k, band * half : (band + 1) * half])
        table[at, k * half : (k + 1) * half] = upper
        table[at + 1, k * half : (k + 1) * half] = lower


def own_source_kernel(
    one, added, stencil_high, stencil_low, edge_high, edge_low, own, after, sum_one, edge_source, table, *, begin
):
    count_r, rows, width = one.shape
    count = sum_one.shape[0]
    columns = table.shape[1]
    size = LAST * rows

    @pl.when(in_product())
    def _():
        split_table(own, 0, table, 0)

        def body(n, carry):
            cut = pl.ds(pl.multiple_of(begin * rows + n * size, size), size)
            weights = (stencil_high[cut], stencil_low[cut])
            more = product(weights, table[0], table[1]).reshape(LAST, rows, width)
            sum_one[pl.ds(n * LAST, LAST)] = one[pl.ds(begin + n * LAST, LAST)] + more
            return carry

        lax.fori_loop(0, count // LAST, body, 0)
        if begin == 0:
            edge_source[...] = product((edge_high[:, 0:columns], edge_low[:, 0:columns]), table[0], table[1])

    @pl.when(jnp.logical_not(in_product()))
    def _():
        sum_one[...] = one[begin : begin + count]

    for k in range(HALO):
        if begin == 0:
            sum_one[k] += added[k]
        if begin + count == count_r:
            sum_one[count - HALO + k] += added[HALO + k]


def own_source(one, added, matrices, own, after, begin, count, flops):
    _, rows, width = one.shape
    edge_rows = matrices[2].shape[0] if begin == 0 else 8
    return pl.pallas_call(
        functools.partial(own_source_kernel, begin=begin),
        in_specs=[*[VMEM] * 7, ANY],
        out_specs=[VMEM] * 2,
        out_shape=[
            jax.ShapeDtypeStruct((count, rows, width), F32),
            jax.ShapeDtypeStruct((edge_rows, width), F32),
        ],
        scratch_shapes=[pltpu.VMEM((2, own.shape[0] * own.shape[1] // 2, width), BF16)],
        compiler_params=pltpu.CompilerParams(vmem_limit_bytes=16 * MIB),
        cost_estimate=pl.CostEstimate(flops=flops, bytes_accessed=flops // 500, transcendentals=0),
        name="own_source",
    )(one, added, *matrices, own, after)


def last_kernel(
    one, one_end, edge_source, packet, potential, tables, up, down, left, right, high, low,
    own_high, own_low, stencil_high, stencil_low, edge_high, edge_low, own, other,
    earlier, latest, field, done, sides, table, ends, sems,
):
    count_r, rows, width = packet.shape
    steps = count_r // LAST
    size = LAST * rows
    columns = table.shape[1]
    is_product = in_product()

    def part(n):
        return pl.ds(n * LAST, LAST)

    def cut(n):
        return pl.ds(pl.multiple_of(n * size, size), size)

    def earliers(n):
        return pltpu.make_async_copy(field.at[pl.ds(HALO + n * LAST, LAST)], earlier.at[part(n)], sems.at[0, n])

    def latests(n):
        return pltpu.make_async_copy(done.at[part(n)], latest.at[part(n)], sems.at[1, n])

    def put_ends(up_value, down_value):
        for k in range(HALO):
            field[k] = up_value[k * rows : (k + 1) * rows]
            field[HALO + count_r + k] = down_value[k * rows : (k + 1) * rows]

    def put(k, lanes, value):
        done[k, :, lanes] = value

    @pl.when(is_product)
    def _():
        split_table(other, 0, table, 0)
        split_table(own, 1, table, 2)
        split_table(other, 1, table, 4)
        ends[...] = edge_source[...] + product(
            (edge_high[:, columns : 2 * columns], edge_low[:, columns : 2 * columns]), table[0], table[1]
        )
        edges = HALO * rows
        long = HALO * count_r
        put_ends(up[...] + ends[:edges], down[...] + ends[edges : 2 * edges])
        put_sides(
            sides, left, right, count_r, ends.at[pl.ds(2 * edges, long)], ends.at[pl.ds(2 * edges + long, long)]
        )

        def weights(n):
            return stencil_high[cut(n)], stencil_low[cut(n)]

        def add(n, carry):
            more = product(weights(n), table[0], table[1]).reshape(LAST, rows, width)
            field[pl.ds(HALO + n * LAST, LAST)] = one[part(n)] + more
            earliers(n).start()
            return carry

        lax.fori_loop(0, steps - 1, add, 0)
        more = product(weights(steps - 1), table[0], table[1]).reshape(LAST, rows, width)
        field[HALO + count_r - LAST : HALO + count_r] = one_end[...] + more
        earliers(steps - 1).start()

        def body(n, carry):
            mine, theirs = (own_high[cut(n)], own_low[cut(n)]), weights(n)

            def more(lanes):
                return product(mine, table[2, :, lanes], table[3, :, lanes]) + product(
                    theirs, table[4, :, lanes], table[5, :, lanes]
                )

            advance(n, LAST, field, sides, packet, potential, tables, high, low, put, more)
            latests(n).start()
            return carry

        lax.fori_loop(0, steps, body, 0)

    @pl.when(jnp.logical_not(is_product))
    def _():
        put_ends(up, down)
        put_sides(sides, left, right, count_r)
        for n in range(steps):
            field[pl.ds(HALO + n * LAST, LAST)] = one[part(n)] if n + 1 < steps else one_end[...]
            earliers(n).start()

        def body(n, carry):
            advance(n, LAST, field, sides, packet, potential, tables, high, low, put)
            latests(n).start()
            return carry

        lax.fori_loop(0, steps, body, 0)

    for n in range(steps):
        earliers(n).wait()
        latests(n).wait()


def last_iteration(own_sums, packet, potential, tables, halos, high, low, matrices, pieces):
    count_r, rows, width = packet.shape
    steps = count_r // LAST
    return pl.pallas_call(
        last_kernel,
        in_specs=[VMEM] * 20,
        out_specs=[HBM, HBM],
        out_shape=[jax.ShapeDtypeStruct(packet.shape, F32)] * 2,
        scratch_shapes=[
            pltpu.VMEM((count_r + 2 * HALO, rows, width), F32),
            pltpu.VMEM(packet.shape, F32),
            pltpu.VMEM((count_r, 8, width), F32),
            pltpu.VMEM((6, pieces[0].shape[0] * pieces[0].shape[1] // 2, width), BF16),
            pltpu.VMEM((2 * HALO * (rows + count_r), width), F32),
            pltpu.SemaphoreType.DMA((2, steps)),
        ],
        compiler_params=pltpu.CompilerParams(vmem_limit_bytes=20 * MIB),
        cost_estimate=pl.CostEstimate(flops=14_000_000_000, bytes_accessed=36 * MIB, transcendentals=0),
        name="last_iteration",
    )(*own_sums, packet, potential, tables, *halos, high, low, *matrices, *pieces)


def neighbours(axis, upward, downward):
    count = lax.axis_size(axis)
    return (
        lax.ppermute(upward, axis, [(i, i + 1) for i in range(count - 1)]),
        lax.ppermute(downward, axis, [(i + 1, i) for i in range(count - 1)]),
    )


def local(packet, previous, potential, rotation, angular, damping, absorber, stencil_index, stencil_weight):
    packet, previous, potential = packet[0], previous[0], potential[0]
    rotation, angular, damping, absorber = rotation[0], angular[0], damping[0], absorber[0]
    count_r, rows, width = packet.shape
    count_rr, count_row = (lax.axis_size(name) for name in ("rr", "row"))
    chips = count_row // CORES
    rotation, damping, absorber = (jnp.swapaxes(value, 0, 1) for value in (rotation, damping, absorber))
    stencil_index, stencil_weight = (jnp.swapaxes(value, 1, 2) for value in (stencil_index, stencil_weight))
    near_packet, near_previous, near_potential = packet, previous, potential
    packet, previous, potential, rotation, damping, absorber, stencil_index, stencil_weight = (
        in_hbm(value)
        for value in (
            packet, previous, potential, rotation, damping, absorber, stencil_index, stencil_weight
        )
    )

    upper, lower, first, last, tables = prepare(
        packet, previous, potential, rotation, damping, absorber, stencil_index, stencil_weight
    )
    columns = count_row * rows * BAND
    left, right = neighbours("row", last, first)
    *matrix, high, low = matrices_of(tables, angular, count_r, columns, first)
    left, right, matrix = lax.optimization_barrier((left, right, matrix))
    table = bands(packet, previous, potential, tables, left, right, high, low)

    half = count_rr // PLANES
    start = count_rr - 1
    plane = ("sect", "rr")
    low_side, high_side = start - half + 1, start - 1
    relays = [count_rr + half - 1, count_rr + start, high_side, low_side]
    crossed = [lax.ppermute(table, plane, [(start, relay)]) for relay in relays]
    one, *edges = first_iteration(
        packet, near_previous, near_potential, tables, upper, lower, left, right, high, low, table
    )
    *crossed, one, edges = lax.optimization_barrier((*crossed, one, edges))
    piece = sum(crossed)
    near = [(low_side, count_rr), (high_side, count_rr + half - 2)]
    near += [(count_rr + half - 1, count_rr + half - 3), (count_rr + start, count_rr + start - 2)]
    opposite = [(low_side, count_rr + low_side), (high_side, count_rr + high_side)]
    arrived = [lax.ppermute(piece, plane, opposite), lax.ppermute(piece, plane, near)]
    top, bottom, first, last = edges
    top, bottom, piece = lax.optimization_barrier((top, bottom, piece))
    up, down = neighbours("rr", bottom, top)
    spread = piece + sum(arrived)
    line = ("sect", "row")

    def around(shift):
        pairs = []
        for chip in range(chips):
            for core in range(CORES):
                pairs.append(
                    (count_row + chip * CORES + core, count_row + ((chip + shift) % chips) * CORES + core)
                )
        return lax.ppermute(spread, line, pairs)

    rest = [around(1), around(3), around(2)]
    edge_matrix_and_ends = finish_edges(
        (up, down, left, right), tables, (top, bottom, first, last), rows, count_r, columns, spread
    )
    *edge_matrix, up, down, first, last, added = edge_matrix_and_ends
    rest[2], edge_matrix, first, last = lax.optimization_barrier((rest[2], edge_matrix, first, last))
    left, right = neighbours("row", last, first)
    own = jnp.stack([spread, rest[0], rest[2], rest[1]], axis=0)
    other = lax.ppermute(
        own, line, [(count_row + i, count_row + i + 1 - 2 * (i % CORES)) for i in range(count_row)]
    )
    own_matrices = (*matrix[:2], *edge_matrix)
    one_begin, edge_source = own_source(one, added, own_matrices, own, own, 0, count_r - LAST, 1_000_000)
    left, right, added, one_begin = lax.optimization_barrier((left, right, added, one_begin))
    one_end, _ = own_source(one, added, own_matrices, own, one_begin, count_r - LAST, LAST, 100_000_000_000)
    own_sums = (one_begin, one_end, edge_source)
    other, own_sums = lax.optimization_barrier((other, own_sums))
    earlier, latest = last_iteration(
        own_sums, near_packet, near_potential, tables, (up, down, left, right), high, low, (*matrix, *edge_matrix), (own, other)
    )
    return latest[None], earlier[None]


def solution(mesh):
    in_specs = (
        P("sect", "rr", "row", None),
        P("sect", "rr", "row", None),
        P("sect", "rr", "row", None),
        P("sect", "rr", "row"),
        P("sect", None, None),
        P("sect", "rr", "row"),
        P("sect", "rr", "row"),
        P(None, "rr", "row"),
        P(None, "rr", "row"),
    )
    out_specs = (P("sect", "rr", "row", None), P("sect", "rr", "row", None))
    return jax.shard_map(local, mesh=mesh, in_specs=in_specs, out_specs=out_specs, check_vma=False)
```

```python
import functools

import jax
import jax.numpy as jnp
from jax import lax
from jax.experimental import pallas as pl
from jax.experimental.pallas import tpu as pltpu
from jax.sharding import PartitionSpec as P

BAND = 2
STENCILS = 4
HALO = 2
LANES = 128
CHUNK = 16
LAST = 16
CORES = 2
PLANES = 2
ROT, RET, INDEX, WEIGHT, TABLES = 0, 1, 2, 6, 10
EXTRA = 2 * STENCILS * HALO
OFBAND = 32
MIB = 1 << 20
F32 = jnp.float32
BF16 = jnp.bfloat16
ANY = pl.BlockSpec(memory_space=pl.ANY)
HBM = pl.BlockSpec(memory_space=pltpu.HBM)
VMEM = pl.BlockSpec(memory_space=pltpu.VMEM)

SIDE1 = -16.0 / 96.0
SIDE2 = 1.0 / 96.0
MIDDLE = 2.0 * 30.0 / 96.0 - 7.5 / 4.0


def halves(value):
    high = value.astype(BF16)
    low = (value - high.astype(F32)).astype(BF16)
    return high, low


def product(left, right_high, right_low):
    high, low = left
    total = jnp.dot(high, right_high, preferred_element_type=F32)
    total += jnp.dot(low, right_high, preferred_element_type=F32)
    return total + jnp.dot(high, right_low, preferred_element_type=F32)


def doubled_hamilton(field, index, start, count, lanes, turned, potential, rotation):
    def at(shift_r, shift_v):
        return field[index + shift_r, pl.ds(start + shift_v, count), lanes]

    middle = at(0, 0)
    near = at(-1, 0) + at(1, 0) + (at(0, -1) + at(0, 1))
    far = at(-2, 0) + at(2, 0) + (at(0, -2) + at(0, 2))
    return (
        SIDE1 * near
        + SIDE2 * far
        + (0.25 * potential + MIDDLE) * middle
        + (0.25 * rotation) * turned
    )


def in_hbm(value):
    return pltpu.with_memory_space_constraint(value, pltpu.HBM)


def holds_bands():
    return (lax.axis_index("sect") == 0) & (lax.axis_index("rr") == lax.axis_size("rr") - 1)


def in_product():
    return lax.axis_index("sect") == 1


def retained_of(damping, absorber):
    return 1.0 - absorber.astype(F32) * (1.0 - damping)


def band_kernel(
    packet, previous, potential, tables, left, right, high, low, out, field, later, turned, held, sems
):
    count_r, rows, width = packet.shape
    base = 16
    wide = rows + 16
    begin = left.shape[0] - OFBAND

    @pl.when(holds_bands())
    def _():
        copies = [
            pltpu.make_async_copy(packet.at[pl.ds(count_r - 6, 6)], field.at[pl.ds(2, 6), pl.ds(base, rows)], sems.at[0]),
            pltpu.make_async_copy(previous.at[pl.ds(count_r - 4, 4)], held.at[0], sems.at[1]),
            pltpu.make_async_copy(potential.at[pl.ds(count_r - 4, 4)], held.at[1], sems.at[2]),
        ]
        later[...] = jnp.zeros_like(later)
        field[0:2] = jnp.zeros_like(field[0:2])
        field[8:10] = jnp.zeros_like(field[8:10])
        for k in range(2, 8):
            field[k, 0:base] = jnp.zeros((base, width), F32)
            field[k, base + rows :] = jnp.zeros((base, width), F32)
        for copy in copies:
            copy.start()
        for k in range(4):
            at = begin + 4 * k
            field[4 + k, base - 4 : base] = left[at : at + 4]
            field[4 + k, base + rows : base + rows + 4] = right[at : at + 4]
        columns = [
            (tables[ROT, :, count_r - 4 + k : count_r - 3 + k], tables[RET, :, count_r - 4 + k : count_r - 3 + k])
            for k in range(4)
        ]
        columns = [tuple(jnp.broadcast_to(c, (rows, LANES)) for c in pair) for pair in columns]
        for copy in copies:
            copy.wait()
        window = field[4:8, base - 8 : base + rows + 8].reshape(4 * wide, width)
        turned[...] = product(halves(window), high[...], low[...])
        for k in range(4):
            rotation, retained = columns[k]
            for at in range(0, width, LANES):
                lanes = slice(at, at + LANES)
                update = doubled_hamilton(
                    field, 4 + k, base, rows, lanes,
                    turned[k * wide + 8 : k * wide + 8 + rows, lanes], held[1, k, :, lanes], rotation,
                ) - retained * held[0, k, :, lanes]
                later[k, base : base + rows, lanes] = retained * update
                if k >= 2:
                    out[(k - 2) * rows : (k - 1) * rows, lanes] = (1.0 - retained) * update
        for k in range(2, 4):
            for slab, place, inside in ((left, base - 8, 6), (right, base + rows, 0)):
                at = begin + 16 + 2 * (k - 2)
                prev, pot, rot, ret = (slab[at + 4 * n : at + 4 * n + 2] for n in range(4))
                update = doubled_hamilton(
                    field, 4 + k, place + inside, 2, slice(None),
                    turned[k * wide + place - base + 8 + inside : k * wide + place - base + 10 + inside], pot, rot,
                ) - ret * prev
                later[k, place + inside : place + inside + 2] = ret * update
        window = later[2:4, base : base + rows].reshape(2 * rows, width)
        turned[0 : 2 * rows] = product(halves(window), high[...], low[...])
        for k in range(2, 4):
            rotation, retained = columns[k]
            for at in range(0, width, LANES):
                lanes = slice(at, at + LANES)
                update = doubled_hamilton(
                    later, k, base, rows, lanes,
                    turned[(k - 2) * rows : (k - 1) * rows, lanes], held[1, k, :, lanes], rotation,
                ) - retained * field[4 + k, base : base + rows, lanes]
                out[k * rows : (k + 1) * rows, lanes] = (1.0 - retained) * update


def bands(packet, previous, potential, tables, left, right, high, low):
    _, rows, width = packet.shape
    return pl.pallas_call(
        band_kernel,
        in_specs=[HBM, HBM, HBM, VMEM, VMEM, VMEM, VMEM, VMEM],
        out_specs=VMEM,
        out_shape=jax.ShapeDtypeStruct((2 * BAND * rows, width), F32),
        scratch_shapes=[
            pltpu.VMEM((10, rows + 32, width), F32),
            pltpu.VMEM((6, rows + 32, width), F32),
            pltpu.VMEM((4 * (rows + 16), width), F32),
            pltpu.VMEM((2, 4, rows, width), F32),
            pltpu.SemaphoreType.DMA((3,)),
        ],
        compiler_params=pltpu.CompilerParams(vmem_limit_bytes=16 * MIB),
        cost_estimate=pl.CostEstimate(flops=400_000_000, bytes_accessed=4 * MIB, transcendentals=0),
        name="both_bands",
    )(packet, previous, potential, tables, left, right, high, low)


def prepare_kernel(
    packet, previous, potential, rotation, damping, absorber, index, weight,
    upper, lower, first, last, tables,
    sides, others, factors, masks, indices, weights, sems,
):
    count_r, rows, width = packet.shape
    small = [
        pltpu.make_async_copy(rotation, factors.at[0], sems.at[0]),
        pltpu.make_async_copy(damping, factors.at[1], sems.at[1]),
        pltpu.make_async_copy(absorber, masks, sems.at[2]),
        pltpu.make_async_copy(index, indices, sems.at[3]),
        pltpu.make_async_copy(weight, weights, sems.at[4]),
    ]
    copies = [
        pltpu.make_async_copy(packet.at[:, pl.ds(0, 8)], sides.at[0], sems.at[5]),
        pltpu.make_async_copy(packet.at[:, pl.ds(rows - 8, 8)], sides.at[1], sems.at[6]),
        pltpu.make_async_copy(previous.at[pl.ds(count_r - BAND, BAND)], others.at[0], sems.at[7]),
        pltpu.make_async_copy(potential.at[pl.ds(count_r - BAND, BAND)], others.at[1], sems.at[8]),
    ]
    for copy in small + copies:
        copy.start()
    for copy in small:
        copy.wait()
    values = [factors[0], retained_of(factors[1], masks[...])]
    values += [indices[n].astype(F32) for n in range(STENCILS)]
    values += [weights[n] for n in range(STENCILS)]
    for n, value in enumerate(values):
        tables[n] = jnp.concatenate([value, jnp.zeros((rows, LANES - count_r), F32)], axis=1)
    columns = HALO * count_r
    lane = lax.broadcasted_iota(jnp.int32, (rows, LANES), 1)
    at_top = jnp.zeros((rows, LANES), F32)
    at_bottom = jnp.zeros((rows, LANES), F32)
    for n, table in enumerate([*range(INDEX, TABLES), RET]):
        value = tables[table]
        at = n * HALO
        here = (lane >= at) & (lane < at + HALO)
        at_top = jnp.where(here, pltpu.roll(value, at, 1), at_top)
        at_bottom = jnp.where(here, pltpu.roll(value, (at + LANES - (count_r - HALO)) % LANES, 1), at_bottom)
        if table != RET:
            first[columns + at : columns + at + HALO, 0:LANES] = value[0:HALO]
            last[columns + at : columns + at + HALO, 0:LANES] = value[rows - HALO : rows]
    upper[...] = at_top
    lower[...] = at_bottom
    begin = columns + EXTRA
    for copy in copies:
        copy.wait()
    for out, n, far, near in ((first, 0, 0, 0), (last, 1, 4, rows - 2)):
        for k in range(4):
            out[begin + 4 * k : begin + 4 * k + 4] = sides[n, count_r - 4 + k, far : far + 4]
        for k in range(BAND):
            at = begin + 16 + 2 * k
            column = count_r - BAND + k
            out[at : at + 2] = others[0, k, near : near + 2]
            out[at + 4 : at + 6] = others[1, k, near : near + 2]
            for m in (ROT, RET):
                value = tables[m, near : near + 2, column : column + 1]
                out[at + 8 + 4 * m : at + 10 + 4 * m] = jnp.broadcast_to(value, (2, width))
    for out, n, near in ((first, 0, 0), (last, 1, 8 - HALO)):
        for k in range(count_r):
            for r in range(HALO):
                out[r * count_r + k : r * count_r + k + 1] = sides[n, k, near + r : near + r + 1]


def prepare(packet, previous, potential, rotation, damping, absorber, index, weight):
    count_r, rows, width = packet.shape
    ends = jax.ShapeDtypeStruct((rows, LANES), F32)
    sides = jax.ShapeDtypeStruct((HALO * count_r + EXTRA + OFBAND, width), F32)
    return pl.pallas_call(
        prepare_kernel,
        in_specs=[HBM] * 8,
        out_specs=[VMEM] * 5,
        out_shape=[ends, ends, sides, sides, jax.ShapeDtypeStruct((TABLES, rows, LANES), F32)],
        scratch_shapes=[
            pltpu.VMEM((2, count_r, 8, width), F32),
            pltpu.VMEM((2, BAND, rows, width), F32),
            pltpu.VMEM((2, rows, count_r), F32),
            pltpu.VMEM((rows, count_r), jnp.int32),
            pltpu.VMEM((STENCILS, rows, count_r), jnp.int32),
            pltpu.VMEM((STENCILS, rows, count_r), F32),
            pltpu.SemaphoreType.DMA((9,)),
        ],
        compiler_params=pltpu.CompilerParams(vmem_limit_bytes=16 * MIB),
        cost_estimate=pl.CostEstimate(flops=1_000_000, bytes_accessed=6 * MIB, transcendentals=0),
        name="prepare",
    )(packet, previous, potential, rotation, damping, absorber, index, weight)


def put_sides(sides, left, right, count_r, left_more=None, right_more=None):
    def body(k, carry):
        for r in range(HALO):
            at = pl.ds(r * count_r + k, 1)
            before, behind = left[at], right[at]
            if left_more is not None:
                before, behind = before + left_more[at], behind + right_more[at]
            sides[k, r : r + 1] = behind
            sides[k, 8 - HALO + r : 8 - HALO + r + 1] = before
        return carry

    lax.fori_loop(0, count_r, body, 0, unroll=8)


def advance(step, chunk, field, sides, previous, potential, tables, high, low, put, more=None):
    rows = previous.shape[1]
    width = previous.shape[2]
    here = step * chunk
    shift = lax.rem(LANES - here, LANES)
    columns = [pltpu.roll(tables[n], shift, 1) for n in (ROT, RET)]
    window = field[pl.ds(HALO + here, chunk)].reshape(chunk * rows, width)
    split = halves(window)
    wide = 2 * LANES
    for tile in range(0, width, wide):
        turned = product(split, high[:, tile : tile + wide], low[:, tile : tile + wide])
        source = None if more is None else more(slice(tile, tile + wide))
        for k in range(chunk):
            rotation = jnp.broadcast_to(0.25 * columns[0][:, k : k + 1], (rows, LANES))
            retained = jnp.broadcast_to(columns[1][:, k : k + 1], (rows, LANES))
            for at in range(tile, tile + wide, LANES):
                lanes = slice(at, at + LANES)

                def row(shift):
                    return field[HALO + here + k + shift, :, lanes]

                middle = row(0)
                ring = jnp.concatenate([middle, sides[here + k, :, lanes]], axis=0)
                around = [pltpu.roll(ring, s, 0)[:rows] for s in (1, rows + 7, 2, rows + 6)]
                near = row(-1) + row(1) + (around[0] + around[1])
                far = row(-2) + row(2) + (around[2] + around[3])
                update = (
                    SIDE1 * near
                    + SIDE2 * far
                    + (0.25 * potential[here + k, :, lanes] + MIDDLE) * middle
                    + rotation * turned[k * rows : (k + 1) * rows, at - tile : at - tile + LANES]
                    - retained * previous[here + k, :, lanes]
                )
                value = retained * update
                if source is not None:
                    value += source[k * rows : (k + 1) * rows, at - tile : at - tile + LANES]
                put(here + k, lanes, value)


def first_kernel(
    packet, previous, potential, tables, upper, lower, left, right, high, low, after,
    done, top, bottom, first, last, field, sides,
):
    count_r, rows, width = packet.shape
    steps = count_r // CHUNK

    field[HALO : HALO + count_r] = packet[...]
    field[0:HALO] = jnp.zeros((HALO, rows, width), F32)
    field[HALO + count_r :] = jnp.zeros((HALO, rows, width), F32)
    put_sides(sides, left, right, count_r)

    def put(k, lanes, value):
        done[k, :, lanes] = value

    def body(n, carry):
        advance(n, CHUNK, field, sides, previous, potential, tables, high, low, put)
        for k in range(CHUNK):
            for r in range(HALO):
                at = pl.ds(r * count_r + n * CHUNK + k, 1)
                first[at] = done[n * CHUNK + k, r : r + 1]
                last[at] = done[n * CHUNK + k, rows - HALO + r : rows - HALO + r + 1]
        return carry

    lax.fori_loop(0, steps, body, 0)
    edges = HALO * rows
    for k in range(HALO):
        here = slice(k * rows, (k + 1) * rows)
        beside = slice(edges + k * rows, edges + (k + 1) * rows)
        top[here] = done[k]
        bottom[here] = done[count_r - HALO + k]
        top[beside] = field[HALO + k]
        bottom[beside] = field[count_r + k]
    top[2 * edges : 2 * edges + rows, 0:LANES] = upper[...]
    bottom[2 * edges : 2 * edges + rows, 0:LANES] = lower[...]


def first_iteration(packet, previous, potential, tables, upper, lower, left, right, high, low, after):
    count_r, rows, width = packet.shape
    ends = jax.ShapeDtypeStruct((2 * HALO * rows + rows, width), F32)
    sides = jax.ShapeDtypeStruct((HALO * count_r, width), F32)
    return pl.pallas_call(
        first_kernel,
        in_specs=[*[VMEM] * 10, ANY],
        out_specs=[VMEM] * 5,
        out_shape=[jax.ShapeDtypeStruct(packet.shape, F32), ends, ends, sides, sides],
        scratch_shapes=[
            pltpu.VMEM((count_r + 2 * HALO, rows, width), F32),
            pltpu.VMEM((count_r, 8, width), F32),
        ],
        compiler_params=pltpu.CompilerParams(vmem_limit_bytes=14 * MIB),
        cost_estimate=pl.CostEstimate(flops=7_000_000_000, bytes_accessed=20 * MIB, transcendentals=0),
        name="first_iteration",
    )(packet, previous, potential, tables, upper, lower, left, right, high, low, after)


def slot_of(value, rows, width):
    per = rows * BAND
    shift_owner = per.bit_length() - 1
    chips = width // per // CORES
    row = lax.axis_index("row")
    index = value.astype(jnp.int32)
    owner = index >> shift_owner
    inside = index & (per - 1)
    core = (owner & 1) ^ (row & 1)
    chip = ((row >> 1) - (owner >> 1)) & (chips - 1)
    slot = ((core * chips + chip) << shift_owner) + (inside & 1) * rows + (inside >> 1)
    return slot.astype(F32)


def fill_rows(at, cut, rows, high, low, begin=0):
    column = lax.broadcasted_iota(jnp.int32, (rows, LANES), 1).astype(F32)
    cut = [jnp.broadcast_to(value, (rows, LANES)) for value in cut]
    for tile in range(0, high.shape[1], LANES):
        here = column + float(begin + tile)
        total = jnp.where(here == cut[0], cut[STENCILS], 0.0)
        for n in range(1, STENCILS):
            total += jnp.where(here == cut[n], cut[STENCILS + n], 0.0)
        upper, lower = halves(total)
        high[pl.ds(at, rows), tile : tile + LANES] = upper
        low[pl.ds(at, rows), tile : tile + LANES] = lower


def stencil_kernel(tables, angular, after, high, low, other_high, other_low, angular_high, angular_low):
    _, rows, _ = tables.shape
    count_r = high.shape[0] // rows
    group = 8
    half = high.shape[1]
    angular_high[...], angular_low[...] = halves(angular[...])

    @pl.when(in_product())
    def _():
        values = [slot_of(tables[INDEX + n], rows, CORES * half) for n in range(STENCILS)]
        values += [tables[WEIGHT + n] for n in range(STENCILS)]

        def body(step, carry):
            shift = lax.rem(LANES - step * group, LANES)
            moved = [pltpu.roll(value, shift, 1) for value in values]
            for k in range(group):
                at = pl.multiple_of((step * group + k) * rows, rows)
                cut = [jnp.broadcast_to(value[:, k : k + 1], (rows, LANES)) for value in moved]
                fill_rows(at, cut, rows, high, low)
                fill_rows(at, cut, rows, other_high, other_low, half)
            return carry

        lax.fori_loop(0, count_r // group, body, 0)


def matrices_of(tables, angular, count_r, columns, after):
    rows = tables.shape[1]
    points = jax.ShapeDtypeStruct((count_r * rows, columns // CORES), BF16)
    return pl.pallas_call(
        stencil_kernel,
        in_specs=[VMEM, VMEM, ANY],
        out_specs=[VMEM] * 6,
        out_shape=[points] * 4 + [jax.ShapeDtypeStruct(angular.shape, BF16)] * 2,
        compiler_params=pltpu.CompilerParams(vmem_limit_bytes=16 * MIB),
        cost_estimate=pl.CostEstimate(flops=15_000_000, bytes_accessed=6 * MIB, transcendentals=0),
        name="stencil_matrix",
    )(tables, angular, after)


def edge_kernel(
    up, down, left, right, tables, top, bottom, first, last, after,
    high, low, whole_up, whole_down, new_first, new_last, added, square, *, rows, count_r,
):
    width = up.shape[1]
    edges = HALO * rows

    def retained(k):
        return jnp.broadcast_to(tables[RET, :, k : k + 1], (rows, width))

    def there(side, k):
        at = 2 * STENCILS * HALO + k
        return jnp.broadcast_to(side[2 * edges : 2 * edges + rows, at : at + 1], (rows, width))

    def packet_row(slab, k):
        return slab[edges + k * rows : edges + (k + 1) * rows]

    added[0] = retained(0) * (SIDE1 * packet_row(up, 1) + SIDE2 * packet_row(up, 0))
    added[1] = retained(1) * (SIDE2 * packet_row(up, 1))
    added[2] = retained(count_r - 2) * (SIDE2 * packet_row(down, 0))
    added[3] = retained(count_r - 1) * (SIDE1 * packet_row(down, 0) + SIDE2 * packet_row(down, 1))
    whole_up[0:rows] = up[0:rows] + there(up, 0) * (SIDE2 * packet_row(top, 0))
    whole_up[rows:edges] = up[rows:edges] + there(up, 1) * (SIDE1 * packet_row(top, 0) + SIDE2 * packet_row(top, 1))
    whole_down[0:rows] = down[0:rows] + there(down, 0) * (SIDE1 * packet_row(bottom, 1) + SIDE2 * packet_row(bottom, 0))
    whole_down[rows:edges] = down[rows:edges] + there(down, 1) * (SIDE2 * packet_row(bottom, 1))
    new_first[...] = first[...]
    new_last[...] = last[...]
    for k in range(HALO):
        for n, r_row in ((k, k), (HALO + k, count_r - HALO + k)):
            for r in range(HALO):
                at = r * count_r + r_row
                new_first[at : at + 1] = first[at : at + 1] + added[n, r : r + 1]
                new_last[at : at + 1] = last[at : at + 1] + added[n, rows - HALO + r : rows - HALO + r + 1]

    @pl.when(in_product())
    def _():
        at = 0
        for side in (up, down):
            value = side[2 * edges : 2 * edges + rows, 0:LANES]
            slots = slot_of(value, rows, high.shape[1])
            for e in range(HALO):
                cut = [
                    (slots if m < STENCILS else value)[:, HALO * m + e : HALO * m + e + 1]
                    for m in range(2 * STENCILS)
                ]
                fill_rows(at, cut, rows, high, low)
                at += rows
        square[...] = jnp.zeros_like(square)
        part = EXTRA // 2
        for n, side in enumerate((left, right)):
            begin = HALO * count_r
            square[n * EXTRA : n * EXTRA + part] = slot_of(side[begin : begin + part, 0:LANES], rows, high.shape[1])
            square[n * EXTRA + part : (n + 1) * EXTRA] = side[begin + part : begin + EXTRA, 0:LANES]
        turned = square[...].T
        for n in range(2):
            for e in range(HALO):
                for begin in range(0, count_r, rows):
                    cut = [
                        turned[begin : begin + rows, n * EXTRA + HALO * m + e : n * EXTRA + HALO * m + e + 1]
                        for m in range(2 * STENCILS)
                    ]
                    fill_rows(at, cut, rows, high, low)
                    at += rows


def finish_edges(halos, tables, edges, rows, count_r, columns, after):
    points = jax.ShapeDtypeStruct((2 * HALO * (rows + count_r), columns), BF16)
    width = edges[0].shape[1]
    return pl.pallas_call(
        functools.partial(edge_kernel, rows=rows, count_r=count_r),
        in_specs=[*[VMEM] * 9, ANY],
        out_specs=[VMEM] * 7,
        out_shape=[
            points, points,
            *[jax.ShapeDtypeStruct((HALO * length, width), F32) for length in (rows, rows, count_r, count_r)],
            jax.ShapeDtypeStruct((2 * HALO, rows, width), F32),
        ],
        scratch_shapes=[pltpu.VMEM((LANES, LANES), F32)],
        compiler_params=pltpu.CompilerParams(vmem_limit_bytes=16 * MIB),
        cost_estimate=pl.CostEstimate(flops=2_000_000, bytes_accessed=3 * MIB, transcendentals=0),
        name="finish_edges",
    )(*halos, tables, *edges, after)


def split_table(pieces, band, table, at):
    half = pieces.shape[1] // 2
    for k in range(pieces.shape[0]):
        upper, lower = halves(pieces[k, band * half : (band + 1) * half])
        table[at, k * half : (k + 1) * half] = upper
        table[at + 1, k * half : (k + 1) * half] = lower


def own_source_kernel(
    one, added, stencil_high, stencil_low, edge_high, edge_low, own, after, sum_one, edge_source, table, *, begin
):
    count_r, rows, width = one.shape
    count = sum_one.shape[0]
    columns = table.shape[1]
    size = LAST * rows

    @pl.when(in_product())
    def _():
        split_table(own, 0, table, 0)

        def body(n, carry):
            cut = pl.ds(pl.multiple_of(begin * rows + n * size, size), size)
            weights = (stencil_high[cut], stencil_low[cut])
            more = product(weights, table[0], table[1]).reshape(LAST, rows, width)
            sum_one[pl.ds(n * LAST, LAST)] = one[pl.ds(begin + n * LAST, LAST)] + more
            return carry

        lax.fori_loop(0, count // LAST, body, 0)
        if begin == 0:
            edge_source[...] = product((edge_high[:, 0:columns], edge_low[:, 0:columns]), table[0], table[1])

    @pl.when(jnp.logical_not(in_product()))
    def _():
        sum_one[...] = one[begin : begin + count]

    for k in range(HALO):
        if begin == 0:
            sum_one[k] += added[k]
        if begin + count == count_r:
            sum_one[count - HALO + k] += added[HALO + k]


def own_source(one, added, matrices, own, after, begin, count, flops):
    _, rows, width = one.shape
    edge_rows = matrices[2].shape[0] if begin == 0 else 8
    return pl.pallas_call(
        functools.partial(own_source_kernel, begin=begin),
        in_specs=[*[VMEM] * 7, ANY],
        out_specs=[VMEM] * 2,
        out_shape=[
            jax.ShapeDtypeStruct((count, rows, width), F32),
            jax.ShapeDtypeStruct((edge_rows, width), F32),
        ],
        scratch_shapes=[pltpu.VMEM((2, own.shape[0] * own.shape[1] // 2, width), BF16)],
        compiler_params=pltpu.CompilerParams(vmem_limit_bytes=16 * MIB),
        cost_estimate=pl.CostEstimate(flops=flops, bytes_accessed=flops // 500, transcendentals=0),
        name="own_source",
    )(one, added, *matrices, own, after)


def last_kernel(
    one, one_end, edge_source, packet, potential, tables, up, down, left, right, high, low,
    own_high, own_low, stencil_high, stencil_low, edge_high, edge_low, own, other,
    earlier, latest, field, done, sides, table, ends, sems,
):
    count_r, rows, width = packet.shape
    steps = count_r // LAST
    size = LAST * rows
    columns = table.shape[1]
    is_product = in_product()

    def part(n):
        return pl.ds(n * LAST, LAST)

    def cut(n):
        return pl.ds(pl.multiple_of(n * size, size), size)

    def earliers(n):
        return pltpu.make_async_copy(field.at[pl.ds(HALO + n * LAST, LAST)], earlier.at[part(n)], sems.at[0, n])

    def latests(n):
        return pltpu.make_async_copy(done.at[part(n)], latest.at[part(n)], sems.at[1, n])

    def put_ends(up_value, down_value):
        for k in range(HALO):
            field[k] = up_value[k * rows : (k + 1) * rows]
            field[HALO + count_r + k] = down_value[k * rows : (k + 1) * rows]

    def put(k, lanes, value):
        done[k, :, lanes] = value

    @pl.when(is_product)
    def _():
        split_table(other, 0, table, 0)
        split_table(own, 1, table, 2)
        split_table(other, 1, table, 4)
        ends[...] = edge_source[...] + product(
            (edge_high[:, columns : 2 * columns], edge_low[:, columns : 2 * columns]), table[0], table[1]
        )
        edges = HALO * rows
        long = HALO * count_r
        put_ends(up[...] + ends[:edges], down[...] + ends[edges : 2 * edges])
        put_sides(
            sides, left, right, count_r, ends.at[pl.ds(2 * edges, long)], ends.at[pl.ds(2 * edges + long, long)]
        )

        def weights(n):
            return stencil_high[cut(n)], stencil_low[cut(n)]

        def add(n, carry):
            more = product(weights(n), table[0], table[1]).reshape(LAST, rows, width)
            field[pl.ds(HALO + n * LAST, LAST)] = one[part(n)] + more
            earliers(n).start()
            return carry

        lax.fori_loop(0, steps - 1, add, 0)
        more = product(weights(steps - 1), table[0], table[1]).reshape(LAST, rows, width)
        field[HALO + count_r - LAST : HALO + count_r] = one_end[...] + more
        earliers(steps - 1).start()

        def body(n, carry):
            mine, theirs = (own_high[cut(n)], own_low[cut(n)]), weights(n)

            def more(lanes):
                return product(mine, table[2, :, lanes], table[3, :, lanes]) + product(
                    theirs, table[4, :, lanes], table[5, :, lanes]
                )

            advance(n, LAST, field, sides, packet, potential, tables, high, low, put, more)
            latests(n).start()
            return carry

        lax.fori_loop(0, steps, body, 0)

    @pl.when(jnp.logical_not(is_product))
    def _():
        put_ends(up, down)
        put_sides(sides, left, right, count_r)
        for n in range(steps):
            field[pl.ds(HALO + n * LAST, LAST)] = one[part(n)] if n + 1 < steps else one_end[...]
            earliers(n).start()

        def body(n, carry):
            advance(n, LAST, field, sides, packet, potential, tables, high, low, put)
            latests(n).start()
            return carry

        lax.fori_loop(0, steps, body, 0)

    for n in range(steps):
        earliers(n).wait()
        latests(n).wait()


def last_iteration(own_sums, packet, potential, tables, halos, high, low, matrices, pieces):
    count_r, rows, width = packet.shape
    steps = count_r // LAST
    return pl.pallas_call(
        last_kernel,
        in_specs=[VMEM] * 20,
        out_specs=[HBM, HBM],
        out_shape=[jax.ShapeDtypeStruct(packet.shape, F32)] * 2,
        scratch_shapes=[
            pltpu.VMEM((count_r + 2 * HALO, rows, width), F32),
            pltpu.VMEM(packet.shape, F32),
            pltpu.VMEM((count_r, 8, width), F32),
            pltpu.VMEM((6, pieces[0].shape[0] * pieces[0].shape[1] // 2, width), BF16),
            pltpu.VMEM((2 * HALO * (rows + count_r), width), F32),
            pltpu.SemaphoreType.DMA((2, steps)),
        ],
        compiler_params=pltpu.CompilerParams(vmem_limit_bytes=20 * MIB),
        cost_estimate=pl.CostEstimate(flops=14_000_000_000, bytes_accessed=36 * MIB, transcendentals=0),
        name="last_iteration",
    )(*own_sums, packet, potential, tables, *halos, high, low, *matrices, *pieces)


def neighbours(axis, upward, downward):
    count = lax.axis_size(axis)
    return (
        lax.ppermute(upward, axis, [(i, i + 1) for i in range(count - 1)]),
        lax.ppermute(downward, axis, [(i + 1, i) for i in range(count - 1)]),
    )


def local(packet, previous, potential, rotation, angular, damping, absorber, stencil_index, stencil_weight):
    packet, previous, potential = packet[0], previous[0], potential[0]
    rotation, angular, damping, absorber = rotation[0], angular[0], damping[0], absorber[0]
    count_r, rows, width = packet.shape
    count_rr, count_row = (lax.axis_size(name) for name in ("rr", "row"))
    chips = count_row // CORES
    rotation, damping, absorber = (jnp.swapaxes(value, 0, 1) for value in (rotation, damping, absorber))
    stencil_index, stencil_weight = (jnp.swapaxes(value, 1, 2) for value in (stencil_index, stencil_weight))
    near_packet, near_previous, near_potential = packet, previous, potential
    packet, previous, potential, rotation, damping, absorber, stencil_index, stencil_weight = (
        in_hbm(value)
        for value in (
            packet, previous, potential, rotation, damping, absorber, stencil_index, stencil_weight
        )
    )

    upper, lower, first, last, tables = prepare(
        packet, previous, potential, rotation, damping, absorber, stencil_index, stencil_weight
    )
    columns = count_row * rows * BAND
    left, right = neighbours("row", last, first)
    *matrix, high, low = matrices_of(tables, angular, count_r, columns, first)
    left, right, matrix = lax.optimization_barrier((left, right, matrix))
    table = bands(packet, previous, potential, tables, left, right, high, low)

    half = count_rr // PLANES
    start = count_rr - 1
    plane = ("sect", "rr")
    low_side, high_side = start - half + 1, start - 1
    relays = [count_rr + half - 1, count_rr + start, high_side, low_side]
    crossed = [lax.ppermute(table, plane, [(start, relay)]) for relay in relays]
    one, *edges = first_iteration(
        near_packet, near_previous, near_potential, tables, upper, lower, left, right, high, low, table
    )
    *crossed, one, edges = lax.optimization_barrier((*crossed, one, edges))
    piece = sum(crossed)
    near = [(low_side, count_rr), (high_side, count_rr + half - 2)]
    near += [(count_rr + half - 1, count_rr + half - 3), (count_rr + start, count_rr + start - 2)]
    opposite = [(low_side, count_rr + low_side), (high_side, count_rr + high_side)]
    arrived = [lax.ppermute(piece, plane, opposite), lax.ppermute(piece, plane, near)]
    top, bottom, first, last = edges
    top, bottom, piece = lax.optimization_barrier((top, bottom, piece))
    up, down = neighbours("rr", bottom, top)
    spread = piece + sum(arrived)
    line = ("sect", "row")

    def around(shift):
        pairs = []
        for chip in range(chips):
            for core in range(CORES):
                pairs.append(
                    (count_row + chip * CORES + core, count_row + ((chip + shift) % chips) * CORES + core)
                )
        return lax.ppermute(spread, line, pairs)

    rest = [around(1), around(3), around(2)]
    edge_matrix_and_ends = finish_edges(
        (up, down, left, right), tables, (top, bottom, first, last), rows, count_r, columns, spread
    )
    *edge_matrix, up, down, first, last, added = edge_matrix_and_ends
    rest[2], edge_matrix, first, last = lax.optimization_barrier((rest[2], edge_matrix, first, last))
    left, right = neighbours("row", last, first)
    own = jnp.stack([spread, rest[0], rest[2], rest[1]], axis=0)
    other = lax.ppermute(
        own, line, [(count_row + i, count_row + i + 1 - 2 * (i % CORES)) for i in range(count_row)]
    )
    own_matrices = (*matrix[:2], *edge_matrix)
    one_begin, edge_source = own_source(one, added, own_matrices, own, own, 0, count_r - LAST, 1_000_000)
    left, right, added, one_begin = lax.optimization_barrier((left, right, added, one_begin))
    one_end, _ = own_source(one, added, own_matrices, own, one_begin, count_r - LAST, LAST, 100_000_000_000)
    own_sums = (one_begin, one_end, edge_source)
    other, own_sums = lax.optimization_barrier((other, own_sums))
    earlier, latest = last_iteration(
        own_sums, near_packet, near_potential, tables, (up, down, left, right), high, low, (*matrix, *edge_matrix), (own, other)
    )
    return latest[None], earlier[None]


def solution(mesh):
    in_specs = (
        P("sect", "rr", "row", None),
        P("sect", "rr", "row", None),
        P("sect", "rr", "row", None),
        P("sect", "rr", "row"),
        P("sect", None, None),
        P("sect", "rr", "row"),
        P("sect", "rr", "row"),
        P(None, "rr", "row"),
        P(None, "rr", "row"),
    )
    out_specs = (P("sect", "rr", "row", None), P("sect", "rr", "row", None))
    return jax.shard_map(local, mesh=mesh, in_specs=in_specs, out_specs=out_specs, check_vma=False)
```
